32 devices in a mesh: grp: 4 (over y, x), orb: 8 (over z, core).
Axes of the slice: x: 2, y: 2, z: 4, core: 2. Of those that a mesh axis runs over, the one named last changes fastest.
Arguments:
- wavevectors: float32 [3, 1024], replicated, may hold values from -3 to 3
- coefficients: bfloat16 [2048, 1024], P(None, 'orb'), may hold values from -0.0017089844 to 0.0017089844
- inverse: float32 [32, 1024, 1024], P(('grp', 'orb')), may hold values from -0.5 to 0.5
- positions: float32 [32, 3, 1024], P(('grp', 'orb')), may hold values from 0 to 10
- displacements: float32 [2, 32, 3, 16], P(None, ('grp', 'orb')), may hold values from -0.3125 to 0.3125
- moved: int32 [2, 32, 16], P(None, ('grp', 'orb')), may hold values from 0 to 1023, as said below
- donor: int32 [8], P('orb'), may hold values from 0 to 3
- take: int32 [32], P(('grp', 'orb')), may hold values 0 or 1
- log_weight: float32 [32], P(('grp', 'orb')), may hold values from -1 to 1
Outputs:
- new_inverse: float32 [32, 1024, 1024], P(('grp', 'orb'))
- drift: float32 [2, 32, 3, 16], P(None, ('grp', 'orb'))
- laplacian: float32 [2, 32, 16], P(None, ('grp', 'orb'))
- new_weight: float32 [32], P(('grp', 'orb'))
The draws below stay inside these ranges and needn't reach their ends.
Inputs may be any that keep to these rules, and one draw needn't show every extreme that they name: `moved`: within a walker slot the 32 entries are distinct electrons.
All inputs are finite; a program needn't handle non-finite values. No bound on the sum of `take` on one device may be relied on, other than what follows from the above.
Results may differ from the reference program's by a relative error of at most 0.004.
Values may be sent and summed in bfloat16 or wider, within the bound.
No kernel may reach another device: no remote copies, remote signals or barrier semaphores. Data moves between devices by JAX's collectives and lax.ppermute only.
A program may use at most 64 MiB of HBM per device.

```python
import jax
import jax.numpy as jnp
from jax import lax

NE = 1024
NPW = 2048
K = 16
UPD = 2
NG = 1024
W = 32
N_GRP = 4
N_ORB = 8


def draw_moved(key, part):
    keys = jax.random.split(jax.random.fold_in(key, 17), W)

    def pick(walker_key):
        return jax.random.permutation(walker_key, NE)[:UPD * K]
    rows = jax.vmap(pick)(keys)
    return rows.reshape(W, UPD, K).transpose(1, 0, 2).astype(jnp.int32)


def place_ends(array, rng, low, high):
    longest = array.shape.index(max(array.shape))
    spots = []
    for shift in (0, 1):
        where = [jax.random.randint(jax.random.fold_in(rng, axis), (), 0, length) for axis, length in enumerate(array.shape)]
        where[longest] = (where[longest] + shift) % array.shape[longest]
        spots.append(tuple(where))
    return array.at[spots[0]].set(low).at[spots[1]].set(high)


def levels(key, extent, pieces, smallest, largest):
    def one(dim, blocks):
        draws = jax.random.uniform(jax.random.fold_in(jax.random.fold_in(key, 6), dim), (blocks,), jnp.float32, smallest / len(pieces), largest / len(pieces))
        return jnp.repeat(jnp.exp(draws), extent[dim] // blocks).reshape((-1,) + (1,) * (len(extent) - dim - 1))

    loudness = one(*pieces[0])
    for cut in pieces[1:]:
        loudness = loudness * one(*cut)
    return loudness


def scatter_about(stream_key, dims, scale, bound, cuts=(), held_as=jnp.bfloat16):
    level = levels(stream_key, dims, cuts, -0.22, 0.18) if cuts else 1.0
    array = jax.random.normal(stream_key, dims, jnp.float32) * scale * level
    return jnp.minimum(jnp.maximum(array, -bound), bound).astype(held_as)


def setup_inputs(seed: int = 0) -> dict:
    seeds = jax.random.split(jax.random.key(seed), 10)
    return {
        "wavevectors": jnp.clip(jax.random.uniform(seeds[0], (3, NG), jnp.float32, -3.0, 3.0), -3.0, 3.0),
        "coefficients": scatter_about(seeds[1], (NPW, NE), 0.0003, 0.0017089844, ((1, 8),)),
        "inverse": jnp.clip(jax.random.uniform(seeds[2], (W, NE, NE), jnp.float32, -0.5, 0.5) * levels(seeds[2], (W, NE, NE), ((0, 32),), -0.4, 0.0), -0.5, 0.5),
        "positions": jnp.clip(10.0 * jax.random.uniform(seeds[3], (W, 3, NE), jnp.float32) ** levels(seeds[3], (W, 3, NE), ((0, 32),), -0.2, 0.2), 0.0, 10.0),
        "displacements": scatter_about(seeds[4], (UPD, W, 3, K), 0.05, 0.3125, ((1, 32),), jnp.float32),
        "moved": draw_moved(jax.random.fold_in(seeds[9], 71), 0),
        "donor": place_ends(jax.random.randint(seeds[6], (N_ORB,), 0, N_GRP), jax.random.fold_in(seeds[6], 1), 0, N_GRP - 1).astype(jnp.int32),
        "take": place_ends((jax.random.randint(seeds[7], (W,), 0, 2) < 1).astype(jnp.int32), jax.random.fold_in(seeds[7], 1), 0, 1),
        "log_weight": jnp.clip(jax.random.uniform(seeds[8], (W,), jnp.float32, -1.0, 1.0) * levels(seeds[8], (W,), ((0, 32),), -0.4, 0.0), -1.0, 1.0),
    }


precise = lax.Precision.HIGHEST

def build_tables(coefficients, wavevectors):
    coeff_f = coefficients.astype(jnp.float32)
    wave_count = wavevectors.shape[1]
    cos_part = coeff_f[:wave_count]
    sin_part = coeff_f[wave_count:]
    parts = [coeff_f]
    for component in range(3):
        scale = wavevectors[component][:, None]
        parts.append(jnp.concatenate([scale * sin_part, -scale * cos_part], 0))
    squared = wavevectors[0] * wavevectors[0] + wavevectors[1] * wavevectors[1] + wavevectors[2] * wavevectors[2]
    doubled = jnp.concatenate([squared, squared], 0)[:, None]
    parts.append(-doubled * coeff_f)
    return jnp.stack(parts, 1).astype(jnp.bfloat16)

def evaluate(points, wavevectors, coefficients, derived):
    count = points.shape[1] // 2
    phases = points[0][:, None] * wavevectors[0][None, :] + points[1][:, None] * wavevectors[1][None, :]
    phases = phases + points[2][:, None] * wavevectors[2][None, :]
    waves = jnp.concatenate([jnp.cos(phases), jnp.sin(phases)], 1).astype(jnp.bfloat16)
    before = jnp.dot(waves[:count].astype(jnp.float32), coefficients.astype(jnp.float32), preferred_element_type=jnp.float32)
    flat = derived.reshape(derived.shape[0], -1)
    after = jnp.dot(waves[count:].astype(jnp.float32), flat.astype(jnp.float32), preferred_element_type=jnp.float32).reshape(count, 5, -1)
    change = after[:, 0] - before
    return jnp.concatenate([change[:, None], after[:, 1:]], 1)

def woodbury(matrix, values, chosen):
    change = values[:, 0]
    columns = matrix[:, chosen]
    ratio_matrix = jnp.eye(change.shape[0], dtype=matrix.dtype) + jnp.dot(change, columns, precision=precise)
    product = jnp.dot(change, matrix, precision=precise)
    solved = jnp.linalg.solve(ratio_matrix, product)
    updated = matrix - jnp.dot(columns, solved, precision=precise)
    log_ratio = jnp.linalg.slogdet(ratio_matrix)[1]
    fresh_columns = updated[:, chosen]
    drift = jnp.einsum('kaj,jk->ak', values[:, 1:4], fresh_columns, precision=precise)
    laplacian = jnp.einsum('kj,jk->k', values[:, 4], fresh_columns, precision=precise)
    return (updated, log_ratio, drift, laplacian)

def reference(wavevectors, coefficients, inverse, positions, displacements, moved, donor, take, log_weight):
    derived = build_tables(coefficients, wavevectors)

    def advance(matrix, places, shifted, chosen):
        before_points = places[:, chosen]
        moved_to = before_points + shifted
        points = jnp.concatenate([before_points, moved_to], 1)
        values = evaluate(points, wavevectors, coefficients, derived)
        updated, log_ratio, drift, laplacian = woodbury(matrix, values, chosen)
        places = places.at[:, chosen].set(moved_to)
        return (updated, places, log_ratio, drift, laplacian)

    def first_pass(items):
        return advance(items[0], items[1], items[2], items[3])
    matrix_one, places_one, ratio_one, drift_one, lap_one = lax.map(first_pass, (inverse, positions, displacements[0], moved[0]))
    walker = jnp.arange(W, dtype=jnp.int32)
    group = walker // N_ORB
    column = walker % N_ORB
    source = donor[column]
    parent = jnp.where(jnp.logical_and(take == 1, group != source), source * N_ORB + column, walker).astype(jnp.int32)
    weight_one = log_weight + ratio_one

    def second_pass(items):
        return advance(matrix_one[items[0]], places_one[items[0]], items[1], items[2])
    matrix_two, places_two, ratio_two, drift_two, lap_two = lax.map(second_pass, (parent, displacements[1], moved[1]))
    final_weight = weight_one[parent] + ratio_two
    return (matrix_two, jnp.stack([drift_one, drift_two]), jnp.stack([lap_one, lap_two]), final_weight)
```

```python
import functools
import math

import jax
import jax.numpy as jnp
from jax import lax
from jax.experimental import pallas as pl
from jax.experimental.pallas import tpu as pltpu
from jax.sharding import PartitionSpec as P

F32 = jnp.float32
BF16 = jnp.bfloat16
LANES = 128
VMEM_BYTES = 40 * 1024 * 1024
precise = lax.Precision.HIGHEST

SIN_HALF = (4.4428679, -7.30744342, 3.59478808, -0.78437403)
COS_HALF = (1.4142135, -6.97885099, 5.73946117, -1.88356299, 0.31069819)


def dot(a, b, dims=((1,), (0,)), exact=False):
    return lax.dot_general(
        a, b, (dims, ((), ())), precision=precise if exact else None, preferred_element_type=F32
    )


def iota(shape, dim):
    return lax.broadcasted_iota(jnp.int32, shape, dim)


def call(kernel, out_shape, in_specs, out_specs, scratch=(), flops=0, moved=0):
    return pl.pallas_call(
        kernel,
        out_shape=out_shape,
        in_specs=in_specs,
        out_specs=out_specs,
        scratch_shapes=list(scratch),
        compiler_params=pltpu.CompilerParams(vmem_limit_bytes=VMEM_BYTES),
        cost_estimate=pl.CostEstimate(flops=flops, bytes_accessed=moved, transcendentals=0),
    )


VM = pl.BlockSpec(memory_space=pltpu.VMEM)
SM = pl.BlockSpec(memory_space=pltpu.SMEM)
ANY = pl.BlockSpec(memory_space=pl.ANY)


def shape(dims, dtype):
    return jax.ShapeDtypeStruct(dims, dtype)


def is_power(n):
    return n & (n - 1) == 0


def pairs(n, step):
    if is_power(n):
        return [(i, i ^ step) for i in range(n)]
    return [(i, (i + step) % n) for i in range(n)]


def distance(n, here, there):
    return here ^ there if is_power(n) else lax.rem(here - there + n, n)


def backward(n, step):
    return step if is_power(n) else (n - step) % n


def start_kernel(count, pos_ref, moved_ref, disp_ref, weight_ref, out_ref):
    electrons = pos_ref.shape[2]
    pos = jnp.concatenate([pos_ref[0], jnp.zeros((5, electrons), F32)], 0)
    pick = (iota((electrons, LANES), 0) == moved_ref[0:1, :]).astype(F32)
    block = iota((8, LANES), 1) // count
    old = dot(pos, pick, exact=True)
    disp = disp_ref[0]
    points = old + jnp.where(block % 2 == 1, disp, 0.0)
    first = jnp.where(block == 0, disp, 0.0)
    out_ref[...] = pos + dot(first, pick, ((1,), (1,)), exact=True)
    out_ref[3:6, 0:LANES] = points[0:3]
    out_ref[6:7, 0:LANES] = moved_ref[1:2, :].astype(F32)
    out_ref[7:8, 0:LANES] = jnp.full((1, LANES), weight_ref[0], F32)


def points_kernel(count, others, role_ref, *refs):
    own_ref = refs[0]
    received = refs[1 : 1 + others]
    moved_ref, disp_ref, points_ref, weight_ref = refs[1 + others :]
    role = role_ref[0]
    parent = own_ref[...]
    for step in range(others):
        parent = jnp.where(role == step + 1, received[step][...], parent)
    electrons = parent.shape[1]
    pick = (iota((electrons, LANES), 0) == moved_ref[1:2, :]).astype(F32)
    block = iota((8, LANES), 1) // count
    old = dot(parent, pick, exact=True)
    later = old + jnp.where(block % 2 == 1, disp_ref[1], 0.0)
    zeros = jnp.zeros((5, LANES), F32)
    mine = jnp.concatenate([own_ref[3:6, 0:LANES], zeros], 0)
    theirs = jnp.concatenate([parent[3:6, 0:LANES], zeros], 0)
    points = jnp.where(block < 2, mine, jnp.where(block < 4, theirs, later))
    points_ref[...] = jnp.broadcast_to(points[None], points_ref.shape)
    weight_ref[...] = parent[7:8, 0:LANES]


def columns_kernel(count, others, chunks, steps, *refs):
    chunk_refs = refs[:chunks]
    moved_ref = refs[chunks]
    received = refs[chunks + 1 : chunks + 1 + others]
    outs = refs[chunks + 1 + others :]
    depth = chunk_refs[0].shape[0]
    electrons = chunk_refs[0].shape[1]
    block = iota((1, LANES), 1) // count
    wanted = jnp.where(block == 0, moved_ref[0:1, :], moved_ref[1:2, :])
    for step in range(others):
        theirs = received[step][6:7, 0:LANES].astype(jnp.int32)
        wanted = jnp.where(block == 2 + step, theirs, wanted)
    pick = (iota((electrons, LANES), 0) == wanted).astype(F32).astype(BF16)
    for chunk in range(chunks):
        rows = slice(chunk * depth, (chunk + 1) * depth)
        found = dot(chunk_refs[chunk][...], pick)
        turned = jnp.transpose(found).astype(BF16)
        for out, step in zip(outs, steps):
            out[0:count, rows] = turned[0:count]
            out[count : 2 * count, rows] = turned[(1 + step) * count : (2 + step) * count]


def table_kernel(coeff_ref, wave_ref, out_ref):
    waves = wave_ref.shape[1]
    width = coeff_ref.shape[1]
    wave = jnp.transpose(jnp.concatenate([wave_ref[...], jnp.zeros((5, waves), F32)], 0))
    cos_part = coeff_ref[0:waves].astype(F32)
    sin_part = coeff_ref[waves:].astype(F32)
    squared = None
    for a in range(3):
        scale = wave[:, a : a + 1]
        where = slice(a * width, (a + 1) * width)
        out_ref[0:waves, where] = (scale * sin_part).astype(BF16)
        out_ref[waves:, where] = (-scale * cos_part).astype(BF16)
        squared = scale * scale if a == 0 else squared + scale * scale
    where = slice(3 * width, 4 * width)
    out_ref[0:waves, where] = (-squared * cos_part).astype(BF16)
    out_ref[waves:, where] = (-squared * sin_part).astype(BF16)


def horner(coefs, u):
    value = coefs[-1] * u + coefs[-2]
    for c in reversed(coefs[:-2]):
        value = value * u + c
    return value


def evaluate_kernel(count, points_ref, wave_ref, coeff_ref, table_ref, out_ref, diff, new):
    walkers = points_ref.shape[0]
    waves = wave_ref.shape[1]
    width = coeff_ref.shape[1]
    step = math.gcd(waves, LANES)

    def one(w, carry):
        column = jnp.transpose(points_ref[w])
        xs = [column[0 : 6 * count, a : a + 1] for a in range(3)]
        row_d = pl.multiple_of(w * (3 * count), count)
        row_n = pl.multiple_of(w * (2 * count), count)
        for at in range(0, waves, step):
            ks = [wave_ref[a : a + 1, at : at + step] * (0.5 / math.pi) for a in range(3)]
            turn = xs[0] * ks[0] + xs[1] * ks[1] + xs[2] * ks[2]
            r = turn - jnp.floor(turn + 0.5)
            u = r * r
            s = r * horner(SIN_HALF, u)
            c = horner(COS_HALF, u)
            for value, base in ((1.0 - s * s, 0), (s * c, waves)):
                where = slice(base + at, base + at + step)
                kept = value.astype(BF16)
                wide = kept.astype(F32)
                part = [wide[i * count : (i + 1) * count] for i in range(6)]
                diff[pl.ds(row_d, count), where] = (part[3] - part[2]).astype(BF16)
                diff[pl.ds(row_d + count, count), where] = (part[5] - part[4]).astype(BF16)
                diff[pl.ds(row_d + 2 * count, count), where] = (part[1] - part[0]).astype(BF16)
                new[pl.ds(row_n, count), where] = kept[5 * count : 6 * count]
                new[pl.ds(row_n + count, count), where] = kept[count : 2 * count]
        return carry

    lax.fori_loop(0, walkers, one, 0)
    change = dot(diff[...], coeff_ref[...]).astype(BF16)
    rest = dot(new[...], table_ref[...]).astype(BF16)
    for w in range(walkers):
        at = w * 3 * count
        out_ref[w, 0 : 2 * count] = change[at : at + 2 * count]
        out_ref[w, 6 * count : 7 * count] = change[at + 2 * count : at + 3 * count]
        for half, base in ((0, 2 * count), (1, 7 * count)):
            row = (2 * w + half) * count
            for a in range(4):
                out_ref[w, base + a * count : base + (a + 1) * count] = rest[
                    row : row + count, a * width : (a + 1) * width
                ]


def eliminate(matrix, size, first):
    row = iota((size, 1), 0).astype(F32)
    free = jnp.ones((size, 1), F32)
    logdet = jnp.zeros((1, 1), F32)
    for k in range(size):
        column = matrix[:, first + k : first + k + 1]
        score = jnp.where(free > 0, jnp.abs(column), -1.0)
        best = jnp.max(score, axis=0, keepdims=True)
        index = jnp.min(jnp.where(score == best, row, float(size)), axis=0, keepdims=True)
        chosen = row == index
        pivot = jnp.sum(jnp.where(chosen, column, 0.0), axis=0, keepdims=True)
        line = jnp.sum(jnp.where(chosen, matrix, 0.0), axis=0, keepdims=True) / pivot
        matrix = jnp.where(chosen, line, matrix - column * line)
        free = jnp.where(chosen, 0.0, free)
        logdet = logdet + jnp.log(jnp.abs(pivot))
    return matrix, logdet


def solve_kernel(count, others, role_ref, vals_ref, own_ref, *refs):
    received = refs[:others]
    weight_ref, change_ref, cols_ref, inv_ref, first_ref, second_ref, out_weight_ref, vals = refs[
        others:
    ]
    pieces, _, width = vals_ref.shape
    for o in range(pieces):
        vals[:, o * width : (o + 1) * width] = vals_ref[o]
    role = role_ref[0]
    cols = own_ref[...].astype(F32)
    for step in range(others):
        cols = jnp.where(role == step + 1, received[step][...].astype(F32), cols)
    cols = cols.astype(BF16)
    cols_ref[...] = cols
    change_ref[...] = vals[0 : 2 * count]
    own = own_ref[0:count]
    for sums_ref, size, matrix_in, part in (
        (first_ref, count, own, vals[6 * count : 11 * count]),
        (second_ref, 2 * count, cols, vals[0 : 6 * count]),
    ):
        wide = part.shape[0]
        products = dot(matrix_in, part, ((1,), (1,)))
        lane = iota((size, wide), 1)
        row = iota((size, wide), 0)
        matrix = jnp.where(lane < size, products, 0.0)
        matrix = matrix + jnp.where(lane == row, 1.0, 0.0) + jnp.where(lane == row + size, 1.0, 0.0)
        matrix, logdet = eliminate(matrix, size, 0)
        joined = dot(matrix, matrix, ((0,), (0,)), exact=True)[size : 2 * size, :]
        line = iota((wide, wide), 0)
        place = iota((wide, wide), 1)
        tile = jnp.where(line == size - count + place % count, 1.0, 0.0)
        spread = dot(joined, tile, exact=True)
        sums_ref[...] = jnp.sum(products * spread, axis=0, keepdims=True)[:, size:]
        if size > count:
            inv_ref[...] = joined[:, 0:size]
            out_weight_ref[...] = weight_ref[...] + logdet


def finish_kernel(sources, chunks, role_ref, change_ref, cols_ref, inv_ref, *refs):
    inputs = refs[:-5]
    out_ref, parent, staged, in_sem, out_sem = refs[-5:]
    depth = inputs[0].shape[0]
    role = role_ref[0]
    for chunk in range(chunks):
        for which, table in enumerate(sources):

            @pl.when(role == which)
            def _():
                pltpu.make_async_copy(
                    inputs[table[chunk]], parent.at[chunk], in_sem.at[chunk]
                ).start()

    total = jnp.zeros((change_ref.shape[0], inputs[0].shape[1]), F32)
    for chunk in range(chunks):
        pltpu.make_async_copy(inputs[chunk], parent.at[chunk], in_sem.at[chunk]).wait()
        total = total + dot(change_ref[:, chunk * depth : (chunk + 1) * depth], parent[chunk])
    solved = dot(inv_ref[...], total, exact=True).astype(BF16)
    copies = []
    for chunk in range(chunks):
        rows = slice(chunk * depth, (chunk + 1) * depth)
        columns = jnp.transpose(cols_ref[:, rows].astype(F32)).astype(BF16)
        staged[chunk] = parent[chunk].astype(F32) - dot(columns, solved)
        copy = pltpu.make_async_copy(staged.at[chunk], out_ref.at[rows], out_sem.at[chunk])
        copy.start()
        copies.append(copy)
    for copy in copies:
        copy.wait()


def branch(own, donor_here, n):
    chunks = len(own)
    if n == 4 and chunks == 4:
        send_x = lambda block: lax.ppermute(block, "grp", pairs(n, 1))
        send_y = lambda block: lax.ppermute(block, "grp", pairs(n, 2))
        x1, y1 = send_x(own[0]), send_y(own[3])
        x2 = send_x(jnp.where(donor_here, own[1], y1))
        y2 = send_y(jnp.where(donor_here, own[2], x1))
        x3 = send_x(jnp.where(donor_here, own[2], y2))
        y3 = send_y(jnp.where(donor_here, own[1], x2))
        arrays = list(own) + [x1, x2, x3, y1, y2, y3]
        a1, a2, a3, b1, b2, b3 = range(chunks, chunks + 6)
        return arrays, [range(chunks), (a1, a2, a3, b3), (a3, b3, b2, b1), (b2, b3, a3, a2)]
    arrays = list(own)
    table = [range(chunks)]
    for step in range(1, n):
        table.append(range(len(arrays), len(arrays) + chunks))
        arrays += [lax.ppermute(block, "grp", pairs(n, step)) for block in own]
    return arrays, table


def per_device(
    n_grp,
    n_orb,
    wavevectors,
    coefficients,
    inverse,
    positions,
    displacements,
    moved,
    donor,
    take,
    log_weight,
):
    electrons = inverse.shape[1]
    count = moved.shape[2]
    plane = coefficients.shape[0]
    local = coefficients.shape[1]
    others = n_grp - 1
    chunks = 4
    group = lax.axis_index("grp")
    source = donor[0]
    apart = distance(n_grp, group, source)
    role = jnp.where(take[0] == 1, apart, 0).astype(jnp.int32).reshape(1)

    tiled = jnp.tile(moved[:, 0], (1, LANES // count))
    disp = jnp.pad(jnp.tile(displacements[:, 0], (1, 1, LANES // count)), ((0, 0), (0, 5), (0, 0)))
    record = call(
        functools.partial(start_kernel, count),
        shape((8, electrons), F32),
        [VM, VM, VM, SM],
        VM,
    )(positions, tiled, disp, log_weight)
    records = [lax.ppermute(record, "grp", pairs(n_grp, s)) for s in range(1, n_grp)]

    depth = electrons // chunks
    own = [inverse[0, c * depth : (c + 1) * depth].astype(BF16) for c in range(chunks)]
    arrays, table = branch(own, apart == 0, n_grp)

    points, weight = call(
        functools.partial(points_kernel, count, others),
        (shape((n_orb, 8, LANES), F32), shape((1, LANES), F32)),
        [SM] + [VM] * (others + 3),
        (VM, VM),
    )(role, record, *records, tiled, disp)
    points = lax.all_to_all(points, "orb", split_axis=0, concat_axis=0, tiled=True)

    steps = [0] + [backward(n_grp, s) for s in range(1, n_grp)]
    columns = call(
        functools.partial(columns_kernel, count, others, chunks, steps),
        tuple(shape((2 * count, electrons), BF16) for _ in steps),
        [VM] * (chunks + 1 + others),
        tuple(VM for _ in steps),
        flops=2 * electrons * electrons * LANES,
        moved=2 * electrons * electrons,
    )(*own, tiled, *records)
    sent = [lax.ppermute(columns[s], "grp", pairs(n_grp, s)) for s in range(1, n_grp)]

    width = -(-local // LANES) * LANES
    coeff = jnp.pad(coefficients, ((0, 0), (0, width - local))) if width > local else coefficients
    derived = call(
        table_kernel,
        shape((plane, 4 * width), BF16),
        [VM, VM],
        VM,
        flops=8 * plane * width,
        moved=10 * plane * width,
    )(coeff, wavevectors)
    block = math.gcd(n_orb, 8)
    values = pl.pallas_call(
        functools.partial(evaluate_kernel, count),
        grid=(n_orb // block,),
        out_shape=shape((n_orb, 11 * count, width), BF16),
        in_specs=[
            pl.BlockSpec((block, 8, LANES), lambda i: (i, 0, 0)),
            pl.BlockSpec(wavevectors.shape, lambda i: (0, 0)),
            pl.BlockSpec(coeff.shape, lambda i: (0, 0)),
            pl.BlockSpec(derived.shape, lambda i: (0, 0)),
        ],
        out_specs=pl.BlockSpec((block, 11 * count, width), lambda i: (i, 0, 0)),
        scratch_shapes=[
            pltpu.VMEM((block * 3 * count, plane), BF16),
            pltpu.VMEM((block * 2 * count, plane), BF16),
        ],
        compiler_params=pltpu.CompilerParams(vmem_limit_bytes=VMEM_BYTES),
        cost_estimate=pl.CostEstimate(
            flops=2 * n_orb * count * plane * width * 11, bytes_accessed=12 * plane * width, transcendentals=0
        ),
    )(points, wavevectors, coeff, derived)
    values = values[:, :, :local]
    values = lax.all_to_all(values, "orb", split_axis=0, concat_axis=0, tiled=True)
    if width > local:
        values = values.transpose(1, 0, 2).reshape(1, 11 * count, electrons)

    change, cols, small, first, second, new_weight = call(
        functools.partial(solve_kernel, count, others),
        (
            shape((2 * count, electrons), BF16),
            shape((2 * count, electrons), BF16),
            shape((2 * count, 2 * count), F32),
            shape((1, 4 * count), F32),
            shape((1, 4 * count), F32),
            shape((1, LANES), F32),
        ),
        [SM] + [VM] * (others + 3),
        (VM,) * 6,
        scratch=[pltpu.VMEM((11 * count, electrons), BF16)],
        flops=2 * electrons * count * count * 16,
        moved=4 * 11 * count * electrons,
    )(role, values, columns[0], *sent, weight)

    updated = call(
        functools.partial(finish_kernel, table, chunks),
        shape((electrons, electrons), F32),
        [SM, VM, VM, VM] + [ANY] * len(arrays),
        ANY,
        scratch=[
            pltpu.VMEM((chunks, depth, electrons), BF16),
            pltpu.VMEM((chunks, depth, electrons), F32),
            pltpu.SemaphoreType.DMA((chunks,)),
            pltpu.SemaphoreType.DMA((chunks,)),
        ],
        flops=4 * electrons * electrons * 2 * count,
        moved=6 * electrons * electrons,
    )(role, change, cols, small, *arrays)

    both = jnp.concatenate([first, second]).reshape(2, 1, 4, count)
    return updated[None], both[:, :, :3], both[:, :, 3], new_weight[0, :1]


def solution(mesh):
    split = ("grp", "orb")
    return jax.shard_map(
        functools.partial(per_device, mesh.shape["grp"], mesh.shape["orb"]),
        mesh=mesh,
        in_specs=(
            P(),
            P(None, "orb"),
            P(split, None, None),
            P(split, None, None),
            P(None, split, None, None),
            P(None, split, None),
            P("orb"),
            P(split),
            P(split),
        ),
        out_specs=(
            P(split, None, None),
            P(None, split, None, None),
            P(None, split, None),
            P(split),
        ),
        check_vma=False,
    )
```

```python
import functools
import math

import jax
import jax.numpy as jnp
from jax import lax
from jax.experimental import pallas as pl
from jax.experimental.pallas import tpu as pltpu
from jax.sharding import PartitionSpec as P

F32 = jnp.float32
BF16 = jnp.bfloat16
LANES = 128
MIB = 1024 * 1024
precise = lax.Precision.HIGHEST

SIN_HALF = (4.4428679, -7.30744342, 3.59478808, -0.78437403)
COS_HALF = (1.4142135, -6.97885099, 5.73946117, -1.88356299, 0.31069819)


def dot(a, b, dims=((1,), (0,)), exact=False):
    return lax.dot_general(
        a, b, (dims, ((), ())), precision=precise if exact else None, preferred_element_type=F32
    )


def iota(shape, dim):
    return lax.broadcasted_iota(jnp.int32, shape, dim)


def call(kernel, out_shape, in_specs, out_specs, scratch=(), flops=0, moved=0, vmem=4):
    return pl.pallas_call(
        kernel,
        out_shape=out_shape,
        in_specs=in_specs,
        out_specs=out_specs,
        scratch_shapes=list(scratch),
        compiler_params=pltpu.CompilerParams(vmem_limit_bytes=vmem * MIB),
        cost_estimate=pl.CostEstimate(flops=flops, bytes_accessed=moved, transcendentals=0),
    )


VM = pl.BlockSpec(memory_space=pltpu.VMEM)
SM = pl.BlockSpec(memory_space=pltpu.SMEM)
ANY = pl.BlockSpec(memory_space=pl.ANY)


def shape(dims, dtype):
    return jax.ShapeDtypeStruct(dims, dtype)


def is_power(n):
    return n & (n - 1) == 0


def pairs(n, step):
    if is_power(n):
        return [(i, i ^ step) for i in range(n)]
    return [(i, (i + step) % n) for i in range(n)]


def distance(n, here, there):
    return here ^ there if is_power(n) else lax.rem(here - there + n, n)


def backward(n, step):
    return step if is_power(n) else (n - step) % n


def start_kernel(count, pos_ref, moved_ref, disp_ref, weight_ref, out_ref, tiled_ref, shift_ref):
    electrons = pos_ref.shape[2]
    copies = LANES // count
    tiled = jnp.concatenate([moved_ref[:, 0, :]] * copies, 1)
    tiled_ref[...] = tiled
    zeros = jnp.zeros((5, LANES), F32)
    for update in range(2):
        shift = jnp.concatenate([disp_ref[update, 0]] * copies, 1)
        shift_ref[update] = jnp.concatenate([shift, zeros], 0)
    pos = jnp.concatenate([pos_ref[0], jnp.zeros((5, electrons), F32)], 0)
    pick = (iota((electrons, LANES), 0) == tiled[0:1, :]).astype(F32)
    block = iota((8, LANES), 1) // count
    old = dot(pos, pick, exact=True)
    disp = shift_ref[0]
    points = old + jnp.where(block % 2 == 1, disp, 0.0)
    first = jnp.where(block == 0, disp, 0.0)
    out_ref[...] = pos + dot(first, pick, ((1,), (1,)), exact=True)
    out_ref[3:6, 0:LANES] = points[0:3]
    out_ref[6:7, 0:LANES] = tiled[1:2, :].astype(F32)
    out_ref[7:8, 0:LANES] = jnp.full((1, LANES), weight_ref[0], F32)


def round_kernel(wanted, inverse_ref, after_ref, *refs):
    outs = refs[: len(wanted)]
    staged, sem = refs[len(wanted) :]
    depth = staged.shape[1]
    copies = []
    for slot, chunk in enumerate(wanted):
        rows = inverse_ref.at[0, pl.ds(chunk * depth, depth)]
        copy = pltpu.make_async_copy(rows, staged.at[slot], sem.at[slot])
        copy.start()
        copies.append(copy)
    for slot, out in enumerate(outs):
        copies[slot].wait()
        out[...] = staged[slot].astype(BF16)


def relay_kernel(flag_ref, own_a, own_b, got_a, got_b, *refs):
    out_a, out_b, token_ref = refs[-3:]
    here = flag_ref[0] == 0

    @pl.when(here)
    def _():
        out_a[...] = own_a[...]
        out_b[...] = own_b[...]

    @pl.when(jnp.logical_not(here))
    def _():
        out_a[...] = got_a[...]
        out_b[...] = got_b[...]

    token_ref[...] = jnp.zeros(token_ref.shape, F32)


def points_kernel(count, others, role_ref, *refs):
    own_ref = refs[0]
    received = refs[1 : 1 + others]
    moved_ref, disp_ref, points_ref, weight_ref = refs[1 + others :]
    role = role_ref[0]
    parent = own_ref[...]
    for step in range(others):
        parent = jnp.where(role == step + 1, received[step][...], parent)
    electrons = parent.shape[1]
    pick = (iota((electrons, LANES), 0) == moved_ref[1:2, :]).astype(F32)
    block = iota((8, LANES), 1) // count
    old = dot(parent, pick, exact=True)
    later = old + jnp.where(block % 2 == 1, disp_ref[1], 0.0)
    zeros = jnp.zeros((5, LANES), F32)
    mine = jnp.concatenate([own_ref[3:6, 0:LANES], zeros], 0)
    theirs = jnp.concatenate([parent[3:6, 0:LANES], zeros], 0)
    points = jnp.where(block < 2, mine, jnp.where(block < 4, theirs, later))
    points_ref[...] = jnp.broadcast_to(points[None], points_ref.shape)
    weight_ref[...] = parent[7:8, 0:LANES]


def columns_kernel(count, others, chunks, steps, *refs):
    chunk_refs = refs[:chunks]
    moved_ref = refs[chunks]
    received = refs[chunks + 1 : chunks + 1 + others]
    outs = refs[chunks + 1 + others :]
    depth = chunk_refs[0].shape[0]
    electrons = chunk_refs[0].shape[1]
    block = iota((1, LANES), 1) // count
    wanted = jnp.where(block == 0, moved_ref[0:1, :], moved_ref[1:2, :])
    for step in range(others):
        theirs = received[step][6:7, 0:LANES].astype(jnp.int32)
        wanted = jnp.where(block == 2 + step, theirs, wanted)
    pick = (iota((electrons, LANES), 0) == wanted).astype(F32).astype(BF16)
    for chunk in range(chunks):
        rows = slice(chunk * depth, (chunk + 1) * depth)
        found = dot(chunk_refs[chunk][...], pick)
        turned = jnp.transpose(found).astype(BF16)
        for out, step in zip(outs, steps):
            out[0:count, rows] = turned[0:count]
            out[count : 2 * count, rows] = turned[(1 + step) * count : (2 + step) * count]


def table_kernel(coeff_ref, wave_ref, out_ref):
    waves = wave_ref.shape[1]
    width = coeff_ref.shape[1]
    wave = jnp.transpose(jnp.concatenate([wave_ref[...], jnp.zeros((5, waves), F32)], 0))
    cos_part = coeff_ref[0:waves].astype(F32)
    sin_part = coeff_ref[waves:].astype(F32)
    squared = None
    for a in range(3):
        scale = wave[:, a : a + 1]
        where = slice(a * width, (a + 1) * width)
        out_ref[0:waves, where] = (scale * sin_part).astype(BF16)
        out_ref[waves:, where] = (-scale * cos_part).astype(BF16)
        squared = scale * scale if a == 0 else squared + scale * scale
    where = slice(3 * width, 4 * width)
    out_ref[0:waves, where] = (-squared * cos_part).astype(BF16)
    out_ref[waves:, where] = (-squared * sin_part).astype(BF16)


def horner(coefs, u):
    value = coefs[-1] * u + coefs[-2]
    for c in reversed(coefs[:-2]):
        value = value * u + c
    return value


def evaluate_kernel(
    count, points_ref, wave_ref, coeff_ref, table_ref, after_ref, out_ref, diff, new
):
    walkers = points_ref.shape[0]
    waves = wave_ref.shape[1]
    width = coeff_ref.shape[1]
    step = math.gcd(waves, LANES)

    def one(w, carry):
        column = jnp.transpose(points_ref[w])
        xs = [column[0 : 6 * count, a : a + 1] for a in range(3)]
        row_d = pl.multiple_of(w * (3 * count), count)
        row_n = pl.multiple_of(w * (2 * count), count)
        for at in range(0, waves, step):
            ks = [wave_ref[a : a + 1, at : at + step] * (0.5 / math.pi) for a in range(3)]
            turn = xs[0] * ks[0] + xs[1] * ks[1] + xs[2] * ks[2]
            r = turn - jnp.floor(turn + 0.5)
            u = r * r
            s = r * horner(SIN_HALF, u)
            c = horner(COS_HALF, u)
            for value, base in ((1.0 - s * s, 0), (s * c, waves)):
                where = slice(base + at, base + at + step)
                kept = value.astype(BF16)
                wide = kept.astype(F32)
                part = [wide[i * count : (i + 1) * count] for i in range(6)]
                diff[pl.ds(row_d, count), where] = (part[3] - part[2]).astype(BF16)
                diff[pl.ds(row_d + count, count), where] = (part[5] - part[4]).astype(BF16)
                diff[pl.ds(row_d + 2 * count, count), where] = (part[1] - part[0]).astype(BF16)
                new[pl.ds(row_n, count), where] = kept[5 * count : 6 * count]
                new[pl.ds(row_n + count, count), where] = kept[count : 2 * count]
        return carry

    lax.fori_loop(0, walkers, one, 0)
    change = dot(diff[...], coeff_ref[...]).astype(BF16)
    rest = dot(new[...], table_ref[...]).astype(BF16)
    for w in range(walkers):
        at = w * 3 * count
        out_ref[w, 0 : 2 * count] = change[at : at + 2 * count]
        out_ref[w, 6 * count : 7 * count] = change[at + 2 * count : at + 3 * count]
        for half, base in ((0, 2 * count), (1, 7 * count)):
            row = (2 * w + half) * count
            for a in range(4):
                out_ref[w, base + a * count : base + (a + 1) * count] = rest[
                    row : row + count, a * width : (a + 1) * width
                ]


def sweep(matrices):
    matrices = list(matrices)
    logs = [jnp.zeros((1, 1), F32) for _ in matrices]
    for k in range(max(m.shape[0] for m in matrices)):
        for which, matrix in enumerate(matrices):
            size = matrix.shape[0]
            if k >= size:
                continue
            pivot = matrix[k : k + 1, k : k + 1]
            inverse = 1.0 / pivot
            column = matrix[:, k : k + 1]
            line = matrix[k : k + 1, :]
            row_here = iota((size, size), 0) == k
            lane_here = iota((size, size), 1) == k
            scaled = line * inverse
            reduced = matrix - column * scaled
            matrix = jnp.where(row_here, scaled, jnp.where(lane_here, column * inverse, reduced))
            matrix = jnp.where(jnp.logical_and(row_here, lane_here), -inverse, matrix)
            matrices[which] = matrix
            logs[which] = logs[which] + jnp.log(pivot)
    return [-m for m in matrices], logs


def solve_kernel(count, others, role_ref, vals_ref, own_ref, *refs):
    received = refs[:others]
    weight_ref, after_ref = refs[others : others + 2]
    change_ref, cols_ref, inv_ref, first_ref, second_ref, out_weight_ref, vals = refs[others + 2 :]
    pieces, _, width = vals_ref.shape
    for o in range(pieces):
        vals[:, o * width : (o + 1) * width] = vals_ref[o]
    role = role_ref[0]
    cols = own_ref[...].astype(F32)
    for step in range(others):
        cols = jnp.where(role == step + 1, received[step][...].astype(F32), cols)
    cols = cols.astype(BF16)
    cols_ref[...] = cols
    change_ref[...] = vals[0 : 2 * count]
    own = own_ref[0:count]
    products, ratios, normal = [], [], []
    for size, matrix, part in (
        (count, own, vals[6 * count : 11 * count]),
        (2 * count, cols, vals[0 : 6 * count]),
    ):
        product = dot(matrix, part, ((1,), (1,)))
        ratio = product[:, 0:size] + jnp.where(iota((size, size), 0) == iota((size, size), 1), 1.0, 0.0)
        products.append(product[:, size:])
        ratios.append(ratio)
        normal.append(dot(ratio, ratio, ((1,), (1,)), exact=True))
    inverses, logs = sweep(normal)
    for inverse, ratio, product, sums_ref in zip(inverses, ratios, products, (first_ref, second_ref)):
        size = ratio.shape[0]
        wide = product.shape[1]
        small = dot(inverse, ratio, exact=True)
        tile = jnp.where(iota((size, wide), 0) == size - count + iota((size, wide), 1) % count, 1.0, 0.0)
        spread = dot(small, tile, exact=True)
        sums_ref[...] = jnp.sum(product * spread, axis=0, keepdims=True)
    inv_ref[...] = small
    out_weight_ref[...] = weight_ref[...] + 0.5 * logs[1]


def finish_kernel(sources, chunks, role_ref, change_ref, cols_ref, inv_ref, *refs):
    inputs = refs[:-5]
    out_ref, parent, staged, in_sem, out_sem = refs[-5:]
    depth = inputs[0].shape[0]
    role = role_ref[0]
    for chunk in range(chunks):
        for which, table in enumerate(sources):

            @pl.when(role == which)
            def _():
                pltpu.make_async_copy(
                    inputs[table[chunk]], parent.at[chunk], in_sem.at[chunk]
                ).start()

    total = jnp.zeros((change_ref.shape[0], inputs[0].shape[1]), F32)
    for chunk in range(chunks):
        pltpu.make_async_copy(inputs[chunk], parent.at[chunk], in_sem.at[chunk]).wait()
        total = total + dot(change_ref[:, chunk * depth : (chunk + 1) * depth], parent[chunk])
    solved = dot(inv_ref[...], total, exact=True).astype(BF16)
    copies = []
    for chunk in range(chunks):
        rows = slice(chunk * depth, (chunk + 1) * depth)
        columns = jnp.transpose(cols_ref[:, rows].astype(F32)).astype(BF16)
        staged[chunk] = parent[chunk].astype(F32) - dot(columns, solved)
        copy = pltpu.make_async_copy(staged.at[chunk], out_ref.at[rows], out_sem.at[chunk])
        copy.start()
        copies.append(copy)
    for copy in copies:
        copy.wait()


def per_device(
    n_grp,
    n_orb,
    wavevectors,
    coefficients,
    inverse,
    positions,
    displacements,
    moved,
    donor,
    take,
    log_weight,
):
    electrons = inverse.shape[1]
    count = moved.shape[2]
    plane = coefficients.shape[0]
    local = coefficients.shape[1]
    others = n_grp - 1
    chunks = 4
    group = lax.axis_index("grp")
    source = donor[0]
    apart = distance(n_grp, group, source)
    role = jnp.where(take[0] == 1, apart, 0).astype(jnp.int32).reshape(1)

    record, tiled, disp = call(
        functools.partial(start_kernel, count),
        (
            shape((8, electrons), F32),
            shape((2, LANES), jnp.int32),
            shape((2, 8, LANES), F32),
        ),
        [VM, VM, VM, SM],
        (VM, VM, VM),
    )(positions, moved, displacements, log_weight)
    records = [lax.ppermute(record, "grp", pairs(n_grp, s)) for s in range(1, n_grp)]

    depth = electrons // chunks
    own = [None] * chunks
    after = record
    for wanted in ((0, chunks - 1), tuple(range(1, chunks - 1))):
        some = call(
            functools.partial(round_kernel, wanted),
            tuple(shape((depth, electrons), BF16) for _ in wanted),
            [ANY, ANY],
            tuple(VM for _ in wanted),
            scratch=[
                pltpu.VMEM((len(wanted), depth, electrons), F32),
                pltpu.SemaphoreType.DMA((len(wanted),)),
            ],
            moved=6 * len(wanted) * depth * electrons,
            vmem=6,
        )(inverse, after)
        for chunk, block in zip(wanted, some):
            own[chunk] = block
        after = some[0]

    points, weight = call(
        functools.partial(points_kernel, count, others),
        (shape((n_orb, 8, LANES), F32), shape((1, LANES), F32)),
        [SM] + [VM] * (others + 3),
        (VM, VM),
    )(role, record, *records, tiled, disp)
    points = lax.all_to_all(points, "orb", split_axis=0, concat_axis=0, tiled=True)

    steps = [0] + [backward(n_grp, s) for s in range(1, n_grp)]
    columns = call(
        functools.partial(columns_kernel, count, others, chunks, steps),
        tuple(shape((2 * count, electrons), BF16) for _ in steps),
        [VM] * (chunks + 1 + others),
        tuple(VM for _ in steps),
        flops=2 * electrons * electrons * LANES,
        moved=2 * electrons * electrons,
        vmem=8,
    )(*own, tiled, *records)
    sent = [lax.ppermute(columns[s], "grp", pairs(n_grp, s)) for s in range(1, n_grp)]

    width = -(-local // LANES) * LANES
    coeff = jnp.pad(coefficients, ((0, 0), (0, width - local))) if width > local else coefficients
    derived = call(
        table_kernel,
        shape((plane, 4 * width), BF16),
        [VM, VM],
        VM,
        flops=8 * plane * width,
        moved=10 * plane * width,
        vmem=8,
    )(coeff, wavevectors)

    apart = apart.astype(jnp.int32).reshape(1)
    arrays = list(own)
    if n_grp == 4:
        send_x = lambda block: lax.ppermute(block, "grp", pairs(n_grp, 1))
        send_y = lambda block: lax.ppermute(block, "grp", pairs(n_grp, 2))

        def relay(mine, got, first):
            kept = shape((depth, electrons), BF16)
            return call(
                relay_kernel,
                (kept, kept, shape((8, LANES), F32)),
                [SM, VM, VM, VM, VM] + [ANY] * len(first),
                (VM, VM, VM),
                moved=4 * depth * electrons,
                vmem=4,
            )(apart, *mine, *got, *first)

        x1, y1 = send_x(own[0]), send_y(own[3])
        relay_x, relay_y, token_1 = relay((own[1], own[2]), (y1, x1), (derived, columns[0]))
        x2, y2 = send_x(relay_x), send_y(relay_y)
        relay_x, relay_y, token_2 = relay((own[2], own[1]), (y2, x2), ())
        x3, y3 = send_x(relay_x), send_y(relay_y)
        arrays += [x1, x2, x3, y1, y2, y3]
        a1, a2, a3, b1, b2, b3 = range(chunks, chunks + 6)
        table = [range(chunks), (a1, a2, a3, b3), (a3, b3, b2, b1), (b2, b3, a3, a2)]
    else:
        token_1 = token_2 = jnp.zeros((8, LANES), F32)
        table = [range(chunks)]
        for step in range(1, n_grp):
            table.append(range(len(arrays), len(arrays) + chunks))
            arrays += [lax.ppermute(block, "grp", pairs(n_grp, step)) for block in own]

    block = math.gcd(n_orb, 8)
    values = pl.pallas_call(
        functools.partial(evaluate_kernel, count),
        grid=(n_orb // block,),
        out_shape=shape((n_orb, 11 * count, width), BF16),
        in_specs=[
            pl.BlockSpec((block, 8, LANES), lambda i: (i, 0, 0)),
            pl.BlockSpec(wavevectors.shape, lambda i: (0, 0)),
            pl.BlockSpec(coeff.shape, lambda i: (0, 0)),
            pl.BlockSpec(derived.shape, lambda i: (0, 0)),
            ANY,
        ],
        out_specs=pl.BlockSpec((block, 11 * count, width), lambda i: (i, 0, 0)),
        scratch_shapes=[
            pltpu.VMEM((block * 3 * count, plane), BF16),
            pltpu.VMEM((block * 2 * count, plane), BF16),
        ],
        compiler_params=pltpu.CompilerParams(vmem_limit_bytes=16 * MIB),
        cost_estimate=pl.CostEstimate(
            flops=2 * n_orb * count * plane * width * 11,
            bytes_accessed=12 * plane * width,
            transcendentals=0,
        ),
    )(points, wavevectors, coeff, derived, token_1)
    values = values[:, :, :local]
    values = lax.all_to_all(values, "orb", split_axis=0, concat_axis=0, tiled=True)
    if width > local:
        values = values.transpose(1, 0, 2).reshape(1, 11 * count, electrons)

    change, cols, small, first, second, new_weight = call(
        functools.partial(solve_kernel, count, others),
        (
            shape((2 * count, electrons), BF16),
            shape((2 * count, electrons), BF16),
            shape((2 * count, 2 * count), F32),
            shape((1, 4 * count), F32),
            shape((1, 4 * count), F32),
            shape((1, LANES), F32),
        ),
        [SM] + [VM] * (others + 3) + [ANY],
        (VM,) * 6,
        scratch=[pltpu.VMEM((11 * count, electrons), BF16)],
        flops=2 * electrons * count * count * 16,
        moved=4 * 11 * count * electrons,
    )(role, values, columns[0], *sent, weight, token_2)

    updated = call(
        functools.partial(finish_kernel, table, chunks),
        shape((electrons, electrons), F32),
        [SM, VM, VM, VM] + [ANY] * len(arrays),
        ANY,
        scratch=[
            pltpu.VMEM((chunks, depth, electrons), BF16),
            pltpu.VMEM((chunks, depth, electrons), F32),
            pltpu.SemaphoreType.DMA((chunks,)),
            pltpu.SemaphoreType.DMA((chunks,)),
        ],
        flops=4 * electrons * electrons * 2 * count,
        moved=6 * electrons * electrons,
        vmem=12,
    )(role, change, cols, small, *arrays)

    both = jnp.concatenate([first, second]).reshape(2, 1, 4, count)
    return updated[None], both[:, :, :3], both[:, :, 3], new_weight[0, :1]


def solution(mesh):
    split = ("grp", "orb")
    return jax.shard_map(
        functools.partial(per_device, mesh.shape["grp"], mesh.shape["orb"]),
        mesh=mesh,
        in_specs=(
            P(),
            P(None, "orb"),
            P(split, None, None),
            P(split, None, None),
            P(None, split, None, None),
            P(None, split, None),
            P("orb"),
            P(split),
            P(split),
        ),
        out_specs=(
            P(split, None, None),
            P(None, split, None, None),
            P(None, split, None),
            P(split),
        ),
        check_vma=False,
    )
```

```python
import functools
import math

import jax
import jax.numpy as jnp
from jax import lax
from jax.experimental import pallas as pl
from jax.experimental.pallas import tpu as pltpu
from jax.sharding import PartitionSpec as P

F32 = jnp.float32
BF16 = jnp.bfloat16
LANES = 128
MIB = 1024 * 1024
precise = lax.Precision.HIGHEST

SIN_HALF = (4.4428679, -7.30744342, 3.59478808, -0.78437403)
COS_HALF = (1.4142135, -6.97885099, 5.73946117, -1.88356299, 0.31069819)


def dot(a, b, dims=((1,), (0,)), exact=False):
    return lax.dot_general(
        a, b, (dims, ((), ())), precision=precise if exact else None, preferred_element_type=F32
    )


def iota(shape, dim):
    return lax.broadcasted_iota(jnp.int32, shape, dim)


def call(
    kernel, out_shape, in_specs, out_specs, scratch=(), flops=0, moved=0, vmem=4, aliases=None
):
    return pl.pallas_call(
        kernel,
        out_shape=out_shape,
        input_output_aliases=aliases or {},
        in_specs=in_specs,
        out_specs=out_specs,
        scratch_shapes=list(scratch),
        compiler_params=pltpu.CompilerParams(vmem_limit_bytes=vmem * MIB),
        cost_estimate=pl.CostEstimate(flops=flops, bytes_accessed=moved, transcendentals=0),
    )


VM = pl.BlockSpec(memory_space=pltpu.VMEM)
SM = pl.BlockSpec(memory_space=pltpu.SMEM)
ANY = pl.BlockSpec(memory_space=pl.ANY)
HBM = pl.BlockSpec(memory_space=pltpu.HBM)


def shape(dims, dtype):
    return jax.ShapeDtypeStruct(dims, dtype)


def is_power(n):
    return n & (n - 1) == 0


def pairs(n, step):
    if is_power(n):
        return [(i, i ^ step) for i in range(n)]
    return [(i, (i + step) % n) for i in range(n)]


def distance(n, here, there):
    return here ^ there if is_power(n) else lax.rem(here - there + n, n)


def backward(n, step):
    return step if is_power(n) else (n - step) % n


def start_kernel(
    count,
    pos_hbm,
    moved_hbm,
    disp_hbm,
    weight_hbm,
    out_ref,
    tiled_ref,
    shift_ref,
    pos_ref,
    moved_ref,
    disp_ref,
    weight_ref,
    sems,
):
    loads = [
        pltpu.make_async_copy(src, dst, sems.at[i])
        for i, (src, dst) in enumerate(
            (
                (moved_hbm, moved_ref),
                (disp_hbm, disp_ref),
                (pos_hbm, pos_ref),
                (weight_hbm, weight_ref),
            )
        )
    ]
    for load in loads:
        load.start()
    electrons = pos_ref.shape[2]
    copies = LANES // count
    loads[0].wait()
    tiled = jnp.concatenate([moved_ref[:, 0, :]] * copies, 1)
    tiled_ref[...] = tiled
    pick = (iota((electrons, LANES), 0) == tiled[0:1, :]).astype(F32)
    block = iota((8, LANES), 1) // count
    zeros = jnp.zeros((5, LANES), F32)
    loads[1].wait()
    for update in range(2):
        shift = jnp.concatenate([disp_ref[3 * update : 3 * update + 3, 0, :]] * copies, 1)
        shift_ref[update] = jnp.concatenate([shift, zeros], 0)
    loads[2].wait()
    pos = jnp.concatenate([pos_ref[:, 0, :], jnp.zeros((5, electrons), F32)], 0)
    old = dot(pos, pick, exact=True)
    disp = shift_ref[0]
    points = old + jnp.where(block % 2 == 1, disp, 0.0)
    first = jnp.where(block == 0, disp, 0.0)
    out_ref[...] = pos + dot(first, pick, ((1,), (1,)), exact=True)
    out_ref[3:6, 0:LANES] = points[0:3]
    out_ref[6:7, 0:LANES] = tiled[1:2, :].astype(F32)
    loads[3].wait()
    out_ref[7:8, 0:LANES] = jnp.full((1, LANES), weight_ref[0], F32)


def round_kernel(inverse_ref, after_ref, *refs):
    outs = refs[:-2]
    staged, sem = refs[-2:]
    depth = staged.shape[1]
    copies = []
    for chunk in range(len(outs)):
        rows = inverse_ref.at[0, pl.ds(chunk * depth, depth)]
        copy = pltpu.make_async_copy(rows, staged.at[chunk], sem.at[chunk])
        copy.start()
        copies.append(copy)
    for chunk, out in enumerate(outs):
        copies[chunk].wait()
        out[...] = staged[chunk].astype(BF16)


def gate_kernel(*refs):
    token_ref = refs[-1]
    token_ref[...] = jnp.zeros(token_ref.shape, F32)


def relay_kernel(flag_ref, own_a, own_b, got_a, got_b, *refs):
    out_a, out_b, token_ref, sems = refs[-4:]

    @pl.when(flag_ref[0] == 0)
    def _():
        copies = [
            pltpu.make_async_copy(own_a, out_a, sems.at[0]),
            pltpu.make_async_copy(own_b, out_b, sems.at[1]),
        ]
        for copy in copies:
            copy.start()
        for copy in copies:
            copy.wait()

    token_ref[...] = jnp.zeros(token_ref.shape, F32)


def points_kernel(count, others, role_ref, *refs):
    own_ref = refs[0]
    received = refs[1 : 1 + others]
    moved_ref, disp_ref, after_ref, points_ref, weight_ref = refs[1 + others :]
    role = role_ref[0]
    parent = own_ref[...]
    for step in range(others):
        parent = jnp.where(role == step + 1, received[step][...], parent)
    electrons = parent.shape[1]
    pick = (iota((electrons, LANES), 0) == moved_ref[1:2, :]).astype(F32)
    block = iota((8, LANES), 1) // count
    old = dot(parent, pick, exact=True)
    later = old + jnp.where(block % 2 == 1, disp_ref[1], 0.0)
    zeros = jnp.zeros((5, LANES), F32)
    mine = jnp.concatenate([own_ref[3:6, 0:LANES], zeros], 0)
    theirs = jnp.concatenate([parent[3:6, 0:LANES], zeros], 0)
    points = jnp.where(block < 2, mine, jnp.where(block < 4, theirs, later))
    points_ref[...] = jnp.broadcast_to(points[None], points_ref.shape)
    weight_ref[...] = parent[7:8, 0:LANES]


def columns_kernel(count, others, chunks, steps, *refs):
    chunk_refs = refs[:chunks]
    moved_ref = refs[chunks]
    received = refs[chunks + 1 : chunks + 1 + others]
    outs = refs[chunks + 1 + others :]
    depth = chunk_refs[0].shape[0]
    electrons = chunk_refs[0].shape[1]
    block = iota((1, LANES), 1) // count
    wanted = jnp.where(block == 0, moved_ref[0:1, :], moved_ref[1:2, :])
    for step in range(others):
        theirs = received[step][6:7, 0:LANES].astype(jnp.int32)
        wanted = jnp.where(block == 2 + step, theirs, wanted)
    pick = (iota((electrons, LANES), 0) == wanted).astype(F32).astype(BF16)
    for chunk in range(chunks):
        rows = slice(chunk * depth, (chunk + 1) * depth)
        found = dot(chunk_refs[chunk][...], pick)
        turned = jnp.transpose(found).astype(BF16)
        for out, step in zip(outs, steps):
            out[0:count, rows] = turned[0:count]
            out[count : 2 * count, rows] = turned[(1 + step) * count : (2 + step) * count]


def table_kernel(coeff_ref, wave_ref, out_ref):
    waves = wave_ref.shape[1]
    width = coeff_ref.shape[1]
    wave = jnp.transpose(jnp.concatenate([wave_ref[...], jnp.zeros((5, waves), F32)], 0))
    out_ref[:, 0:width] = coeff_ref[...]
    cos_part = coeff_ref[0:waves].astype(F32)
    sin_part = coeff_ref[waves:].astype(F32)
    squared = None
    for a in range(3):
        scale = wave[:, a : a + 1]
        where = slice((a + 1) * width, (a + 2) * width)
        out_ref[0:waves, where] = (scale * sin_part).astype(BF16)
        out_ref[waves:, where] = (-scale * cos_part).astype(BF16)
        squared = scale * scale if a == 0 else squared + scale * scale
    where = slice(4 * width, 5 * width)
    out_ref[0:waves, where] = (-squared * cos_part).astype(BF16)
    out_ref[waves:, where] = (-squared * sin_part).astype(BF16)


def horner(coefs, u):
    value = coefs[-1] * u + coefs[-2]
    for c in reversed(coefs[:-2]):
        value = value * u + c
    return value


def evaluate_kernel(
    count, points_ref, wave_ref, table_ref, after_ref, out_ref, diff, new
):
    walkers = points_ref.shape[0]
    waves = wave_ref.shape[1]
    width = table_ref.shape[1] // 5
    step = math.gcd(waves, LANES)

    def one(w, carry):
        column = jnp.transpose(points_ref[w])
        xs = [column[0 : 6 * count, a : a + 1] for a in range(3)]
        row_d = pl.multiple_of(w * (3 * count), count)
        row_n = pl.multiple_of(w * (2 * count), count)
        for at in range(0, waves, step):
            ks = [wave_ref[a : a + 1, at : at + step] * (0.5 / math.pi) for a in range(3)]
            turn = xs[0] * ks[0] + xs[1] * ks[1] + xs[2] * ks[2]
            r = turn - jnp.floor(turn + 0.5)
            u = r * r
            s = r * horner(SIN_HALF, u)
            c = horner(COS_HALF, u)
            for value, base in ((1.0 - s * s, 0), (s * c, waves)):
                where = slice(base + at, base + at + step)
                kept = value.astype(BF16)
                wide = kept.astype(F32)
                part = [wide[i * count : (i + 1) * count] for i in range(6)]
                diff[pl.ds(row_d, count), where] = (part[3] - part[2]).astype(BF16)
                diff[pl.ds(row_d + count, count), where] = (part[5] - part[4]).astype(BF16)
                diff[pl.ds(row_d + 2 * count, count), where] = (part[1] - part[0]).astype(BF16)
                new[pl.ds(row_n, count), where] = kept[5 * count : 6 * count]
                new[pl.ds(row_n + count, count), where] = kept[count : 2 * count]
        return carry

    lax.fori_loop(0, walkers, one, 0)
    change = dot(diff[...], table_ref[:, 0:width]).astype(BF16)
    rest = dot(new[...], table_ref[:, width:]).astype(BF16)
    for w in range(walkers):
        at = w * 3 * count
        out_ref[w, 0 : 2 * count] = change[at : at + 2 * count]
        out_ref[w, 6 * count : 7 * count] = change[at + 2 * count : at + 3 * count]
        for half, base in ((0, 2 * count), (1, 7 * count)):
            row = (2 * w + half) * count
            for a in range(4):
                out_ref[w, base + a * count : base + (a + 1) * count] = rest[
                    row : row + count, a * width : (a + 1) * width
                ]


def sweep(matrices):
    matrices = list(matrices)
    logs = [jnp.zeros((1, 1), F32) for _ in matrices]
    for k in range(max(m.shape[0] for m in matrices)):
        for which, matrix in enumerate(matrices):
            size = matrix.shape[0]
            if k >= size:
                continue
            pivot = matrix[k : k + 1, k : k + 1]
            inverse = 1.0 / pivot
            column = matrix[:, k : k + 1]
            line = matrix[k : k + 1, :]
            row_here = iota((size, size), 0) == k
            lane_here = iota((size, size), 1) == k
            scaled = line * inverse
            reduced = matrix - column * scaled
            matrix = jnp.where(row_here, scaled, jnp.where(lane_here, column * inverse, reduced))
            matrix = jnp.where(jnp.logical_and(row_here, lane_here), -inverse, matrix)
            matrices[which] = matrix
            logs[which] = logs[which] + jnp.log(pivot)
    return [-m for m in matrices], logs


def solve_kernel(count, others, role_ref, vals_ref, own_ref, *refs):
    received = refs[:others]
    weight_ref, after_ref = refs[others : others + 2]
    change_ref, cols_ref, inv_ref, drift_ref, lap_ref, out_weight_ref, vals = refs[others + 2 :]
    pieces, _, width = vals_ref.shape
    for o in range(pieces):
        vals[:, o * width : (o + 1) * width] = vals_ref[o]
    role = role_ref[0]
    cols = own_ref[...].astype(F32)
    for step in range(others):
        cols = jnp.where(role == step + 1, received[step][...].astype(F32), cols)
    cols = cols.astype(BF16)
    cols_ref[...] = cols
    change_ref[...] = vals[0 : 2 * count]
    own = own_ref[0:count]
    products, ratios, normal = [], [], []
    for size, matrix, part in (
        (count, own, vals[6 * count : 11 * count]),
        (2 * count, cols, vals[0 : 6 * count]),
    ):
        product = dot(matrix, part, ((1,), (1,)))
        ratio = product[:, 0:size] + jnp.where(iota((size, size), 0) == iota((size, size), 1), 1.0, 0.0)
        products.append(product[:, size:])
        ratios.append(ratio)
        normal.append(dot(ratio, ratio, ((1,), (1,)), exact=True))
    inverses, logs = sweep(normal)
    for update, (inverse, ratio, product) in enumerate(zip(inverses, ratios, products)):
        size = ratio.shape[0]
        wide = product.shape[1]
        small = dot(inverse, ratio, exact=True)
        tile = jnp.where(iota((size, wide), 0) == size - count + iota((size, wide), 1) % count, 1.0, 0.0)
        spread = dot(small, tile, exact=True)
        sums = jnp.sum(product * spread, axis=0, keepdims=True)
        for a in range(3):
            drift_ref[3 * update + a] = sums[:, a * count : (a + 1) * count]
        lap_ref[update] = sums[:, 3 * count : 4 * count]
    inv_ref[...] = small
    out_weight_ref[...] = weight_ref[...] + 0.5 * logs[1]


def finish_kernel(sources, chunks, role_ref, change_ref, cols_ref, inv_ref, *refs):
    inputs = refs[:-5]
    out_ref, parent, staged, in_sem, out_sem = refs[-5:]
    depth = inputs[0].shape[0]
    role = role_ref[0]
    for chunk in range(chunks):
        for which, table in enumerate(sources):

            @pl.when(role == which)
            def _():
                pltpu.make_async_copy(
                    inputs[table[chunk]], parent.at[chunk], in_sem.at[chunk]
                ).start()

    total = jnp.zeros((change_ref.shape[0], inputs[0].shape[1]), F32)
    for chunk in range(chunks):
        pltpu.make_async_copy(inputs[chunk], parent.at[chunk], in_sem.at[chunk]).wait()
        total = total + dot(change_ref[:, chunk * depth : (chunk + 1) * depth], parent[chunk])
    solved = dot(inv_ref[...], total, exact=True).astype(BF16)
    copies = []
    for chunk in range(chunks):
        rows = slice(chunk * depth, (chunk + 1) * depth)
        columns = jnp.transpose(cols_ref[:, rows].astype(F32)).astype(BF16)
        staged[chunk] = parent[chunk].astype(F32) - dot(columns, solved)
        copy = pltpu.make_async_copy(staged.at[chunk], out_ref.at[rows], out_sem.at[chunk])
        copy.start()
        copies.append(copy)
    for copy in copies:
        copy.wait()


def per_device(
    n_grp,
    n_orb,
    wavevectors,
    coefficients,
    inverse,
    positions,
    displacements,
    moved,
    donor,
    take,
    log_weight,
):
    electrons = inverse.shape[1]
    count = moved.shape[2]
    plane = coefficients.shape[0]
    local = coefficients.shape[1]
    others = n_grp - 1
    chunks = 4
    group = lax.axis_index("grp")
    source = donor[0]
    apart = distance(n_grp, group, source)
    role = jnp.where(take[0] == 1, apart, 0).astype(jnp.int32).reshape(1)

    record, tiled, disp = call(
        functools.partial(start_kernel, count),
        (
            shape((8, electrons), F32),
            shape((2, LANES), jnp.int32),
            shape((2, 8, LANES), F32),
        ),
        [HBM, HBM, HBM, HBM],
        (VM, VM, VM),
        scratch=[
            pltpu.VMEM((3, 1, electrons), F32),
            pltpu.VMEM((2, 1, count), jnp.int32),
            pltpu.VMEM((6, 1, count), F32),
            pltpu.SMEM((1,), F32),
            pltpu.SemaphoreType.DMA((4,)),
        ],
    )(
        positions.reshape(3, 1, electrons), moved, displacements.reshape(6, 1, count), log_weight
    )
    records = [lax.ppermute(record, "grp", pairs(n_grp, s)) for s in range(1, n_grp)]

    depth = electrons // chunks
    kept = shape((depth, electrons), BF16)
    token = shape((8, LANES), F32)
    own = list(
        call(
            round_kernel,
            (kept,) * chunks,
            [HBM, ANY],
            (VM,) * chunks,
            scratch=[
                pltpu.VMEM((chunks, depth, electrons), F32),
                pltpu.SemaphoreType.DMA((chunks,)),
            ],
            moved=6 * electrons * electrons,
            vmem=8,
        )(inverse, record)
    )
    own[0], own[-1], token_0 = call(
        gate_kernel,
        (kept, kept, token),
        [ANY] * (2 + others),
        (ANY, ANY, VM),
        aliases={0: 0, 1: 1},
        vmem=1,
    )(own[0], own[-1], *records)

    points, weight = call(
        functools.partial(points_kernel, count, others),
        (shape((n_orb, 8, LANES), F32), shape((1, LANES), F32)),
        [SM] + [VM] * (others + 3) + [ANY],
        (VM, VM),
    )(role, record, *records, tiled, disp, token_0)
    points = lax.all_to_all(points, "orb", split_axis=0, concat_axis=0, tiled=True)

    steps = [0] + [backward(n_grp, s) for s in range(1, n_grp)]
    columns = call(
        functools.partial(columns_kernel, count, others, chunks, steps),
        tuple(shape((2 * count, electrons), BF16) for _ in steps),
        [VM] * (chunks + 1 + others),
        tuple(VM for _ in steps),
        flops=2 * electrons * electrons * LANES,
        moved=2 * electrons * electrons,
        vmem=8,
    )(*own, tiled, *records)
    sent = [lax.ppermute(columns[s], "grp", pairs(n_grp, s)) for s in range(1, n_grp)]

    width = -(-local // LANES) * LANES
    coeff = jnp.pad(coefficients, ((0, 0), (0, width - local))) if width > local else coefficients
    derived = call(
        table_kernel,
        shape((plane, 5 * width), BF16),
        [VM, VM],
        VM,
        flops=8 * plane * width,
        moved=10 * plane * width,
        vmem=8,
    )(coeff, wavevectors)

    apart = apart.astype(jnp.int32).reshape(1)
    arrays = list(own)
    if n_grp == 4:
        send_x = lambda block: lax.ppermute(block, "grp", pairs(n_grp, 1))
        send_y = lambda block: lax.ppermute(block, "grp", pairs(n_grp, 2))

        def relay(mine, got, first):
            return call(
                relay_kernel,
                (kept, kept, token),
                [SM] + [ANY] * (4 + len(first)),
                (ANY, ANY, VM),
                scratch=[pltpu.SemaphoreType.DMA((2,))],
                aliases={3: 0, 4: 1},
                vmem=1,
            )(apart, *mine, *got, *first)

        x1, y1 = send_x(own[0]), send_y(own[3])
        y1, x1, token_1 = relay((own[1], own[2]), (y1, x1), (derived, columns[0], weight))
        x2, y2 = send_x(y1), send_y(x1)
        y2, x2, token_2 = relay((own[2], own[1]), (y2, x2), sent)
        x3, y3 = send_x(y2), send_y(x2)
        arrays += [x1, x2, x3, y1, y2, y3]
        a1, a2, a3, b1, b2, b3 = range(chunks, chunks + 6)
        table = [range(chunks), (a1, a2, a3, b3), (a3, b3, b2, b1), (b2, b3, a3, a2)]
    else:
        token_1 = token_2 = jnp.zeros((8, LANES), F32)
        table = [range(chunks)]
        for step in range(1, n_grp):
            table.append(range(len(arrays), len(arrays) + chunks))
            arrays += [lax.ppermute(block, "grp", pairs(n_grp, step)) for block in own]

    block = math.gcd(n_orb, 8)
    values = pl.pallas_call(
        functools.partial(evaluate_kernel, count),
        grid=(n_orb // block,),
        out_shape=shape((n_orb, 11 * count, width), BF16),
        in_specs=[
            pl.BlockSpec((block, 8, LANES), lambda i: (i, 0, 0)),
            pl.BlockSpec(wavevectors.shape, lambda i: (0, 0)),
            pl.BlockSpec(derived.shape, lambda i: (0, 0)),
            ANY,
        ],
        out_specs=pl.BlockSpec((block, 11 * count, width), lambda i: (i, 0, 0)),
        scratch_shapes=[
            pltpu.VMEM((block * 3 * count, plane), BF16),
            pltpu.VMEM((block * 2 * count, plane), BF16),
        ],
        compiler_params=pltpu.CompilerParams(vmem_limit_bytes=16 * MIB),
        cost_estimate=pl.CostEstimate(
            flops=2 * n_orb * count * plane * width * 11,
            bytes_accessed=12 * plane * width,
            transcendentals=0,
        ),
    )(points, wavevectors, derived, token_1)
    values = values[:, :, :local]
    values = lax.all_to_all(values, "orb", split_axis=0, concat_axis=0, tiled=True)
    if width > local:
        values = values.transpose(1, 0, 2).reshape(1, 11 * count, electrons)

    change, cols, small, drift, laplacian, new_weight = call(
        functools.partial(solve_kernel, count, others),
        (
            shape((2 * count, electrons), BF16),
            shape((2 * count, electrons), BF16),
            shape((2 * count, 2 * count), F32),
            shape((6, 1, count), F32),
            shape((2, 1, count), F32),
            shape((1, LANES), F32),
        ),
        [SM] + [VM] * (others + 3) + [ANY],
        (VM,) * 6,
        scratch=[pltpu.VMEM((11 * count, electrons), BF16)],
        flops=2 * electrons * count * count * 16,
        moved=4 * 11 * count * electrons,
    )(role, values, columns[0], *sent, weight, token_2)

    updated = call(
        functools.partial(finish_kernel, table, chunks),
        shape((electrons, electrons), F32),
        [SM, VM, VM, VM] + [ANY] * len(arrays),
        ANY,
        scratch=[
            pltpu.VMEM((chunks, depth, electrons), BF16),
            pltpu.VMEM((chunks, depth, electrons), F32),
            pltpu.SemaphoreType.DMA((chunks,)),
            pltpu.SemaphoreType.DMA((chunks,)),
        ],
        flops=4 * electrons * electrons * 2 * count,
        moved=6 * electrons * electrons,
        vmem=12,
    )(role, change, cols, small, *arrays)

    return updated[None], drift.reshape(2, 1, 3, count), laplacian, new_weight[0, :1]


def solution(mesh):
    split = ("grp", "orb")
    return jax.shard_map(
        functools.partial(per_device, mesh.shape["grp"], mesh.shape["orb"]),
        mesh=mesh,
        in_specs=(
            P(),
            P(None, "orb"),
            P(split, None, None),
            P(split, None, None),
            P(None, split, None, None),
            P(None, split, None),
            P("orb"),
            P(split),
            P(split),
        ),
        out_specs=(
            P(split, None, None),
            P(None, split, None, None),
            P(None, split, None),
            P(split),
        ),
        check_vma=False,
    )
```

```python
import functools
import math

import jax
import jax.numpy as jnp
from jax import lax
from jax.experimental import pallas as pl
from jax.experimental.pallas import tpu as pltpu
from jax.sharding import PartitionSpec as P

F32 = jnp.float32
BF16 = jnp.bfloat16
LANES = 128
MIB = 1024 * 1024
precise = lax.Precision.HIGHEST

SIN_HALF = (4.4428679, -7.30744342, 3.59478808, -0.78437403)
COS_HALF = (1.4142135, -6.97885099, 5.73946117, -1.88356299, 0.31069819)


def dot(a, b, dims=((1,), (0,)), exact=False):
    return lax.dot_general(
        a, b, (dims, ((), ())), precision=precise if exact else None, preferred_element_type=F32
    )


def iota(shape, dim):
    return lax.broadcasted_iota(jnp.int32, shape, dim)


def call(
    kernel, out_shape, in_specs, out_specs, scratch=(), flops=0, moved=0, vmem=4, aliases=None
):
    return pl.pallas_call(
        kernel,
        out_shape=out_shape,
        input_output_aliases=aliases or {},
        in_specs=in_specs,
        out_specs=out_specs,
        scratch_shapes=list(scratch),
        compiler_params=pltpu.CompilerParams(vmem_limit_bytes=vmem * MIB),
        cost_estimate=pl.CostEstimate(flops=flops, bytes_accessed=moved, transcendentals=0),
    )


VM = pl.BlockSpec(memory_space=pltpu.VMEM)
SM = pl.BlockSpec(memory_space=pltpu.SMEM)
ANY = pl.BlockSpec(memory_space=pl.ANY)
HBM = pl.BlockSpec(memory_space=pltpu.HBM)


def shape(dims, dtype):
    return jax.ShapeDtypeStruct(dims, dtype)


def in_hbm(*arrays):
    return tuple(pltpu.with_memory_space_constraint(a, pltpu.HBM) for a in arrays)


def is_power(n):
    return n & (n - 1) == 0


def pairs(n, step):
    if is_power(n):
        return [(i, i ^ step) for i in range(n)]
    return [(i, (i + step) % n) for i in range(n)]


def distance(n, here, there):
    return here ^ there if is_power(n) else lax.rem(here - there + n, n)


def backward(n, step):
    return step if is_power(n) else (n - step) % n


def start_kernel(
    count,
    pos_hbm,
    moved_hbm,
    disp_hbm,
    weight_ref,
    out_ref,
    tiled_ref,
    shift_ref,
    pos_ref,
    moved_ref,
    disp_ref,
    sems,
):
    loads = [
        pltpu.make_async_copy(src, dst, sems.at[i])
        for i, (src, dst) in enumerate(
            (
                (moved_hbm, moved_ref),
                (disp_hbm, disp_ref),
                (pos_hbm, pos_ref),
            )
        )
    ]
    for load in loads:
        load.start()
    electrons = pos_ref.shape[2]
    copies = LANES // count
    loads[0].wait()
    tiled = jnp.concatenate([moved_ref[:, 0, :]] * copies, 1)
    tiled_ref[...] = tiled
    pick = (iota((electrons, LANES), 0) == tiled[0:1, :]).astype(F32)
    block = iota((8, LANES), 1) // count
    zeros = jnp.zeros((5, LANES), F32)
    loads[1].wait()
    for update in range(2):
        shift = jnp.concatenate([disp_ref[3 * update : 3 * update + 3, 0, :]] * copies, 1)
        shift_ref[update] = jnp.concatenate([shift, zeros], 0)
    loads[2].wait()
    pos = jnp.concatenate([pos_ref[:, 0, :], jnp.zeros((5, electrons), F32)], 0)
    old = dot(pos, pick, exact=True)
    disp = shift_ref[0]
    points = old + jnp.where(block % 2 == 1, disp, 0.0)
    first = jnp.where(block == 0, disp, 0.0)
    out_ref[...] = pos + dot(first, pick, ((1,), (1,)), exact=True)
    out_ref[3:6, 0:LANES] = points[0:3]
    out_ref[6:7, 0:LANES] = tiled[1:2, :].astype(F32)
    out_ref[7:8, 0:LANES] = jnp.full((1, LANES), weight_ref[0], F32)


def round_kernel(inverse_ref, after_ref, *refs):
    outs = refs[:-2]
    staged, sem = refs[-2:]
    depth = staged.shape[1]
    copies = []
    for chunk in range(len(outs)):
        rows = inverse_ref.at[0, pl.ds(chunk * depth, depth)]
        copy = pltpu.make_async_copy(rows, staged.at[chunk], sem.at[chunk])
        copy.start()
        copies.append(copy)
    for chunk, out in enumerate(outs):
        copies[chunk].wait()
        out[...] = staged[chunk].astype(BF16)


def gate_kernel(*refs):
    token_ref = refs[-1]
    token_ref[...] = jnp.zeros(token_ref.shape, F32)


def relay_kernel(flag_ref, own_a, own_b, got_a, got_b, *refs):
    out_a, out_b, token_ref, sems = refs[-4:]

    @pl.when(flag_ref[0] == 0)
    def _():
        copies = [
            pltpu.make_async_copy(own_a, out_a, sems.at[0]),
            pltpu.make_async_copy(own_b, out_b, sems.at[1]),
        ]
        for copy in copies:
            copy.start()
        for copy in copies:
            copy.wait()

    token_ref[...] = jnp.zeros(token_ref.shape, F32)


def points_kernel(count, others, role_ref, *refs):
    own_ref = refs[0]
    received = refs[1 : 1 + others]
    moved_ref, disp_ref, after_ref, points_ref, weight_ref = refs[1 + others :]
    role = role_ref[0]
    parent = own_ref[...]
    for step in range(others):
        parent = jnp.where(role == step + 1, received[step][...], parent)
    electrons = parent.shape[1]
    pick = (iota((electrons, LANES), 0) == moved_ref[1:2, :]).astype(F32)
    block = iota((8, LANES), 1) // count
    old = dot(parent, pick, exact=True)
    later = old + jnp.where(block % 2 == 1, disp_ref[1], 0.0)
    zeros = jnp.zeros((5, LANES), F32)
    mine = jnp.concatenate([own_ref[3:6, 0:LANES], zeros], 0)
    theirs = jnp.concatenate([parent[3:6, 0:LANES], zeros], 0)
    points = jnp.where(block < 2, mine, jnp.where(block < 4, theirs, later))
    points_ref[...] = jnp.broadcast_to(points[None], points_ref.shape)
    weight_ref[...] = parent[7:8, 0:LANES]


def columns_kernel(count, others, chunks, steps, *refs):
    chunk_refs = refs[:chunks]
    moved_ref = refs[chunks]
    received = refs[chunks + 1 : chunks + 1 + others]
    outs = refs[chunks + 1 + others :]
    depth = chunk_refs[0].shape[0]
    electrons = chunk_refs[0].shape[1]
    block = iota((1, LANES), 1) // count
    wanted = jnp.where(block == 0, moved_ref[0:1, :], moved_ref[1:2, :])
    for step in range(others):
        theirs = received[step][6:7, 0:LANES].astype(jnp.int32)
        wanted = jnp.where(block == 2 + step, theirs, wanted)
    pick = (iota((electrons, LANES), 0) == wanted).astype(F32).astype(BF16)
    for chunk in range(chunks):
        rows = slice(chunk * depth, (chunk + 1) * depth)
        found = dot(chunk_refs[chunk][...], pick)
        turned = jnp.transpose(found).astype(BF16)
        for out, step in zip(outs, steps):
            out[0:count, rows] = turned[0:count]
            out[count : 2 * count, rows] = turned[(1 + step) * count : (2 + step) * count]


def table_kernel(coeff_hbm, wave_hbm, out_ref, coeff_ref, wave_ref, sems):
    loads = [
        pltpu.make_async_copy(wave_hbm, wave_ref, sems.at[0]),
        pltpu.make_async_copy(coeff_hbm, coeff_ref, sems.at[1]),
    ]
    for load in loads:
        load.start()
    for load in loads:
        load.wait()
    waves = wave_ref.shape[1]
    width = coeff_ref.shape[1]
    wave = jnp.transpose(jnp.concatenate([wave_ref[...], jnp.zeros((5, waves), F32)], 0))
    out_ref[:, 0:width] = coeff_ref[...]
    cos_part = coeff_ref[0:waves].astype(F32)
    sin_part = coeff_ref[waves:].astype(F32)
    squared = None
    for a in range(3):
        scale = wave[:, a : a + 1]
        where = slice((a + 1) * width, (a + 2) * width)
        out_ref[0:waves, where] = (scale * sin_part).astype(BF16)
        out_ref[waves:, where] = (-scale * cos_part).astype(BF16)
        squared = scale * scale if a == 0 else squared + scale * scale
    where = slice(4 * width, 5 * width)
    out_ref[0:waves, where] = (-squared * cos_part).astype(BF16)
    out_ref[waves:, where] = (-squared * sin_part).astype(BF16)


def horner(coefs, u):
    value = coefs[-1] * u + coefs[-2]
    for c in reversed(coefs[:-2]):
        value = value * u + c
    return value


def evaluate_kernel(
    count, points_ref, wave_ref, table_ref, after_ref, out_ref, diff, new
):
    walkers = points_ref.shape[0]
    waves = wave_ref.shape[1]
    width = table_ref.shape[1] // 5
    step = math.gcd(waves, LANES)

    def one(w, carry):
        column = jnp.transpose(points_ref[w])
        xs = [column[0 : 6 * count, a : a + 1] for a in range(3)]
        row_d = pl.multiple_of(w * (3 * count), count)
        row_n = pl.multiple_of(w * (2 * count), count)
        for at in range(0, waves, step):
            ks = [wave_ref[a : a + 1, at : at + step] * (0.5 / math.pi) for a in range(3)]
            turn = xs[0] * ks[0] + xs[1] * ks[1] + xs[2] * ks[2]
            r = turn - jnp.floor(turn + 0.5)
            u = r * r
            s = r * horner(SIN_HALF, u)
            c = horner(COS_HALF, u)
            for value, base in ((1.0 - s * s, 0), (s * c, waves)):
                where = slice(base + at, base + at + step)
                kept = value.astype(BF16)
                wide = kept.astype(F32)
                part = [wide[i * count : (i + 1) * count] for i in range(6)]
                diff[pl.ds(row_d, count), where] = (part[3] - part[2]).astype(BF16)
                diff[pl.ds(row_d + count, count), where] = (part[5] - part[4]).astype(BF16)
                diff[pl.ds(row_d + 2 * count, count), where] = (part[1] - part[0]).astype(BF16)
                new[pl.ds(row_n, count), where] = kept[5 * count : 6 * count]
                new[pl.ds(row_n + count, count), where] = kept[count : 2 * count]
        return carry

    lax.fori_loop(0, walkers, one, 0)
    change = dot(diff[...], table_ref[:, 0:width]).astype(BF16)
    rest = dot(new[...], table_ref[:, width:]).astype(BF16)
    for w in range(walkers):
        at = w * 3 * count
        out_ref[w, 0 : 2 * count] = change[at : at + 2 * count]
        out_ref[w, 6 * count : 7 * count] = change[at + 2 * count : at + 3 * count]
        for half, base in ((0, 2 * count), (1, 7 * count)):
            row = (2 * w + half) * count
            for a in range(4):
                out_ref[w, base + a * count : base + (a + 1) * count] = rest[
                    row : row + count, a * width : (a + 1) * width
                ]


def sweep(matrices):
    matrices = list(matrices)
    logs = [jnp.zeros((1, 1), F32) for _ in matrices]
    for k in range(max(m.shape[0] for m in matrices)):
        for which, matrix in enumerate(matrices):
            size = matrix.shape[0]
            if k >= size:
                continue
            pivot = matrix[k : k + 1, k : k + 1]
            inverse = 1.0 / pivot
            column = matrix[:, k : k + 1]
            line = matrix[k : k + 1, :]
            row_here = iota((size, size), 0) == k
            lane_here = iota((size, size), 1) == k
            scaled = line * inverse
            reduced = matrix - column * scaled
            matrix = jnp.where(row_here, scaled, jnp.where(lane_here, column * inverse, reduced))
            matrix = jnp.where(jnp.logical_and(row_here, lane_here), -inverse, matrix)
            matrices[which] = matrix
            logs[which] = logs[which] + jnp.log(pivot)
    return [-m for m in matrices], logs


def solve_kernel(count, others, role_ref, vals_ref, own_ref, *refs):
    received = refs[:others]
    weight_ref, after_ref = refs[others : others + 2]
    change_ref, cols_ref, inv_ref, drift_ref, lap_ref, out_weight_ref, vals = refs[others + 2 :]
    pieces, _, width = vals_ref.shape
    for o in range(pieces):
        vals[:, o * width : (o + 1) * width] = vals_ref[o]
    role = role_ref[0]
    cols = own_ref[...].astype(F32)
    for step in range(others):
        cols = jnp.where(role == step + 1, received[step][...].astype(F32), cols)
    cols = cols.astype(BF16)
    cols_ref[...] = cols
    change_ref[...] = vals[0 : 2 * count]
    own = own_ref[0:count]
    products, ratios, normal = [], [], []
    for size, matrix, part in (
        (count, own, vals[6 * count : 11 * count]),
        (2 * count, cols, vals[0 : 6 * count]),
    ):
        product = dot(matrix, part, ((1,), (1,)))
        ratio = product[:, 0:size] + jnp.where(iota((size, size), 0) == iota((size, size), 1), 1.0, 0.0)
        products.append(product[:, size:])
        ratios.append(ratio)
        normal.append(dot(ratio, ratio, ((1,), (1,)), exact=True))
    inverses, logs = sweep(normal)
    for update, (inverse, ratio, product) in enumerate(zip(inverses, ratios, products)):
        size = ratio.shape[0]
        wide = product.shape[1]
        small = dot(inverse, ratio, exact=True)
        tile = jnp.where(iota((size, wide), 0) == size - count + iota((size, wide), 1) % count, 1.0, 0.0)
        spread = dot(small, tile, exact=True)
        sums = jnp.sum(product * spread, axis=0, keepdims=True)
        for a in range(3):
            drift_ref[3 * update + a] = sums[:, a * count : (a + 1) * count]
        lap_ref[update] = sums[:, 3 * count : 4 * count]
    inv_ref[...] = small
    out_weight_ref[...] = weight_ref[...] + 0.5 * logs[1]


def finish_kernel(sources, chunks, role_ref, change_ref, cols_ref, inv_ref, *refs):
    inputs = refs[:-5]
    out_ref, parent, staged, in_sem, out_sem = refs[-5:]
    depth = inputs[0].shape[0]
    role = role_ref[0]
    for chunk in range(chunks):
        for which, table in enumerate(sources):

            @pl.when(role == which)
            def _():
                pltpu.make_async_copy(
                    inputs[table[chunk]], parent.at[chunk], in_sem.at[chunk]
                ).start()

    total = jnp.zeros((change_ref.shape[0], inputs[0].shape[1]), F32)
    for chunk in range(chunks):
        pltpu.make_async_copy(inputs[chunk], parent.at[chunk], in_sem.at[chunk]).wait()
        total = total + dot(change_ref[:, chunk * depth : (chunk + 1) * depth], parent[chunk])
    solved = dot(inv_ref[...], total, exact=True).astype(BF16)
    copies = []
    for chunk in range(chunks):
        rows = slice(chunk * depth, (chunk + 1) * depth)
        columns = jnp.transpose(cols_ref[:, rows].astype(F32)).astype(BF16)
        staged[chunk] = parent[chunk].astype(F32) - dot(columns, solved)
        copy = pltpu.make_async_copy(staged.at[chunk], out_ref.at[rows], out_sem.at[chunk])
        copy.start()
        copies.append(copy)
    for copy in copies:
        copy.wait()


def per_device(
    n_grp,
    n_orb,
    wavevectors,
    coefficients,
    inverse,
    positions,
    displacements,
    moved,
    donor,
    take,
    log_weight,
):
    electrons = inverse.shape[1]
    count = moved.shape[2]
    plane = coefficients.shape[0]
    local = coefficients.shape[1]
    others = n_grp - 1
    chunks = 4
    group = lax.axis_index("grp")
    source = donor[0]
    apart = distance(n_grp, group, source)
    role = jnp.where(take[0] == 1, apart, 0).astype(jnp.int32).reshape(1)

    record, tiled, disp = call(
        functools.partial(start_kernel, count),
        (
            shape((8, electrons), F32),
            shape((2, LANES), jnp.int32),
            shape((2, 8, LANES), F32),
        ),
        [HBM, HBM, HBM, SM],
        (VM, VM, VM),
        scratch=[
            pltpu.VMEM((3, 1, electrons), F32),
            pltpu.VMEM((2, 1, count), jnp.int32),
            pltpu.VMEM((6, 1, count), F32),
            pltpu.SemaphoreType.DMA((3,)),
        ],
    )(
        *in_hbm(
            positions.reshape(3, 1, electrons), moved, displacements.reshape(6, 1, count)
        ),
        log_weight,
    )
    records = [lax.ppermute(record, "grp", pairs(n_grp, s)) for s in range(1, n_grp)]

    depth = electrons // chunks
    kept = shape((depth, electrons), BF16)
    token = shape((8, LANES), F32)
    own = list(
        call(
            round_kernel,
            (kept,) * chunks,
            [HBM, ANY],
            (VM,) * chunks,
            scratch=[
                pltpu.VMEM((chunks, depth, electrons), F32),
                pltpu.SemaphoreType.DMA((chunks,)),
            ],
            moved=6 * electrons * electrons,
            vmem=8,
        )(*in_hbm(inverse), record)
    )
    own[0], own[-1], token_0 = call(
        gate_kernel,
        (kept, kept, token),
        [ANY] * (2 + others),
        (ANY, ANY, VM),
        aliases={0: 0, 1: 1},
        vmem=1,
    )(own[0], own[-1], *records)

    points, weight = call(
        functools.partial(points_kernel, count, others),
        (shape((n_orb, 8, LANES), F32), shape((1, LANES), F32)),
        [SM] + [VM] * (others + 3) + [ANY],
        (VM, VM),
    )(role, record, *records, tiled, disp, token_0)
    points = lax.all_to_all(points, "orb", split_axis=0, concat_axis=0, tiled=True)

    steps = [0] + [backward(n_grp, s) for s in range(1, n_grp)]
    columns = call(
        functools.partial(columns_kernel, count, others, chunks, steps),
        tuple(shape((2 * count, electrons), BF16) for _ in steps),
        [VM] * (chunks + 1 + others),
        tuple(VM for _ in steps),
        flops=2 * electrons * electrons * LANES,
        moved=2 * electrons * electrons,
        vmem=8,
    )(*own, tiled, *records)
    sent = [lax.ppermute(columns[s], "grp", pairs(n_grp, s)) for s in range(1, n_grp)]

    width = -(-local // LANES) * LANES
    coeff = jnp.pad(coefficients, ((0, 0), (0, width - local))) if width > local else coefficients
    derived = call(
        table_kernel,
        shape((plane, 5 * width), BF16),
        [HBM, HBM],
        VM,
        scratch=[
            pltpu.VMEM((plane, width), BF16),
            pltpu.VMEM(wavevectors.shape, F32),
            pltpu.SemaphoreType.DMA((2,)),
        ],
        flops=8 * plane * width,
        moved=10 * plane * width,
        vmem=8,
    )(*in_hbm(coeff, wavevectors))

    apart = apart.astype(jnp.int32).reshape(1)
    arrays = list(own)
    if n_grp == 4:
        send_x = lambda block: lax.ppermute(block, "grp", pairs(n_grp, 1))
        send_y = lambda block: lax.ppermute(block, "grp", pairs(n_grp, 2))

        def relay(mine, got, first):
            return call(
                relay_kernel,
                (kept, kept, token),
                [SM] + [ANY] * (4 + len(first)),
                (ANY, ANY, VM),
                scratch=[pltpu.SemaphoreType.DMA((2,))],
                aliases={3: 0, 4: 1},
                vmem=1,
            )(apart, *mine, *got, *first)

        x1, y1 = send_x(own[0]), send_y(own[3])
        y1, x1, token_1 = relay((own[1], own[2]), (y1, x1), (derived, points, *sent))
        x2, y2 = send_x(y1), send_y(x1)
        y2, x2, token_2 = relay((own[2], own[1]), (y2, x2), ())
        x3, y3 = send_x(y2), send_y(x2)
        arrays += [x1, x2, x3, y1, y2, y3]
        a1, a2, a3, b1, b2, b3 = range(chunks, chunks + 6)
        table = [range(chunks), (a1, a2, a3, b3), (a3, b3, b2, b1), (b2, b3, a3, a2)]
    else:
        token_1 = token_2 = jnp.zeros((8, LANES), F32)
        table = [range(chunks)]
        for step in range(1, n_grp):
            table.append(range(len(arrays), len(arrays) + chunks))
            arrays += [lax.ppermute(block, "grp", pairs(n_grp, step)) for block in own]

    block = math.gcd(n_orb, 8)
    values = pl.pallas_call(
        functools.partial(evaluate_kernel, count),
        grid=(n_orb // block,),
        out_shape=shape((n_orb, 11 * count, width), BF16),
        in_specs=[
            pl.BlockSpec((block, 8, LANES), lambda i: (i, 0, 0)),
            pl.BlockSpec(wavevectors.shape, lambda i: (0, 0)),
            pl.BlockSpec(derived.shape, lambda i: (0, 0)),
            ANY,
        ],
        out_specs=pl.BlockSpec((block, 11 * count, width), lambda i: (i, 0, 0)),
        scratch_shapes=[
            pltpu.VMEM((block * 3 * count, plane), BF16),
            pltpu.VMEM((block * 2 * count, plane), BF16),
        ],
        compiler_params=pltpu.CompilerParams(vmem_limit_bytes=16 * MIB),
        cost_estimate=pl.CostEstimate(
            flops=2 * n_orb * count * plane * width * 11,
            bytes_accessed=12 * plane * width,
            transcendentals=0,
        ),
    )(points, wavevectors, derived, token_1)
    values = values[:, :, :local]
    values = lax.all_to_all(values, "orb", split_axis=0, concat_axis=0, tiled=True)
    if width > local:
        values = values.transpose(1, 0, 2).reshape(1, 11 * count, electrons)

    change, cols, small, drift, laplacian, new_weight = call(
        functools.partial(solve_kernel, count, others),
        (
            shape((2 * count, electrons), BF16),
            shape((2 * count, electrons), BF16),
            shape((2 * count, 2 * count), F32),
            shape((6, 1, count), F32),
            shape((2, 1, count), F32),
            shape((1, LANES), F32),
        ),
        [SM] + [VM] * (others + 3) + [ANY],
        (VM,) * 6,
        scratch=[pltpu.VMEM((11 * count, electrons), BF16)],
        flops=2 * electrons * count * count * 16,
        moved=4 * 11 * count * electrons,
    )(role, values, columns[0], *sent, weight, token_2)

    updated = call(
        functools.partial(finish_kernel, table, chunks),
        shape((electrons, electrons), F32),
        [SM, VM, VM, VM] + [ANY] * len(arrays),
        ANY,
        scratch=[
            pltpu.VMEM((chunks, depth, electrons), BF16),
            pltpu.VMEM((chunks, depth, electrons), F32),
            pltpu.SemaphoreType.DMA((chunks,)),
            pltpu.SemaphoreType.DMA((chunks,)),
        ],
        flops=4 * electrons * electrons * 2 * count,
        moved=6 * electrons * electrons,
        vmem=12,
    )(role, change, cols, small, *arrays)

    return updated[None], drift.reshape(2, 1, 3, count), laplacian, new_weight[0, :1]


def solution(mesh):
    split = ("grp", "orb")
    return jax.shard_map(
        functools.partial(per_device, mesh.shape["grp"], mesh.shape["orb"]),
        mesh=mesh,
        in_specs=(
            P(),
            P(None, "orb"),
            P(split, None, None),
            P(split, None, None),
            P(None, split, None, None),
            P(None, split, None),
            P("orb"),
            P(split),
            P(split),
        ),
        out_specs=(
            P(split, None, None),
            P(None, split, None, None),
            P(None, split, None),
            P(split),
        ),
        check_vma=False,
    )
```

```python
import functools
import math

import jax
import jax.numpy as jnp
from jax import lax
from jax.experimental import pallas as pl
from jax.experimental.pallas import tpu as pltpu
from jax.sharding import PartitionSpec as P

F32 = jnp.float32
BF16 = jnp.bfloat16
LANES = 128
ROWS = 16
MIB = 1024 * 1024
precise = lax.Precision.HIGHEST

SIN_HALF = (4.4428679, -7.30744342, 3.59478808, -0.78437403)
COS_HALF = (1.4142135, -6.97885099, 5.73946117, -1.88356299, 0.31069819)


def dot(a, b, dims=((1,), (0,)), exact=False):
    return lax.dot_general(
        a, b, (dims, ((), ())), precision=precise if exact else None, preferred_element_type=F32
    )


def iota(shape, dim):
    return lax.broadcasted_iota(jnp.int32, shape, dim)


def call(
    kernel, out_shape, in_specs, out_specs, scratch=(), flops=0, moved=0, vmem=4, aliases=None
):
    return pl.pallas_call(
        kernel,
        out_shape=out_shape,
        input_output_aliases=aliases or {},
        in_specs=in_specs,
        out_specs=out_specs,
        scratch_shapes=list(scratch),
        compiler_params=pltpu.CompilerParams(vmem_limit_bytes=vmem * MIB),
        cost_estimate=pl.CostEstimate(flops=flops, bytes_accessed=moved, transcendentals=0),
    )


VM = pl.BlockSpec(memory_space=pltpu.VMEM)
SM = pl.BlockSpec(memory_space=pltpu.SMEM)
ANY = pl.BlockSpec(memory_space=pl.ANY)
HBM = pl.BlockSpec(memory_space=pltpu.HBM)


def shape(dims, dtype):
    return jax.ShapeDtypeStruct(dims, dtype)


def in_hbm(*arrays):
    return tuple(pltpu.with_memory_space_constraint(a, pltpu.HBM) for a in arrays)


def is_power(n):
    return n & (n - 1) == 0


def pairs(n, step):
    if is_power(n):
        return [(i, i ^ step) for i in range(n)]
    return [(i, (i + step) % n) for i in range(n)]


def distance(n, here, there):
    return here ^ there if is_power(n) else lax.rem(here - there + n, n)


def backward(n, step):
    return step if is_power(n) else (n - step) % n


def start_kernel(
    count,
    pos_hbm,
    moved_hbm,
    disp_hbm,
    weight_ref,
    out_ref,
    tiled_ref,
    shift_ref,
    pos_ref,
    moved_ref,
    disp_ref,
    sems,
):
    loads = [
        pltpu.make_async_copy(src, dst, sems.at[i])
        for i, (src, dst) in enumerate(
            (
                (moved_hbm, moved_ref),
                (disp_hbm, disp_ref),
                (pos_hbm, pos_ref),
            )
        )
    ]
    for load in loads:
        load.start()
    electrons = pos_ref.shape[2]
    copies = LANES // count
    loads[0].wait()
    tiled = jnp.concatenate([moved_ref[:, 0, :]] * copies, 1)
    tiled_ref[...] = tiled
    pick = (iota((electrons, LANES), 0) == tiled[0:1, :]).astype(F32)
    block = iota((8, LANES), 1) // count
    zeros = jnp.zeros((5, LANES), F32)
    loads[1].wait()
    for update in range(2):
        shift = jnp.concatenate([disp_ref[3 * update : 3 * update + 3, 0, :]] * copies, 1)
        shift_ref[update] = jnp.concatenate([shift, zeros], 0)
    loads[2].wait()
    pos = jnp.concatenate([pos_ref[:, 0, :], jnp.zeros((5, electrons), F32)], 0)
    old = dot(pos, pick, exact=True)
    disp = shift_ref[0]
    points = old + jnp.where(block % 2 == 1, disp, 0.0)
    first = jnp.where(block == 0, disp, 0.0)
    out_ref[...] = pos + dot(first, pick, ((1,), (1,)), exact=True)
    out_ref[3:6, 0:LANES] = points[0:3]
    out_ref[6:7, 0:LANES] = tiled[1:2, :].astype(F32)
    out_ref[7:8, 0:LANES] = jnp.full((1, LANES), weight_ref[0], F32)


def rows_of(ref, chunk, depth):
    return ref.at[0, pl.ds(chunk * depth, depth)]


def round_kernel(wanted, inverse_hbm, after_ref, *refs):
    outs = refs[: len(wanted)]
    staged, rounded, in_sem, out_sem = refs[len(wanted) :]
    depth = staged.shape[1]
    loads, stores = [], []
    for slot, chunk in enumerate(wanted):
        load = pltpu.make_async_copy(
            rows_of(inverse_hbm, chunk, depth), staged.at[slot], in_sem.at[slot]
        )
        load.start()
        loads.append(load)
    for slot, out in enumerate(outs):
        loads[slot].wait()
        rounded[slot] = staged[slot].astype(BF16)
        store = pltpu.make_async_copy(rounded.at[slot], out, out_sem.at[slot])
        store.start()
        stores.append(store)
    for store in stores:
        store.wait()


def gate_kernel(*refs):
    token_ref = refs[-1]
    token_ref[...] = jnp.zeros(token_ref.shape, F32)


def relay_kernel(flag_ref, own_a, own_b, got_a, got_b, *refs):
    out_a, out_b, token_ref, sems = refs[-4:]
    for here, pair in ((True, (own_a, own_b)), (False, (got_a, got_b))):

        @pl.when((flag_ref[0] == 0) == here)
        def _():
            copies = [
                pltpu.make_async_copy(pair[0], out_a, sems.at[0]),
                pltpu.make_async_copy(pair[1], out_b, sems.at[1]),
            ]
            for copy in copies:
                copy.start()
            for copy in copies:
                copy.wait()

    token_ref[...] = jnp.zeros(token_ref.shape, F32)


def points_kernel(count, others, role_ref, *refs):
    own_ref = refs[0]
    received = refs[1 : 1 + others]
    moved_ref, disp_ref, after_ref, points_ref, weight_ref = refs[1 + others :]
    role = role_ref[0]
    parent = own_ref[...]
    for step in range(others):
        parent = jnp.where(role == step + 1, received[step][...], parent)
    electrons = parent.shape[1]
    pick = (iota((electrons, LANES), 0) == moved_ref[1:2, :]).astype(F32)
    block = iota((8, LANES), 1) // count
    old = dot(parent, pick, exact=True)
    later = old + jnp.where(block % 2 == 1, disp_ref[1], 0.0)
    zeros = jnp.zeros((5, LANES), F32)
    mine = jnp.concatenate([own_ref[3:6, 0:LANES], zeros], 0)
    theirs = jnp.concatenate([parent[3:6, 0:LANES], zeros], 0)
    points = jnp.where(block < 2, mine, jnp.where(block < 4, theirs, later))
    points = jnp.concatenate([points, jnp.zeros((ROWS - 8, LANES), F32)], 0)
    points_ref[...] = jnp.broadcast_to(points[None], points_ref.shape)
    weight_ref[...] = parent[7:8, 0:LANES]


def derive(coeff_ref, wave_ref, out_ref):
    waves = wave_ref.shape[1]
    width = coeff_ref.shape[1]
    wave = jnp.transpose(jnp.concatenate([wave_ref[...], jnp.zeros((5, waves), F32)], 0))
    out_ref[:, 0:width] = coeff_ref[...]
    cos_part = coeff_ref[0:waves].astype(F32)
    sin_part = coeff_ref[waves:].astype(F32)
    squared = None
    for a in range(3):
        scale = wave[:, a : a + 1]
        where = slice((a + 1) * width, (a + 2) * width)
        out_ref[0:waves, where] = (scale * sin_part).astype(BF16)
        out_ref[waves:, where] = (-scale * cos_part).astype(BF16)
        squared = scale * scale if a == 0 else squared + scale * scale
    where = slice(4 * width, 5 * width)
    out_ref[0:waves, where] = (-squared * cos_part).astype(BF16)
    out_ref[waves:, where] = (-squared * sin_part).astype(BF16)


def prepare_kernel(
    count, others, chunks, wanted, steps, coeff_hbm, wave_hbm, inverse_hbm, moved_ref, *refs
):
    received = refs[:others]
    table_ref = refs[others + 1]
    outs = refs[others + 2 : others + 2 + len(wanted)]
    columns = refs[others + 2 + len(wanted) : -7]
    coeff_ref, wave_ref, staged, rounded, small_sem, in_sem, out_sem = refs[-7:]
    depth, electrons = staged.shape[1:]
    wave_load = pltpu.make_async_copy(wave_hbm, wave_ref, small_sem.at[0])
    coeff_load = pltpu.make_async_copy(coeff_hbm, coeff_ref, small_sem.at[1])
    wave_load.start()
    coeff_load.start()
    loads, stores = [], []
    for chunk in range(chunks):
        load = pltpu.make_async_copy(
            rows_of(inverse_hbm, chunk, depth), staged.at[chunk], in_sem.at[chunk]
        )
        load.start()
        loads.append(load)
    block = iota((1, LANES), 1) // count
    number = jnp.where(block == 0, moved_ref[0:1, :], moved_ref[1:2, :])
    for step in range(others):
        theirs = received[step][6:7, 0:LANES].astype(jnp.int32)
        number = jnp.where(block == 2 + step, theirs, number)
    pick = (iota((electrons, LANES), 0) == number).astype(F32).astype(BF16)
    wave_load.wait()
    coeff_load.wait()
    derive(coeff_ref, wave_ref, table_ref)
    for chunk in range(chunks):
        rows = slice(chunk * depth, (chunk + 1) * depth)
        loads[chunk].wait()
        rounded[chunk] = staged[chunk].astype(BF16)
        if chunk in wanted:
            slot = wanted.index(chunk)
            store = pltpu.make_async_copy(rounded.at[chunk], outs[slot], out_sem.at[slot])
            store.start()
            stores.append(store)
        turned = jnp.transpose(dot(rounded[chunk], pick)).astype(BF16)
        for out, step in zip(columns, steps):
            out[0:count, rows] = turned[0:count]
            out[count : 2 * count, rows] = turned[(1 + step) * count : (2 + step) * count]
    for store in stores:
        store.wait()


def horner(coefs, u):
    value = coefs[-1] * u + coefs[-2]
    for c in reversed(coefs[:-2]):
        value = value * u + c
    return value


def evaluate_kernel(count, points_ref, wave_ref, table_ref, *refs):
    out_ref, diff, new = refs[-3:]
    walkers = points_ref.shape[0]
    waves = wave_ref.shape[1]
    width = table_ref.shape[1] // 5
    step = math.gcd(waves, LANES)

    def one(w, carry):
        column = jnp.transpose(points_ref[w, 0:8])
        xs = [column[0 : 6 * count, a : a + 1] for a in range(3)]
        row_d = pl.multiple_of(w * (3 * count), count)
        row_n = pl.multiple_of(w * (2 * count), count)
        for at in range(0, waves, step):
            ks = [wave_ref[a : a + 1, at : at + step] * (0.5 / math.pi) for a in range(3)]
            turn = xs[0] * ks[0] + xs[1] * ks[1] + xs[2] * ks[2]
            r = turn - jnp.floor(turn + 0.5)
            u = r * r
            s = r * horner(SIN_HALF, u)
            c = horner(COS_HALF, u)
            for value, base in ((1.0 - s * s, 0), (s * c, waves)):
                where = slice(base + at, base + at + step)
                kept = value.astype(BF16)
                wide = kept.astype(F32)
                part = [wide[i * count : (i + 1) * count] for i in range(6)]
                diff[pl.ds(row_d, count), where] = (part[3] - part[2]).astype(BF16)
                diff[pl.ds(row_d + count, count), where] = (part[5] - part[4]).astype(BF16)
                diff[pl.ds(row_d + 2 * count, count), where] = (part[1] - part[0]).astype(BF16)
                new[pl.ds(row_n, count), where] = kept[5 * count : 6 * count]
                new[pl.ds(row_n + count, count), where] = kept[count : 2 * count]
        return carry

    lax.fori_loop(0, walkers, one, 0)
    change = dot(diff[...], table_ref[:, 0:width]).astype(BF16)
    rest = dot(new[...], table_ref[:, width:]).astype(BF16)
    for w in range(walkers):
        at = w * 3 * count
        out_ref[w, 0 : 2 * count] = change[at : at + 2 * count]
        out_ref[w, 6 * count : 7 * count] = change[at + 2 * count : at + 3 * count]
        for half, base in ((0, 2 * count), (1, 7 * count)):
            row = (2 * w + half) * count
            for a in range(4):
                out_ref[w, base + a * count : base + (a + 1) * count] = rest[
                    row : row + count, a * width : (a + 1) * width
                ]


def sweep(matrices):
    matrices = list(matrices)
    logs = [jnp.zeros((1, 1), F32) for _ in matrices]
    for k in range(max(m.shape[0] for m in matrices)):
        for which, matrix in enumerate(matrices):
            size = matrix.shape[0]
            if k >= size:
                continue
            pivot = matrix[k : k + 1, k : k + 1]
            inverse = 1.0 / pivot
            column = matrix[:, k : k + 1]
            line = matrix[k : k + 1, :]
            row_here = iota((size, size), 0) == k
            lane_here = iota((size, size), 1) == k
            scaled = line * inverse
            reduced = matrix - column * scaled
            matrix = jnp.where(row_here, scaled, jnp.where(lane_here, column * inverse, reduced))
            matrix = jnp.where(jnp.logical_and(row_here, lane_here), -inverse, matrix)
            matrices[which] = matrix
            logs[which] = logs[which] + jnp.log(pivot)
    return [-m for m in matrices], logs


def solve_kernel(count, others, role_ref, vals_ref, own_ref, *refs):
    received = refs[:others]
    weight_ref, after_ref = refs[others : others + 2]
    change_ref, cols_ref, inv_ref, drift_ref, lap_ref, out_weight_ref, vals = refs[others + 2 :]
    pieces, _, width = vals_ref.shape
    for o in range(pieces):
        vals[:, o * width : (o + 1) * width] = vals_ref[o]
    role = role_ref[0]
    cols = own_ref[...].astype(F32)
    for step in range(others):
        cols = jnp.where(role == step + 1, received[step][...].astype(F32), cols)
    cols = cols.astype(BF16)
    cols_ref[...] = cols
    change_ref[...] = vals[0 : 2 * count]
    own = own_ref[0:count]
    products, ratios, normal = [], [], []
    for size, matrix, part in (
        (count, own, vals[6 * count : 11 * count]),
        (2 * count, cols, vals[0 : 6 * count]),
    ):
        product = dot(matrix, part, ((1,), (1,)))
        ratio = product[:, 0:size] + jnp.where(iota((size, size), 0) == iota((size, size), 1), 1.0, 0.0)
        products.append(product[:, size:])
        ratios.append(ratio)
        normal.append(dot(ratio, ratio, ((1,), (1,)), exact=True))
    inverses, logs = sweep(normal)
    for update, (inverse, ratio, product) in enumerate(zip(inverses, ratios, products)):
        size = ratio.shape[0]
        wide = product.shape[1]
        small = dot(inverse, ratio, exact=True)
        tile = jnp.where(iota((size, wide), 0) == size - count + iota((size, wide), 1) % count, 1.0, 0.0)
        spread = dot(small, tile, exact=True)
        sums = jnp.sum(product * spread, axis=0, keepdims=True)
        for a in range(3):
            drift_ref[3 * update + a] = sums[:, a * count : (a + 1) * count]
        lap_ref[update] = sums[:, 3 * count : 4 * count]
    inv_ref[...] = small
    out_weight_ref[...] = weight_ref[...] + 0.5 * logs[1]


def finish_kernel(sources, chunks, role_ref, change_ref, cols_ref, inv_ref, *refs):
    inputs = refs[:-5]
    out_ref, parent, staged, in_sem, out_sem = refs[-5:]
    depth = inputs[0].shape[0]
    role = role_ref[0]
    for chunk in range(chunks):
        for which, table in enumerate(sources):

            @pl.when(role == which)
            def _():
                pltpu.make_async_copy(
                    inputs[table[chunk]], parent.at[chunk], in_sem.at[chunk]
                ).start()

    total = jnp.zeros((change_ref.shape[0], inputs[0].shape[1]), F32)
    for chunk in range(chunks):
        pltpu.make_async_copy(inputs[chunk], parent.at[chunk], in_sem.at[chunk]).wait()
        total = total + dot(change_ref[:, chunk * depth : (chunk + 1) * depth], parent[chunk])
    solved = dot(inv_ref[...], total, exact=True).astype(BF16)
    copies = []
    for chunk in range(chunks):
        rows = slice(chunk * depth, (chunk + 1) * depth)
        columns = jnp.transpose(cols_ref[:, rows].astype(F32)).astype(BF16)
        staged[chunk] = parent[chunk].astype(F32) - dot(columns, solved)
        copy = pltpu.make_async_copy(staged.at[chunk], out_ref.at[rows], out_sem.at[chunk])
        copy.start()
        copies.append(copy)
    for copy in copies:
        copy.wait()


def per_device(
    n_grp,
    n_orb,
    wavevectors,
    coefficients,
    inverse,
    positions,
    displacements,
    moved,
    donor,
    take,
    log_weight,
):
    electrons = inverse.shape[1]
    count = moved.shape[2]
    plane = coefficients.shape[0]
    local = coefficients.shape[1]
    others = n_grp - 1
    chunks = 4
    group = lax.axis_index("grp")
    source = donor[0]
    apart = distance(n_grp, group, source)
    role = jnp.where(take[0] == 1, apart, 0).astype(jnp.int32).reshape(1)

    record, tiled, disp = call(
        functools.partial(start_kernel, count),
        (
            shape((8, electrons), F32),
            shape((2, LANES), jnp.int32),
            shape((2, 8, LANES), F32),
        ),
        [HBM, HBM, HBM, SM],
        (VM, VM, VM),
        scratch=[
            pltpu.VMEM((3, 1, electrons), F32),
            pltpu.VMEM((2, 1, count), jnp.int32),
            pltpu.VMEM((6, 1, count), F32),
            pltpu.SemaphoreType.DMA((3,)),
        ],
    )(
        *in_hbm(
            positions.reshape(3, 1, electrons), moved, displacements.reshape(6, 1, count)
        ),
        log_weight,
    )
    records = [lax.ppermute(record, "grp", pairs(n_grp, s)) for s in range(1, n_grp)]

    depth = electrons // chunks
    kept = pltpu.HBM((depth, electrons), BF16)
    token = shape((8, LANES), F32)
    own = [None] * chunks
    ends = (0, chunks - 1)
    middle = tuple(range(1, chunks - 1))
    own[0], own[-1] = call(
        functools.partial(round_kernel, ends),
        (kept,) * 2,
        [HBM, ANY],
        (HBM,) * 2,
        scratch=[
            pltpu.VMEM((2, depth, electrons), F32),
            pltpu.VMEM((2, depth, electrons), BF16),
            pltpu.SemaphoreType.DMA((2,)),
            pltpu.SemaphoreType.DMA((2,)),
        ],
        moved=3 * electrons * electrons,
        vmem=6,
    )(*in_hbm(inverse), record)
    own[0], own[-1], token_0 = call(
        gate_kernel,
        (kept, kept, token),
        [ANY] * (2 + others),
        (ANY, ANY, VM),
        aliases={0: 0, 1: 1},
        vmem=1,
    )(*in_hbm(own[0], own[-1]), *records)

    points, weight = call(
        functools.partial(points_kernel, count, others),
        (shape((n_orb, ROWS, LANES), F32), shape((1, LANES), F32)),
        [SM] + [VM] * (others + 3) + [ANY],
        (VM, VM),
    )(role, record, *records, tiled, disp, token_0)
    points = lax.all_to_all(points, "orb", split_axis=0, concat_axis=0, tiled=True)

    width = -(-local // LANES) * LANES
    coeff = jnp.pad(coefficients, ((0, 0), (0, width - local))) if width > local else coefficients
    steps = [0] + [backward(n_grp, s) for s in range(1, n_grp)]
    derived, *prepared = call(
        functools.partial(prepare_kernel, count, others, chunks, middle, steps),
        (shape((plane, 5 * width), BF16),)
        + (kept,) * len(middle)
        + tuple(shape((2 * count, electrons), BF16) for _ in steps),
        [HBM, HBM, HBM] + [VM] * (1 + others) + [ANY],
        (VM,) + (HBM,) * len(middle) + (VM,) * len(steps),
        scratch=[
            pltpu.VMEM((plane, width), BF16),
            pltpu.VMEM(wavevectors.shape, F32),
            pltpu.VMEM((chunks, depth, electrons), F32),
            pltpu.VMEM((chunks, depth, electrons), BF16),
            pltpu.SemaphoreType.DMA((2,)),
            pltpu.SemaphoreType.DMA((chunks,)),
            pltpu.SemaphoreType.DMA((len(middle),)),
        ],
        flops=2 * electrons * electrons * LANES + 8 * plane * width,
        moved=6 * electrons * electrons + 10 * plane * width,
        vmem=16,
    )(*in_hbm(coeff, wavevectors, inverse), tiled, *records, weight)
    for chunk, block in zip(middle, prepared):
        own[chunk] = block
    columns = prepared[len(middle) :]
    sent = [lax.ppermute(columns[s], "grp", pairs(n_grp, s)) for s in range(1, n_grp)]

    apart = apart.astype(jnp.int32).reshape(1)
    arrays = list(own)
    if n_grp == 4:
        send_x = lambda block: lax.ppermute(block, "grp", pairs(n_grp, 1))
        send_y = lambda block: lax.ppermute(block, "grp", pairs(n_grp, 2))

        def relay(mine, got, first):
            return call(
                relay_kernel,
                (kept, kept, token),
                [SM] + [ANY] * (4 + len(first)),
                (HBM, HBM, VM),
                scratch=[pltpu.SemaphoreType.DMA((2,))],
                vmem=1,
            )(apart, *in_hbm(*mine), *got, *first)

        x1, y1 = send_x(own[0]), send_y(own[3])
        y1, x1, token_1 = relay((own[1], own[2]), (y1, x1), (derived, points, *sent))
        x2, y2 = send_x(y1), send_y(x1)
        y2, x2, token_2 = relay((own[2], own[1]), (y2, x2), ())
        x3, y3 = send_x(y2), send_y(x2)
        arrays += [x1, x2, y1, y2, x3, y3]
        settled = len(arrays) - 2
        a1, a2, b1, b2, a3, b3 = range(chunks, chunks + 6)
        table = [range(chunks), (a1, a2, a3, b3), (a3, b3, b2, b1), (b2, b3, a3, a2)]
    else:
        token_1 = token_2 = jnp.zeros((8, LANES), F32)
        settled = chunks
        table = [range(chunks)]
        for step in range(1, n_grp):
            table.append(range(len(arrays), len(arrays) + chunks))
            arrays += [lax.ppermute(block, "grp", pairs(n_grp, step)) for block in own]

    block = math.gcd(n_orb, 8)
    values = pl.pallas_call(
        functools.partial(evaluate_kernel, count),
        grid=(n_orb // block,),
        out_shape=shape((n_orb, 11 * count, width), BF16),
        in_specs=[
            pl.BlockSpec((block, ROWS, LANES), lambda i: (i, 0, 0)),
            pl.BlockSpec(wavevectors.shape, lambda i: (0, 0)),
            pl.BlockSpec(derived.shape, lambda i: (0, 0)),
        ]
        + [ANY],
        out_specs=pl.BlockSpec((block, 11 * count, width), lambda i: (i, 0, 0)),
        scratch_shapes=[
            pltpu.VMEM((block * 3 * count, plane), BF16),
            pltpu.VMEM((block * 2 * count, plane), BF16),
        ],
        compiler_params=pltpu.CompilerParams(vmem_limit_bytes=16 * MIB),
        cost_estimate=pl.CostEstimate(
            flops=2 * n_orb * count * plane * width * 11,
            bytes_accessed=12 * plane * width,
            transcendentals=0,
        ),
    )(points, wavevectors, derived, token_1)
    values = values[:, :, :local]
    values = lax.all_to_all(values, "orb", split_axis=0, concat_axis=0, tiled=True)
    if width > local:
        values = values.transpose(1, 0, 2).reshape(1, 11 * count, electrons)

    change, cols, small, drift, laplacian, new_weight = call(
        functools.partial(solve_kernel, count, others),
        (
            shape((2 * count, electrons), BF16),
            shape((2 * count, electrons), BF16),
            shape((2 * count, 2 * count), F32),
            shape((6, 1, count), F32),
            shape((2, 1, count), F32),
            shape((1, LANES), F32),
        ),
        [SM] + [VM] * (others + 3) + [ANY],
        (VM,) * 6,
        scratch=[pltpu.VMEM((11 * count, electrons), BF16)],
        flops=2 * electrons * count * count * 16,
        moved=4 * 11 * count * electrons,
    )(role, values, columns[0], *sent, weight, token_2)

    updated = call(
        functools.partial(finish_kernel, table, chunks),
        shape((electrons, electrons), F32),
        [SM, VM, VM, VM] + [ANY] * len(arrays),
        HBM,
        scratch=[
            pltpu.VMEM((chunks, depth, electrons), BF16),
            pltpu.VMEM((chunks, depth, electrons), F32),
            pltpu.SemaphoreType.DMA((chunks,)),
            pltpu.SemaphoreType.DMA((chunks,)),
        ],
        flops=4 * electrons * electrons * 2 * count,
        moved=6 * electrons * electrons,
        vmem=12,
    )(role, change, cols, small, *in_hbm(*arrays[:settled]), *arrays[settled:])

    return updated[None], drift.reshape(2, 1, 3, count), laplacian, new_weight[0, :1]


def solution(mesh):
    split = ("grp", "orb")
    return jax.shard_map(
        functools.partial(per_device, mesh.shape["grp"], mesh.shape["orb"]),
        mesh=mesh,
        in_specs=(
            P(),
            P(None, "orb"),
            P(split, None, None),
            P(split, None, None),
            P(None, split, None, None),
            P(None, split, None),
            P("orb"),
            P(split),
            P(split),
        ),
        out_specs=(
            P(split, None, None),
            P(None, split, None, None),
            P(None, split, None),
            P(split),
        ),
        check_vma=False,
    )
```

```python
import functools
import math

import jax
import jax.numpy as jnp
from jax import lax
from jax.experimental import pallas as pl
from jax.experimental.pallas import tpu as pltpu
from jax.sharding import PartitionSpec as P

F32 = jnp.float32
BF16 = jnp.bfloat16
LANES = 128
ROWS = 16
MIB = 1024 * 1024
precise = lax.Precision.HIGHEST

SIN_HALF = (4.4428679, -7.30744342, 3.59478808, -0.78437403)
COS_HALF = (1.4142135, -6.97885099, 5.73946117, -1.88356299, 0.31069819)


def dot(a, b, dims=((1,), (0,)), exact=False):
    return lax.dot_general(
        a, b, (dims, ((), ())), precision=precise if exact else None, preferred_element_type=F32
    )


def iota(shape, dim):
    return lax.broadcasted_iota(jnp.int32, shape, dim)


def call(
    kernel, out_shape, in_specs, out_specs, scratch=(), flops=0, moved=0, vmem=4, aliases=None
):
    return pl.pallas_call(
        kernel,
        out_shape=out_shape,
        input_output_aliases=aliases or {},
        in_specs=in_specs,
        out_specs=out_specs,
        scratch_shapes=list(scratch),
        compiler_params=pltpu.CompilerParams(vmem_limit_bytes=vmem * MIB),
        cost_estimate=pl.CostEstimate(flops=flops, bytes_accessed=moved, transcendentals=0),
    )


VM = pl.BlockSpec(memory_space=pltpu.VMEM)
SM = pl.BlockSpec(memory_space=pltpu.SMEM)
ANY = pl.BlockSpec(memory_space=pl.ANY)
HBM = pl.BlockSpec(memory_space=pltpu.HBM)


def shape(dims, dtype):
    return jax.ShapeDtypeStruct(dims, dtype)


def in_hbm(*arrays):
    return tuple(pltpu.with_memory_space_constraint(a, pltpu.HBM) for a in arrays)


def is_power(n):
    return n & (n - 1) == 0


def pairs(n, step):
    if is_power(n):
        return [(i, i ^ step) for i in range(n)]
    return [(i, (i + step) % n) for i in range(n)]


def distance(n, here, there):
    return here ^ there if is_power(n) else lax.rem(here - there + n, n)


def backward(n, step):
    return step if is_power(n) else (n - step) % n


def start_kernel(
    count,
    pos_hbm,
    moved_hbm,
    disp_hbm,
    weight_ref,
    out_ref,
    tiled_ref,
    shift_ref,
    pos_ref,
    moved_ref,
    disp_ref,
    sems,
):
    loads = [
        pltpu.make_async_copy(src, dst, sems.at[i])
        for i, (src, dst) in enumerate(
            (
                (moved_hbm, moved_ref),
                (disp_hbm, disp_ref),
                (pos_hbm, pos_ref),
            )
        )
    ]
    for load in loads:
        load.start()
    electrons = pos_ref.shape[2]
    copies = LANES // count
    loads[0].wait()
    tiled = jnp.concatenate([moved_ref[:, 0, :]] * copies, 1)
    tiled_ref[...] = tiled
    pick = (iota((electrons, LANES), 0) == tiled[0:1, :]).astype(F32)
    block = iota((8, LANES), 1) // count
    zeros = jnp.zeros((5, LANES), F32)
    loads[1].wait()
    for update in range(2):
        shift = jnp.concatenate([disp_ref[3 * update : 3 * update + 3, 0, :]] * copies, 1)
        shift_ref[update] = jnp.concatenate([shift, zeros], 0)
    loads[2].wait()
    pos = jnp.concatenate([pos_ref[:, 0, :], jnp.zeros((5, electrons), F32)], 0)
    old = dot(pos, pick, exact=True)
    disp = shift_ref[0]
    points = old + jnp.where(block % 2 == 1, disp, 0.0)
    first = jnp.where(block == 0, disp, 0.0)
    out_ref[...] = pos + dot(first, pick, ((1,), (1,)), exact=True)
    out_ref[3:6, 0:LANES] = points[0:3]
    out_ref[6:7, 0:LANES] = tiled[1:2, :].astype(F32)
    out_ref[7:8, 0:LANES] = jnp.full((1, LANES), weight_ref[0], F32)


def rows_of(ref, chunk, depth):
    return ref.at[0, pl.ds(chunk * depth, depth)]


def round_kernel(wanted, inverse_hbm, after_ref, *refs):
    outs = refs[: len(wanted)]
    staged, rounded, in_sem, out_sem = refs[len(wanted) :]
    depth = staged.shape[1]
    loads, stores = [], []
    for slot, chunk in enumerate(wanted):
        load = pltpu.make_async_copy(
            rows_of(inverse_hbm, chunk, depth), staged.at[slot], in_sem.at[slot]
        )
        load.start()
        loads.append(load)
    for slot, out in enumerate(outs):
        loads[slot].wait()
        rounded[slot] = staged[slot].astype(BF16)
        store = pltpu.make_async_copy(rounded.at[slot], out, out_sem.at[slot])
        store.start()
        stores.append(store)
    for store in stores:
        store.wait()


def gate_kernel(*refs):
    token_ref = refs[-1]
    token_ref[...] = jnp.zeros(token_ref.shape, F32)


def relay_kernel(flag_ref, own_a, own_b, got_a, got_b, *refs):
    out_a, out_b, token_ref, staged, in_sem, out_sem = refs[-6:]
    pieces, depth, _ = staged.shape

    @pl.when(flag_ref[0] == 0)
    def _():
        loads, stores = [], []
        for piece in range(pieces):
            own, out = (own_a, out_a) if piece < pieces // 2 else (own_b, out_b)
            rows = pl.ds(piece % (pieces // 2) * depth, depth)
            loads.append(
                pltpu.make_async_copy(own.at[rows], staged.at[piece], in_sem.at[piece])
            )
            stores.append(
                pltpu.make_async_copy(staged.at[piece], out.at[rows], out_sem.at[piece])
            )
        for load in loads:
            load.start()
        for load, store in zip(loads, stores):
            load.wait()
            store.start()
        for store in stores:
            store.wait()

    token_ref[...] = jnp.zeros(token_ref.shape, F32)


def points_kernel(count, others, role_ref, *refs):
    own_ref = refs[0]
    received = refs[1 : 1 + others]
    moved_ref, disp_ref, after_ref, points_ref, weight_ref = refs[1 + others :]
    role = role_ref[0]
    parent = own_ref[...]
    for step in range(others):
        parent = jnp.where(role == step + 1, received[step][...], parent)
    electrons = parent.shape[1]
    pick = (iota((electrons, LANES), 0) == moved_ref[1:2, :]).astype(F32)
    block = iota((8, LANES), 1) // count
    old = dot(parent, pick, exact=True)
    later = old + jnp.where(block % 2 == 1, disp_ref[1], 0.0)
    zeros = jnp.zeros((5, LANES), F32)
    mine = jnp.concatenate([own_ref[3:6, 0:LANES], zeros], 0)
    theirs = jnp.concatenate([parent[3:6, 0:LANES], zeros], 0)
    points = jnp.where(block < 2, mine, jnp.where(block < 4, theirs, later))
    points = jnp.concatenate([points, jnp.zeros((ROWS - 8, LANES), F32)], 0)
    points_ref[...] = jnp.broadcast_to(points[None], points_ref.shape)
    weight_ref[...] = parent[7:8, 0:LANES]


def derive(coeff_ref, wave_ref, out_ref):
    waves = wave_ref.shape[1]
    width = coeff_ref.shape[1]
    wave = jnp.transpose(jnp.concatenate([wave_ref[...], jnp.zeros((5, waves), F32)], 0))
    out_ref[:, 0:width] = coeff_ref[...]
    cos_part = coeff_ref[0:waves].astype(F32)
    sin_part = coeff_ref[waves:].astype(F32)
    squared = None
    for a in range(3):
        scale = wave[:, a : a + 1]
        where = slice((a + 1) * width, (a + 2) * width)
        out_ref[0:waves, where] = (scale * sin_part).astype(BF16)
        out_ref[waves:, where] = (-scale * cos_part).astype(BF16)
        squared = scale * scale if a == 0 else squared + scale * scale
    where = slice(4 * width, 5 * width)
    out_ref[0:waves, where] = (-squared * cos_part).astype(BF16)
    out_ref[waves:, where] = (-squared * sin_part).astype(BF16)


def prepare_kernel(
    count, others, chunks, wanted, steps, coeff_hbm, wave_hbm, inverse_hbm, moved_ref, *refs
):
    received = refs[:others]
    table_ref = refs[others + 1]
    outs = refs[others + 2 : others + 2 + len(wanted)]
    columns = refs[others + 2 + len(wanted) : -7]
    coeff_ref, wave_ref, staged, rounded, small_sem, in_sem, out_sem = refs[-7:]
    depth, electrons = staged.shape[1:]
    wave_load = pltpu.make_async_copy(wave_hbm, wave_ref, small_sem.at[0])
    coeff_load = pltpu.make_async_copy(coeff_hbm, coeff_ref, small_sem.at[1])
    wave_load.start()
    coeff_load.start()
    loads, stores = [], []
    for chunk in range(chunks):
        load = pltpu.make_async_copy(
            rows_of(inverse_hbm, chunk, depth), staged.at[chunk], in_sem.at[chunk]
        )
        load.start()
        loads.append(load)
    block = iota((1, LANES), 1) // count
    number = jnp.where(block == 0, moved_ref[0:1, :], moved_ref[1:2, :])
    for step in range(others):
        theirs = received[step][6:7, 0:LANES].astype(jnp.int32)
        number = jnp.where(block == 2 + step, theirs, number)
    pick = (iota((electrons, LANES), 0) == number).astype(F32).astype(BF16)
    wave_load.wait()
    coeff_load.wait()
    derive(coeff_ref, wave_ref, table_ref)
    for chunk in range(chunks):
        rows = slice(chunk * depth, (chunk + 1) * depth)
        loads[chunk].wait()
        rounded[chunk] = staged[chunk].astype(BF16)
        if chunk in wanted:
            slot = wanted.index(chunk)
            store = pltpu.make_async_copy(rounded.at[chunk], outs[slot], out_sem.at[slot])
            store.start()
            stores.append(store)
        turned = jnp.transpose(dot(rounded[chunk], pick)).astype(BF16)
        for out, step in zip(columns, steps):
            out[0:count, rows] = turned[0:count]
            out[count : 2 * count, rows] = turned[(1 + step) * count : (2 + step) * count]
    for store in stores:
        store.wait()


def horner(coefs, u):
    value = coefs[-1] * u + coefs[-2]
    for c in reversed(coefs[:-2]):
        value = value * u + c
    return value


def evaluate_kernel(count, points_ref, wave_ref, table_ref, *refs):
    out_ref, diff, new = refs[-3:]
    walkers = points_ref.shape[0]
    waves = wave_ref.shape[1]
    width = table_ref.shape[1] // 5
    step = math.gcd(waves, LANES)

    def one(w, carry):
        column = jnp.transpose(points_ref[w, 0:8])
        xs = [column[0 : 6 * count, a : a + 1] for a in range(3)]
        row_d = pl.multiple_of(w * (3 * count), count)
        row_n = pl.multiple_of(w * (2 * count), count)
        for at in range(0, waves, step):
            ks = [wave_ref[a : a + 1, at : at + step] * (0.5 / math.pi) for a in range(3)]
            turn = xs[0] * ks[0] + xs[1] * ks[1] + xs[2] * ks[2]
            r = turn - jnp.floor(turn + 0.5)
            u = r * r
            s = r * horner(SIN_HALF, u)
            c = horner(COS_HALF, u)
            for value, base in ((1.0 - s * s, 0), (s * c, waves)):
                where = slice(base + at, base + at + step)
                kept = value.astype(BF16)
                wide = kept.astype(F32)
                part = [wide[i * count : (i + 1) * count] for i in range(6)]
                diff[pl.ds(row_d, count), where] = (part[3] - part[2]).astype(BF16)
                diff[pl.ds(row_d + count, count), where] = (part[5] - part[4]).astype(BF16)
                diff[pl.ds(row_d + 2 * count, count), where] = (part[1] - part[0]).astype(BF16)
                new[pl.ds(row_n, count), where] = kept[5 * count : 6 * count]
                new[pl.ds(row_n + count, count), where] = kept[count : 2 * count]
        return carry

    lax.fori_loop(0, walkers, one, 0)
    change = dot(diff[...], table_ref[:, 0:width]).astype(BF16)
    rest = dot(new[...], table_ref[:, width:]).astype(BF16)
    for w in range(walkers):
        at = w * 3 * count
        out_ref[w, 0 : 2 * count] = change[at : at + 2 * count]
        out_ref[w, 6 * count : 7 * count] = change[at + 2 * count : at + 3 * count]
        for half, base in ((0, 2 * count), (1, 7 * count)):
            row = (2 * w + half) * count
            for a in range(4):
                out_ref[w, base + a * count : base + (a + 1) * count] = rest[
                    row : row + count, a * width : (a + 1) * width
                ]


def sweep(matrices):
    matrices = list(matrices)
    logs = [jnp.zeros((1, 1), F32) for _ in matrices]
    for k in range(max(m.shape[0] for m in matrices)):
        for which, matrix in enumerate(matrices):
            size = matrix.shape[0]
            if k >= size:
                continue
            pivot = matrix[k : k + 1, k : k + 1]
            inverse = 1.0 / pivot
            column = matrix[:, k : k + 1]
            line = matrix[k : k + 1, :]
            row_here = iota((size, size), 0) == k
            lane_here = iota((size, size), 1) == k
            scaled = line * inverse
            reduced = matrix - column * scaled
            matrix = jnp.where(row_here, scaled, jnp.where(lane_here, column * inverse, reduced))
            matrix = jnp.where(jnp.logical_and(row_here, lane_here), -inverse, matrix)
            matrices[which] = matrix
            logs[which] = logs[which] + jnp.log(pivot)
    return [-m for m in matrices], logs


def solve_kernel(count, others, role_ref, vals_ref, own_ref, *refs):
    received = refs[:others]
    weight_ref, after_ref = refs[others : others + 2]
    change_ref, cols_ref, inv_ref, drift_ref, lap_ref, out_weight_ref, vals = refs[others + 2 :]
    pieces, _, width = vals_ref.shape
    for o in range(pieces):
        vals[:, o * width : (o + 1) * width] = vals_ref[o]
    role = role_ref[0]
    cols = own_ref[...].astype(F32)
    for step in range(others):
        cols = jnp.where(role == step + 1, received[step][...].astype(F32), cols)
    cols = cols.astype(BF16)
    cols_ref[...] = cols
    change_ref[...] = vals[0 : 2 * count]
    own = own_ref[0:count]
    products, ratios, normal = [], [], []
    for size, matrix, part in (
        (count, own, vals[6 * count : 11 * count]),
        (2 * count, cols, vals[0 : 6 * count]),
    ):
        product = dot(matrix, part, ((1,), (1,)))
        ratio = product[:, 0:size] + jnp.where(iota((size, size), 0) == iota((size, size), 1), 1.0, 0.0)
        products.append(product[:, size:])
        ratios.append(ratio)
        normal.append(dot(ratio, ratio, ((1,), (1,)), exact=True))
    inverses, logs = sweep(normal)
    for update, (inverse, ratio, product) in enumerate(zip(inverses, ratios, products)):
        size = ratio.shape[0]
        wide = product.shape[1]
        small = dot(inverse, ratio, exact=True)
        tile = jnp.where(iota((size, wide), 0) == size - count + iota((size, wide), 1) % count, 1.0, 0.0)
        spread = dot(small, tile, exact=True)
        sums = jnp.sum(product * spread, axis=0, keepdims=True)
        for a in range(3):
            drift_ref[3 * update + a] = sums[:, a * count : (a + 1) * count]
        lap_ref[update] = sums[:, 3 * count : 4 * count]
    inv_ref[...] = small
    out_weight_ref[...] = weight_ref[...] + 0.5 * logs[1]


def finish_kernel(sources, chunks, role_ref, change_ref, cols_ref, inv_ref, *refs):
    inputs = refs[:-5]
    out_ref, parent, staged, in_sem, out_sem = refs[-5:]
    depth = inputs[0].shape[0]
    role = role_ref[0]
    for chunk in range(chunks):
        for which, table in enumerate(sources):

            @pl.when(role == which)
            def _():
                pltpu.make_async_copy(
                    inputs[table[chunk]], parent.at[chunk], in_sem.at[chunk]
                ).start()

    total = jnp.zeros((change_ref.shape[0], inputs[0].shape[1]), F32)
    for chunk in range(chunks):
        pltpu.make_async_copy(inputs[chunk], parent.at[chunk], in_sem.at[chunk]).wait()
        total = total + dot(change_ref[:, chunk * depth : (chunk + 1) * depth], parent[chunk])
    solved = dot(inv_ref[...], total, exact=True).astype(BF16)
    copies = []
    for chunk in range(chunks):
        rows = slice(chunk * depth, (chunk + 1) * depth)
        columns = jnp.transpose(cols_ref[:, rows].astype(F32)).astype(BF16)
        staged[chunk] = parent[chunk].astype(F32) - dot(columns, solved)
        copy = pltpu.make_async_copy(staged.at[chunk], out_ref.at[rows], out_sem.at[chunk])
        copy.start()
        copies.append(copy)
    for copy in copies:
        copy.wait()


def per_device(
    n_grp,
    n_orb,
    wavevectors,
    coefficients,
    inverse,
    positions,
    displacements,
    moved,
    donor,
    take,
    log_weight,
):
    electrons = inverse.shape[1]
    count = moved.shape[2]
    plane = coefficients.shape[0]
    local = coefficients.shape[1]
    others = n_grp - 1
    chunks = 4
    group = lax.axis_index("grp")
    source = donor[0]
    apart = distance(n_grp, group, source)
    role = jnp.where(take[0] == 1, apart, 0).astype(jnp.int32).reshape(1)

    record, tiled, disp = call(
        functools.partial(start_kernel, count),
        (
            shape((8, electrons), F32),
            shape((2, LANES), jnp.int32),
            shape((2, 8, LANES), F32),
        ),
        [HBM, HBM, HBM, SM],
        (VM, VM, VM),
        scratch=[
            pltpu.VMEM((3, 1, electrons), F32),
            pltpu.VMEM((2, 1, count), jnp.int32),
            pltpu.VMEM((6, 1, count), F32),
            pltpu.SemaphoreType.DMA((3,)),
        ],
    )(
        *in_hbm(
            positions.reshape(3, 1, electrons), moved, displacements.reshape(6, 1, count)
        ),
        log_weight,
    )
    records = [lax.ppermute(record, "grp", pairs(n_grp, s)) for s in range(1, n_grp)]

    depth = electrons // chunks
    kept = shape((depth, electrons), BF16)
    token = shape((8, LANES), F32)
    own = [None] * chunks
    ends = (0, chunks - 1)
    middle = tuple(range(1, chunks - 1))
    own[0], own[-1] = call(
        functools.partial(round_kernel, ends),
        (kept,) * 2,
        [HBM, ANY],
        (ANY,) * 2,
        scratch=[
            pltpu.VMEM((2, depth, electrons), F32),
            pltpu.VMEM((2, depth, electrons), BF16),
            pltpu.SemaphoreType.DMA((2,)),
            pltpu.SemaphoreType.DMA((2,)),
        ],
        moved=3 * electrons * electrons,
        vmem=6,
    )(*in_hbm(inverse), record)
    own[0], own[-1], token_0 = call(
        gate_kernel,
        (kept, kept, token),
        [ANY] * (2 + others),
        (ANY, ANY, VM),
        aliases={0: 0, 1: 1},
        vmem=1,
    )(own[0], own[-1], *records)

    points, weight = call(
        functools.partial(points_kernel, count, others),
        (shape((n_orb, ROWS, LANES), F32), shape((1, LANES), F32)),
        [SM] + [VM] * (others + 3) + [ANY],
        (VM, VM),
    )(role, record, *records, tiled, disp, token_0)
    points = lax.all_to_all(points, "orb", split_axis=0, concat_axis=0, tiled=True)

    width = -(-local // LANES) * LANES
    coeff = jnp.pad(coefficients, ((0, 0), (0, width - local))) if width > local else coefficients
    steps = [0] + [backward(n_grp, s) for s in range(1, n_grp)]
    derived, *prepared = call(
        functools.partial(prepare_kernel, count, others, chunks, middle, steps),
        (shape((plane, 5 * width), BF16),)
        + (pltpu.HBM((depth, electrons), BF16),) * len(middle)
        + tuple(shape((2 * count, electrons), BF16) for _ in steps),
        [HBM, HBM, HBM] + [VM] * (1 + others) + [ANY],
        (VM,) + (ANY,) * len(middle) + (VM,) * len(steps),
        scratch=[
            pltpu.VMEM((plane, width), BF16),
            pltpu.VMEM(wavevectors.shape, F32),
            pltpu.VMEM((chunks, depth, electrons), F32),
            pltpu.VMEM((chunks, depth, electrons), BF16),
            pltpu.SemaphoreType.DMA((2,)),
            pltpu.SemaphoreType.DMA((chunks,)),
            pltpu.SemaphoreType.DMA((len(middle),)),
        ],
        flops=2 * electrons * electrons * LANES + 8 * plane * width,
        moved=6 * electrons * electrons + 10 * plane * width,
        vmem=16,
    )(*in_hbm(coeff, wavevectors, inverse), tiled, *records, weight)
    for chunk, block in zip(middle, prepared):
        own[chunk] = block
    columns = prepared[len(middle) :]
    sent = [lax.ppermute(columns[s], "grp", pairs(n_grp, s)) for s in range(1, n_grp)]

    apart = apart.astype(jnp.int32).reshape(1)
    arrays = list(own)
    if n_grp == 4:
        send_x = lambda block: lax.ppermute(block, "grp", pairs(n_grp, 1))
        send_y = lambda block: lax.ppermute(block, "grp", pairs(n_grp, 2))

        def relay(mine, got, first):
            return call(
                relay_kernel,
                (kept, kept, token),
                [SM] + [ANY] * (4 + len(first)),
                (ANY, ANY, VM),
                scratch=[
                    pltpu.VMEM((4, depth // 2, electrons), BF16),
                    pltpu.SemaphoreType.DMA((4,)),
                    pltpu.SemaphoreType.DMA((4,)),
                ],
                aliases={3: 0, 4: 1},
                vmem=2,
            )(apart, *in_hbm(*mine), *got, *first)

        x1, y1 = send_x(own[0]), send_y(own[3])
        y1, x1, token_1 = relay((own[1], own[2]), (y1, x1), (derived, points, *sent))
        x2, y2 = send_x(y1), send_y(x1)
        y2, x2, token_2 = relay((own[2], own[1]), (y2, x2), ())
        x3, y3 = send_x(y2), send_y(x2)
        arrays += [x1, x2, y1, y2, x3, y3]
        a1, a2, b1, b2, a3, b3 = range(chunks, chunks + 6)
        table = [range(chunks), (a1, a2, a3, b3), (a3, b3, b2, b1), (b2, b3, a3, a2)]
    else:
        token_1 = token_2 = jnp.zeros((8, LANES), F32)
        table = [range(chunks)]
        for step in range(1, n_grp):
            table.append(range(len(arrays), len(arrays) + chunks))
            arrays += [lax.ppermute(block, "grp", pairs(n_grp, step)) for block in own]

    block = math.gcd(n_orb, 8)
    values = pl.pallas_call(
        functools.partial(evaluate_kernel, count),
        grid=(n_orb // block,),
        out_shape=shape((n_orb, 11 * count, width), BF16),
        in_specs=[
            pl.BlockSpec((block, ROWS, LANES), lambda i: (i, 0, 0)),
            pl.BlockSpec(wavevectors.shape, lambda i: (0, 0)),
            pl.BlockSpec(derived.shape, lambda i: (0, 0)),
        ]
        + [ANY],
        out_specs=pl.BlockSpec((block, 11 * count, width), lambda i: (i, 0, 0)),
        scratch_shapes=[
            pltpu.VMEM((block * 3 * count, plane), BF16),
            pltpu.VMEM((block * 2 * count, plane), BF16),
        ],
        compiler_params=pltpu.CompilerParams(vmem_limit_bytes=8 * MIB),
        cost_estimate=pl.CostEstimate(
            flops=2 * n_orb * count * plane * width * 11,
            bytes_accessed=12 * plane * width,
            transcendentals=0,
        ),
    )(points, wavevectors, derived, token_1)
    values = values[:, :, :local]
    values = lax.all_to_all(values, "orb", split_axis=0, concat_axis=0, tiled=True)
    if width > local:
        values = values.transpose(1, 0, 2).reshape(1, 11 * count, electrons)

    change, cols, small, drift, laplacian, new_weight = call(
        functools.partial(solve_kernel, count, others),
        (
            shape((2 * count, electrons), BF16),
            shape((2 * count, electrons), BF16),
            shape((2 * count, 2 * count), F32),
            shape((6, 1, count), F32),
            shape((2, 1, count), F32),
            shape((1, LANES), F32),
        ),
        [SM] + [VM] * (others + 3) + [ANY],
        (VM,) * 6,
        scratch=[pltpu.VMEM((11 * count, electrons), BF16)],
        flops=2 * electrons * count * count * 16,
        moved=4 * 11 * count * electrons,
    )(role, values, columns[0], *sent, weight, token_2)

    updated = call(
        functools.partial(finish_kernel, table, chunks),
        shape((electrons, electrons), F32),
        [SM, VM, VM, VM] + [ANY] * len(arrays),
        HBM,
        scratch=[
            pltpu.VMEM((chunks, depth, electrons), BF16),
            pltpu.VMEM((chunks, depth, electrons), F32),
            pltpu.SemaphoreType.DMA((chunks,)),
            pltpu.SemaphoreType.DMA((chunks,)),
        ],
        flops=4 * electrons * electrons * 2 * count,
        moved=6 * electrons * electrons,
        vmem=12,
    )(role, change, cols, small, *in_hbm(*own), *arrays[chunks:])

    return updated[None], drift.reshape(2, 1, 3, count), laplacian, new_weight[0, :1]


def solution(mesh):
    split = ("grp", "orb")
    return jax.shard_map(
        functools.partial(per_device, mesh.shape["grp"], mesh.shape["orb"]),
        mesh=mesh,
        in_specs=(
            P(),
            P(None, "orb"),
            P(split, None, None),
            P(split, None, None),
            P(None, split, None, None),
            P(None, split, None),
            P("orb"),
            P(split),
            P(split),
        ),
        out_specs=(
            P(split, None, None),
            P(None, split, None, None),
            P(None, split, None),
            P(split),
        ),
        check_vma=False,
    )
```

```python
import functools
import math

import jax
import jax.numpy as jnp
from jax import lax
from jax.experimental import pallas as pl
from jax.experimental.pallas import tpu as pltpu
from jax.sharding import PartitionSpec as P

F32 = jnp.float32
BF16 = jnp.bfloat16
LANES = 128
ROWS = 16
DIRECT_POINTS = False
DIRECT_VALUES = False
MIB = 1024 * 1024
precise = lax.Precision.HIGHEST

SIN_HALF = (4.4428679, -7.30744342, 3.59478808, -0.78437403)
COS_HALF = (1.4142135, -6.97885099, 5.73946117, -1.88356299, 0.31069819)


def dot(a, b, dims=((1,), (0,)), exact=False):
    return lax.dot_general(
        a, b, (dims, ((), ())), precision=precise if exact else None, preferred_element_type=F32
    )


def iota(shape, dim):
    return lax.broadcasted_iota(jnp.int32, shape, dim)


def call(
    kernel, out_shape, in_specs, out_specs, scratch=(), flops=0, moved=0, vmem=4, aliases=None
):
    return pl.pallas_call(
        kernel,
        out_shape=out_shape,
        input_output_aliases=aliases or {},
        in_specs=in_specs,
        out_specs=out_specs,
        scratch_shapes=list(scratch),
        compiler_params=pltpu.CompilerParams(vmem_limit_bytes=vmem * MIB),
        cost_estimate=pl.CostEstimate(flops=flops, bytes_accessed=moved, transcendentals=0),
    )


VM = pl.BlockSpec(memory_space=pltpu.VMEM)
SM = pl.BlockSpec(memory_space=pltpu.SMEM)
ANY = pl.BlockSpec(memory_space=pl.ANY)
HBM = pl.BlockSpec(memory_space=pltpu.HBM)


def shape(dims, dtype):
    return jax.ShapeDtypeStruct(dims, dtype)


def in_hbm(*arrays):
    return tuple(pltpu.with_memory_space_constraint(a, pltpu.HBM) for a in arrays)


def is_power(n):
    return n & (n - 1) == 0


def pairs(n, step):
    if is_power(n):
        return [(i, i ^ step) for i in range(n)]
    return [(i, (i + step) % n) for i in range(n)]


def distance(n, here, there):
    return here ^ there if is_power(n) else lax.rem(here - there + n, n)


def backward(n, step):
    return step if is_power(n) else (n - step) % n


def start_kernel(
    count,
    pos_hbm,
    moved_hbm,
    disp_hbm,
    weight_ref,
    out_ref,
    tiled_ref,
    shift_ref,
    pos_ref,
    moved_ref,
    disp_ref,
    sems,
):
    loads = [
        pltpu.make_async_copy(src, dst, sems.at[i])
        for i, (src, dst) in enumerate(
            (
                (moved_hbm, moved_ref),
                (disp_hbm, disp_ref),
                (pos_hbm, pos_ref),
            )
        )
    ]
    for load in loads:
        load.start()
    electrons = pos_ref.shape[2]
    copies = LANES // count
    loads[0].wait()
    tiled = jnp.concatenate([moved_ref[:, 0, :]] * copies, 1)
    tiled_ref[...] = tiled
    pick = (iota((electrons, LANES), 0) == tiled[0:1, :]).astype(F32)
    block = iota((8, LANES), 1) // count
    zeros = jnp.zeros((5, LANES), F32)
    loads[1].wait()
    for update in range(2):
        shift = jnp.concatenate([disp_ref[3 * update : 3 * update + 3, 0, :]] * copies, 1)
        shift_ref[update] = jnp.concatenate([shift, zeros], 0)
    loads[2].wait()
    pos = jnp.concatenate([pos_ref[:, 0, :], jnp.zeros((5, electrons), F32)], 0)
    old = dot(pos, pick, exact=True)
    disp = shift_ref[0]
    points = old + jnp.where(block % 2 == 1, disp, 0.0)
    first = jnp.where(block == 0, disp, 0.0)
    out_ref[...] = pos + dot(first, pick, ((1,), (1,)), exact=True)
    out_ref[3:6, 0:LANES] = points[0:3]
    out_ref[6:7, 0:LANES] = tiled[0:1, :].astype(F32)
    out_ref[7:8, 0:LANES] = jnp.full((1, LANES), weight_ref[0], F32)


def rows_of(ref, chunk, depth):
    return ref.at[0, pl.ds(chunk * depth, depth)]


def round_kernel(wanted, inverse_hbm, after_ref, *refs):
    outs = refs[: len(wanted)]
    staged, rounded, in_sem, out_sem = refs[len(wanted) :]
    depth = staged.shape[1]
    loads, stores = [], []
    for slot, chunk in enumerate(wanted):
        load = pltpu.make_async_copy(
            rows_of(inverse_hbm, chunk, depth), staged.at[slot], in_sem.at[slot]
        )
        load.start()
        loads.append(load)
    for slot, out in enumerate(outs):
        loads[slot].wait()
        rounded[slot] = staged[slot].astype(BF16)
        store = pltpu.make_async_copy(rounded.at[slot], out, out_sem.at[slot])
        store.start()
        stores.append(store)
    for store in stores:
        store.wait()


def gate_kernel(*refs):
    token_ref = refs[-1]
    token_ref[...] = jnp.zeros(token_ref.shape, F32)


def relay_kernel(flag_ref, own_a, own_b, got_a, got_b, *refs):
    out_a, out_b, token_ref, staged, in_sem, out_sem = refs[-6:]
    pieces, depth, _ = staged.shape

    @pl.when(flag_ref[0] == 0)
    def _():
        loads, stores = [], []
        for piece in range(pieces):
            own, out = (own_a, out_a) if piece < pieces // 2 else (own_b, out_b)
            rows = pl.ds(piece % (pieces // 2) * depth, depth)
            loads.append(
                pltpu.make_async_copy(own.at[rows], staged.at[piece], in_sem.at[piece])
            )
            stores.append(
                pltpu.make_async_copy(staged.at[piece], out.at[rows], out_sem.at[piece])
            )
        for load in loads:
            load.start()
        for load, store in zip(loads, stores):
            load.wait()
            store.start()
        for store in stores:
            store.wait()

    token_ref[...] = jnp.zeros(token_ref.shape, F32)


def points_kernel(count, others, role_ref, *refs):
    own_ref = refs[0]
    received = refs[1 : 1 + others]
    moved_ref, disp_ref, after_ref, points_ref, weight_ref, number_ref = refs[1 + others :]
    role = role_ref[0]
    parent = own_ref[...]
    for step in range(others):
        parent = jnp.where(role == step + 1, received[step][...], parent)
    electrons = parent.shape[1]
    pick = (iota((electrons, LANES), 0) == moved_ref[1:2, :]).astype(F32)
    block = iota((8, LANES), 1) // count
    old = dot(parent, pick, exact=True)
    later = old + jnp.where(block % 2 == 1, disp_ref[1], 0.0)
    zeros = jnp.zeros((5, LANES), F32)
    mine = jnp.concatenate([own_ref[3:6, 0:LANES], zeros], 0)
    theirs = jnp.concatenate([parent[3:6, 0:LANES], zeros], 0)
    points = jnp.where(block < 2, mine, jnp.where(block < 4, theirs, later))
    if len(points_ref.shape) == 2:
        points_ref[...] = points
    else:
        points = jnp.concatenate([points, jnp.zeros((ROWS - 8, LANES), F32)], 0)
        points_ref[...] = jnp.broadcast_to(points[None], points_ref.shape)
    weight_ref[...] = parent[7:8, 0:LANES]
    before = parent[6:7, 0:LANES].astype(jnp.int32)
    number_ref[...] = jnp.where(
        block[0:1] == 0, before, jnp.where(block[0:1] == 1, moved_ref[1:2, :], -1)
    )


def derive(coeff_ref, wave_ref, out_ref):
    waves = wave_ref.shape[1]
    width = coeff_ref.shape[1]
    wave = jnp.transpose(jnp.concatenate([wave_ref[...], jnp.zeros((5, waves), F32)], 0))
    out_ref[:, 0:width] = coeff_ref[...]
    cos_part = coeff_ref[0:waves].astype(F32)
    sin_part = coeff_ref[waves:].astype(F32)
    squared = None
    for a in range(3):
        scale = wave[:, a : a + 1]
        where = slice((a + 1) * width, (a + 2) * width)
        out_ref[0:waves, where] = (scale * sin_part).astype(BF16)
        out_ref[waves:, where] = (-scale * cos_part).astype(BF16)
        squared = scale * scale if a == 0 else squared + scale * scale
    where = slice(4 * width, 5 * width)
    out_ref[0:waves, where] = (-squared * cos_part).astype(BF16)
    out_ref[waves:, where] = (-squared * sin_part).astype(BF16)


def prepare_kernel(wanted, coeff_hbm, wave_hbm, inverse_hbm, after_ref, table_ref, *refs):
    outs = refs[: len(wanted)]
    coeff_ref, wave_ref, staged, rounded, small_sem, in_sem, out_sem = refs[len(wanted) :]
    depth = staged.shape[1]
    wave_load = pltpu.make_async_copy(wave_hbm, wave_ref, small_sem.at[0])
    coeff_load = pltpu.make_async_copy(coeff_hbm, coeff_ref, small_sem.at[1])
    wave_load.start()
    coeff_load.start()
    loads, stores = [], []
    for slot, chunk in enumerate(wanted):
        load = pltpu.make_async_copy(
            rows_of(inverse_hbm, chunk, depth), staged.at[slot], in_sem.at[slot]
        )
        load.start()
        loads.append(load)
    wave_load.wait()
    coeff_load.wait()
    derive(coeff_ref, wave_ref, table_ref)
    for slot, out in enumerate(outs):
        loads[slot].wait()
        rounded[slot] = staged[slot].astype(BF16)
        store = pltpu.make_async_copy(rounded.at[slot], out, out_sem.at[slot])
        store.start()
        stores.append(store)
    for store in stores:
        store.wait()


def horner(coefs, u):
    value = coefs[-1] * u + coefs[-2]
    for c in reversed(coefs[:-2]):
        value = value * u + c
    return value


def evaluate_kernel(count, sources, targets, *refs):
    points = refs[:sources]
    wave_ref, table_ref = refs[sources : sources + 2]
    outs = refs[sources + 3 : -3]
    diff, new, gathered = refs[-3:]
    walkers = gathered.shape[0]
    for w in range(walkers):
        gathered[w] = points[w][...] if sources > 1 else points[0][w, 0:8]
    waves = wave_ref.shape[1]
    width = table_ref.shape[1] // 5
    step = math.gcd(waves, LANES)

    def one(w, carry):
        column = jnp.transpose(gathered[w])
        xs = [column[0 : 6 * count, a : a + 1] for a in range(3)]
        row_d = pl.multiple_of(w * (3 * count), count)
        row_n = pl.multiple_of(w * (2 * count), count)
        for at in range(0, waves, step):
            ks = [wave_ref[a : a + 1, at : at + step] * (0.5 / math.pi) for a in range(3)]
            turn = xs[0] * ks[0] + xs[1] * ks[1] + xs[2] * ks[2]
            r = turn - jnp.floor(turn + 0.5)
            u = r * r
            s = r * horner(SIN_HALF, u)
            c = horner(COS_HALF, u)
            for value, base in ((1.0 - s * s, 0), (s * c, waves)):
                where = slice(base + at, base + at + step)
                kept = value.astype(BF16)
                wide = kept.astype(F32)
                part = [wide[i * count : (i + 1) * count] for i in range(6)]
                diff[pl.ds(row_d, count), where] = (part[3] - part[2]).astype(BF16)
                diff[pl.ds(row_d + count, count), where] = (part[5] - part[4]).astype(BF16)
                diff[pl.ds(row_d + 2 * count, count), where] = (part[1] - part[0]).astype(BF16)
                new[pl.ds(row_n, count), where] = kept[5 * count : 6 * count]
                new[pl.ds(row_n + count, count), where] = kept[count : 2 * count]
        return carry

    lax.fori_loop(0, walkers, one, 0)
    change = dot(diff[...], table_ref[:, 0:width]).astype(BF16)
    rest = dot(new[...], table_ref[:, width:]).astype(BF16)
    for w in range(walkers):
        out_ref = outs[w] if targets > 1 else outs[0].at[w]
        at = w * 3 * count
        out_ref[0 : 2 * count] = change[at : at + 2 * count]
        out_ref[6 * count : 7 * count] = change[at + 2 * count : at + 3 * count]
        for half, base in ((0, 2 * count), (1, 7 * count)):
            row = (2 * w + half) * count
            for a in range(4):
                out_ref[base + a * count : base + (a + 1) * count] = rest[
                    row : row + count, a * width : (a + 1) * width
                ]


def sweep(matrix):
    size = matrix.shape[0]
    log = jnp.zeros((1, 1), F32)
    for k in range(size):
        pivot = matrix[k : k + 1, k : k + 1]
        inverse = 1.0 / pivot
        column = matrix[:, k : k + 1]
        line = matrix[k : k + 1, :]
        row_here = iota((size, size), 0) == k
        lane_here = iota((size, size), 1) == k
        scaled = line * inverse
        reduced = matrix - column * scaled
        matrix = jnp.where(row_here, scaled, jnp.where(lane_here, column * inverse, reduced))
        matrix = jnp.where(jnp.logical_and(row_here, lane_here), -inverse, matrix)
        log = log + jnp.log(pivot)
    return -matrix, log


def ratio_of(products, size):
    eye = jnp.where(iota((size, size), 0) == iota((size, size), 1), 1.0, 0.0)
    ratio = products[0:size, 0:size] + eye
    inverse, log = sweep(dot(ratio, ratio, ((0,), (0,)), exact=True))
    return ratio, inverse, 0.5 * log


def moved_sums(products, ratio, inverse, count):
    size = ratio.shape[0]
    turned = dot(ratio, inverse, exact=True)[size - count :]
    tile = jnp.concatenate([turned] * 4, 0)
    part = products[size : size + 4 * count, 0:size] * tile
    return dot(jnp.ones((8, size), F32), part, ((1,), (1,)), exact=True)[0:1]


def first_kernel(count, sources, me_ref, moved_ref, *refs):
    values = refs[:sources]
    blocks = refs[sources:-6]
    drift_ref, lap_ref, later_ref, vals, columns = refs[-5:]
    rows = later_ref.shape[0]
    if sources > 1:
        width = values[0].shape[1]
        for step in range(sources):
            at = pl.multiple_of((me_ref[0] ^ step) * width, width)
            later_ref[:, pl.ds(at, width)] = values[step][0:rows]
            vals[:, pl.ds(at, width)] = values[step][rows:]
    else:
        pieces, _, width = values[0].shape
        for piece in range(pieces):
            where = slice(piece * width, (piece + 1) * width)
            later_ref[:, where] = values[0][piece, 0:rows]
            vals[:, where] = values[0][piece, rows:]
    depth, electrons = blocks[0].shape
    block = iota((1, LANES), 1) // count
    number = jnp.where(block == 0, moved_ref[0:1, :], -1)
    pick = (iota((electrons, LANES), 0) == number).astype(F32).astype(BF16)
    for chunk, ref in enumerate(blocks):
        columns[chunk * depth : (chunk + 1) * depth] = dot(ref[...], pick).astype(BF16)
    products = dot(vals[...], columns[...])
    ratio, inverse, _ = ratio_of(products, count)
    sums = moved_sums(products, ratio, inverse, count)
    for a in range(3):
        drift_ref[a] = sums[:, a * count : (a + 1) * count]
    lap_ref[0] = sums[:, 3 * count : 4 * count]


def finish_kernel(
    count, sources, chunks, role_ref, number_ref, later_ref, weight_ref, drift_in, lap_in, *refs
):
    inputs = refs[:-9]
    out_ref, drift_ref, lap_ref, out_weight_ref, parent, staged, columns, in_sem, out_sem = refs[-9:]
    depth, electrons = inputs[0].shape
    size = 2 * count
    role = role_ref[0]
    for chunk in range(chunks):
        for which, table in enumerate(sources):

            @pl.when(role == which)
            def _():
                pltpu.make_async_copy(
                    inputs[table[chunk]], parent.at[chunk], in_sem.at[chunk]
                ).start()

    pick = (iota((electrons, LANES), 0) == number_ref[...]).astype(F32).astype(BF16)
    total = jnp.zeros((size, electrons), F32)
    for chunk in range(chunks):
        rows = slice(chunk * depth, (chunk + 1) * depth)
        pltpu.make_async_copy(inputs[chunk], parent.at[chunk], in_sem.at[chunk]).wait()
        columns[rows] = dot(parent[chunk], pick).astype(BF16)
        total = total + dot(later_ref[0:size, rows], parent[chunk])
    products = dot(later_ref[...], columns[...])
    ratio, inverse, log = ratio_of(products, size)
    small = dot(inverse, ratio, ((1,), (1,)), exact=True)
    solved = dot(small, total, exact=True).astype(BF16)
    solved = jnp.concatenate([solved, jnp.zeros((LANES - size, electrons), BF16)], 0)
    copies = []
    for chunk in range(chunks):
        rows = slice(chunk * depth, (chunk + 1) * depth)
        staged[chunk] = parent[chunk].astype(F32) - dot(columns[rows], solved)
        copy = pltpu.make_async_copy(staged.at[chunk], out_ref.at[rows], out_sem.at[chunk])
        copy.start()
        copies.append(copy)
    sums = moved_sums(products, ratio, inverse, count)
    drift_ref[0:3] = drift_in[...]
    lap_ref[0:1] = lap_in[...]
    for a in range(3):
        drift_ref[3 + a] = sums[:, a * count : (a + 1) * count]
    lap_ref[1] = sums[:, 3 * count : 4 * count]
    out_weight_ref[...] = weight_ref[...] + log
    for copy in copies:
        copy.wait()


def per_device(
    n_grp,
    n_orb,
    wavevectors,
    coefficients,
    inverse,
    positions,
    displacements,
    moved,
    donor,
    take,
    log_weight,
):
    electrons = inverse.shape[1]
    count = moved.shape[2]
    plane = coefficients.shape[0]
    local = coefficients.shape[1]
    others = n_grp - 1
    chunks = 4
    group = lax.axis_index("grp")
    source = donor[0]
    apart = distance(n_grp, group, source)
    role = jnp.where(take[0] == 1, apart, 0).astype(jnp.int32).reshape(1)

    record, tiled, disp = call(
        functools.partial(start_kernel, count),
        (
            shape((8, electrons), F32),
            shape((2, LANES), jnp.int32),
            shape((2, 8, LANES), F32),
        ),
        [HBM, HBM, HBM, SM],
        (VM, VM, VM),
        scratch=[
            pltpu.VMEM((3, 1, electrons), F32),
            pltpu.VMEM((2, 1, count), jnp.int32),
            pltpu.VMEM((6, 1, count), F32),
            pltpu.SemaphoreType.DMA((3,)),
        ],
    )(
        *in_hbm(
            positions.reshape(3, 1, electrons), moved, displacements.reshape(6, 1, count)
        ),
        log_weight,
    )
    records = [lax.ppermute(record, "grp", pairs(n_grp, s)) for s in range(1, n_grp)]

    depth = electrons // chunks
    kept = shape((depth, electrons), BF16)
    token = shape((8, LANES), F32)
    own = [None] * chunks
    ends = (0, chunks - 1)
    middle = tuple(range(1, chunks - 1))
    own[0], own[-1] = call(
        functools.partial(round_kernel, ends),
        (kept,) * 2,
        [HBM, ANY],
        (ANY,) * 2,
        scratch=[
            pltpu.VMEM((2, depth, electrons), F32),
            pltpu.VMEM((2, depth, electrons), BF16),
            pltpu.SemaphoreType.DMA((2,)),
            pltpu.SemaphoreType.DMA((2,)),
        ],
        moved=3 * electrons * electrons,
        vmem=6,
    )(*in_hbm(inverse), record)
    own[0], own[-1], token_0 = call(
        gate_kernel,
        (kept, kept, token),
        [ANY] * (2 + others),
        (ANY, ANY, VM),
        aliases={0: 0, 1: 1},
        vmem=1,
    )(own[0], own[-1], *records)

    few = is_power(n_orb) and local % LANES == 0
    direct = few and DIRECT_POINTS
    sources = n_orb if direct else 1
    points, weight, number = call(
        functools.partial(points_kernel, count, others),
        (
            shape((8, LANES) if direct else (n_orb, ROWS, LANES), F32),
            shape((1, LANES), F32),
            shape((1, LANES), jnp.int32),
        ),
        [SM] + [VM] * (others + 3) + [ANY],
        (VM, VM, VM),
    )(role, record, *records, tiled, disp, token_0)
    if direct:
        points = [points] + [lax.ppermute(points, "orb", pairs(n_orb, s)) for s in range(1, n_orb)]
    else:
        points = [lax.all_to_all(points, "orb", split_axis=0, concat_axis=0, tiled=True)]

    width = -(-local // LANES) * LANES
    coeff = jnp.pad(coefficients, ((0, 0), (0, width - local))) if width > local else coefficients
    derived, *prepared = call(
        functools.partial(prepare_kernel, middle),
        (shape((plane, 5 * width), BF16),)
        + (pltpu.HBM((depth, electrons), BF16),) * len(middle),
        [HBM, HBM, HBM, ANY],
        (VM,) + (ANY,) * len(middle),
        scratch=[
            pltpu.VMEM((plane, width), BF16),
            pltpu.VMEM(wavevectors.shape, F32),
            pltpu.VMEM((len(middle), depth, electrons), F32),
            pltpu.VMEM((len(middle), depth, electrons), BF16),
            pltpu.SemaphoreType.DMA((2,)),
            pltpu.SemaphoreType.DMA((len(middle),)),
            pltpu.SemaphoreType.DMA((len(middle),)),
        ],
        flops=8 * plane * width,
        moved=3 * electrons * electrons + 10 * plane * width,
        vmem=12,
    )(*in_hbm(coeff, wavevectors, inverse), weight)
    for chunk, ready in zip(middle, prepared):
        own[chunk] = ready

    apart = apart.astype(jnp.int32).reshape(1)
    arrays = list(own)
    if n_grp == 4:
        send_x = lambda block: lax.ppermute(block, "grp", pairs(n_grp, 1))
        send_y = lambda block: lax.ppermute(block, "grp", pairs(n_grp, 2))

        def relay(mine, got, first):
            return call(
                relay_kernel,
                (kept, kept, token),
                [SM] + [ANY] * (4 + len(first)),
                (ANY, ANY, VM),
                scratch=[
                    pltpu.VMEM((4, depth // 2, electrons), BF16),
                    pltpu.SemaphoreType.DMA((4,)),
                    pltpu.SemaphoreType.DMA((4,)),
                ],
                aliases={3: 0, 4: 1},
                vmem=2,
            )(apart, *in_hbm(*mine), *got, *first)

        x1, y1 = send_x(own[0]), send_y(own[3])
        y1, x1, token_1 = relay((own[1], own[2]), (y1, x1), (derived, *points))
        x2, y2 = send_x(y1), send_y(x1)
    else:
        token_1 = token_2 = jnp.zeros((8, LANES), F32)
        table = [range(chunks)]
        for step in range(1, n_grp):
            table.append(range(len(arrays), len(arrays) + chunks))
            arrays += [lax.ppermute(block, "grp", pairs(n_grp, step)) for block in own]

    height = 11 * count
    spread = few and DIRECT_VALUES
    targets = n_orb if spread else 1
    block = n_orb if few else math.gcd(n_orb, 8)
    whole = lambda array: pl.BlockSpec(array.shape, lambda i: (0,) * array.ndim)
    if direct:
        point_specs = [whole(p) for p in points]
    else:
        point_specs = [pl.BlockSpec((block, ROWS, LANES), lambda i: (i, 0, 0))]
    if spread:
        out_shapes = (shape((height, width), BF16),) * n_orb
        out_specs = tuple(whole(o) for o in out_shapes)
    else:
        out_shapes = (shape((n_orb, height, width), BF16),)
        out_specs = (pl.BlockSpec((block, height, width), lambda i: (i, 0, 0)),)
    values = pl.pallas_call(
        functools.partial(evaluate_kernel, count, sources, targets),
        grid=(n_orb // block,),
        out_shape=out_shapes,
        in_specs=point_specs + [whole(wavevectors), whole(derived), ANY],
        out_specs=out_specs,
        scratch_shapes=[
            pltpu.VMEM((block * 3 * count, plane), BF16),
            pltpu.VMEM((block * 2 * count, plane), BF16),
            pltpu.VMEM((block, 8, LANES), F32),
        ],
        compiler_params=pltpu.CompilerParams(vmem_limit_bytes=8 * MIB),
        cost_estimate=pl.CostEstimate(
            flops=2 * n_orb * count * plane * width * 11,
            bytes_accessed=12 * plane * width,
            transcendentals=0,
        ),
    )(*points, wavevectors, derived, token_1)
    computed = values[0]
    if spread:
        values = [values[0]] + [
            lax.ppermute(values[s], "orb", pairs(n_orb, s)) for s in range(1, n_orb)
        ]
    else:
        values = values[0][:, :, :local]
        values = lax.all_to_all(values, "orb", split_axis=0, concat_axis=0, tiled=True)
        if width > local:
            values = values.transpose(1, 0, 2).reshape(1, height, electrons)
        values = [values]

    if n_grp == 4:
        y2, x2, token_2 = relay((own[2], own[1]), (y2, x2), (computed,))
        x3, y3 = send_x(y2), send_y(x2)
        arrays += [x1, x2, y1, y2, x3, y3]
        a1, a2, b1, b2, a3, b3 = range(chunks, chunks + 6)
        table = [range(chunks), (a1, a2, a3, b3), (a3, b3, b2, b1), (b2, b3, a3, a2)]

    here = lax.axis_index("orb").astype(jnp.int32).reshape(1)
    drift, laplacian, later = call(
        functools.partial(first_kernel, count, targets),
        (
            shape((3, 1, count), F32),
            shape((1, 1, count), F32),
            shape((6 * count, electrons), BF16),
        ),
        [SM, VM] + [VM] * (targets + chunks) + [ANY],
        (VM, VM, VM),
        scratch=[
            pltpu.VMEM((5 * count, electrons), BF16),
            pltpu.VMEM((electrons, LANES), BF16),
        ],
        flops=2 * electrons * electrons * LANES,
        moved=2 * electrons * electrons,
        vmem=8,
    )(here, tiled, *values, *own, token_2)

    updated, drift, laplacian, new_weight = call(
        functools.partial(finish_kernel, count, table, chunks),
        (
            shape((electrons, electrons), F32),
            shape((6, 1, count), F32),
            shape((2, 1, count), F32),
            shape((1, LANES), F32),
        ),
        [SM] + [VM] * 5 + [ANY] * len(arrays),
        (HBM, VM, VM, VM),
        scratch=[
            pltpu.VMEM((chunks, depth, electrons), BF16),
            pltpu.VMEM((chunks, depth, electrons), F32),
            pltpu.VMEM((electrons, LANES), BF16),
            pltpu.SemaphoreType.DMA((chunks,)),
            pltpu.SemaphoreType.DMA((chunks,)),
        ],
        flops=4 * electrons * electrons * 2 * count,
        moved=6 * electrons * electrons,
        vmem=12,
    )(role, number, later, weight, drift, laplacian, *in_hbm(*own), *arrays[chunks:])

    return updated[None], drift.reshape(2, 1, 3, count), laplacian, new_weight[0, :1]


def solution(mesh):
    split = ("grp", "orb")
    return jax.shard_map(
        functools.partial(per_device, mesh.shape["grp"], mesh.shape["orb"]),
        mesh=mesh,
        in_specs=(
            P(),
            P(None, "orb"),
            P(split, None, None),
            P(split, None, None),
            P(None, split, None, None),
            P(None, split, None),
            P("orb"),
            P(split),
            P(split),
        ),
        out_specs=(
            P(split, None, None),
            P(None, split, None, None),
            P(None, split, None),
            P(split),
        ),
        check_vma=False,
    )
```

```python
import functools
import math

import jax
import jax.numpy as jnp
from jax import lax
from jax.experimental import pallas as pl
from jax.experimental.pallas import tpu as pltpu
from jax.sharding import PartitionSpec as P

F32 = jnp.float32
BF16 = jnp.bfloat16
LANES = 128
ROWS = 16
DIRECT_POINTS = False
DIRECT_VALUES = False
MIB = 1024 * 1024
precise = lax.Precision.HIGHEST

SIN_HALF = (4.4428679, -7.30744342, 3.59478808, -0.78437403)
COS_HALF = (1.4142135, -6.97885099, 5.73946117, -1.88356299, 0.31069819)


def dot(a, b, dims=((1,), (0,)), exact=False):
    return lax.dot_general(
        a, b, (dims, ((), ())), precision=precise if exact else None, preferred_element_type=F32
    )


def iota(shape, dim):
    return lax.broadcasted_iota(jnp.int32, shape, dim)


def call(
    kernel, out_shape, in_specs, out_specs, scratch=(), flops=0, moved=0, vmem=4, aliases=None
):
    return pl.pallas_call(
        kernel,
        out_shape=out_shape,
        input_output_aliases=aliases or {},
        in_specs=in_specs,
        out_specs=out_specs,
        scratch_shapes=list(scratch),
        compiler_params=pltpu.CompilerParams(vmem_limit_bytes=vmem * MIB),
        cost_estimate=pl.CostEstimate(flops=flops, bytes_accessed=moved, transcendentals=0),
    )


VM = pl.BlockSpec(memory_space=pltpu.VMEM)
SM = pl.BlockSpec(memory_space=pltpu.SMEM)
ANY = pl.BlockSpec(memory_space=pl.ANY)
HBM = pl.BlockSpec(memory_space=pltpu.HBM)


def shape(dims, dtype):
    return jax.ShapeDtypeStruct(dims, dtype)


def in_hbm(*arrays):
    return tuple(pltpu.with_memory_space_constraint(a, pltpu.HBM) for a in arrays)


def is_power(n):
    return n & (n - 1) == 0


def pairs(n, step):
    if is_power(n):
        return [(i, i ^ step) for i in range(n)]
    return [(i, (i + step) % n) for i in range(n)]


def distance(n, here, there):
    return here ^ there if is_power(n) else lax.rem(here - there + n, n)


def backward(n, step):
    return step if is_power(n) else (n - step) % n


def start_kernel(
    count,
    pos_hbm,
    moved_hbm,
    disp_hbm,
    weight_ref,
    out_ref,
    tiled_ref,
    shift_ref,
    pos_ref,
    moved_ref,
    disp_ref,
    sems,
):
    loads = [
        pltpu.make_async_copy(src, dst, sems.at[i])
        for i, (src, dst) in enumerate(
            (
                (moved_hbm, moved_ref),
                (disp_hbm, disp_ref),
                (pos_hbm, pos_ref),
            )
        )
    ]
    for load in loads:
        load.start()
    electrons = pos_ref.shape[2]
    copies = LANES // count
    loads[0].wait()
    tiled = jnp.concatenate([moved_ref[:, 0, :]] * copies, 1)
    tiled_ref[...] = tiled
    pick = (iota((electrons, LANES), 0) == tiled[0:1, :]).astype(F32)
    block = iota((8, LANES), 1) // count
    zeros = jnp.zeros((5, LANES), F32)
    loads[1].wait()
    for update in range(2):
        shift = jnp.concatenate([disp_ref[3 * update : 3 * update + 3, 0, :]] * copies, 1)
        shift_ref[update] = jnp.concatenate([shift, zeros], 0)
    loads[2].wait()
    pos = jnp.concatenate([pos_ref[:, 0, :], jnp.zeros((5, electrons), F32)], 0)
    old = dot(pos, pick, exact=True)
    disp = shift_ref[0]
    points = old + jnp.where(block % 2 == 1, disp, 0.0)
    first = jnp.where(block == 0, disp, 0.0)
    out_ref[...] = pos + dot(first, pick, ((1,), (1,)), exact=True)
    out_ref[3:6, 0:LANES] = points[0:3]
    out_ref[6:7, 0:LANES] = tiled[0:1, :].astype(F32)
    out_ref[7:8, 0:LANES] = jnp.full((1, LANES), weight_ref[0], F32)


def rows_of(ref, chunk, depth):
    return ref.at[0, pl.ds(chunk * depth, depth)]


def round_kernel(wanted, inverse_hbm, after_ref, *refs):
    outs = refs[: len(wanted)]
    staged, rounded, in_sem, out_sem = refs[len(wanted) :]
    depth = staged.shape[1]
    loads, stores = [], []
    for slot, chunk in enumerate(wanted):
        load = pltpu.make_async_copy(
            rows_of(inverse_hbm, chunk, depth), staged.at[slot], in_sem.at[slot]
        )
        load.start()
        loads.append(load)
    for slot, out in enumerate(outs):
        loads[slot].wait()
        rounded[slot] = staged[slot].astype(BF16)
        store = pltpu.make_async_copy(rounded.at[slot], out, out_sem.at[slot])
        store.start()
        stores.append(store)
    for store in stores:
        store.wait()


def gate_kernel(*refs):
    token_ref = refs[-1]
    token_ref[...] = jnp.zeros(token_ref.shape, F32)


def relay_kernel(flag_ref, own_a, own_b, got_a, got_b, *refs):
    out_a, out_b, token_ref, staged, in_sem, out_sem = refs[-6:]
    pieces, depth, _ = staged.shape

    @pl.when(flag_ref[0] == 0)
    def _():
        loads, stores = [], []
        for piece in range(pieces):
            own, out = (own_a, out_a) if piece < pieces // 2 else (own_b, out_b)
            rows = pl.ds(piece % (pieces // 2) * depth, depth)
            loads.append(
                pltpu.make_async_copy(own.at[rows], staged.at[piece], in_sem.at[piece])
            )
            stores.append(
                pltpu.make_async_copy(staged.at[piece], out.at[rows], out_sem.at[piece])
            )
        for load in loads:
            load.start()
        for load, store in zip(loads, stores):
            load.wait()
            store.start()
        for store in stores:
            store.wait()

    token_ref[...] = jnp.zeros(token_ref.shape, F32)


def points_kernel(count, others, role_ref, *refs):
    own_ref = refs[0]
    received = refs[1 : 1 + others]
    moved_ref, disp_ref, after_ref, points_ref, weight_ref, number_ref = refs[1 + others :]
    role = role_ref[0]
    parent = own_ref[...]
    for step in range(others):
        parent = jnp.where(role == step + 1, received[step][...], parent)
    electrons = parent.shape[1]
    pick = (iota((electrons, LANES), 0) == moved_ref[1:2, :]).astype(F32)
    block = iota((8, LANES), 1) // count
    old = dot(parent, pick, exact=True)
    later = old + jnp.where(block % 2 == 1, disp_ref[1], 0.0)
    zeros = jnp.zeros((5, LANES), F32)
    mine = jnp.concatenate([own_ref[3:6, 0:LANES], zeros], 0)
    theirs = jnp.concatenate([parent[3:6, 0:LANES], zeros], 0)
    points = jnp.where(block < 2, mine, jnp.where(block < 4, theirs, later))
    if len(points_ref.shape) == 2:
        points_ref[...] = points
    else:
        points = jnp.concatenate([points, jnp.zeros((ROWS - 8, LANES), F32)], 0)
        points_ref[...] = jnp.broadcast_to(points[None], points_ref.shape)
    weight_ref[...] = parent[7:8, 0:LANES]
    before = parent[6:7, 0:LANES].astype(jnp.int32)
    number_ref[...] = jnp.where(
        block[0:1] == 0, before, jnp.where(block[0:1] == 1, moved_ref[1:2, :], -1)
    )


def derive(coeff_ref, wave_ref, out_ref):
    waves = wave_ref.shape[1]
    width = coeff_ref.shape[1]
    wave = jnp.transpose(jnp.concatenate([wave_ref[...], jnp.zeros((5, waves), F32)], 0))
    out_ref[:, 0:width] = coeff_ref[...]
    cos_part = coeff_ref[0:waves].astype(F32)
    sin_part = coeff_ref[waves:].astype(F32)
    squared = None
    for a in range(3):
        scale = wave[:, a : a + 1]
        where = slice((a + 1) * width, (a + 2) * width)
        out_ref[0:waves, where] = (scale * sin_part).astype(BF16)
        out_ref[waves:, where] = (-scale * cos_part).astype(BF16)
        squared = scale * scale if a == 0 else squared + scale * scale
    where = slice(4 * width, 5 * width)
    out_ref[0:waves, where] = (-squared * cos_part).astype(BF16)
    out_ref[waves:, where] = (-squared * sin_part).astype(BF16)


def prepare_kernel(wanted, coeff_hbm, wave_hbm, inverse_hbm, after_ref, table_ref, *refs):
    outs = refs[: len(wanted)]
    coeff_ref, wave_ref, staged, rounded, small_sem, in_sem, out_sem = refs[len(wanted) :]
    depth = staged.shape[1]
    wave_load = pltpu.make_async_copy(wave_hbm, wave_ref, small_sem.at[0])
    coeff_load = pltpu.make_async_copy(coeff_hbm, coeff_ref, small_sem.at[1])
    wave_load.start()
    coeff_load.start()
    loads, stores = [], []
    for slot, chunk in enumerate(wanted):
        load = pltpu.make_async_copy(
            rows_of(inverse_hbm, chunk, depth), staged.at[slot], in_sem.at[slot]
        )
        load.start()
        loads.append(load)
    wave_load.wait()
    coeff_load.wait()
    derive(coeff_ref, wave_ref, table_ref)
    for slot, out in enumerate(outs):
        loads[slot].wait()
        rounded[slot] = staged[slot].astype(BF16)
        store = pltpu.make_async_copy(rounded.at[slot], out, out_sem.at[slot])
        store.start()
        stores.append(store)
    for store in stores:
        store.wait()


def horner(coefs, u):
    value = coefs[-1] * u + coefs[-2]
    for c in reversed(coefs[:-2]):
        value = value * u + c
    return value


def evaluate_kernel(count, sources, targets, *refs):
    points = refs[:sources]
    wave_ref, table_ref = refs[sources : sources + 2]
    outs = refs[sources + 3 : -3]
    diff, new, gathered = refs[-3:]
    walkers = gathered.shape[0]
    for w in range(walkers):
        gathered[w] = points[w][...] if sources > 1 else points[0][w, 0:8]
    waves = wave_ref.shape[1]
    width = table_ref.shape[1] // 5
    step = math.gcd(waves, LANES)

    def one(w, carry):
        column = jnp.transpose(gathered[w])
        xs = [column[0 : 6 * count, a : a + 1] for a in range(3)]
        row_d = pl.multiple_of(w * (3 * count), count)
        row_n = pl.multiple_of(w * (2 * count), count)
        for at in range(0, waves, step):
            ks = [wave_ref[a : a + 1, at : at + step] * (0.5 / math.pi) for a in range(3)]
            turn = xs[0] * ks[0] + xs[1] * ks[1] + xs[2] * ks[2]
            r = turn - jnp.floor(turn + 0.5)
            u = r * r
            s = r * horner(SIN_HALF, u)
            c = horner(COS_HALF, u)
            for value, base in ((1.0 - s * s, 0), (s * c, waves)):
                where = slice(base + at, base + at + step)
                kept = value.astype(BF16)
                wide = kept.astype(F32)
                part = [wide[i * count : (i + 1) * count] for i in range(6)]
                diff[pl.ds(row_d, count), where] = (part[3] - part[2]).astype(BF16)
                diff[pl.ds(row_d + count, count), where] = (part[5] - part[4]).astype(BF16)
                diff[pl.ds(row_d + 2 * count, count), where] = (part[1] - part[0]).astype(BF16)
                new[pl.ds(row_n, count), where] = kept[5 * count : 6 * count]
                new[pl.ds(row_n + count, count), where] = kept[count : 2 * count]
        return carry

    lax.fori_loop(0, walkers, one, 0)
    change = dot(diff[...], table_ref[:, 0:width]).astype(BF16)
    rest = dot(new[...], table_ref[:, width:]).astype(BF16)
    for w in range(walkers):
        out_ref = outs[w] if targets > 1 else outs[0].at[w]
        at = w * 3 * count
        out_ref[0 : 2 * count] = change[at : at + 2 * count]
        out_ref[6 * count : 7 * count] = change[at + 2 * count : at + 3 * count]
        for half, base in ((0, 2 * count), (1, 7 * count)):
            row = (2 * w + half) * count
            for a in range(4):
                out_ref[base + a * count : base + (a + 1) * count] = rest[
                    row : row + count, a * width : (a + 1) * width
                ]


def sweep(matrix):
    size = matrix.shape[0]
    log = jnp.zeros((1, 1), F32)
    row = iota((size, size), 0)
    lane = iota((size, size), 1)
    place = iota((1, size), 1)
    for k in range(0, size, 2):
        a = matrix[k : k + 1, k : k + 1]
        b = matrix[k : k + 1, k + 1 : k + 2]
        d = matrix[k + 1 : k + 2, k + 1 : k + 2]
        column_0, column_1 = matrix[:, k : k + 1], matrix[:, k + 1 : k + 2]
        line_0, line_1 = matrix[k : k + 1, :], matrix[k + 1 : k + 2, :]
        det = a * d - b * b
        scale = 1.0 / det
        a, b, d = a * scale, b * scale, d * scale
        scaled_0 = d * line_0 - b * line_1
        scaled_1 = a * line_1 - b * line_0
        reduced = matrix - column_0 * scaled_0 - column_1 * scaled_1
        edge_0 = d * column_0 - b * column_1
        edge_1 = a * column_1 - b * column_0
        scaled_0 = jnp.where(place == k, -d, jnp.where(place == k + 1, b, scaled_0))
        scaled_1 = jnp.where(place == k, b, jnp.where(place == k + 1, -a, scaled_1))
        matrix = jnp.where(lane == k, edge_0, jnp.where(lane == k + 1, edge_1, reduced))
        matrix = jnp.where(row == k, scaled_0, jnp.where(row == k + 1, scaled_1, matrix))
        log = log + jnp.log(det)
    return -matrix, log


def ratio_of(products, size):
    eye = jnp.where(iota((size, size), 0) == iota((size, size), 1), 1.0, 0.0)
    ratio = products[0:size, 0:size] + eye
    inverse, log = sweep(dot(ratio, ratio, ((0,), (0,)), exact=True))
    return ratio, inverse, 0.5 * log


def moved_sums(products, ratio, inverse, count):
    size = ratio.shape[0]
    turned = dot(ratio, inverse, exact=True)[size - count :]
    tile = jnp.concatenate([turned] * 4, 0)
    part = products[size : size + 4 * count, 0:size] * tile
    return dot(jnp.ones((8, size), F32), part, ((1,), (1,)), exact=True)[0:1]


def columns_kernel(count, inverse_hbm, moved_ref, after_ref, out_ref, staged, sem):
    chunks, depth, electrons = staged.shape
    loads = []
    for chunk in range(chunks):
        load = pltpu.make_async_copy(
            rows_of(inverse_hbm, chunk, depth), staged.at[chunk], sem.at[chunk]
        )
        load.start()
        loads.append(load)
    block = iota((1, LANES), 1) // count
    number = jnp.where(block == 0, moved_ref[0:1, :], -1)
    pick = (iota((electrons, LANES), 0) == number).astype(F32).astype(BF16)
    for chunk in range(chunks):
        loads[chunk].wait()
        found = dot(staged[chunk].astype(BF16), pick)
        out_ref[chunk * depth : (chunk + 1) * depth] = found.astype(BF16)


def first_kernel(count, sources, me_ref, *refs):
    values = refs[:sources]
    columns, drift_ref, lap_ref, later_ref, vals = refs[sources:]
    rows = later_ref.shape[0]
    if sources > 1:
        width = values[0].shape[1]
        for step in range(sources):
            at = pl.multiple_of((me_ref[0] ^ step) * width, width)
            later_ref[:, pl.ds(at, width)] = values[step][0:rows]
            vals[:, pl.ds(at, width)] = values[step][rows:]
    else:
        pieces, _, width = values[0].shape
        for piece in range(pieces):
            where = slice(piece * width, (piece + 1) * width)
            later_ref[:, where] = values[0][piece, 0:rows]
            vals[:, where] = values[0][piece, rows:]
    products = dot(vals[...], columns[...])
    ratio, inverse, _ = ratio_of(products, count)
    sums = moved_sums(products, ratio, inverse, count)
    for a in range(3):
        drift_ref[a] = sums[:, a * count : (a + 1) * count]
    lap_ref[0] = sums[:, 3 * count : 4 * count]


def finish_kernel(
    count,
    sources,
    role_ref,
    number_ref,
    later_ref,
    weight_ref,
    drift_in,
    lap_in,
    inverse_hbm,
    *refs,
):
    inputs = refs[:-9]
    out_ref, drift_ref, lap_ref, out_weight_ref, parent, staged, columns, in_sem, out_sem = refs[-9:]
    chunks, depth, electrons = parent.shape
    size = 2 * count
    role = role_ref[0]
    mine = role == 0
    for chunk in range(chunks):
        own = pltpu.make_async_copy(
            rows_of(inverse_hbm, chunk, depth), staged.at[chunk], in_sem.at[chunk]
        )
        pl.when(mine)(own.start)
        for which, table in enumerate(sources):
            if which:
                sent = pltpu.make_async_copy(
                    inputs[table[chunk]], parent.at[chunk], in_sem.at[chunk]
                )
                pl.when(role == which)(sent.start)

    pick = (iota((electrons, LANES), 0) == number_ref[...]).astype(F32).astype(BF16)
    for chunk in range(chunks):
        own = pltpu.make_async_copy(
            rows_of(inverse_hbm, chunk, depth), staged.at[chunk], in_sem.at[chunk]
        )
        sent = pltpu.make_async_copy(inputs[0], parent.at[chunk], in_sem.at[chunk])

        @pl.when(mine)
        def _():
            own.wait()
            parent[chunk] = staged[chunk].astype(BF16)

        @pl.when(jnp.logical_not(mine))
        def _():
            sent.wait()
            staged[chunk] = parent[chunk].astype(F32)

    for chunk in range(chunks):
        rows = slice(chunk * depth, (chunk + 1) * depth)
        columns[rows] = dot(parent[chunk], pick).astype(BF16)
    products = dot(later_ref[...], columns[...])
    ratio, inverse, log = ratio_of(products, size)
    total = jnp.zeros((size, electrons), F32)
    for chunk in range(chunks):
        rows = slice(chunk * depth, (chunk + 1) * depth)
        total = total + dot(later_ref[0:size, rows], parent[chunk])
    small = dot(inverse, ratio, ((1,), (1,)), exact=True)
    solved = dot(small, total, exact=True).astype(BF16)
    solved = jnp.concatenate([solved, jnp.zeros((LANES - size, electrons), BF16)], 0)
    copies = []
    for chunk in range(chunks):
        rows = slice(chunk * depth, (chunk + 1) * depth)
        staged[chunk] = staged[chunk] - dot(columns[rows], solved)
        copy = pltpu.make_async_copy(staged.at[chunk], out_ref.at[rows], out_sem.at[chunk])
        copy.start()
        copies.append(copy)
    sums = moved_sums(products, ratio, inverse, count)
    drift_ref[0:3] = drift_in[...]
    lap_ref[0:1] = lap_in[...]
    for a in range(3):
        drift_ref[3 + a] = sums[:, a * count : (a + 1) * count]
    lap_ref[1] = sums[:, 3 * count : 4 * count]
    out_weight_ref[...] = weight_ref[...] + log
    for copy in copies:
        copy.wait()


def per_device(
    n_grp,
    n_orb,
    wavevectors,
    coefficients,
    inverse,
    positions,
    displacements,
    moved,
    donor,
    take,
    log_weight,
):
    electrons = inverse.shape[1]
    count = moved.shape[2]
    plane = coefficients.shape[0]
    local = coefficients.shape[1]
    others = n_grp - 1
    chunks = 4
    group = lax.axis_index("grp")
    source = donor[0]
    apart = distance(n_grp, group, source)
    role = jnp.where(take[0] == 1, apart, 0).astype(jnp.int32).reshape(1)

    record, tiled, disp = call(
        functools.partial(start_kernel, count),
        (
            shape((8, electrons), F32),
            shape((2, LANES), jnp.int32),
            shape((2, 8, LANES), F32),
        ),
        [HBM, HBM, HBM, SM],
        (VM, VM, VM),
        scratch=[
            pltpu.VMEM((3, 1, electrons), F32),
            pltpu.VMEM((2, 1, count), jnp.int32),
            pltpu.VMEM((6, 1, count), F32),
            pltpu.SemaphoreType.DMA((3,)),
        ],
    )(
        *in_hbm(
            positions.reshape(3, 1, electrons), moved, displacements.reshape(6, 1, count)
        ),
        log_weight,
    )
    records = [lax.ppermute(record, "grp", pairs(n_grp, s)) for s in range(1, n_grp)]

    depth = electrons // chunks
    kept = shape((depth, electrons), BF16)
    token = shape((8, LANES), F32)
    own = [None] * chunks
    ends = (0, chunks - 1)
    middle = tuple(range(1, chunks - 1))
    own[0], own[-1] = call(
        functools.partial(round_kernel, ends),
        (kept,) * 2,
        [HBM, ANY],
        (ANY,) * 2,
        scratch=[
            pltpu.VMEM((2, depth, electrons), F32),
            pltpu.VMEM((2, depth, electrons), BF16),
            pltpu.SemaphoreType.DMA((2,)),
            pltpu.SemaphoreType.DMA((2,)),
        ],
        moved=3 * electrons * electrons,
        vmem=6,
    )(*in_hbm(inverse), record)
    own[0], own[-1], token_0 = call(
        gate_kernel,
        (kept, kept, token),
        [ANY] * (2 + others),
        (ANY, ANY, VM),
        aliases={0: 0, 1: 1},
        vmem=1,
    )(own[0], own[-1], *records)

    few = is_power(n_orb) and local % LANES == 0
    direct = few and DIRECT_POINTS
    sources = n_orb if direct else 1
    points, weight, number = call(
        functools.partial(points_kernel, count, others),
        (
            shape((8, LANES) if direct else (n_orb, ROWS, LANES), F32),
            shape((1, LANES), F32),
            shape((1, LANES), jnp.int32),
        ),
        [SM] + [VM] * (others + 3) + [ANY],
        (VM, VM, VM),
    )(role, record, *records, tiled, disp, token_0)
    if direct:
        points = [points] + [lax.ppermute(points, "orb", pairs(n_orb, s)) for s in range(1, n_orb)]
    else:
        points = [lax.all_to_all(points, "orb", split_axis=0, concat_axis=0, tiled=True)]

    width = -(-local // LANES) * LANES
    coeff = jnp.pad(coefficients, ((0, 0), (0, width - local))) if width > local else coefficients
    derived, *prepared = call(
        functools.partial(prepare_kernel, middle),
        (shape((plane, 5 * width), BF16),)
        + (pltpu.HBM((depth, electrons), BF16),) * len(middle),
        [HBM, HBM, HBM, ANY],
        (VM,) + (ANY,) * len(middle),
        scratch=[
            pltpu.VMEM((plane, width), BF16),
            pltpu.VMEM(wavevectors.shape, F32),
            pltpu.VMEM((len(middle), depth, electrons), F32),
            pltpu.VMEM((len(middle), depth, electrons), BF16),
            pltpu.SemaphoreType.DMA((2,)),
            pltpu.SemaphoreType.DMA((len(middle),)),
            pltpu.SemaphoreType.DMA((len(middle),)),
        ],
        flops=8 * plane * width,
        moved=3 * electrons * electrons + 10 * plane * width,
        vmem=12,
    )(*in_hbm(coeff, wavevectors, inverse), weight)
    for chunk, ready in zip(middle, prepared):
        own[chunk] = ready

    apart = apart.astype(jnp.int32).reshape(1)
    arrays = []
    if n_grp == 4:
        send_x = lambda block: lax.ppermute(block, "grp", pairs(n_grp, 1))
        send_y = lambda block: lax.ppermute(block, "grp", pairs(n_grp, 2))

        def relay(mine, got, first):
            return call(
                relay_kernel,
                (kept, kept, token),
                [SM] + [ANY] * (4 + len(first)),
                (ANY, ANY, VM),
                scratch=[
                    pltpu.VMEM((4, depth // 2, electrons), BF16),
                    pltpu.SemaphoreType.DMA((4,)),
                    pltpu.SemaphoreType.DMA((4,)),
                ],
                aliases={3: 0, 4: 1},
                vmem=2,
            )(apart, *in_hbm(*mine), *got, *first)

        x1, y1 = send_x(own[0]), send_y(own[3])
        y1, x1, token_1 = relay((own[1], own[2]), (y1, x1), (derived, *points))
        x2, y2 = send_x(y1), send_y(x1)
    else:
        token_1 = token_2 = jnp.zeros((8, LANES), F32)
        table = [()]
        for step in range(1, n_grp):
            table.append(range(len(arrays), len(arrays) + chunks))
            arrays += [lax.ppermute(block, "grp", pairs(n_grp, step)) for block in own]

    height = 11 * count
    spread = few and DIRECT_VALUES
    targets = n_orb if spread else 1
    block = n_orb if few else math.gcd(n_orb, 8)
    whole = lambda array: pl.BlockSpec(array.shape, lambda i: (0,) * array.ndim)
    if direct:
        point_specs = [whole(p) for p in points]
    else:
        point_specs = [pl.BlockSpec((block, ROWS, LANES), lambda i: (i, 0, 0))]
    if spread:
        out_shapes = (shape((height, width), BF16),) * n_orb
        out_specs = tuple(whole(o) for o in out_shapes)
    else:
        out_shapes = (shape((n_orb, height, width), BF16),)
        out_specs = (pl.BlockSpec((block, height, width), lambda i: (i, 0, 0)),)
    values = pl.pallas_call(
        functools.partial(evaluate_kernel, count, sources, targets),
        grid=(n_orb // block,),
        out_shape=out_shapes,
        in_specs=point_specs + [whole(wavevectors), whole(derived), ANY],
        out_specs=out_specs,
        scratch_shapes=[
            pltpu.VMEM((block * 3 * count, plane), BF16),
            pltpu.VMEM((block * 2 * count, plane), BF16),
            pltpu.VMEM((block, 8, LANES), F32),
        ],
        compiler_params=pltpu.CompilerParams(vmem_limit_bytes=8 * MIB),
        cost_estimate=pl.CostEstimate(
            flops=2 * n_orb * count * plane * width * 11,
            bytes_accessed=12 * plane * width,
            transcendentals=0,
        ),
    )(*points, wavevectors, derived, token_1)
    computed = values[0]
    if spread:
        values = [values[0]] + [
            lax.ppermute(values[s], "orb", pairs(n_orb, s)) for s in range(1, n_orb)
        ]
    else:
        values = values[0][:, :, :local]
        values = lax.all_to_all(values, "orb", split_axis=0, concat_axis=0, tiled=True)
        if width > local:
            values = values.transpose(1, 0, 2).reshape(1, height, electrons)
        values = [values]

    if n_grp == 4:
        y2, x2, token_2 = relay((own[2], own[1]), (y2, x2), (computed,))
        x3, y3 = send_x(y2), send_y(x2)
        arrays += [x1, x2, y1, y2, x3, y3]
        a1, a2, b1, b2, a3, b3 = range(6)
        table = [(), (a1, a2, a3, b3), (a3, b3, b2, b1), (b2, b3, a3, a2)]

    columns = call(
        functools.partial(columns_kernel, count),
        shape((electrons, LANES), BF16),
        [HBM, VM, ANY],
        VM,
        scratch=[
            pltpu.VMEM((chunks, depth, electrons), F32),
            pltpu.SemaphoreType.DMA((chunks,)),
        ],
        flops=2 * electrons * electrons * LANES,
        moved=4 * electrons * electrons,
        vmem=8,
    )(*in_hbm(inverse), tiled, token_2)

    here = lax.axis_index("orb").astype(jnp.int32).reshape(1)
    drift, laplacian, later = call(
        functools.partial(first_kernel, count, targets),
        (
            shape((3, 1, count), F32),
            shape((1, 1, count), F32),
            shape((6 * count, electrons), BF16),
        ),
        [SM] + [VM] * (targets + 1),
        (VM, VM, VM),
        scratch=[pltpu.VMEM((5 * count, electrons), BF16)],
        flops=2 * electrons * 11 * count * LANES,
        moved=44 * count * electrons,
    )(here, *values, columns)

    updated, drift, laplacian, new_weight = call(
        functools.partial(finish_kernel, count, table),
        (
            shape((electrons, electrons), F32),
            shape((6, 1, count), F32),
            shape((2, 1, count), F32),
            shape((1, LANES), F32),
        ),
        [SM] + [VM] * 5 + [HBM] + [ANY] * len(arrays),
        (HBM, VM, VM, VM),
        scratch=[
            pltpu.VMEM((chunks, depth, electrons), BF16),
            pltpu.VMEM((chunks, depth, electrons), F32),
            pltpu.VMEM((electrons, LANES), BF16),
            pltpu.SemaphoreType.DMA((chunks,)),
            pltpu.SemaphoreType.DMA((chunks,)),
        ],
        flops=4 * electrons * electrons * 2 * count,
        moved=6 * electrons * electrons,
        vmem=12,
    )(role, number, later, weight, drift, laplacian, *in_hbm(inverse), *arrays)

    return updated[None], drift.reshape(2, 1, 3, count), laplacian, new_weight[0, :1]


def solution(mesh):
    split = ("grp", "orb")
    return jax.shard_map(
        functools.partial(per_device, mesh.shape["grp"], mesh.shape["orb"]),
        mesh=mesh,
        in_specs=(
            P(),
            P(None, "orb"),
            P(split, None, None),
            P(split, None, None),
            P(None, split, None, None),
            P(None, split, None),
            P("orb"),
            P(split),
            P(split),
        ),
        out_specs=(
            P(split, None, None),
            P(None, split, None, None),
            P(None, split, None),
            P(split),
        ),
        check_vma=False,
    )
```

```python
import functools
import math

import jax
import jax.numpy as jnp
from jax import lax
from jax.experimental import pallas as pl
from jax.experimental.pallas import tpu as pltpu
from jax.sharding import PartitionSpec as P

F32 = jnp.float32
BF16 = jnp.bfloat16
LANES = 128
ROWS = 16
DIRECT_POINTS = False
DIRECT_VALUES = False
MIB = 1024 * 1024
precise = lax.Precision.HIGHEST

SIN_HALF = (4.4428679, -7.30744342, 3.59478808, -0.78437403)
COS_HALF = (1.4142135, -6.97885099, 5.73946117, -1.88356299, 0.31069819)


def dot(a, b, dims=((1,), (0,)), exact=False):
    return lax.dot_general(
        a, b, (dims, ((), ())), precision=precise if exact else None, preferred_element_type=F32
    )


def iota(shape, dim):
    return lax.broadcasted_iota(jnp.int32, shape, dim)


def call(
    kernel, out_shape, in_specs, out_specs, scratch=(), flops=0, moved=0, vmem=4, aliases=None
):
    return pl.pallas_call(
        kernel,
        out_shape=out_shape,
        input_output_aliases=aliases or {},
        in_specs=in_specs,
        out_specs=out_specs,
        scratch_shapes=list(scratch),
        compiler_params=pltpu.CompilerParams(vmem_limit_bytes=vmem * MIB),
        cost_estimate=pl.CostEstimate(flops=flops, bytes_accessed=moved, transcendentals=0),
    )


VM = pl.BlockSpec(memory_space=pltpu.VMEM)
SM = pl.BlockSpec(memory_space=pltpu.SMEM)
ANY = pl.BlockSpec(memory_space=pl.ANY)
HBM = pl.BlockSpec(memory_space=pltpu.HBM)


def shape(dims, dtype):
    return jax.ShapeDtypeStruct(dims, dtype)


def in_hbm(*arrays):
    return tuple(pltpu.with_memory_space_constraint(a, pltpu.HBM) for a in arrays)


def is_power(n):
    return n & (n - 1) == 0


def pairs(n, step):
    if is_power(n):
        return [(i, i ^ step) for i in range(n)]
    return [(i, (i + step) % n) for i in range(n)]


def distance(n, here, there):
    return here ^ there if is_power(n) else lax.rem(here - there + n, n)


def backward(n, step):
    return step if is_power(n) else (n - step) % n


def start_kernel(
    count,
    pos_hbm,
    moved_hbm,
    disp_hbm,
    weight_ref,
    out_ref,
    tiled_ref,
    shift_ref,
    pos_ref,
    moved_ref,
    disp_ref,
    sems,
):
    loads = [
        pltpu.make_async_copy(src, dst, sems.at[i])
        for i, (src, dst) in enumerate(
            (
                (moved_hbm, moved_ref),
                (disp_hbm, disp_ref),
                (pos_hbm, pos_ref),
            )
        )
    ]
    for load in loads:
        load.start()
    electrons = pos_ref.shape[2]
    copies = LANES // count
    loads[0].wait()
    tiled = jnp.concatenate([moved_ref[:, 0, :]] * copies, 1)
    tiled_ref[...] = tiled
    pick = (iota((electrons, LANES), 0) == tiled[0:1, :]).astype(F32)
    block = iota((8, LANES), 1) // count
    zeros = jnp.zeros((5, LANES), F32)
    loads[1].wait()
    for update in range(2):
        shift = jnp.concatenate([disp_ref[3 * update : 3 * update + 3, 0, :]] * copies, 1)
        shift_ref[update] = jnp.concatenate([shift, zeros], 0)
    loads[2].wait()
    pos = jnp.concatenate([pos_ref[:, 0, :], jnp.zeros((5, electrons), F32)], 0)
    old = dot(pos, pick, exact=True)
    disp = shift_ref[0]
    points = old + jnp.where(block % 2 == 1, disp, 0.0)
    first = jnp.where(block == 0, disp, 0.0)
    out_ref[...] = pos + dot(first, pick, ((1,), (1,)), exact=True)
    out_ref[3:6, 0:LANES] = points[0:3]
    out_ref[6:7, 0:LANES] = tiled[0:1, :].astype(F32)
    out_ref[7:8, 0:LANES] = jnp.full((1, LANES), weight_ref[0], F32)


def rows_of(ref, chunk, depth):
    return ref.at[0, pl.ds(chunk * depth, depth)]


def round_kernel(wanted, inverse_hbm, after_ref, *refs):
    outs = refs[: len(wanted)]
    staged, rounded, in_sem, out_sem = refs[len(wanted) :]
    depth = staged.shape[1]
    loads, stores = [], []
    for slot, chunk in enumerate(wanted):
        load = pltpu.make_async_copy(
            rows_of(inverse_hbm, chunk, depth), staged.at[slot], in_sem.at[slot]
        )
        load.start()
        loads.append(load)
    for slot, out in enumerate(outs):
        loads[slot].wait()
        rounded[slot] = staged[slot].astype(BF16)
        store = pltpu.make_async_copy(rounded.at[slot], out, out_sem.at[slot])
        store.start()
        stores.append(store)
    for store in stores:
        store.wait()


def gate_kernel(*refs):
    token_ref = refs[-1]
    token_ref[...] = jnp.zeros(token_ref.shape, F32)


def relay_kernel(flag_ref, own_a, own_b, got_a, got_b, *refs):
    out_a, out_b, token_ref, staged, in_sem, out_sem = refs[-6:]
    pieces, depth, _ = staged.shape

    @pl.when(flag_ref[0] == 0)
    def _():
        loads, stores = [], []
        for piece in range(pieces):
            own, out = (own_a, out_a) if piece < pieces // 2 else (own_b, out_b)
            rows = pl.ds(piece % (pieces // 2) * depth, depth)
            loads.append(
                pltpu.make_async_copy(own.at[rows], staged.at[piece], in_sem.at[piece])
            )
            stores.append(
                pltpu.make_async_copy(staged.at[piece], out.at[rows], out_sem.at[piece])
            )
        for load in loads:
            load.start()
        for load, store in zip(loads, stores):
            load.wait()
            store.start()
        for store in stores:
            store.wait()

    token_ref[...] = jnp.zeros(token_ref.shape, F32)


def points_kernel(count, others, role_ref, *refs):
    own_ref = refs[0]
    received = refs[1 : 1 + others]
    moved_ref, disp_ref, after_ref, points_ref, weight_ref, number_ref = refs[1 + others :]
    role = role_ref[0]
    parent = own_ref[...]
    for step in range(others):
        parent = jnp.where(role == step + 1, received[step][...], parent)
    electrons = parent.shape[1]
    pick = (iota((electrons, LANES), 0) == moved_ref[1:2, :]).astype(F32)
    block = iota((8, LANES), 1) // count
    old = dot(parent, pick, exact=True)
    later = old + jnp.where(block % 2 == 1, disp_ref[1], 0.0)
    zeros = jnp.zeros((5, LANES), F32)
    mine = jnp.concatenate([own_ref[3:6, 0:LANES], zeros], 0)
    theirs = jnp.concatenate([parent[3:6, 0:LANES], zeros], 0)
    points = jnp.where(block < 2, mine, jnp.where(block < 4, theirs, later))
    if len(points_ref.shape) == 2:
        points_ref[...] = points
    else:
        points = jnp.concatenate([points, jnp.zeros((ROWS - 8, LANES), F32)], 0)
        points_ref[...] = jnp.broadcast_to(points[None], points_ref.shape)
    weight_ref[...] = parent[7:8, 0:LANES]
    before = parent[6:7, 0:LANES].astype(jnp.int32)
    number_ref[...] = jnp.where(
        block[0:1] == 0, before, jnp.where(block[0:1] == 1, moved_ref[1:2, :], -1)
    )


def derive(coeff_ref, wave_ref, out_ref):
    waves = wave_ref.shape[1]
    width = coeff_ref.shape[1]
    wave = jnp.transpose(jnp.concatenate([wave_ref[...], jnp.zeros((5, waves), F32)], 0))
    out_ref[:, 0:width] = coeff_ref[...]
    cos_part = coeff_ref[0:waves].astype(F32)
    sin_part = coeff_ref[waves:].astype(F32)
    squared = None
    for a in range(3):
        scale = wave[:, a : a + 1]
        where = slice((a + 1) * width, (a + 2) * width)
        out_ref[0:waves, where] = (scale * sin_part).astype(BF16)
        out_ref[waves:, where] = (-scale * cos_part).astype(BF16)
        squared = scale * scale if a == 0 else squared + scale * scale
    where = slice(4 * width, 5 * width)
    out_ref[0:waves, where] = (-squared * cos_part).astype(BF16)
    out_ref[waves:, where] = (-squared * sin_part).astype(BF16)


def prepare_kernel(wanted, coeff_hbm, wave_hbm, inverse_hbm, after_ref, table_ref, *refs):
    outs = refs[: len(wanted)]
    coeff_ref, wave_ref, staged, rounded, small_sem, in_sem, out_sem = refs[len(wanted) :]
    depth = staged.shape[1]
    wave_load = pltpu.make_async_copy(wave_hbm, wave_ref, small_sem.at[0])
    coeff_load = pltpu.make_async_copy(coeff_hbm, coeff_ref, small_sem.at[1])
    wave_load.start()
    coeff_load.start()
    loads, stores = [], []
    for slot, chunk in enumerate(wanted):
        load = pltpu.make_async_copy(
            rows_of(inverse_hbm, chunk, depth), staged.at[slot], in_sem.at[slot]
        )
        load.start()
        loads.append(load)
    wave_load.wait()
    coeff_load.wait()
    derive(coeff_ref, wave_ref, table_ref)
    for slot, out in enumerate(outs):
        loads[slot].wait()
        rounded[slot] = staged[slot].astype(BF16)
        store = pltpu.make_async_copy(rounded.at[slot], out, out_sem.at[slot])
        store.start()
        stores.append(store)
    for store in stores:
        store.wait()


def horner(coefs, u):
    value = coefs[-1] * u + coefs[-2]
    for c in reversed(coefs[:-2]):
        value = value * u + c
    return value


def evaluate_kernel(count, sources, targets, *refs):
    points = refs[:sources]
    wave_ref, table_ref = refs[sources : sources + 2]
    outs = refs[sources + 3 : -3]
    diff, new, gathered = refs[-3:]
    walkers = gathered.shape[0]
    for w in range(walkers):
        gathered[w] = points[w][...] if sources > 1 else points[0][w, 0:8]
    waves = wave_ref.shape[1]
    width = table_ref.shape[1] // 5
    step = math.gcd(waves, LANES)

    def one(w, carry):
        column = jnp.transpose(gathered[w])
        xs = [column[0 : 6 * count, a : a + 1] for a in range(3)]
        row_d = pl.multiple_of(w * (3 * count), count)
        row_n = pl.multiple_of(w * (2 * count), count)
        for at in range(0, waves, step):
            ks = [wave_ref[a : a + 1, at : at + step] * (0.5 / math.pi) for a in range(3)]
            turn = xs[0] * ks[0] + xs[1] * ks[1] + xs[2] * ks[2]
            r = turn - jnp.floor(turn + 0.5)
            u = r * r
            s = r * horner(SIN_HALF, u)
            c = horner(COS_HALF, u)
            for value, base in ((1.0 - s * s, 0), (s * c, waves)):
                where = slice(base + at, base + at + step)
                kept = value.astype(BF16)
                wide = kept.astype(F32)
                part = [wide[i * count : (i + 1) * count] for i in range(6)]
                diff[pl.ds(row_d, count), where] = (part[3] - part[2]).astype(BF16)
                diff[pl.ds(row_d + count, count), where] = (part[5] - part[4]).astype(BF16)
                diff[pl.ds(row_d + 2 * count, count), where] = (part[1] - part[0]).astype(BF16)
                new[pl.ds(row_n, count), where] = kept[5 * count : 6 * count]
                new[pl.ds(row_n + count, count), where] = kept[count : 2 * count]
        return carry

    lax.fori_loop(0, walkers, one, 0)
    change = dot(diff[...], table_ref[:, 0:width]).astype(BF16)
    rest = dot(new[...], table_ref[:, width:]).astype(BF16)
    for w in range(walkers):
        out_ref = outs[w] if targets > 1 else outs[0].at[w]
        at = w * 3 * count
        out_ref[0 : 2 * count] = change[at : at + 2 * count]
        out_ref[6 * count : 7 * count] = change[at + 2 * count : at + 3 * count]
        for half, base in ((0, 2 * count), (1, 7 * count)):
            row = (2 * w + half) * count
            for a in range(4):
                out_ref[base + a * count : base + (a + 1) * count] = rest[
                    row : row + count, a * width : (a + 1) * width
                ]


def sweep(matrix):
    size = matrix.shape[0]
    log = jnp.zeros((1, 1), F32)
    row = iota((size, size), 0)
    lane = iota((size, size), 1)
    place = iota((1, size), 1)
    for k in range(0, size, 2):
        a = matrix[k : k + 1, k : k + 1]
        b = matrix[k : k + 1, k + 1 : k + 2]
        d = matrix[k + 1 : k + 2, k + 1 : k + 2]
        column_0, column_1 = matrix[:, k : k + 1], matrix[:, k + 1 : k + 2]
        line_0, line_1 = matrix[k : k + 1, :], matrix[k + 1 : k + 2, :]
        det = a * d - b * b
        scale = 1.0 / det
        a, b, d = a * scale, b * scale, d * scale
        scaled_0 = d * line_0 - b * line_1
        scaled_1 = a * line_1 - b * line_0
        reduced = matrix - column_0 * scaled_0 - column_1 * scaled_1
        edge_0 = d * column_0 - b * column_1
        edge_1 = a * column_1 - b * column_0
        scaled_0 = jnp.where(place == k, -d, jnp.where(place == k + 1, b, scaled_0))
        scaled_1 = jnp.where(place == k, b, jnp.where(place == k + 1, -a, scaled_1))
        matrix = jnp.where(lane == k, edge_0, jnp.where(lane == k + 1, edge_1, reduced))
        matrix = jnp.where(row == k, scaled_0, jnp.where(row == k + 1, scaled_1, matrix))
        log = log + jnp.log(det)
    return -matrix, log


def ratio_of(products, size):
    eye = jnp.where(iota((size, size), 0) == iota((size, size), 1), 1.0, 0.0)
    ratio = products[0:size, 0:size] + eye
    inverse, log = sweep(dot(ratio, ratio, ((0,), (0,)), exact=True))
    return ratio, inverse, 0.5 * log


def moved_sums(products, ratio, inverse, count):
    size = ratio.shape[0]
    turned = dot(ratio, inverse, exact=True)[size - count :]
    tile = jnp.concatenate([turned] * 4, 0)
    part = products[size : size + 4 * count, 0:size] * tile
    return dot(jnp.ones((8, size), F32), part, ((1,), (1,)), exact=True)[0:1]


def columns_kernel(count, inverse_hbm, moved_ref, after_ref, out_ref, staged, sem):
    chunks, depth, electrons = staged.shape
    loads = []
    for chunk in range(chunks):
        load = pltpu.make_async_copy(
            rows_of(inverse_hbm, chunk, depth), staged.at[chunk], sem.at[chunk]
        )
        load.start()
        loads.append(load)
    block = iota((1, LANES), 1) // count
    number = jnp.where(block == 0, moved_ref[0:1, :], -1)
    pick = (iota((electrons, LANES), 0) == number).astype(F32).astype(BF16)
    for chunk in range(chunks):
        loads[chunk].wait()
        found = dot(staged[chunk].astype(BF16), pick)
        out_ref[chunk * depth : (chunk + 1) * depth] = found.astype(BF16)


def first_kernel(count, sources, me_ref, *refs):
    values = refs[:sources]
    columns, drift_ref, lap_ref, later_ref, vals = refs[sources:]
    rows = later_ref.shape[0]
    if sources > 1:
        width = values[0].shape[1]
        for step in range(sources):
            at = pl.multiple_of((me_ref[0] ^ step) * width, width)
            later_ref[:, pl.ds(at, width)] = values[step][0:rows]
            vals[:, pl.ds(at, width)] = values[step][rows:]
    else:
        pieces, _, width = values[0].shape
        for piece in range(pieces):
            where = slice(piece * width, (piece + 1) * width)
            later_ref[:, where] = values[0][piece, 0:rows]
            vals[:, where] = values[0][piece, rows:]
    products = dot(vals[...], columns[...])
    ratio, inverse, _ = ratio_of(products, count)
    sums = moved_sums(products, ratio, inverse, count)
    for a in range(3):
        drift_ref[a] = sums[:, a * count : (a + 1) * count]
    lap_ref[0] = sums[:, 3 * count : 4 * count]


def pick_from(number_ref, electrons):
    return (iota((electrons, LANES), 0) == number_ref[...]).astype(F32).astype(BF16)


def chunk_at(plan, role, slot):
    chunk = jnp.int32(plan[0][slot][0])
    for which in range(1, len(plan)):
        chunk = jnp.where(role == which, plan[which][slot][0], chunk)
    return chunk


def load_slots(plan, slots, role, inverse_hbm, inputs, parent, staged, sem):
    depth = parent.shape[1]
    for slot in slots:
        own = pltpu.make_async_copy(
            rows_of(inverse_hbm, plan[0][slot][0], depth), staged.at[slot], sem.at[slot]
        )
        pl.when(role == 0)(own.start)
        for which in range(1, len(plan)):
            sent = pltpu.make_async_copy(
                inputs[plan[which][slot][1]], parent.at[slot], sem.at[slot]
            )
            pl.when(role == which)(sent.start)


def settle_slots(plan, slots, role, inverse_hbm, inputs, parent, staged, sem):
    depth = parent.shape[1]
    for slot in slots:
        own = pltpu.make_async_copy(
            rows_of(inverse_hbm, plan[0][slot][0], depth), staged.at[slot], sem.at[slot]
        )
        sent = pltpu.make_async_copy(inputs[0], parent.at[slot], sem.at[slot])

        @pl.when(role == 0)
        def _():
            own.wait()
            parent[slot] = staged[slot].astype(BF16)

        @pl.when(role != 0)
        def _():
            sent.wait()
            staged[slot] = parent[slot].astype(F32)


def early_kernel(count, plan, role_ref, number_ref, later_ref, inverse_hbm, *refs):
    inputs = refs[:-6]
    columns_ref, products_ref, total_ref, parent, staged, sem = refs[-6:]
    slots, depth, electrons = parent.shape
    role = role_ref[0]
    load_slots(plan, range(slots), role, inverse_hbm, inputs, parent, staged, sem)
    pick = pick_from(number_ref, electrons)
    settle_slots(plan, range(slots), role, inverse_hbm, inputs, parent, staged, sem)
    products, total = None, None
    for slot in range(slots):
        columns = dot(parent[slot], pick).astype(BF16)
        columns_ref[slot] = columns
        at = pl.multiple_of(chunk_at(plan, role, slot) * depth, depth)
        rows = later_ref[:, pl.ds(at, depth)]
        part = dot(rows, columns)
        more = dot(rows[0 : 2 * count], parent[slot])
        products = part if slot == 0 else products + part
        total = more if slot == 0 else total + more
    products_ref[...] = products
    total_ref[...] = total


def finish_kernel(
    count,
    plan,
    role_ref,
    number_ref,
    later_ref,
    weight_ref,
    drift_in,
    lap_in,
    early_ref,
    products_ref,
    total_ref,
    inverse_hbm,
    *refs,
):
    inputs = refs[:-8]
    out_ref, drift_ref, lap_ref, out_weight_ref, parent, staged, in_sem, out_sem = refs[-8:]
    chunks, depth, electrons = parent.shape
    done = early_ref.shape[0]
    late = range(done, chunks)
    size = 2 * count
    role = role_ref[0]
    loads = (role, inverse_hbm, inputs, parent, staged, in_sem)
    load_slots(plan, list(late) + list(range(done)), *loads)
    pick = pick_from(number_ref, electrons)
    settle_slots(plan, late, *loads)
    columns = [early_ref[slot] for slot in range(done)]
    products = products_ref[...]
    rows = []
    for slot in late:
        columns.append(dot(parent[slot], pick).astype(BF16))
        at = pl.multiple_of(chunk_at(plan, role, slot) * depth, depth)
        rows.append(later_ref[:, pl.ds(at, depth)])
        products = products + dot(rows[-1], columns[-1])
    settle_slots(plan, range(done), *loads)
    ratio, inverse, log = ratio_of(products, size)
    total = total_ref[...]
    for slot, part in zip(late, rows):
        total = total + dot(part[0:size], parent[slot])
    small = dot(inverse, ratio, ((1,), (1,)), exact=True)
    solved = dot(small, total, exact=True).astype(BF16)
    solved = jnp.concatenate([solved, jnp.zeros((LANES - size, electrons), BF16)], 0)
    copies = []
    for slot in range(chunks):
        staged[slot] = staged[slot] - dot(columns[slot], solved)
        at = pl.multiple_of(chunk_at(plan, role, slot) * depth, depth)
        copy = pltpu.make_async_copy(
            staged.at[slot], out_ref.at[pl.ds(at, depth)], out_sem.at[slot]
        )
        copy.start()
        copies.append(copy)
    sums = moved_sums(products, ratio, inverse, count)
    drift_ref[0:3] = drift_in[...]
    lap_ref[0:1] = lap_in[...]
    for a in range(3):
        drift_ref[3 + a] = sums[:, a * count : (a + 1) * count]
    lap_ref[1] = sums[:, 3 * count : 4 * count]
    out_weight_ref[...] = weight_ref[...] + log
    for copy in copies:
        copy.wait()


def per_device(
    n_grp,
    n_orb,
    wavevectors,
    coefficients,
    inverse,
    positions,
    displacements,
    moved,
    donor,
    take,
    log_weight,
):
    electrons = inverse.shape[1]
    count = moved.shape[2]
    plane = coefficients.shape[0]
    local = coefficients.shape[1]
    others = n_grp - 1
    chunks = 4

    apart = distance(n_grp, lax.axis_index("grp"), donor[0]).astype(jnp.int32).reshape(1)
    role = jnp.where(take == 1, apart, 0)
    record, tiled, disp = call(
        functools.partial(start_kernel, count),
        (
            shape((8, electrons), F32),
            shape((2, LANES), jnp.int32),
            shape((2, 8, LANES), F32),
        ),
        [HBM, HBM, HBM, SM],
        (VM, VM, VM),
        scratch=[
            pltpu.VMEM((3, 1, electrons), F32),
            pltpu.VMEM((2, 1, count), jnp.int32),
            pltpu.VMEM((6, 1, count), F32),
            pltpu.SemaphoreType.DMA((3,)),
        ],
    )(
        *in_hbm(
            positions.reshape(3, 1, electrons),
            moved,
            displacements.reshape(6, 1, count),
        ),
        log_weight,
    )
    records = [lax.ppermute(record, "grp", pairs(n_grp, s)) for s in range(1, n_grp)]

    depth = electrons // chunks
    kept = shape((depth, electrons), BF16)
    token = shape((8, LANES), F32)
    own = [None] * chunks
    ends = (0, chunks - 1)
    middle = tuple(range(1, chunks - 1))
    own[0], own[-1] = call(
        functools.partial(round_kernel, ends),
        (kept,) * 2,
        [HBM, ANY],
        (ANY,) * 2,
        scratch=[
            pltpu.VMEM((2, depth, electrons), F32),
            pltpu.VMEM((2, depth, electrons), BF16),
            pltpu.SemaphoreType.DMA((2,)),
            pltpu.SemaphoreType.DMA((2,)),
        ],
        moved=3 * electrons * electrons,
        vmem=6,
    )(*in_hbm(inverse), record)
    own[0], own[-1], token_0 = call(
        gate_kernel,
        (kept, kept, token),
        [ANY] * (2 + others) + [SM, SM],
        (ANY, ANY, VM),
        aliases={0: 0, 1: 1},
        vmem=1,
    )(own[0], own[-1], *records, role, apart)

    few = is_power(n_orb) and local % LANES == 0
    direct = few and DIRECT_POINTS
    sources = n_orb if direct else 1
    points, weight, number = call(
        functools.partial(points_kernel, count, others),
        (
            shape((8, LANES) if direct else (n_orb, ROWS, LANES), F32),
            shape((1, LANES), F32),
            shape((1, LANES), jnp.int32),
        ),
        [SM] + [VM] * (others + 3) + [ANY],
        (VM, VM, VM),
    )(role, record, *records, tiled, disp, token_0)
    if direct:
        points = [points] + [lax.ppermute(points, "orb", pairs(n_orb, s)) for s in range(1, n_orb)]
    else:
        points = [lax.all_to_all(points, "orb", split_axis=0, concat_axis=0, tiled=True)]

    width = -(-local // LANES) * LANES
    coeff = jnp.pad(coefficients, ((0, 0), (0, width - local))) if width > local else coefficients
    derived, *prepared = call(
        functools.partial(prepare_kernel, middle),
        (shape((plane, 5 * width), BF16),)
        + (pltpu.HBM((depth, electrons), BF16),) * len(middle),
        [HBM, HBM, HBM, ANY],
        (VM,) + (ANY,) * len(middle),
        scratch=[
            pltpu.VMEM((plane, width), BF16),
            pltpu.VMEM(wavevectors.shape, F32),
            pltpu.VMEM((len(middle), depth, electrons), F32),
            pltpu.VMEM((len(middle), depth, electrons), BF16),
            pltpu.SemaphoreType.DMA((2,)),
            pltpu.SemaphoreType.DMA((len(middle),)),
            pltpu.SemaphoreType.DMA((len(middle),)),
        ],
        flops=8 * plane * width,
        moved=3 * electrons * electrons + 10 * plane * width,
        vmem=12,
    )(*in_hbm(coeff, wavevectors, inverse), weight)
    for chunk, ready in zip(middle, prepared):
        own[chunk] = ready

    arrays = []
    if n_grp == 4:
        send_x = lambda block: lax.ppermute(block, "grp", pairs(n_grp, 1))
        send_y = lambda block: lax.ppermute(block, "grp", pairs(n_grp, 2))

        def relay(mine, got, first):
            return call(
                relay_kernel,
                (kept, kept, token),
                [SM] + [ANY] * (4 + len(first)),
                (ANY, ANY, VM),
                scratch=[
                    pltpu.VMEM((4, depth // 2, electrons), BF16),
                    pltpu.SemaphoreType.DMA((4,)),
                    pltpu.SemaphoreType.DMA((4,)),
                ],
                aliases={3: 0, 4: 1},
                vmem=2,
            )(apart, *in_hbm(*mine), *got, *first)

        x1, y1 = send_x(own[0]), send_y(own[3])
        y1, x1, token_1 = relay((own[1], own[2]), (y1, x1), (derived, *points))
        x2, y2 = send_x(y1), send_y(x1)
    else:
        token_1 = token_2 = jnp.zeros((8, LANES), F32)
        plan = [tuple((chunk, 0) for chunk in range(chunks))]
        for step in range(1, n_grp):
            plan.append(tuple((chunk, len(arrays) + chunk) for chunk in range(chunks)))
            arrays += [lax.ppermute(block, "grp", pairs(n_grp, step)) for block in own]
        settled = len(arrays)

    height = 11 * count
    spread = few and DIRECT_VALUES
    targets = n_orb if spread else 1
    block = n_orb if few else math.gcd(n_orb, 8)
    whole = lambda array: pl.BlockSpec(array.shape, lambda i: (0,) * array.ndim)
    if direct:
        point_specs = [whole(p) for p in points]
    else:
        point_specs = [pl.BlockSpec((block, ROWS, LANES), lambda i: (i, 0, 0))]
    if spread:
        out_shapes = (shape((height, width), BF16),) * n_orb
        out_specs = tuple(whole(o) for o in out_shapes)
    else:
        out_shapes = (shape((n_orb, height, width), BF16),)
        out_specs = (pl.BlockSpec((block, height, width), lambda i: (i, 0, 0)),)
    values = pl.pallas_call(
        functools.partial(evaluate_kernel, count, sources, targets),
        grid=(n_orb // block,),
        out_shape=out_shapes,
        in_specs=point_specs + [whole(wavevectors), whole(derived), ANY],
        out_specs=out_specs,
        scratch_shapes=[
            pltpu.VMEM((block * 3 * count, plane), BF16),
            pltpu.VMEM((block * 2 * count, plane), BF16),
            pltpu.VMEM((block, 8, LANES), F32),
        ],
        compiler_params=pltpu.CompilerParams(vmem_limit_bytes=8 * MIB),
        cost_estimate=pl.CostEstimate(
            flops=2 * n_orb * count * plane * width * 11,
            bytes_accessed=12 * plane * width,
            transcendentals=0,
        ),
    )(*points, wavevectors, derived, token_1)
    computed = values[0]
    if spread:
        values = [values[0]] + [
            lax.ppermute(values[s], "orb", pairs(n_orb, s)) for s in range(1, n_orb)
        ]
    else:
        values = values[0][:, :, :local]
        values = lax.all_to_all(values, "orb", split_axis=0, concat_axis=0, tiled=True)
        if width > local:
            values = values.transpose(1, 0, 2).reshape(1, height, electrons)
        values = [values]

    if n_grp == 4:
        y2, x2, token_2 = relay((own[2], own[1]), (y2, x2), (computed,))
        x3, y3 = send_x(y2), send_y(x2)
        arrays = [x1, x2, y1, y2, x3, y3]
        a1, a2, b1, b2, a3, b3 = range(6)
        first, second, third, fourth = range(chunks)
        plan = [
            tuple((chunk, 0) for chunk in range(chunks)),
            ((first, a1), (second, a2), (third, a3), (fourth, b3)),
            ((fourth, b1), (third, b2), (first, a3), (second, b3)),
            ((fourth, a2), (first, b2), (third, a3), (second, b3)),
        ]
        settled = 4

    columns = call(
        functools.partial(columns_kernel, count),
        shape((electrons, LANES), BF16),
        [HBM, VM, ANY],
        VM,
        scratch=[
            pltpu.VMEM((chunks, depth, electrons), F32),
            pltpu.SemaphoreType.DMA((chunks,)),
        ],
        flops=2 * electrons * electrons * LANES,
        moved=4 * electrons * electrons,
        vmem=8,
    )(*in_hbm(inverse), tiled, token_2)

    here = lax.axis_index("orb").astype(jnp.int32).reshape(1)
    drift, laplacian, later = call(
        functools.partial(first_kernel, count, targets),
        (
            shape((3, 1, count), F32),
            shape((1, 1, count), F32),
            shape((6 * count, electrons), BF16),
        ),
        [SM] + [VM] * (targets + 1),
        (VM, VM, VM),
        scratch=[pltpu.VMEM((5 * count, electrons), BF16)],
        flops=2 * electrons * 11 * count * LANES,
        moved=44 * count * electrons,
    )(here, *values, columns)

    early = 2
    work = 2 * electrons * 2 * count
    early_columns, products, total = call(
        functools.partial(early_kernel, count, plan),
        (
            shape((early, depth, LANES), BF16),
            shape((6 * count, LANES), F32),
            shape((2 * count, electrons), F32),
        ),
        [SM, VM, VM, HBM] + [ANY] * settled,
        (VM, VM, VM),
        scratch=[
            pltpu.VMEM((early, depth, electrons), BF16),
            pltpu.VMEM((early, depth, electrons), F32),
            pltpu.SemaphoreType.DMA((early,)),
        ],
        flops=early * depth * work,
        moved=2 * early * depth * electrons,
        vmem=8,
    )(role, number, later, *in_hbm(inverse), *arrays[:settled])

    updated, drift, laplacian, new_weight = call(
        functools.partial(finish_kernel, count, plan),
        (
            shape((electrons, electrons), F32),
            shape((6, 1, count), F32),
            shape((2, 1, count), F32),
            shape((1, LANES), F32),
        ),
        [SM] + [VM] * 8 + [HBM] + [ANY] * len(arrays),
        (HBM, VM, VM, VM),
        scratch=[
            pltpu.VMEM((chunks, depth, electrons), BF16),
            pltpu.VMEM((chunks, depth, electrons), F32),
            pltpu.SemaphoreType.DMA((chunks,)),
            pltpu.SemaphoreType.DMA((chunks,)),
        ],
        flops=2 * electrons * work,
        moved=6 * electrons * electrons,
        vmem=12,
    )(
        role,
        number,
        later,
        weight,
        drift,
        laplacian,
        early_columns,
        products,
        total,
        *in_hbm(inverse),
        *arrays,
    )

    return updated[None], drift.reshape(2, 1, 3, count), laplacian, new_weight[0, :1]


def solution(mesh):
    split = ("grp", "orb")
    return jax.shard_map(
        functools.partial(per_device, mesh.shape["grp"], mesh.shape["orb"]),
        mesh=mesh,
        in_specs=(
            P(),
            P(None, "orb"),
            P(split, None, None),
            P(split, None, None),
            P(None, split, None, None),
            P(None, split, None),
            P("orb"),
            P(split),
            P(split),
        ),
        out_specs=(
            P(split, None, None),
            P(None, split, None, None),
            P(None, split, None),
            P(split),
        ),
        check_vma=False,
    )
```

```python
import functools
import math

import jax
import jax.numpy as jnp
from jax import lax
from jax.experimental import pallas as pl
from jax.experimental.pallas import tpu as pltpu
from jax.sharding import PartitionSpec as P

F32 = jnp.float32
BF16 = jnp.bfloat16
LANES = 128
ROWS = 16
DIRECT_POINTS = False
DIRECT_VALUES = False
MIB = 1024 * 1024
precise = lax.Precision.HIGHEST

SIN_HALF = (4.4428679, -7.30744342, 3.59478808, -0.78437403)
COS_HALF = (1.4142135, -6.97885099, 5.73946117, -1.88356299, 0.31069819)


def dot(a, b, dims=((1,), (0,)), exact=False):
    return lax.dot_general(
        a, b, (dims, ((), ())), precision=precise if exact else None, preferred_element_type=F32
    )


def iota(shape, dim):
    return lax.broadcasted_iota(jnp.int32, shape, dim)


def call(
    kernel, out_shape, in_specs, out_specs, scratch=(), flops=0, moved=0, vmem=4, aliases=None
):
    return pl.pallas_call(
        kernel,
        out_shape=out_shape,
        input_output_aliases=aliases or {},
        in_specs=in_specs,
        out_specs=out_specs,
        scratch_shapes=list(scratch),
        compiler_params=pltpu.CompilerParams(vmem_limit_bytes=vmem * MIB),
        cost_estimate=pl.CostEstimate(flops=flops, bytes_accessed=moved, transcendentals=0),
    )


VM = pl.BlockSpec(memory_space=pltpu.VMEM)
SM = pl.BlockSpec(memory_space=pltpu.SMEM)
ANY = pl.BlockSpec(memory_space=pl.ANY)
HBM = pl.BlockSpec(memory_space=pltpu.HBM)


def shape(dims, dtype):
    return jax.ShapeDtypeStruct(dims, dtype)


def in_hbm(*arrays):
    return tuple(pltpu.with_memory_space_constraint(a, pltpu.HBM) for a in arrays)


def is_power(n):
    return n & (n - 1) == 0


def pairs(n, step):
    if is_power(n):
        return [(i, i ^ step) for i in range(n)]
    return [(i, (i + step) % n) for i in range(n)]


def distance(n, here, there):
    return here ^ there if is_power(n) else lax.rem(here - there + n, n)


def backward(n, step):
    return step if is_power(n) else (n - step) % n


def start_kernel(
    count,
    pos_hbm,
    moved_hbm,
    disp_hbm,
    weight_ref,
    out_ref,
    tiled_ref,
    shift_ref,
    pos_ref,
    moved_ref,
    disp_ref,
    sems,
):
    loads = [
        pltpu.make_async_copy(src, dst, sems.at[i])
        for i, (src, dst) in enumerate(
            (
                (moved_hbm, moved_ref),
                (disp_hbm, disp_ref),
                (pos_hbm, pos_ref),
            )
        )
    ]
    for load in loads:
        load.start()
    electrons = pos_ref.shape[2]
    copies = LANES // count
    loads[0].wait()
    tiled = jnp.concatenate([moved_ref[:, 0, :]] * copies, 1)
    tiled_ref[...] = tiled
    pick = (iota((electrons, LANES), 0) == tiled[0:1, :]).astype(F32)
    block = iota((8, LANES), 1) // count
    zeros = jnp.zeros((5, LANES), F32)
    loads[1].wait()
    for update in range(2):
        shift = jnp.concatenate([disp_ref[3 * update : 3 * update + 3, 0, :]] * copies, 1)
        shift_ref[update] = jnp.concatenate([shift, zeros], 0)
    loads[2].wait()
    pos = jnp.concatenate([pos_ref[:, 0, :], jnp.zeros((5, electrons), F32)], 0)
    old = dot(pos, pick, exact=True)
    disp = shift_ref[0]
    points = old + jnp.where(block % 2 == 1, disp, 0.0)
    first = jnp.where(block == 0, disp, 0.0)
    out_ref[...] = pos + dot(first, pick, ((1,), (1,)), exact=True)
    out_ref[3:6, 0:LANES] = points[0:3]
    out_ref[6:7, 0:LANES] = tiled[0:1, :].astype(F32)
    out_ref[7:8, 0:LANES] = jnp.full((1, LANES), weight_ref[0], F32)


def rows_of(ref, chunk, depth):
    return ref.at[0, pl.ds(chunk * depth, depth)]


def round_kernel(wanted, inverse_hbm, after_ref, *refs):
    outs = refs[: len(wanted)]
    staged, rounded, in_sem, out_sem = refs[len(wanted) :]
    depth = staged.shape[1]
    loads, stores = [], []
    for slot, chunk in enumerate(wanted):
        load = pltpu.make_async_copy(
            rows_of(inverse_hbm, chunk, depth), staged.at[slot], in_sem.at[slot]
        )
        load.start()
        loads.append(load)
    for slot, out in enumerate(outs):
        loads[slot].wait()
        rounded[slot] = staged[slot].astype(BF16)
        store = pltpu.make_async_copy(rounded.at[slot], out, out_sem.at[slot])
        store.start()
        stores.append(store)
    for store in stores:
        store.wait()


def gate_kernel(*refs):
    token_ref = refs[-1]
    token_ref[...] = jnp.zeros(token_ref.shape, F32)


def relay_kernel(flag_ref, own_a, own_b, got_a, got_b, *refs):
    out_a, out_b, token_ref, staged, in_sem, out_sem = refs[-6:]
    pieces, depth, _ = staged.shape

    @pl.when(flag_ref[0] == 0)
    def _():
        loads, stores = [], []
        for piece in range(pieces):
            own, out = (own_a, out_a) if piece < pieces // 2 else (own_b, out_b)
            rows = pl.ds(piece % (pieces // 2) * depth, depth)
            loads.append(
                pltpu.make_async_copy(own.at[rows], staged.at[piece], in_sem.at[piece])
            )
            stores.append(
                pltpu.make_async_copy(staged.at[piece], out.at[rows], out_sem.at[piece])
            )
        for load in loads:
            load.start()
        for load, store in zip(loads, stores):
            load.wait()
            store.start()
        for store in stores:
            store.wait()

    token_ref[...] = jnp.zeros(token_ref.shape, F32)


def points_kernel(count, others, donor_ref, take_ref, *refs):
    own_ref = refs[0]
    received = refs[1 : 1 + others]
    moved_ref, disp_ref, after_ref, points_ref, weight_ref, number_ref = refs[1 + others : -2]
    role_ref, apart_ref = refs[-2:]
    apart = distance(others + 1, lax.axis_index("grp"), donor_ref[0, 0])
    role = jnp.where(take_ref[0, 0] == 1, apart, 0)
    apart_ref[0] = apart
    role_ref[0] = role
    parent = own_ref[...]
    for step in range(others):
        parent = jnp.where(role == step + 1, received[step][...], parent)
    electrons = parent.shape[1]
    pick = (iota((electrons, LANES), 0) == moved_ref[1:2, :]).astype(F32)
    block = iota((8, LANES), 1) // count
    old = dot(parent, pick, exact=True)
    later = old + jnp.where(block % 2 == 1, disp_ref[1], 0.0)
    zeros = jnp.zeros((5, LANES), F32)
    mine = jnp.concatenate([own_ref[3:6, 0:LANES], zeros], 0)
    theirs = jnp.concatenate([parent[3:6, 0:LANES], zeros], 0)
    points = jnp.where(block < 2, mine, jnp.where(block < 4, theirs, later))
    if len(points_ref.shape) == 2:
        points_ref[...] = points
    else:
        points = jnp.concatenate([points, jnp.zeros((ROWS - 8, LANES), F32)], 0)
        points_ref[...] = jnp.broadcast_to(points[None], points_ref.shape)
    weight_ref[...] = parent[7:8, 0:LANES]
    before = parent[6:7, 0:LANES].astype(jnp.int32)
    number_ref[...] = jnp.where(
        block[0:1] == 0, before, jnp.where(block[0:1] == 1, moved_ref[1:2, :], -1)
    )


def derive(coeff_ref, wave_ref, out_ref):
    waves = wave_ref.shape[1]
    width = coeff_ref.shape[1]
    wave = jnp.transpose(jnp.concatenate([wave_ref[...], jnp.zeros((5, waves), F32)], 0))
    out_ref[:, 0:width] = coeff_ref[...]
    cos_part = coeff_ref[0:waves].astype(F32)
    sin_part = coeff_ref[waves:].astype(F32)
    squared = None
    for a in range(3):
        scale = wave[:, a : a + 1]
        where = slice((a + 1) * width, (a + 2) * width)
        out_ref[0:waves, where] = (scale * sin_part).astype(BF16)
        out_ref[waves:, where] = (-scale * cos_part).astype(BF16)
        squared = scale * scale if a == 0 else squared + scale * scale
    where = slice(4 * width, 5 * width)
    out_ref[0:waves, where] = (-squared * cos_part).astype(BF16)
    out_ref[waves:, where] = (-squared * sin_part).astype(BF16)


def prepare_kernel(wanted, coeff_hbm, wave_hbm, inverse_hbm, after_ref, table_ref, *refs):
    outs = refs[: len(wanted)]
    coeff_ref, wave_ref, staged, rounded, small_sem, in_sem, out_sem = refs[len(wanted) :]
    depth = staged.shape[1]
    wave_load = pltpu.make_async_copy(wave_hbm, wave_ref, small_sem.at[0])
    coeff_load = pltpu.make_async_copy(coeff_hbm, coeff_ref, small_sem.at[1])
    wave_load.start()
    coeff_load.start()
    loads, stores = [], []
    for slot, chunk in enumerate(wanted):
        load = pltpu.make_async_copy(
            rows_of(inverse_hbm, chunk, depth), staged.at[slot], in_sem.at[slot]
        )
        load.start()
        loads.append(load)
    wave_load.wait()
    coeff_load.wait()
    derive(coeff_ref, wave_ref, table_ref)
    for slot, out in enumerate(outs):
        loads[slot].wait()
        rounded[slot] = staged[slot].astype(BF16)
        store = pltpu.make_async_copy(rounded.at[slot], out, out_sem.at[slot])
        store.start()
        stores.append(store)
    for store in stores:
        store.wait()


def horner(coefs, u):
    value = coefs[-1] * u + coefs[-2]
    for c in reversed(coefs[:-2]):
        value = value * u + c
    return value


def evaluate_kernel(count, sources, targets, *refs):
    points = refs[:sources]
    wave_ref, table_ref = refs[sources : sources + 2]
    outs = refs[sources + 3 : -3]
    diff, new, gathered = refs[-3:]
    walkers = gathered.shape[0]
    for w in range(walkers):
        gathered[w] = points[w][...] if sources > 1 else points[0][w, 0:8]
    waves = wave_ref.shape[1]
    width = table_ref.shape[1] // 5
    step = math.gcd(waves, LANES)

    def one(w, carry):
        column = jnp.transpose(gathered[w])
        xs = [column[0 : 6 * count, a : a + 1] for a in range(3)]
        row_d = pl.multiple_of(w * (3 * count), count)
        row_n = pl.multiple_of(w * (2 * count), count)
        for at in range(0, waves, step):
            ks = [wave_ref[a : a + 1, at : at + step] * (0.5 / math.pi) for a in range(3)]
            turn = xs[0] * ks[0] + xs[1] * ks[1] + xs[2] * ks[2]
            r = turn - jnp.floor(turn + 0.5)
            u = r * r
            s = r * horner(SIN_HALF, u)
            c = horner(COS_HALF, u)
            for value, base in ((1.0 - s * s, 0), (s * c, waves)):
                where = slice(base + at, base + at + step)
                kept = value.astype(BF16)
                wide = kept.astype(F32)
                part = [wide[i * count : (i + 1) * count] for i in range(6)]
                diff[pl.ds(row_d, count), where] = (part[3] - part[2]).astype(BF16)
                diff[pl.ds(row_d + count, count), where] = (part[5] - part[4]).astype(BF16)
                diff[pl.ds(row_d + 2 * count, count), where] = (part[1] - part[0]).astype(BF16)
                new[pl.ds(row_n, count), where] = kept[5 * count : 6 * count]
                new[pl.ds(row_n + count, count), where] = kept[count : 2 * count]
        return carry

    lax.fori_loop(0, walkers, one, 0)
    change = dot(diff[...], table_ref[:, 0:width]).astype(BF16)
    rest = dot(new[...], table_ref[:, width:]).astype(BF16)
    for w in range(walkers):
        out_ref = outs[w] if targets > 1 else outs[0].at[w]
        at = w * 3 * count
        out_ref[0 : 2 * count] = change[at : at + 2 * count]
        out_ref[6 * count : 7 * count] = change[at + 2 * count : at + 3 * count]
        for half, base in ((0, 2 * count), (1, 7 * count)):
            row = (2 * w + half) * count
            for a in range(4):
                out_ref[base + a * count : base + (a + 1) * count] = rest[
                    row : row + count, a * width : (a + 1) * width
                ]


def pair_inverse(a, b, d):
    det = a * d - b * b
    scale = 1.0 / det
    return d * scale, -b * scale, a * scale, det


def sweep(matrix):
    size = matrix.shape[0]
    log = jnp.zeros((1, 1), F32)
    row = iota((size, size), 0)
    lane = iota((size, size), 1)
    place = iota((1, size), 1)
    for k in range(0, size, 4):
        columns = [jnp.broadcast_to(matrix[:, k + j : k + j + 1], (size, size)) for j in range(4)]
        lines = [matrix[k + i : k + i + 1, :] for i in range(4)]
        at = lambda i, j: columns[j][k + i : k + i + 1, :]
        a00, a01, a11, det_a = pair_inverse(at(0, 0), at(0, 1), at(1, 1))
        b00, b01, b10, b11 = at(0, 2), at(0, 3), at(1, 2), at(1, 3)
        t00, t01 = a00 * b00 + a01 * b10, a00 * b01 + a01 * b11
        t10, t11 = a01 * b00 + a11 * b10, a01 * b01 + a11 * b11
        d00 = at(2, 2) - (b00 * t00 + b10 * t10)
        d01 = at(2, 3) - (b00 * t01 + b10 * t11)
        d11 = at(3, 3) - (b01 * t01 + b11 * t11)
        s00, s01, s11, det_s = pair_inverse(d00, d01, d11)
        u00, u01 = -(t00 * s00 + t01 * s01), -(t00 * s01 + t01 * s11)
        u10, u11 = -(t10 * s00 + t11 * s01), -(t10 * s01 + t11 * s11)
        q00, q01 = a00 - (u00 * t00 + u01 * t01), a01 - (u00 * t10 + u01 * t11)
        q11 = a11 - (u10 * t10 + u11 * t11)
        pivot = (
            (q00, q01, u00, u01),
            (q01, q11, u10, u11),
            (u00, u10, s00, s01),
            (u01, u11, s01, s11),
        )
        reduced = matrix
        scaled, edges = [], []
        for i in range(4):
            line = pivot[i][0] * lines[0] + pivot[i][1] * lines[1]
            line = line + (pivot[i][2] * lines[2] + pivot[i][3] * lines[3])
            reduced = reduced - columns[i] * line
            for j in range(4):
                line = jnp.where(place == k + j, -pivot[i][j], line)
            scaled.append(line)
            edge = pivot[i][0] * columns[0] + pivot[i][1] * columns[1]
            edges.append(edge + (pivot[i][2] * columns[2] + pivot[i][3] * columns[3]))
        matrix = reduced
        for i in range(4):
            matrix = jnp.where(lane == k + i, edges[i], matrix)
        for i in range(4):
            matrix = jnp.where(row == k + i, scaled[i], matrix)
        log = log + (jnp.log(det_a[:, 0:1]) + jnp.log(det_s[:, 0:1]))
    return -matrix, log


def ratio_of(products, size):
    eye = jnp.where(iota((size, size), 0) == iota((size, size), 1), 1.0, 0.0)
    ratio = products[0:size, 0:size] + eye
    inverse, log = sweep(dot(ratio, ratio, ((0,), (0,)), exact=True))
    return ratio, inverse, 0.5 * log


def moved_sums(products, ratio, inverse, count):
    size = ratio.shape[0]
    turned = dot(ratio, inverse, exact=True)[size - count :]
    tile = jnp.concatenate([turned] * 4, 0)
    part = products[size : size + 4 * count, 0:size] * tile
    return dot(jnp.ones((8, size), F32), part, ((1,), (1,)), exact=True)[0:1]


def columns_kernel(count, inverse_hbm, moved_ref, after_ref, out_ref, staged, sem):
    chunks, depth, electrons = staged.shape
    loads = []
    for chunk in range(chunks):
        load = pltpu.make_async_copy(
            rows_of(inverse_hbm, chunk, depth), staged.at[chunk], sem.at[chunk]
        )
        load.start()
        loads.append(load)
    block = iota((1, LANES), 1) // count
    number = jnp.where(block == 0, moved_ref[0:1, :], -1)
    pick = (iota((electrons, LANES), 0) == number).astype(F32).astype(BF16)
    for chunk in range(chunks):
        loads[chunk].wait()
        found = dot(staged[chunk].astype(BF16), pick)
        out_ref[chunk * depth : (chunk + 1) * depth] = found.astype(BF16)


def first_kernel(count, sources, me_ref, *refs):
    values = refs[:sources]
    columns, drift_ref, lap_ref, later_ref, vals = refs[sources:]
    rows = later_ref.shape[0]
    if sources > 1:
        width = values[0].shape[1]
        for step in range(sources):
            at = pl.multiple_of((me_ref[0] ^ step) * width, width)
            later_ref[:, pl.ds(at, width)] = values[step][0:rows]
            vals[:, pl.ds(at, width)] = values[step][rows:]
    else:
        pieces, _, width = values[0].shape
        for piece in range(pieces):
            where = slice(piece * width, (piece + 1) * width)
            later_ref[:, where] = values[0][piece, 0:rows]
            vals[:, where] = values[0][piece, rows:]
    products = dot(vals[...], columns[...])
    ratio, inverse, _ = ratio_of(products, count)
    sums = moved_sums(products, ratio, inverse, count)
    for a in range(3):
        drift_ref[a] = sums[:, a * count : (a + 1) * count]
    lap_ref[0] = sums[:, 3 * count : 4 * count]


def pick_from(number_ref, electrons):
    return (iota((electrons, LANES), 0) == number_ref[...]).astype(F32).astype(BF16)


def chunk_at(plan, role, slot):
    chunk = jnp.int32(plan[0][slot][0])
    for which in range(1, len(plan)):
        chunk = jnp.where(role == which, plan[which][slot][0], chunk)
    return chunk


def load_slots(plan, slots, role, inverse_hbm, inputs, parent, staged, sem):
    depth = parent.shape[1]
    for slot in slots:
        own = pltpu.make_async_copy(
            rows_of(inverse_hbm, plan[0][slot][0], depth), staged.at[slot], sem.at[slot]
        )
        pl.when(role == 0)(own.start)
        for which in range(1, len(plan)):
            sent = pltpu.make_async_copy(
                inputs[plan[which][slot][1]], parent.at[slot], sem.at[slot]
            )
            pl.when(role == which)(sent.start)


def settle_slots(plan, slots, role, inverse_hbm, inputs, parent, staged, sem):
    depth = parent.shape[1]
    for slot in slots:
        own = pltpu.make_async_copy(
            rows_of(inverse_hbm, plan[0][slot][0], depth), staged.at[slot], sem.at[slot]
        )
        sent = pltpu.make_async_copy(inputs[0], parent.at[slot], sem.at[slot])

        @pl.when(role == 0)
        def _():
            own.wait()
            parent[slot] = staged[slot].astype(BF16)

        @pl.when(role != 0)
        def _():
            sent.wait()


def early_kernel(count, plan, role_ref, number_ref, later_ref, inverse_hbm, *refs):
    inputs = refs[:-6]
    columns_ref, products_ref, total_ref, parent, staged, sem = refs[-6:]
    slots, depth, electrons = parent.shape
    role = role_ref[0]
    load_slots(plan, range(slots), role, inverse_hbm, inputs, parent, staged, sem)
    pick = pick_from(number_ref, electrons)
    settle_slots(plan, range(slots), role, inverse_hbm, inputs, parent, staged, sem)
    products, total = None, None
    for slot in range(slots):
        columns = dot(parent[slot], pick).astype(BF16)
        columns_ref[slot] = columns
        at = pl.multiple_of(chunk_at(plan, role, slot) * depth, depth)
        rows = later_ref[:, pl.ds(at, depth)]
        part = dot(rows, columns)
        more = dot(rows[0 : 2 * count], parent[slot])
        products = part if slot == 0 else products + part
        total = more if slot == 0 else total + more
    products_ref[...] = products
    total_ref[...] = total


def finish_kernel(
    count,
    plan,
    role_ref,
    number_ref,
    later_ref,
    weight_ref,
    drift_in,
    lap_in,
    early_ref,
    products_ref,
    total_ref,
    inverse_hbm,
    *refs,
):
    inputs = refs[:-8]
    out_ref, drift_ref, lap_ref, out_weight_ref, parent, staged, in_sem, out_sem = refs[-8:]
    chunks, depth, electrons = parent.shape
    done = early_ref.shape[0]
    late = range(done, chunks)
    size = 2 * count
    role = role_ref[0]
    loads = (role, inverse_hbm, inputs, parent, staged, in_sem)
    load_slots(plan, list(late) + list(range(done)), *loads)
    pick = pick_from(number_ref, electrons)
    settle_slots(plan, late, *loads)
    columns = [early_ref[slot] for slot in range(done)]
    products = products_ref[...]
    rows = []
    for slot in late:
        columns.append(dot(parent[slot], pick).astype(BF16))
        at = pl.multiple_of(chunk_at(plan, role, slot) * depth, depth)
        rows.append(later_ref[:, pl.ds(at, depth)])
        products = products + dot(rows[-1], columns[-1])
    ratio, inverse, log = ratio_of(products, size)
    total = total_ref[...]
    for slot, part in zip(late, rows):
        total = total + dot(part[0:size], parent[slot])
    small = dot(inverse, ratio, ((1,), (1,)), exact=True)
    high = small.astype(BF16)
    halves = jnp.concatenate([high, (small - high.astype(F32)).astype(BF16)], 1)
    rounded = total.astype(BF16)
    solved = dot(halves, jnp.concatenate([rounded, rounded], 0)).astype(BF16)
    solved = jnp.concatenate([solved, jnp.zeros((LANES - size, electrons), BF16)], 0)
    settle_slots(plan, range(done), *loads)
    copies = []
    for slot in list(late) + list(range(done)):
        at = pl.multiple_of(chunk_at(plan, role, slot) * depth, depth)
        copy = pltpu.make_async_copy(
            staged.at[slot], out_ref.at[pl.ds(at, depth)], out_sem.at[slot]
        )
        copies.append((slot, copy))

    def write(before):
        for slot, copy in copies:
            staged[slot] = before(slot) - dot(columns[slot], solved)
            copy.start()

    pl.when(role == 0)(lambda: write(lambda slot: staged[slot]))
    pl.when(role != 0)(lambda: write(lambda slot: parent[slot].astype(F32)))
    sums = moved_sums(products, ratio, inverse, count)
    drift_ref[0:3] = drift_in[...]
    lap_ref[0:1] = lap_in[...]
    for a in range(3):
        drift_ref[3 + a] = sums[:, a * count : (a + 1) * count]
    lap_ref[1] = sums[:, 3 * count : 4 * count]
    out_weight_ref[...] = weight_ref[...] + log
    for _, copy in copies:
        copy.wait()


def per_device(
    n_grp,
    n_orb,
    wavevectors,
    coefficients,
    inverse,
    positions,
    displacements,
    moved,
    donor,
    take,
    log_weight,
):
    electrons = inverse.shape[1]
    count = moved.shape[2]
    plane = coefficients.shape[0]
    local = coefficients.shape[1]
    others = n_grp - 1
    chunks = 4

    record, tiled, disp = call(
        functools.partial(start_kernel, count),
        (
            shape((8, electrons), F32),
            shape((2, LANES), jnp.int32),
            shape((2, 8, LANES), F32),
        ),
        [HBM, HBM, HBM, SM],
        (VM, VM, VM),
        scratch=[
            pltpu.VMEM((3, 1, electrons), F32),
            pltpu.VMEM((2, 1, count), jnp.int32),
            pltpu.VMEM((6, 1, count), F32),
            pltpu.SemaphoreType.DMA((3,)),
        ],
    )(
        *in_hbm(
            positions.reshape(3, 1, electrons),
            moved,
            displacements.reshape(6, 1, count),
        ),
        log_weight,
    )
    records = [lax.ppermute(record, "grp", pairs(n_grp, s)) for s in range(1, n_grp)]

    depth = electrons // chunks
    kept = shape((depth, electrons), BF16)
    token = shape((8, LANES), F32)
    own = [None] * chunks
    ends = (0, chunks - 1)
    middle = tuple(range(1, chunks - 1))
    own[0], own[-1] = call(
        functools.partial(round_kernel, ends),
        (kept,) * 2,
        [HBM, ANY],
        (ANY,) * 2,
        scratch=[
            pltpu.VMEM((2, depth, electrons), F32),
            pltpu.VMEM((2, depth, electrons), BF16),
            pltpu.SemaphoreType.DMA((2,)),
            pltpu.SemaphoreType.DMA((2,)),
        ],
        moved=3 * electrons * electrons,
        vmem=6,
    )(*in_hbm(inverse), record)
    own[0], own[-1], token_0 = call(
        gate_kernel,
        (kept, kept, token),
        [ANY] * (2 + others),
        (ANY, ANY, VM),
        aliases={0: 0, 1: 1},
        vmem=1,
    )(own[0], own[-1], *records)

    few = is_power(n_orb) and local % LANES == 0
    direct = few and DIRECT_POINTS
    sources = n_orb if direct else 1
    points, weight, number, role, apart = call(
        functools.partial(points_kernel, count, others),
        (
            shape((8, LANES) if direct else (n_orb, ROWS, LANES), F32),
            shape((1, LANES), F32),
            shape((1, LANES), jnp.int32),
            shape((1,), jnp.int32),
            shape((1,), jnp.int32),
        ),
        [VM, VM] + [VM] * (others + 3) + [ANY],
        (VM, VM, VM, SM, SM),
    )(donor.reshape(1, 1), take.reshape(1, 1), record, *records, tiled, disp, token_0)
    if direct:
        points = [points] + [lax.ppermute(points, "orb", pairs(n_orb, s)) for s in range(1, n_orb)]
    else:
        points = [lax.all_to_all(points, "orb", split_axis=0, concat_axis=0, tiled=True)]

    width = -(-local // LANES) * LANES
    coeff = jnp.pad(coefficients, ((0, 0), (0, width - local))) if width > local else coefficients
    derived, *prepared = call(
        functools.partial(prepare_kernel, middle),
        (shape((plane, 5 * width), BF16),)
        + (pltpu.HBM((depth, electrons), BF16),) * len(middle),
        [HBM, HBM, HBM, ANY],
        (VM,) + (ANY,) * len(middle),
        scratch=[
            pltpu.VMEM((plane, width), BF16),
            pltpu.VMEM(wavevectors.shape, F32),
            pltpu.VMEM((len(middle), depth, electrons), F32),
            pltpu.VMEM((len(middle), depth, electrons), BF16),
            pltpu.SemaphoreType.DMA((2,)),
            pltpu.SemaphoreType.DMA((len(middle),)),
            pltpu.SemaphoreType.DMA((len(middle),)),
        ],
        flops=8 * plane * width,
        moved=3 * electrons * electrons + 10 * plane * width,
        vmem=12,
    )(*in_hbm(coeff, wavevectors, inverse), weight)
    for chunk, ready in zip(middle, prepared):
        own[chunk] = ready

    arrays = []
    if n_grp == 4:
        send_x = lambda block: lax.ppermute(block, "grp", pairs(n_grp, 1))
        send_y = lambda block: lax.ppermute(block, "grp", pairs(n_grp, 2))

        def relay(mine, got, first):
            return call(
                relay_kernel,
                (kept, kept, token),
                [SM] + [ANY] * (4 + len(first)),
                (ANY, ANY, VM),
                scratch=[
                    pltpu.VMEM((8, depth // 4, electrons), BF16),
                    pltpu.SemaphoreType.DMA((8,)),
                    pltpu.SemaphoreType.DMA((8,)),
                ],
                aliases={3: 0, 4: 1},
                vmem=2,
            )(apart, *in_hbm(*mine), *got, *first)

        x1, y1 = send_x(own[0]), send_y(own[3])
        y1, x1, token_1 = relay((own[1], own[2]), (y1, x1), (derived, *points))
        x2, y2 = send_x(y1), send_y(x1)
    else:
        token_1 = token_2 = jnp.zeros((8, LANES), F32)
        plan = [tuple((chunk, 0) for chunk in range(chunks))]
        for step in range(1, n_grp):
            plan.append(tuple((chunk, len(arrays) + chunk) for chunk in range(chunks)))
            arrays += [lax.ppermute(block, "grp", pairs(n_grp, step)) for block in own]
        settled = len(arrays)

    height = 11 * count
    spread = few and DIRECT_VALUES
    targets = n_orb if spread else 1
    block = n_orb if few else math.gcd(n_orb, 8)
    whole = lambda array: pl.BlockSpec(array.shape, lambda i: (0,) * array.ndim)
    if direct:
        point_specs = [whole(p) for p in points]
    else:
        point_specs = [pl.BlockSpec((block, ROWS, LANES), lambda i: (i, 0, 0))]
    if spread:
        out_shapes = (shape((height, width), BF16),) * n_orb
        out_specs = tuple(whole(o) for o in out_shapes)
    else:
        out_shapes = (shape((n_orb, height, width), BF16),)
        out_specs = (pl.BlockSpec((block, height, width), lambda i: (i, 0, 0)),)
    values = pl.pallas_call(
        functools.partial(evaluate_kernel, count, sources, targets),
        grid=(n_orb // block,),
        out_shape=out_shapes,
        in_specs=point_specs + [whole(wavevectors), whole(derived), ANY],
        out_specs=out_specs,
        scratch_shapes=[
            pltpu.VMEM((block * 3 * count, plane), BF16),
            pltpu.VMEM((block * 2 * count, plane), BF16),
            pltpu.VMEM((block, 8, LANES), F32),
        ],
        compiler_params=pltpu.CompilerParams(vmem_limit_bytes=8 * MIB),
        cost_estimate=pl.CostEstimate(
            flops=2 * n_orb * count * plane * width * 11,
            bytes_accessed=12 * plane * width,
            transcendentals=0,
        ),
    )(*points, wavevectors, derived, token_1)
    computed = values[0]
    if spread:
        values = [values[0]] + [
            lax.ppermute(values[s], "orb", pairs(n_orb, s)) for s in range(1, n_orb)
        ]
    else:
        values = values[0][:, :, :local]
        values = lax.all_to_all(values, "orb", split_axis=0, concat_axis=0, tiled=True)
        if width > local:
            values = values.transpose(1, 0, 2).reshape(1, height, electrons)
        values = [values]

    if n_grp == 4:
        y2, x2, token_2 = relay((own[2], own[1]), (y2, x2), (computed,))
        x3, y3 = send_x(y2), send_y(x2)
        arrays = [x1, x2, y1, y2, x3, y3]
        a1, a2, b1, b2, a3, b3 = range(6)
        first, second, third, fourth = range(chunks)
        plan = [
            tuple((chunk, 0) for chunk in range(chunks)),
            ((first, a1), (second, a2), (third, a3), (fourth, b3)),
            ((fourth, b1), (third, b2), (first, a3), (second, b3)),
            ((fourth, a2), (first, b2), (third, a3), (second, b3)),
        ]
        settled = 4

    columns = call(
        functools.partial(columns_kernel, count),
        shape((electrons, LANES), BF16),
        [HBM, VM, ANY],
        VM,
        scratch=[
            pltpu.VMEM((chunks, depth, electrons), F32),
            pltpu.SemaphoreType.DMA((chunks,)),
        ],
        flops=2 * electrons * electrons * LANES,
        moved=4 * electrons * electrons,
        vmem=8,
    )(*in_hbm(inverse), tiled, token_2)

    here = lax.axis_index("orb").astype(jnp.int32).reshape(1)
    drift, laplacian, later = call(
        functools.partial(first_kernel, count, targets),
        (
            shape((3, 1, count), F32),
            shape((1, 1, count), F32),
            shape((6 * count, electrons), BF16),
        ),
        [SM] + [VM] * (targets + 1),
        (VM, VM, VM),
        scratch=[pltpu.VMEM((5 * count, electrons), BF16)],
        flops=2 * electrons * 11 * count * LANES,
        moved=44 * count * electrons,
    )(here, *values, columns)

    early = 2
    work = 2 * electrons * 2 * count
    early_columns, products, total = call(
        functools.partial(early_kernel, count, plan),
        (
            shape((early, depth, LANES), BF16),
            shape((6 * count, LANES), F32),
            shape((2 * count, electrons), F32),
        ),
        [SM, VM, VM, HBM] + [ANY] * settled,
        (VM, VM, VM),
        scratch=[
            pltpu.VMEM((early, depth, electrons), BF16),
            pltpu.VMEM((early, depth, electrons), F32),
            pltpu.SemaphoreType.DMA((early,)),
        ],
        flops=early * depth * work,
        moved=2 * early * depth * electrons,
        vmem=8,
    )(role, number, later, *in_hbm(inverse), *arrays[:settled])

    updated, drift, laplacian, new_weight = call(
        functools.partial(finish_kernel, count, plan),
        (
            shape((electrons, electrons), F32),
            shape((6, 1, count), F32),
            shape((2, 1, count), F32),
            shape((1, LANES), F32),
        ),
        [SM] + [VM] * 8 + [HBM] + [ANY] * len(arrays),
        (HBM, VM, VM, VM),
        scratch=[
            pltpu.VMEM((chunks, depth, electrons), BF16),
            pltpu.VMEM((chunks, depth, electrons), F32),
            pltpu.SemaphoreType.DMA((chunks,)),
            pltpu.SemaphoreType.DMA((chunks,)),
        ],
        flops=2 * electrons * work,
        moved=6 * electrons * electrons,
        vmem=12,
    )(
        role,
        number,
        later,
        weight,
        drift,
        laplacian,
        early_columns,
        products,
        total,
        *in_hbm(inverse),
        *arrays,
    )

    return updated[None], drift.reshape(2, 1, 3, count), laplacian, new_weight[0, :1]


def solution(mesh):
    split = ("grp", "orb")
    return jax.shard_map(
        functools.partial(per_device, mesh.shape["grp"], mesh.shape["orb"]),
        mesh=mesh,
        in_specs=(
            P(),
            P(None, "orb"),
            P(split, None, None),
            P(split, None, None),
            P(None, split, None, None),
            P(None, split, None),
            P("orb"),
            P(split),
            P(split),
        ),
        out_specs=(
            P(split, None, None),
            P(None, split, None, None),
            P(None, split, None),
            P(split),
        ),
        check_vma=False,
    )
```

```python
import functools
import math

import jax
import jax.numpy as jnp
from jax import lax
from jax.experimental import pallas as pl
from jax.experimental.pallas import tpu as pltpu
from jax.sharding import PartitionSpec as P

F32 = jnp.float32
BF16 = jnp.bfloat16
LANES = 128
ROWS = 16
DIRECT_POINTS = False
DIRECT_VALUES = False
MIB = 1024 * 1024
precise = lax.Precision.HIGHEST

SIN_HALF = (4.4428679, -7.30744342, 3.59478808, -0.78437403)
COS_HALF = (1.4142135, -6.97885099, 5.73946117, -1.88356299, 0.31069819)


def dot(a, b, dims=((1,), (0,)), exact=False):
    return lax.dot_general(
        a, b, (dims, ((), ())), precision=precise if exact else None, preferred_element_type=F32
    )


def iota(shape, dim):
    return lax.broadcasted_iota(jnp.int32, shape, dim)


def call(
    kernel, out_shape, in_specs, out_specs, scratch=(), flops=0, moved=0, vmem=4, aliases=None
):
    return pl.pallas_call(
        kernel,
        out_shape=out_shape,
        input_output_aliases=aliases or {},
        in_specs=in_specs,
        out_specs=out_specs,
        scratch_shapes=list(scratch),
        compiler_params=pltpu.CompilerParams(vmem_limit_bytes=vmem * MIB),
        cost_estimate=pl.CostEstimate(flops=flops, bytes_accessed=moved, transcendentals=0),
    )


VM = pl.BlockSpec(memory_space=pltpu.VMEM)
SM = pl.BlockSpec(memory_space=pltpu.SMEM)
ANY = pl.BlockSpec(memory_space=pl.ANY)
HBM = pl.BlockSpec(memory_space=pltpu.HBM)


def shape(dims, dtype):
    return jax.ShapeDtypeStruct(dims, dtype)


def in_hbm(*arrays):
    return tuple(pltpu.with_memory_space_constraint(a, pltpu.HBM) for a in arrays)


def is_power(n):
    return n & (n - 1) == 0


def pairs(n, step):
    if is_power(n):
        return [(i, i ^ step) for i in range(n)]
    return [(i, (i + step) % n) for i in range(n)]


def distance(n, here, there):
    return here ^ there if is_power(n) else lax.rem(here - there + n, n)


def backward(n, step):
    return step if is_power(n) else (n - step) % n


def start_kernel(
    count,
    pos_hbm,
    moved_hbm,
    disp_hbm,
    weight_ref,
    out_ref,
    tiled_ref,
    shift_ref,
    pos_ref,
    moved_ref,
    disp_ref,
    sems,
):
    loads = [
        pltpu.make_async_copy(src, dst, sems.at[i])
        for i, (src, dst) in enumerate(
            (
                (moved_hbm, moved_ref),
                (disp_hbm, disp_ref),
                (pos_hbm, pos_ref),
            )
        )
    ]
    for load in loads:
        load.start()
    electrons = pos_ref.shape[2]
    copies = LANES // count
    loads[0].wait()
    tiled = jnp.concatenate([moved_ref[:, 0, :]] * copies, 1)
    tiled_ref[...] = tiled
    pick = (iota((electrons, LANES), 0) == tiled[0:1, :]).astype(F32)
    block = iota((8, LANES), 1) // count
    zeros = jnp.zeros((5, LANES), F32)
    loads[1].wait()
    for update in range(2):
        shift = jnp.concatenate([disp_ref[3 * update : 3 * update + 3, 0, :]] * copies, 1)
        shift_ref[update] = jnp.concatenate([shift, zeros], 0)
    loads[2].wait()
    pos = jnp.concatenate([pos_ref[:, 0, :], jnp.zeros((5, electrons), F32)], 0)
    old = dot(pos, pick, exact=True)
    disp = shift_ref[0]
    points = old + jnp.where(block % 2 == 1, disp, 0.0)
    first = jnp.where(block == 0, disp, 0.0)
    out_ref[...] = pos + dot(first, pick, ((1,), (1,)), exact=True)
    out_ref[3:6, 0:LANES] = points[0:3]
    out_ref[6:7, 0:LANES] = tiled[0:1, :].astype(F32)
    out_ref[7:8, 0:LANES] = jnp.full((1, LANES), weight_ref[0], F32)


def rows_of(ref, chunk, depth):
    return ref.at[0, pl.ds(chunk * depth, depth)]


def round_kernel(wanted, inverse_hbm, after_ref, *refs):
    outs = refs[: len(wanted)]
    staged, rounded, in_sem, out_sem = refs[len(wanted) :]
    depth = staged.shape[1]
    loads, stores = [], []
    for slot, chunk in enumerate(wanted):
        load = pltpu.make_async_copy(
            rows_of(inverse_hbm, chunk, depth), staged.at[slot], in_sem.at[slot]
        )
        load.start()
        loads.append(load)
    for slot, out in enumerate(outs):
        loads[slot].wait()
        rounded[slot] = staged[slot].astype(BF16)
        store = pltpu.make_async_copy(rounded.at[slot], out, out_sem.at[slot])
        store.start()
        stores.append(store)
    for store in stores:
        store.wait()


def gate_kernel(*refs):
    token_ref = refs[-1]
    token_ref[...] = jnp.zeros(token_ref.shape, F32)


def relay_kernel(flag_ref, own_a, own_b, got_a, got_b, *refs):
    out_a, out_b, token_ref, staged, in_sem, out_sem = refs[-6:]
    pieces, depth, _ = staged.shape

    @pl.when(flag_ref[0] == 0)
    def _():
        loads, stores = [], []
        for piece in range(pieces):
            own, out = (own_a, out_a) if piece < pieces // 2 else (own_b, out_b)
            rows = pl.ds(piece % (pieces // 2) * depth, depth)
            loads.append(
                pltpu.make_async_copy(own.at[rows], staged.at[piece], in_sem.at[piece])
            )
            stores.append(
                pltpu.make_async_copy(staged.at[piece], out.at[rows], out_sem.at[piece])
            )
        for load in loads:
            load.start()
        for load, store in zip(loads, stores):
            load.wait()
            store.start()
        for store in stores:
            store.wait()

    token_ref[...] = jnp.zeros(token_ref.shape, F32)


def points_kernel(count, others, donor_ref, take_ref, *refs):
    own_ref = refs[0]
    received = refs[1 : 1 + others]
    moved_ref, disp_ref, after_ref, points_ref, weight_ref, number_ref = refs[1 + others : -2]
    role_ref, apart_ref = refs[-2:]
    apart = distance(others + 1, lax.axis_index("grp"), donor_ref[0, 0])
    role = jnp.where(take_ref[0, 0] == 1, apart, 0)
    apart_ref[0] = apart
    role_ref[0] = role
    parent = own_ref[...]
    for step in range(others):
        parent = jnp.where(role == step + 1, received[step][...], parent)
    electrons = parent.shape[1]
    pick = (iota((electrons, LANES), 0) == moved_ref[1:2, :]).astype(F32)
    block = iota((8, LANES), 1) // count
    old = dot(parent, pick, exact=True)
    later = old + jnp.where(block % 2 == 1, disp_ref[1], 0.0)
    zeros = jnp.zeros((5, LANES), F32)
    mine = jnp.concatenate([own_ref[3:6, 0:LANES], zeros], 0)
    theirs = jnp.concatenate([parent[3:6, 0:LANES], zeros], 0)
    points = jnp.where(block < 2, mine, jnp.where(block < 4, theirs, later))
    if len(points_ref.shape) == 2:
        points_ref[...] = points
    else:
        points = jnp.concatenate([points, jnp.zeros((ROWS - 8, LANES), F32)], 0)
        points_ref[...] = jnp.broadcast_to(points[None], points_ref.shape)
    weight_ref[...] = parent[7:8, 0:LANES]
    before = parent[6:7, 0:LANES].astype(jnp.int32)
    number_ref[...] = jnp.where(
        block[0:1] == 0, before, jnp.where(block[0:1] == 1, moved_ref[1:2, :], -1)
    )


def derive(coeff_ref, wave_ref, out_ref):
    waves = wave_ref.shape[1]
    width = coeff_ref.shape[1]
    wave = jnp.transpose(jnp.concatenate([wave_ref[...], jnp.zeros((5, waves), F32)], 0))
    out_ref[:, 0:width] = coeff_ref[...]
    cos_part = coeff_ref[0:waves].astype(F32)
    sin_part = coeff_ref[waves:].astype(F32)
    squared = None
    for a in range(3):
        scale = wave[:, a : a + 1]
        where = slice((a + 1) * width, (a + 2) * width)
        out_ref[0:waves, where] = (scale * sin_part).astype(BF16)
        out_ref[waves:, where] = (-scale * cos_part).astype(BF16)
        squared = scale * scale if a == 0 else squared + scale * scale
    where = slice(4 * width, 5 * width)
    out_ref[0:waves, where] = (-squared * cos_part).astype(BF16)
    out_ref[waves:, where] = (-squared * sin_part).astype(BF16)


def prepare_kernel(wanted, coeff_hbm, wave_hbm, inverse_hbm, after_ref, table_ref, *refs):
    outs = refs[: len(wanted)]
    coeff_ref, wave_ref, staged, rounded, small_sem, in_sem, out_sem = refs[len(wanted) :]
    depth = staged.shape[1]
    wave_load = pltpu.make_async_copy(wave_hbm, wave_ref, small_sem.at[0])
    coeff_load = pltpu.make_async_copy(coeff_hbm, coeff_ref, small_sem.at[1])
    wave_load.start()
    coeff_load.start()
    loads, stores = [], []
    for slot, chunk in enumerate(wanted):
        load = pltpu.make_async_copy(
            rows_of(inverse_hbm, chunk, depth), staged.at[slot], in_sem.at[slot]
        )
        load.start()
        loads.append(load)
    wave_load.wait()
    coeff_load.wait()
    derive(coeff_ref, wave_ref, table_ref)
    for slot, out in enumerate(outs):
        loads[slot].wait()
        rounded[slot] = staged[slot].astype(BF16)
        store = pltpu.make_async_copy(rounded.at[slot], out, out_sem.at[slot])
        store.start()
        stores.append(store)
    for store in stores:
        store.wait()


def horner(coefs, u):
    value = coefs[-1] * u + coefs[-2]
    for c in reversed(coefs[:-2]):
        value = value * u + c
    return value


def evaluate_kernel(count, sources, targets, *refs):
    points = refs[:sources]
    wave_ref, table_ref = refs[sources : sources + 2]
    outs = refs[sources + 3 : -3]
    diff, new, gathered = refs[-3:]
    walkers = gathered.shape[0]
    for w in range(walkers):
        gathered[w] = points[w][...] if sources > 1 else points[0][w, 0:8]
    waves = wave_ref.shape[1]
    width = table_ref.shape[1] // 5
    step = math.gcd(waves, LANES)

    def one(w, carry):
        column = jnp.transpose(gathered[w])
        xs = [column[0 : 6 * count, a : a + 1] for a in range(3)]
        row_d = pl.multiple_of(w * (3 * count), count)
        row_n = pl.multiple_of(w * (2 * count), count)
        for at in range(0, waves, step):
            ks = [wave_ref[a : a + 1, at : at + step] * (0.5 / math.pi) for a in range(3)]
            turn = xs[0] * ks[0] + xs[1] * ks[1] + xs[2] * ks[2]
            r = turn - jnp.floor(turn + 0.5)
            u = r * r
            s = r * horner(SIN_HALF, u)
            c = horner(COS_HALF, u)
            for value, base in ((1.0 - s * s, 0), (s * c, waves)):
                where = slice(base + at, base + at + step)
                kept = value.astype(BF16)
                wide = kept.astype(F32)
                part = [wide[i * count : (i + 1) * count] for i in range(6)]
                diff[pl.ds(row_d, count), where] = (part[3] - part[2]).astype(BF16)
                diff[pl.ds(row_d + count, count), where] = (part[5] - part[4]).astype(BF16)
                diff[pl.ds(row_d + 2 * count, count), where] = (part[1] - part[0]).astype(BF16)
                new[pl.ds(row_n, count), where] = kept[5 * count : 6 * count]
                new[pl.ds(row_n + count, count), where] = kept[count : 2 * count]
        return carry

    lax.fori_loop(0, walkers, one, 0)
    change = dot(diff[...], table_ref[:, 0:width]).astype(BF16)
    rest = dot(new[...], table_ref[:, width:]).astype(BF16)
    for w in range(walkers):
        out_ref = outs[w] if targets > 1 else outs[0].at[w]
        at = w * 3 * count
        out_ref[0 : 2 * count] = change[at : at + 2 * count]
        out_ref[6 * count : 7 * count] = change[at + 2 * count : at + 3 * count]
        for half, base in ((0, 2 * count), (1, 7 * count)):
            row = (2 * w + half) * count
            for a in range(4):
                out_ref[base + a * count : base + (a + 1) * count] = rest[
                    row : row + count, a * width : (a + 1) * width
                ]


def pair_inverse(a, b, d):
    det = a * d - b * b
    scale = 1.0 / det
    return d * scale, -b * scale, a * scale, det


def sweep(matrix):
    size = matrix.shape[0]
    log = jnp.zeros((1, 1), F32)
    row = iota((size, size), 0)
    lane = iota((size, size), 1)
    place = iota((1, size), 1)
    for k in range(0, size, 4):
        columns = [jnp.broadcast_to(matrix[:, k + j : k + j + 1], (size, size)) for j in range(4)]
        lines = [matrix[k + i : k + i + 1, :] for i in range(4)]
        at = lambda i, j: columns[j][k + i : k + i + 1, :]
        a00, a01, a11, det_a = pair_inverse(at(0, 0), at(0, 1), at(1, 1))
        b00, b01, b10, b11 = at(0, 2), at(0, 3), at(1, 2), at(1, 3)
        t00, t01 = a00 * b00 + a01 * b10, a00 * b01 + a01 * b11
        t10, t11 = a01 * b00 + a11 * b10, a01 * b01 + a11 * b11
        d00 = at(2, 2) - (b00 * t00 + b10 * t10)
        d01 = at(2, 3) - (b00 * t01 + b10 * t11)
        d11 = at(3, 3) - (b01 * t01 + b11 * t11)
        s00, s01, s11, det_s = pair_inverse(d00, d01, d11)
        u00, u01 = -(t00 * s00 + t01 * s01), -(t00 * s01 + t01 * s11)
        u10, u11 = -(t10 * s00 + t11 * s01), -(t10 * s01 + t11 * s11)
        q00, q01 = a00 - (u00 * t00 + u01 * t01), a01 - (u00 * t10 + u01 * t11)
        q11 = a11 - (u10 * t10 + u11 * t11)
        pivot = (
            (q00, q01, u00, u01),
            (q01, q11, u10, u11),
            (u00, u10, s00, s01),
            (u01, u11, s01, s11),
        )
        reduced = matrix
        scaled, edges = [], []
        for i in range(4):
            line = pivot[i][0] * lines[0] + pivot[i][1] * lines[1]
            line = line + (pivot[i][2] * lines[2] + pivot[i][3] * lines[3])
            reduced = reduced - columns[i] * line
            for j in range(4):
                line = jnp.where(place == k + j, -pivot[i][j], line)
            scaled.append(line)
            edge = pivot[i][0] * columns[0] + pivot[i][1] * columns[1]
            edges.append(edge + (pivot[i][2] * columns[2] + pivot[i][3] * columns[3]))
        matrix = reduced
        for i in range(4):
            matrix = jnp.where(lane == k + i, edges[i], matrix)
        for i in range(4):
            matrix = jnp.where(row == k + i, scaled[i], matrix)
        log = log + (jnp.log(det_a[:, 0:1]) + jnp.log(det_s[:, 0:1]))
    return -matrix, log


def ratio_of(products, size):
    eye = jnp.where(iota((size, size), 0) == iota((size, size), 1), 1.0, 0.0)
    ratio = products[0:size, 0:size] + eye
    inverse, log = sweep(dot(ratio, ratio, ((0,), (0,)), exact=True))
    return ratio, inverse, 0.5 * log


def moved_sums(products, ratio, inverse, count):
    size = ratio.shape[0]
    turned = dot(ratio, inverse, exact=True)[size - count :]
    tile = jnp.concatenate([turned] * 4, 0)
    part = products[size : size + 4 * count, 0:size] * tile
    return dot(jnp.ones((8, size), F32), part, ((1,), (1,)), exact=True)[0:1]


def columns_kernel(count, inverse_hbm, moved_ref, after_ref, out_ref, staged, sem):
    chunks, depth, electrons = staged.shape
    loads = []
    for chunk in range(chunks):
        load = pltpu.make_async_copy(
            rows_of(inverse_hbm, chunk, depth), staged.at[chunk], sem.at[chunk]
        )
        load.start()
        loads.append(load)
    block = iota((1, LANES), 1) // count
    number = jnp.where(block == 0, moved_ref[0:1, :], -1)
    pick = (iota((electrons, LANES), 0) == number).astype(F32).astype(BF16)
    for chunk in range(chunks):
        loads[chunk].wait()
        found = dot(staged[chunk].astype(BF16), pick)
        out_ref[chunk * depth : (chunk + 1) * depth] = found.astype(BF16)


def first_kernel(count, sources, me_ref, *refs):
    values = refs[:sources]
    columns, drift_ref, lap_ref, later_ref, vals = refs[sources:]
    rows = later_ref.shape[0]
    if sources > 1:
        width = values[0].shape[1]
        for step in range(sources):
            at = pl.multiple_of((me_ref[0] ^ step) * width, width)
            later_ref[:, pl.ds(at, width)] = values[step][0:rows]
            vals[:, pl.ds(at, width)] = values[step][rows:]
    else:
        pieces, _, width = values[0].shape
        for piece in range(pieces):
            where = slice(piece * width, (piece + 1) * width)
            later_ref[:, where] = values[0][piece, 0:rows]
            vals[:, where] = values[0][piece, rows:]
    products = dot(vals[...], columns[...])
    ratio, inverse, _ = ratio_of(products, count)
    sums = moved_sums(products, ratio, inverse, count)
    for a in range(3):
        drift_ref[a] = sums[:, a * count : (a + 1) * count]
    lap_ref[0] = sums[:, 3 * count : 4 * count]


def pick_from(number_ref, electrons):
    return (iota((electrons, LANES), 0) == number_ref[...]).astype(F32).astype(BF16)


def chunk_at(plan, role, slot):
    chunk = jnp.int32(plan[0][slot][0])
    for which in range(1, len(plan)):
        chunk = jnp.where(role == which, plan[which][slot][0], chunk)
    return chunk


def load_slots(plan, slots, role, inputs, parent, sem):
    for slot in slots:
        for which in range(len(plan)):
            load = pltpu.make_async_copy(
                inputs[plan[which][slot][1]], parent.at[slot], sem.at[slot]
            )
            pl.when(role == which)(load.start)


def wait_slots(slots, inputs, parent, sem):
    for slot in slots:
        pltpu.make_async_copy(inputs[0], parent.at[slot], sem.at[slot]).wait()


def early_kernel(count, plan, role_ref, number_ref, later_ref, *refs):
    inputs = refs[:-5]
    columns_ref, products_ref, total_ref, parent, sem = refs[-5:]
    slots, depth, electrons = parent.shape
    role = role_ref[0]
    load_slots(plan, range(slots), role, inputs, parent, sem)
    pick = pick_from(number_ref, electrons)
    wait_slots(range(slots), inputs, parent, sem)
    products, total = None, None
    for slot in range(slots):
        columns = dot(parent[slot], pick).astype(BF16)
        columns_ref[slot] = columns
        at = pl.multiple_of(chunk_at(plan, role, slot) * depth, depth)
        rows = later_ref[:, pl.ds(at, depth)]
        part = dot(rows, columns)
        more = dot(rows[0 : 2 * count], parent[slot])
        products = part if slot == 0 else products + part
        total = more if slot == 0 else total + more
    products_ref[...] = products
    total_ref[...] = total


def finish_kernel(
    count,
    plan,
    role_ref,
    number_ref,
    later_ref,
    weight_ref,
    drift_in,
    lap_in,
    early_ref,
    products_ref,
    total_ref,
    inverse_hbm,
    *refs,
):
    inputs = refs[:-9]
    out_ref, drift_ref, lap_ref, out_weight_ref = refs[-9:-5]
    parent, staged, in_sem, own_sem, out_sem = refs[-5:]
    chunks, depth, electrons = parent.shape
    done = early_ref.shape[0]
    late = range(done, chunks)
    size = 2 * count
    role = role_ref[0]
    own = [
        pltpu.make_async_copy(
            rows_of(inverse_hbm, plan[0][slot][0], depth), staged.at[slot], own_sem.at[slot]
        )
        for slot in range(chunks)
    ]
    load_slots(plan, list(late) + list(range(done)), role, inputs, parent, in_sem)
    for load in own:
        pl.when(role == 0)(load.start)
    pick = pick_from(number_ref, electrons)
    wait_slots(late, inputs, parent, in_sem)
    columns = [early_ref[slot] for slot in range(done)]
    products = products_ref[...]
    rows = []
    for slot in late:
        columns.append(dot(parent[slot], pick).astype(BF16))
        at = pl.multiple_of(chunk_at(plan, role, slot) * depth, depth)
        rows.append(later_ref[:, pl.ds(at, depth)])
        products = products + dot(rows[-1], columns[-1])
    ratio, inverse, log = ratio_of(products, size)
    total = total_ref[...]
    for slot, part in zip(late, rows):
        total = total + dot(part[0:size], parent[slot])
    small = dot(inverse, ratio, ((1,), (1,)), exact=True)
    high = small.astype(BF16)
    halves = jnp.concatenate([high, (small - high.astype(F32)).astype(BF16)], 1)
    rounded = total.astype(BF16)
    solved = dot(halves, jnp.concatenate([rounded, rounded], 0)).astype(BF16)
    solved = jnp.concatenate([solved, jnp.zeros((LANES - size, electrons), BF16)], 0)
    wait_slots(range(done), inputs, parent, in_sem)
    copies = []
    for slot in list(late) + list(range(done)):
        at = pl.multiple_of(chunk_at(plan, role, slot) * depth, depth)
        copy = pltpu.make_async_copy(
            staged.at[slot], out_ref.at[pl.ds(at, depth)], out_sem.at[slot]
        )
        copies.append((slot, copy))

    def kept(slot):
        own[slot].wait()
        return staged[slot]

    def write(before):
        for slot, copy in copies:
            staged[slot] = before(slot) - dot(columns[slot], solved)
            copy.start()

    pl.when(role == 0)(lambda: write(kept))
    pl.when(role != 0)(lambda: write(lambda slot: parent[slot].astype(F32)))
    sums = moved_sums(products, ratio, inverse, count)
    drift_ref[0:3] = drift_in[...]
    lap_ref[0:1] = lap_in[...]
    for a in range(3):
        drift_ref[3 + a] = sums[:, a * count : (a + 1) * count]
    lap_ref[1] = sums[:, 3 * count : 4 * count]
    out_weight_ref[...] = weight_ref[...] + log
    for _, copy in copies:
        copy.wait()


def per_device(
    n_grp,
    n_orb,
    wavevectors,
    coefficients,
    inverse,
    positions,
    displacements,
    moved,
    donor,
    take,
    log_weight,
):
    electrons = inverse.shape[1]
    count = moved.shape[2]
    plane = coefficients.shape[0]
    local = coefficients.shape[1]
    others = n_grp - 1
    chunks = 4

    record, tiled, disp = call(
        functools.partial(start_kernel, count),
        (
            shape((8, electrons), F32),
            shape((2, LANES), jnp.int32),
            shape((2, 8, LANES), F32),
        ),
        [HBM, HBM, HBM, SM],
        (VM, VM, VM),
        scratch=[
            pltpu.VMEM((3, 1, electrons), F32),
            pltpu.VMEM((2, 1, count), jnp.int32),
            pltpu.VMEM((6, 1, count), F32),
            pltpu.SemaphoreType.DMA((3,)),
        ],
    )(
        *in_hbm(
            positions.reshape(3, 1, electrons),
            moved,
            displacements.reshape(6, 1, count),
        ),
        log_weight,
    )
    records = [lax.ppermute(record, "grp", pairs(n_grp, s)) for s in range(1, n_grp)]

    depth = electrons // chunks
    kept = shape((depth, electrons), BF16)
    token = shape((8, LANES), F32)
    own = [None] * chunks
    ends = (0, chunks - 1)
    middle = tuple(range(1, chunks - 1))
    own[0], own[-1] = call(
        functools.partial(round_kernel, ends),
        (kept,) * 2,
        [HBM, ANY],
        (ANY,) * 2,
        scratch=[
            pltpu.VMEM((2, depth, electrons), F32),
            pltpu.VMEM((2, depth, electrons), BF16),
            pltpu.SemaphoreType.DMA((2,)),
            pltpu.SemaphoreType.DMA((2,)),
        ],
        moved=3 * electrons * electrons,
        vmem=6,
    )(*in_hbm(inverse), record)
    own[0], own[-1], token_0 = call(
        gate_kernel,
        (kept, kept, token),
        [ANY] * (2 + others),
        (ANY, ANY, VM),
        aliases={0: 0, 1: 1},
        vmem=1,
    )(own[0], own[-1], *records)

    few = is_power(n_orb) and local % LANES == 0
    direct = few and DIRECT_POINTS
    sources = n_orb if direct else 1
    points, weight, number, role, apart = call(
        functools.partial(points_kernel, count, others),
        (
            shape((8, LANES) if direct else (n_orb, ROWS, LANES), F32),
            shape((1, LANES), F32),
            shape((1, LANES), jnp.int32),
            shape((1,), jnp.int32),
            shape((1,), jnp.int32),
        ),
        [VM, VM] + [VM] * (others + 3) + [ANY],
        (VM, VM, VM, SM, SM),
    )(donor.reshape(1, 1), take.reshape(1, 1), record, *records, tiled, disp, token_0)
    if direct:
        points = [points] + [lax.ppermute(points, "orb", pairs(n_orb, s)) for s in range(1, n_orb)]
    else:
        points = [lax.all_to_all(points, "orb", split_axis=0, concat_axis=0, tiled=True)]

    width = -(-local // LANES) * LANES
    coeff = jnp.pad(coefficients, ((0, 0), (0, width - local))) if width > local else coefficients
    derived, *prepared = call(
        functools.partial(prepare_kernel, middle),
        (shape((plane, 5 * width), BF16),)
        + (pltpu.HBM((depth, electrons), BF16),) * len(middle),
        [HBM, HBM, HBM, ANY],
        (VM,) + (ANY,) * len(middle),
        scratch=[
            pltpu.VMEM((plane, width), BF16),
            pltpu.VMEM(wavevectors.shape, F32),
            pltpu.VMEM((len(middle), depth, electrons), F32),
            pltpu.VMEM((len(middle), depth, electrons), BF16),
            pltpu.SemaphoreType.DMA((2,)),
            pltpu.SemaphoreType.DMA((len(middle),)),
            pltpu.SemaphoreType.DMA((len(middle),)),
        ],
        flops=8 * plane * width,
        moved=3 * electrons * electrons + 10 * plane * width,
        vmem=12,
    )(*in_hbm(coeff, wavevectors, inverse), weight)
    for chunk, ready in zip(middle, prepared):
        own[chunk] = ready

    arrays = list(own)
    if n_grp == 4:
        send_x = lambda block: lax.ppermute(block, "grp", pairs(n_grp, 1))
        send_y = lambda block: lax.ppermute(block, "grp", pairs(n_grp, 2))

        def relay(mine, got, first):
            return call(
                relay_kernel,
                (kept, kept, token),
                [SM] + [ANY] * (4 + len(first)),
                (ANY, ANY, VM),
                scratch=[
                    pltpu.VMEM((2, depth, electrons), BF16),
                    pltpu.SemaphoreType.DMA((2,)),
                    pltpu.SemaphoreType.DMA((2,)),
                ],
                aliases={3: 0, 4: 1},
                vmem=2,
            )(apart, *in_hbm(*mine), *got, *first)

        x1, y1 = send_x(own[0]), send_y(own[3])
        y1, x1, token_1 = relay((own[1], own[2]), (y1, x1), (derived, *points))
        x2, y2 = send_x(y1), send_y(x1)
    else:
        token_1 = token_2 = jnp.zeros((8, LANES), F32)
        plan = [tuple((chunk, chunk) for chunk in range(chunks))]
        for step in range(1, n_grp):
            plan.append(tuple((chunk, len(arrays) + chunk) for chunk in range(chunks)))
            arrays += [lax.ppermute(block, "grp", pairs(n_grp, step)) for block in own]
        settled = len(arrays)

    height = 11 * count
    spread = few and DIRECT_VALUES
    targets = n_orb if spread else 1
    block = n_orb if few else math.gcd(n_orb, 8)
    whole = lambda array: pl.BlockSpec(array.shape, lambda i: (0,) * array.ndim)
    if direct:
        point_specs = [whole(p) for p in points]
    else:
        point_specs = [pl.BlockSpec((block, ROWS, LANES), lambda i: (i, 0, 0))]
    if spread:
        out_shapes = (shape((height, width), BF16),) * n_orb
        out_specs = tuple(whole(o) for o in out_shapes)
    else:
        out_shapes = (shape((n_orb, height, width), BF16),)
        out_specs = (pl.BlockSpec((block, height, width), lambda i: (i, 0, 0)),)
    values = pl.pallas_call(
        functools.partial(evaluate_kernel, count, sources, targets),
        grid=(n_orb // block,),
        out_shape=out_shapes,
        in_specs=point_specs + [whole(wavevectors), whole(derived), ANY],
        out_specs=out_specs,
        scratch_shapes=[
            pltpu.VMEM((block * 3 * count, plane), BF16),
            pltpu.VMEM((block * 2 * count, plane), BF16),
            pltpu.VMEM((block, 8, LANES), F32),
        ],
        compiler_params=pltpu.CompilerParams(vmem_limit_bytes=8 * MIB),
        cost_estimate=pl.CostEstimate(
            flops=2 * n_orb * count * plane * width * 11,
            bytes_accessed=12 * plane * width,
            transcendentals=0,
        ),
    )(*points, wavevectors, derived, token_1)
    computed = values[0]
    if spread:
        values = [values[0]] + [
            lax.ppermute(values[s], "orb", pairs(n_orb, s)) for s in range(1, n_orb)
        ]
    else:
        values = values[0][:, :, :local]
        values = lax.all_to_all(values, "orb", split_axis=0, concat_axis=0, tiled=True)
        if width > local:
            values = values.transpose(1, 0, 2).reshape(1, height, electrons)
        values = [values]

    if n_grp == 4:
        y2, x2, token_2 = relay((own[2], own[1]), (y2, x2), (computed,))
        x3, y3 = send_x(y2), send_y(x2)
        arrays = own + [x1, x2, y1, y2, x3, y3]
        a1, a2, b1, b2, a3, b3 = range(chunks, chunks + 6)
        first, second, third, fourth = range(chunks)
        plan = [
            tuple((chunk, chunk) for chunk in range(chunks)),
            ((first, a1), (second, a2), (third, a3), (fourth, b3)),
            ((fourth, b1), (third, b2), (first, a3), (second, b3)),
            ((fourth, a2), (first, b2), (third, a3), (second, b3)),
        ]
        settled = chunks + 4

    columns = call(
        functools.partial(columns_kernel, count),
        shape((electrons, LANES), BF16),
        [HBM, VM, ANY],
        VM,
        scratch=[
            pltpu.VMEM((chunks, depth, electrons), F32),
            pltpu.SemaphoreType.DMA((chunks,)),
        ],
        flops=2 * electrons * electrons * LANES,
        moved=4 * electrons * electrons,
        vmem=8,
    )(*in_hbm(inverse), tiled, token_2)

    here = lax.axis_index("orb").astype(jnp.int32).reshape(1)
    drift, laplacian, later = call(
        functools.partial(first_kernel, count, targets),
        (
            shape((3, 1, count), F32),
            shape((1, 1, count), F32),
            shape((6 * count, electrons), BF16),
        ),
        [SM] + [VM] * (targets + 1),
        (VM, VM, VM),
        scratch=[pltpu.VMEM((5 * count, electrons), BF16)],
        flops=2 * electrons * 11 * count * LANES,
        moved=44 * count * electrons,
    )(here, *values, columns)

    early = 2
    work = 2 * electrons * 2 * count
    early_columns, products, total = call(
        functools.partial(early_kernel, count, plan),
        (
            shape((early, depth, LANES), BF16),
            shape((6 * count, LANES), F32),
            shape((2 * count, electrons), F32),
        ),
        [SM, VM, VM] + [ANY] * settled,
        (VM, VM, VM),
        scratch=[
            pltpu.VMEM((early, depth, electrons), BF16),
            pltpu.SemaphoreType.DMA((early,)),
        ],
        flops=early * depth * work,
        moved=2 * early * depth * electrons,
        vmem=8,
    )(role, number, later, *in_hbm(*own), *arrays[chunks:settled])

    updated, drift, laplacian, new_weight = call(
        functools.partial(finish_kernel, count, plan),
        (
            shape((electrons, electrons), F32),
            shape((6, 1, count), F32),
            shape((2, 1, count), F32),
            shape((1, LANES), F32),
        ),
        [SM] + [VM] * 8 + [HBM] + [ANY] * len(arrays),
        (HBM, VM, VM, VM),
        scratch=[
            pltpu.VMEM((chunks, depth, electrons), BF16),
            pltpu.VMEM((chunks, depth, electrons), F32),
            pltpu.SemaphoreType.DMA((chunks,)),
            pltpu.SemaphoreType.DMA((chunks,)),
            pltpu.SemaphoreType.DMA((chunks,)),
        ],
        flops=2 * electrons * work,
        moved=6 * electrons * electrons,
        vmem=12,
    )(
        role,
        number,
        later,
        weight,
        drift,
        laplacian,
        early_columns,
        products,
        total,
        *in_hbm(inverse, *own),
        *arrays[chunks:],
    )

    return updated[None], drift.reshape(2, 1, 3, count), laplacian, new_weight[0, :1]


def solution(mesh):
    split = ("grp", "orb")
    return jax.shard_map(
        functools.partial(per_device, mesh.shape["grp"], mesh.shape["orb"]),
        mesh=mesh,
        in_specs=(
            P(),
            P(None, "orb"),
            P(split, None, None),
            P(split, None, None),
            P(None, split, None, None),
            P(None, split, None),
            P("orb"),
            P(split),
            P(split),
        ),
        out_specs=(
            P(split, None, None),
            P(None, split, None, None),
            P(None, split, None),
            P(split),
        ),
        check_vma=False,
    )
```

```python
import functools
import math

import jax
import jax.numpy as jnp
from jax import lax
from jax.experimental import pallas as pl
from jax.experimental.pallas import tpu as pltpu
from jax.sharding import PartitionSpec as P

F32 = jnp.float32
BF16 = jnp.bfloat16
LANES = 128
ROWS = 16
DIRECT_POINTS = False
DIRECT_VALUES = False
MIB = 1024 * 1024
precise = lax.Precision.HIGHEST

SIN_HALF = (4.4428679, -7.30744342, 3.59478808, -0.78437403)
COS_HALF = (1.4142135, -6.97885099, 5.73946117, -1.88356299, 0.31069819)


def dot(a, b, dims=((1,), (0,)), exact=False):
    return lax.dot_general(
        a, b, (dims, ((), ())), precision=precise if exact else None, preferred_element_type=F32
    )


def iota(shape, dim):
    return lax.broadcasted_iota(jnp.int32, shape, dim)


def call(
    kernel, out_shape, in_specs, out_specs, scratch=(), flops=0, moved=0, vmem=4, aliases=None
):
    return pl.pallas_call(
        kernel,
        out_shape=out_shape,
        input_output_aliases=aliases or {},
        in_specs=in_specs,
        out_specs=out_specs,
        scratch_shapes=list(scratch),
        compiler_params=pltpu.CompilerParams(vmem_limit_bytes=vmem * MIB),
        cost_estimate=pl.CostEstimate(flops=flops, bytes_accessed=moved, transcendentals=0),
    )


VM = pl.BlockSpec(memory_space=pltpu.VMEM)
SM = pl.BlockSpec(memory_space=pltpu.SMEM)
ANY = pl.BlockSpec(memory_space=pl.ANY)
HBM = pl.BlockSpec(memory_space=pltpu.HBM)


def shape(dims, dtype):
    return jax.ShapeDtypeStruct(dims, dtype)


def in_hbm(*arrays):
    return tuple(pltpu.with_memory_space_constraint(a, pltpu.HBM) for a in arrays)


def is_power(n):
    return n & (n - 1) == 0


def pairs(n, step):
    if is_power(n):
        return [(i, i ^ step) for i in range(n)]
    return [(i, (i + step) % n) for i in range(n)]


def distance(n, here, there):
    return here ^ there if is_power(n) else lax.rem(here - there + n, n)


def backward(n, step):
    return step if is_power(n) else (n - step) % n


def start_kernel(
    count,
    pos_hbm,
    moved_hbm,
    disp_hbm,
    weight_ref,
    out_ref,
    tiled_ref,
    shift_ref,
    pos_ref,
    moved_ref,
    disp_ref,
    sems,
):
    loads = [
        pltpu.make_async_copy(src, dst, sems.at[i])
        for i, (src, dst) in enumerate(
            (
                (moved_hbm, moved_ref),
                (disp_hbm, disp_ref),
                (pos_hbm, pos_ref),
            )
        )
    ]
    for load in loads:
        load.start()
    electrons = pos_ref.shape[2]
    copies = LANES // count
    loads[0].wait()
    tiled = jnp.concatenate([moved_ref[:, 0, :]] * copies, 1)
    tiled_ref[...] = tiled
    pick = (iota((electrons, LANES), 0) == tiled[0:1, :]).astype(F32)
    block = iota((8, LANES), 1) // count
    zeros = jnp.zeros((5, LANES), F32)
    loads[1].wait()
    for update in range(2):
        shift = jnp.concatenate([disp_ref[3 * update : 3 * update + 3, 0, :]] * copies, 1)
        shift_ref[update] = jnp.concatenate([shift, zeros], 0)
    loads[2].wait()
    pos = jnp.concatenate([pos_ref[:, 0, :], jnp.zeros((5, electrons), F32)], 0)
    old = dot(pos, pick, exact=True)
    disp = shift_ref[0]
    points = old + jnp.where(block % 2 == 1, disp, 0.0)
    first = jnp.where(block == 0, disp, 0.0)
    out_ref[...] = pos + dot(first, pick, ((1,), (1,)), exact=True)
    out_ref[3:6, 0:LANES] = points[0:3]
    out_ref[6:7, 0:LANES] = tiled[0:1, :].astype(F32)
    out_ref[7:8, 0:LANES] = jnp.full((1, LANES), weight_ref[0], F32)


def rows_of(ref, chunk, depth):
    return ref.at[0, pl.ds(chunk * depth, depth)]


def round_kernel(wanted, inverse_hbm, after_ref, *refs):
    outs = refs[: len(wanted)]
    staged, rounded, in_sem, out_sem = refs[len(wanted) :]
    depth = staged.shape[1]
    loads, stores = [], []
    for slot, chunk in enumerate(wanted):
        load = pltpu.make_async_copy(
            rows_of(inverse_hbm, chunk, depth), staged.at[slot], in_sem.at[slot]
        )
        load.start()
        loads.append(load)
    for slot, out in enumerate(outs):
        loads[slot].wait()
        rounded[slot] = staged[slot].astype(BF16)
        store = pltpu.make_async_copy(rounded.at[slot], out, out_sem.at[slot])
        store.start()
        stores.append(store)
    for store in stores:
        store.wait()


def gate_kernel(*refs):
    token_ref = refs[-1]
    token_ref[...] = jnp.zeros(token_ref.shape, F32)


def relay_kernel(flag_ref, own_a, own_b, got_a, got_b, *refs):
    out_a, out_b, token_ref, staged, in_sem, out_sem = refs[-6:]
    pieces, depth, _ = staged.shape

    @pl.when(flag_ref[0] == 0)
    def _():
        loads, stores = [], []
        for piece in range(pieces):
            own, out = (own_a, out_a) if piece < pieces // 2 else (own_b, out_b)
            rows = pl.ds(piece % (pieces // 2) * depth, depth)
            loads.append(
                pltpu.make_async_copy(own.at[rows], staged.at[piece], in_sem.at[piece])
            )
            stores.append(
                pltpu.make_async_copy(staged.at[piece], out.at[rows], out_sem.at[piece])
            )
        for load in loads:
            load.start()
        for load, store in zip(loads, stores):
            load.wait()
            store.start()
        for store in stores:
            store.wait()

    token_ref[...] = jnp.zeros(token_ref.shape, F32)


def points_kernel(count, others, role_ref, *refs):
    own_ref = refs[0]
    received = refs[1 : 1 + others]
    moved_ref, disp_ref, after_ref, points_ref, weight_ref, number_ref = refs[1 + others :]
    role = role_ref[0]
    parent = own_ref[...]
    for step in range(others):
        parent = jnp.where(role == step + 1, received[step][...], parent)
    electrons = parent.shape[1]
    pick = (iota((electrons, LANES), 0) == moved_ref[1:2, :]).astype(F32)
    block = iota((8, LANES), 1) // count
    old = dot(parent, pick, exact=True)
    later = old + jnp.where(block % 2 == 1, disp_ref[1], 0.0)
    zeros = jnp.zeros((5, LANES), F32)
    mine = jnp.concatenate([own_ref[3:6, 0:LANES], zeros], 0)
    theirs = jnp.concatenate([parent[3:6, 0:LANES], zeros], 0)
    points = jnp.where(block < 2, mine, jnp.where(block < 4, theirs, later))
    if len(points_ref.shape) == 2:
        points_ref[...] = points
    else:
        points = jnp.concatenate([points, jnp.zeros((ROWS - 8, LANES), F32)], 0)
        points_ref[...] = jnp.broadcast_to(points[None], points_ref.shape)
    weight_ref[...] = parent[7:8, 0:LANES]
    before = parent[6:7, 0:LANES].astype(jnp.int32)
    number_ref[...] = jnp.where(
        block[0:1] == 0, before, jnp.where(block[0:1] == 1, moved_ref[1:2, :], -1)
    )


def derive(coeff_ref, wave_ref, out_ref):
    waves = wave_ref.shape[1]
    width = coeff_ref.shape[1]
    wave = jnp.transpose(jnp.concatenate([wave_ref[...], jnp.zeros((5, waves), F32)], 0))
    out_ref[:, 0:width] = coeff_ref[...]
    cos_part = coeff_ref[0:waves].astype(F32)
    sin_part = coeff_ref[waves:].astype(F32)
    squared = None
    for a in range(3):
        scale = wave[:, a : a + 1]
        where = slice((a + 1) * width, (a + 2) * width)
        out_ref[0:waves, where] = (scale * sin_part).astype(BF16)
        out_ref[waves:, where] = (-scale * cos_part).astype(BF16)
        squared = scale * scale if a == 0 else squared + scale * scale
    where = slice(4 * width, 5 * width)
    out_ref[0:waves, where] = (-squared * cos_part).astype(BF16)
    out_ref[waves:, where] = (-squared * sin_part).astype(BF16)


def prepare_kernel(wanted, coeff_hbm, wave_hbm, inverse_hbm, after_ref, table_ref, *refs):
    outs = refs[: len(wanted)]
    coeff_ref, wave_ref, staged, rounded, small_sem, in_sem, out_sem = refs[len(wanted) :]
    depth = staged.shape[1]
    wave_load = pltpu.make_async_copy(wave_hbm, wave_ref, small_sem.at[0])
    coeff_load = pltpu.make_async_copy(coeff_hbm, coeff_ref, small_sem.at[1])
    wave_load.start()
    coeff_load.start()
    loads, stores = [], []
    for slot, chunk in enumerate(wanted):
        load = pltpu.make_async_copy(
            rows_of(inverse_hbm, chunk, depth), staged.at[slot], in_sem.at[slot]
        )
        load.start()
        loads.append(load)
    wave_load.wait()
    coeff_load.wait()
    derive(coeff_ref, wave_ref, table_ref)
    for slot, out in enumerate(outs):
        loads[slot].wait()
        rounded[slot] = staged[slot].astype(BF16)
        store = pltpu.make_async_copy(rounded.at[slot], out, out_sem.at[slot])
        store.start()
        stores.append(store)
    for store in stores:
        store.wait()


def horner(coefs, u):
    value = coefs[-1] * u + coefs[-2]
    for c in reversed(coefs[:-2]):
        value = value * u + c
    return value


def evaluate_kernel(count, sources, targets, *refs):
    points = refs[:sources]
    wave_ref, table_ref = refs[sources : sources + 2]
    outs = refs[sources + 3 : -4]
    diff, new, gathered, spread = refs[-4:]
    walkers = gathered.shape[0]
    for w in range(walkers):
        gathered[w] = points[w][...] if sources > 1 else points[0][w, 0:8]
    waves = wave_ref.shape[1]
    width = table_ref.shape[1] // 5
    step = math.gcd(waves, LANES)

    def one(w, carry):
        column = jnp.transpose(gathered[w])
        for a in range(3):
            spread[a] = jnp.broadcast_to(column[0 : 6 * count, a : a + 1], (6 * count, step))
        row_d = pl.multiple_of(w * (3 * count), count)
        row_n = pl.multiple_of(w * (2 * count), count)
        for at in range(0, waves, step):
            ks = [wave_ref[a : a + 1, at : at + step] * (0.5 / math.pi) for a in range(3)]
            for pair, diff_at, new_at in ((0, 2, 1), (1, 0, None), (2, 1, 0)):
                rows = slice(2 * pair * count, 2 * (pair + 1) * count)
                turn = spread[0, rows] * ks[0] + spread[1, rows] * ks[1] + spread[2, rows] * ks[2]
                r = turn - jnp.floor(turn + 0.5)
                u = r * r
                s = r * horner(SIN_HALF, u)
                c = horner(COS_HALF, u)
                for value, base in ((1.0 - s * s, 0), (s * c, waves)):
                    where = slice(base + at, base + at + step)
                    kept = value.astype(BF16)
                    wide = kept.astype(F32)
                    change = (wide[count:] - wide[:count]).astype(BF16)
                    diff[pl.ds(row_d + diff_at * count, count), where] = change
                    if new_at is not None:
                        new[pl.ds(row_n + new_at * count, count), where] = kept[count:]
        return carry

    lax.fori_loop(0, walkers, one, 0)
    change = dot(diff[...], table_ref[:, 0:width]).astype(BF16)
    rest = dot(new[...], table_ref[:, width:]).astype(BF16)
    for w in range(walkers):
        out_ref = outs[w] if targets > 1 else outs[0].at[w]
        at = w * 3 * count
        out_ref[0 : 2 * count] = change[at : at + 2 * count]
        out_ref[6 * count : 7 * count] = change[at + 2 * count : at + 3 * count]
        for half, base in ((0, 2 * count), (1, 7 * count)):
            row = (2 * w + half) * count
            for a in range(4):
                out_ref[base + a * count : base + (a + 1) * count] = rest[
                    row : row + count, a * width : (a + 1) * width
                ]


def pair_inverse(a, b, d):
    det = a * d - b * b
    scale = 1.0 / det
    return d * scale, -b * scale, a * scale, det


def sweep(matrix):
    size = matrix.shape[0]
    log = jnp.zeros((1, 1), F32)
    row = iota((size, size), 0)
    lane = iota((size, size), 1)
    place = iota((1, size), 1)
    for k in range(0, size, 4):
        columns = [jnp.broadcast_to(matrix[:, k + j : k + j + 1], (size, size)) for j in range(4)]
        lines = [matrix[k + i : k + i + 1, :] for i in range(4)]
        at = lambda i, j: columns[j][k + i : k + i + 1, :]
        a00, a01, a11, det_a = pair_inverse(at(0, 0), at(0, 1), at(1, 1))
        b00, b01, b10, b11 = at(0, 2), at(0, 3), at(1, 2), at(1, 3)
        t00, t01 = a00 * b00 + a01 * b10, a00 * b01 + a01 * b11
        t10, t11 = a01 * b00 + a11 * b10, a01 * b01 + a11 * b11
        d00 = at(2, 2) - (b00 * t00 + b10 * t10)
        d01 = at(2, 3) - (b00 * t01 + b10 * t11)
        d11 = at(3, 3) - (b01 * t01 + b11 * t11)
        s00, s01, s11, det_s = pair_inverse(d00, d01, d11)
        u00, u01 = -(t00 * s00 + t01 * s01), -(t00 * s01 + t01 * s11)
        u10, u11 = -(t10 * s00 + t11 * s01), -(t10 * s01 + t11 * s11)
        q00, q01 = a00 - (u00 * t00 + u01 * t01), a01 - (u00 * t10 + u01 * t11)
        q11 = a11 - (u10 * t10 + u11 * t11)
        pivot = (
            (q00, q01, u00, u01),
            (q01, q11, u10, u11),
            (u00, u10, s00, s01),
            (u01, u11, s01, s11),
        )
        reduced = matrix
        scaled, edges = [], []
        for i in range(4):
            line = pivot[i][0] * lines[0] + pivot[i][1] * lines[1]
            line = line + (pivot[i][2] * lines[2] + pivot[i][3] * lines[3])
            reduced = reduced - columns[i] * line
            for j in range(4):
                line = jnp.where(place == k + j, -pivot[i][j], line)
            scaled.append(line)
            edge = pivot[i][0] * columns[0] + pivot[i][1] * columns[1]
            edges.append(edge + (pivot[i][2] * columns[2] + pivot[i][3] * columns[3]))
        matrix = reduced
        for i in range(4):
            matrix = jnp.where(lane == k + i, edges[i], matrix)
        for i in range(4):
            matrix = jnp.where(row == k + i, scaled[i], matrix)
        log = log + (jnp.log(det_a[:, 0:1]) + jnp.log(det_s[:, 0:1]))
    return -matrix, log


def ratio_of(products, size):
    eye = jnp.where(iota((size, size), 0) == iota((size, size), 1), 1.0, 0.0)
    ratio = products[0:size, 0:size] + eye
    inverse, log = sweep(dot(ratio, ratio, ((0,), (0,)), exact=True))
    return ratio, inverse, 0.5 * log


def moved_sums(products, ratio, inverse, count):
    size = ratio.shape[0]
    turned = dot(ratio, inverse, exact=True)[size - count :]
    tile = jnp.concatenate([turned] * 4, 0)
    part = products[size : size + 4 * count, 0:size] * tile
    return dot(jnp.ones((8, size), F32), part, ((1,), (1,)), exact=True)[0:1]


def columns_kernel(count, inverse_hbm, moved_ref, after_ref, out_ref, staged, sem):
    chunks, depth, electrons = staged.shape
    loads = []
    for chunk in range(chunks):
        load = pltpu.make_async_copy(
            rows_of(inverse_hbm, chunk, depth), staged.at[chunk], sem.at[chunk]
        )
        load.start()
        loads.append(load)
    block = iota((1, LANES), 1) // count
    number = jnp.where(block == 0, moved_ref[0:1, :], -1)
    pick = (iota((electrons, LANES), 0) == number).astype(F32).astype(BF16)
    for chunk in range(chunks):
        loads[chunk].wait()
        found = dot(staged[chunk].astype(BF16), pick)
        out_ref[chunk * depth : (chunk + 1) * depth] = found.astype(BF16)


def pick_from(number_ref, electrons):
    return (iota((electrons, LANES), 0) == number_ref[...]).astype(F32).astype(BF16)


def chunk_at(plan, role, slot):
    chunk = jnp.int32(plan[0][slot][0])
    for which in range(1, len(plan)):
        chunk = jnp.where(role == which, plan[which][slot][0], chunk)
    return chunk


def load_slots(plan, slots, role, inputs, parent, sem):
    for slot in slots:
        for which in range(len(plan)):
            load = pltpu.make_async_copy(
                inputs[plan[which][slot][1]], parent.at[slot], sem.at[slot]
            )
            pl.when(role == which)(load.start)


def wait_slots(slots, inputs, parent, sem):
    for slot in slots:
        pltpu.make_async_copy(inputs[0], parent.at[slot], sem.at[slot]).wait()


def middle_kernel(count, sources, plan, me_ref, role_ref, number_ref, *refs):
    values = refs[:sources]
    own_columns = refs[sources]
    inputs = refs[sources + 1 : -9]
    drift_ref, lap_ref, later_ref, columns_ref, products_ref, total_ref = refs[-9:-3]
    vals, parent, sem = refs[-3:]
    slots, depth, electrons = parent.shape
    role = role_ref[0]
    load_slots(plan, range(slots), role, inputs, parent, sem)
    rows = later_ref.shape[0]
    if sources > 1:
        width = values[0].shape[1]
        for step in range(sources):
            at = pl.multiple_of((me_ref[0] ^ step) * width, width)
            later_ref[:, pl.ds(at, width)] = values[step][0:rows]
            vals[:, pl.ds(at, width)] = values[step][rows:]
    else:
        pieces, _, width = values[0].shape
        for piece in range(pieces):
            where = slice(piece * width, (piece + 1) * width)
            later_ref[:, where] = values[0][piece, 0:rows]
            vals[:, where] = values[0][piece, rows:]
    pick = pick_from(number_ref, electrons)
    wait_slots(range(slots), inputs, parent, sem)
    own = dot(vals[...], own_columns[...])
    products, total = None, None
    for slot in range(slots):
        columns = dot(parent[slot], pick).astype(BF16)
        columns_ref[slot] = columns
        at = pl.multiple_of(chunk_at(plan, role, slot) * depth, depth)
        part = later_ref[:, pl.ds(at, depth)]
        product = dot(part, columns)
        more = dot(part[0 : 2 * count], parent[slot])
        products = product if slot == 0 else products + product
        total = more if slot == 0 else total + more
    products_ref[...] = products
    total_ref[...] = total
    ratio, inverse, _ = ratio_of(own, count)
    sums = moved_sums(own, ratio, inverse, count)
    for a in range(3):
        drift_ref[a] = sums[:, a * count : (a + 1) * count]
    lap_ref[0] = sums[:, 3 * count : 4 * count]


def finish_kernel(
    count,
    plan,
    role_ref,
    number_ref,
    later_ref,
    weight_ref,
    drift_in,
    lap_in,
    early_ref,
    products_ref,
    total_ref,
    inverse_hbm,
    *refs,
):
    inputs = refs[:-9]
    out_ref, drift_ref, lap_ref, out_weight_ref = refs[-9:-5]
    parent, staged, in_sem, own_sem, out_sem = refs[-5:]
    chunks, depth, electrons = parent.shape
    done = early_ref.shape[0]
    late = range(done, chunks)
    size = 2 * count
    role = role_ref[0]
    own = [
        pltpu.make_async_copy(
            rows_of(inverse_hbm, plan[0][slot][0], depth), staged.at[slot], own_sem.at[slot]
        )
        for slot in range(chunks)
    ]
    load_slots(plan, list(late) + list(range(done)), role, inputs, parent, in_sem)
    for load in own:
        pl.when(role == 0)(load.start)
    pick = pick_from(number_ref, electrons)
    wait_slots(late, inputs, parent, in_sem)
    columns = [early_ref[slot] for slot in range(done)]
    products = products_ref[...]
    rows = []
    for slot in late:
        columns.append(dot(parent[slot], pick).astype(BF16))
        at = pl.multiple_of(chunk_at(plan, role, slot) * depth, depth)
        rows.append(later_ref[:, pl.ds(at, depth)])
        products = products + dot(rows[-1], columns[-1])
    ratio, inverse, log = ratio_of(products, size)
    total = total_ref[...]
    for slot, part in zip(late, rows):
        total = total + dot(part[0:size], parent[slot])
    small = dot(inverse, ratio, ((1,), (1,)), exact=True)
    high = small.astype(BF16)
    halves = jnp.concatenate([high, (small - high.astype(F32)).astype(BF16)], 1)
    rounded = total.astype(BF16)
    solved = dot(halves, jnp.concatenate([rounded, rounded], 0)).astype(BF16)
    solved = jnp.concatenate([solved, jnp.zeros((LANES - size, electrons), BF16)], 0)
    wait_slots(range(done), inputs, parent, in_sem)
    copies = []
    for slot in list(late) + list(range(done)):
        at = pl.multiple_of(chunk_at(plan, role, slot) * depth, depth)
        copy = pltpu.make_async_copy(
            staged.at[slot], out_ref.at[pl.ds(at, depth)], out_sem.at[slot]
        )
        copies.append((slot, copy))

    def kept(slot):
        own[slot].wait()
        return staged[slot]

    def write(before):
        for slot, copy in copies:
            staged[slot] = before(slot) - dot(columns[slot], solved)
            copy.start()

    pl.when(role == 0)(lambda: write(kept))
    pl.when(role != 0)(lambda: write(lambda slot: parent[slot].astype(F32)))
    sums = moved_sums(products, ratio, inverse, count)
    drift_ref[0:3] = drift_in[...]
    lap_ref[0:1] = lap_in[...]
    for a in range(3):
        drift_ref[3 + a] = sums[:, a * count : (a + 1) * count]
    lap_ref[1] = sums[:, 3 * count : 4 * count]
    out_weight_ref[...] = weight_ref[...] + log
    for _, copy in copies:
        copy.wait()


def per_device(
    n_grp,
    n_orb,
    wavevectors,
    coefficients,
    inverse,
    positions,
    displacements,
    moved,
    donor,
    take,
    log_weight,
):
    electrons = inverse.shape[1]
    count = moved.shape[2]
    plane = coefficients.shape[0]
    local = coefficients.shape[1]
    others = n_grp - 1
    chunks = 4

    apart = distance(n_grp, lax.axis_index("grp"), donor[0])
    role = jnp.where(take[0] == 1, apart, 0).astype(jnp.int32).reshape(1)
    apart = apart.astype(jnp.int32).reshape(1)

    record, tiled, disp = call(
        functools.partial(start_kernel, count),
        (
            shape((8, electrons), F32),
            shape((2, LANES), jnp.int32),
            shape((2, 8, LANES), F32),
        ),
        [HBM, HBM, HBM, SM],
        (VM, VM, VM),
        scratch=[
            pltpu.VMEM((3, 1, electrons), F32),
            pltpu.VMEM((2, 1, count), jnp.int32),
            pltpu.VMEM((6, 1, count), F32),
            pltpu.SemaphoreType.DMA((3,)),
        ],
    )(
        *in_hbm(
            positions.reshape(3, 1, electrons),
            moved,
            displacements.reshape(6, 1, count),
        ),
        log_weight,
    )
    records = [lax.ppermute(record, "grp", pairs(n_grp, s)) for s in range(1, n_grp)]

    depth = electrons // chunks
    kept = shape((depth, electrons), BF16)
    token = shape((8, LANES), F32)
    own = [None] * chunks
    ends = (0, chunks - 1)
    middle = tuple(range(1, chunks - 1))
    own[0], own[-1] = call(
        functools.partial(round_kernel, ends),
        (kept,) * 2,
        [HBM, ANY],
        (ANY,) * 2,
        scratch=[
            pltpu.VMEM((2, depth, electrons), F32),
            pltpu.VMEM((2, depth, electrons), BF16),
            pltpu.SemaphoreType.DMA((2,)),
            pltpu.SemaphoreType.DMA((2,)),
        ],
        moved=3 * electrons * electrons,
        vmem=6,
    )(*in_hbm(inverse), record)
    own[0], own[-1], token_0 = call(
        gate_kernel,
        (kept, kept, token),
        [ANY] * (2 + others),
        (ANY, ANY, VM),
        aliases={0: 0, 1: 1},
        vmem=1,
    )(own[0], own[-1], *records)

    few = is_power(n_orb) and local % LANES == 0
    direct = few and DIRECT_POINTS
    sources = n_orb if direct else 1
    points, weight, number = call(
        functools.partial(points_kernel, count, others),
        (
            shape((8, LANES) if direct else (n_orb, ROWS, LANES), F32),
            shape((1, LANES), F32),
            shape((1, LANES), jnp.int32),
        ),
        [SM] + [VM] * (others + 3) + [ANY],
        (VM, VM, VM),
    )(role, record, *records, tiled, disp, token_0)
    if direct:
        points = [points] + [lax.ppermute(points, "orb", pairs(n_orb, s)) for s in range(1, n_orb)]
    else:
        points = [lax.all_to_all(points, "orb", split_axis=0, concat_axis=0, tiled=True)]

    width = -(-local // LANES) * LANES
    coeff = jnp.pad(coefficients, ((0, 0), (0, width - local))) if width > local else coefficients
    derived, *prepared = call(
        functools.partial(prepare_kernel, middle),
        (shape((plane, 5 * width), BF16),)
        + (pltpu.HBM((depth, electrons), BF16),) * len(middle),
        [HBM, HBM, HBM, ANY],
        (VM,) + (ANY,) * len(middle),
        scratch=[
            pltpu.VMEM((plane, width), BF16),
            pltpu.VMEM(wavevectors.shape, F32),
            pltpu.VMEM((len(middle), depth, electrons), F32),
            pltpu.VMEM((len(middle), depth, electrons), BF16),
            pltpu.SemaphoreType.DMA((2,)),
            pltpu.SemaphoreType.DMA((len(middle),)),
            pltpu.SemaphoreType.DMA((len(middle),)),
        ],
        flops=8 * plane * width,
        moved=3 * electrons * electrons + 10 * plane * width,
        vmem=12,
    )(*in_hbm(coeff, wavevectors, inverse), weight)
    for chunk, ready in zip(middle, prepared):
        own[chunk] = ready

    arrays = list(own)
    if n_grp == 4:
        send_x = lambda block: lax.ppermute(block, "grp", pairs(n_grp, 1))
        send_y = lambda block: lax.ppermute(block, "grp", pairs(n_grp, 2))

        def relay(mine, got, first):
            return call(
                relay_kernel,
                (kept, kept, token),
                [SM] + [ANY] * (4 + len(first)),
                (ANY, ANY, VM),
                scratch=[
                    pltpu.VMEM((4, depth // 2, electrons), BF16),
                    pltpu.SemaphoreType.DMA((4,)),
                    pltpu.SemaphoreType.DMA((4,)),
                ],
                aliases={3: 0, 4: 1},
                vmem=2,
            )(apart, *in_hbm(*mine), *got, *first)

        x1, y1 = send_x(own[0]), send_y(own[3])
        y1, x1, token_1 = relay((own[1], own[2]), (y1, x1), (derived, *points))
        x2, y2 = send_x(y1), send_y(x1)
    else:
        token_1 = token_2 = jnp.zeros((8, LANES), F32)
        plan = [tuple((chunk, chunk) for chunk in range(chunks))]
        for step in range(1, n_grp):
            plan.append(tuple((chunk, len(arrays) + chunk) for chunk in range(chunks)))
            arrays += [lax.ppermute(block, "grp", pairs(n_grp, step)) for block in own]
        settled = len(arrays)

    height = 11 * count
    spread = few and DIRECT_VALUES
    targets = n_orb if spread else 1
    block = n_orb if few else math.gcd(n_orb, 8)
    whole = lambda array: pl.BlockSpec(array.shape, lambda i: (0,) * array.ndim)
    if direct:
        point_specs = [whole(p) for p in points]
    else:
        point_specs = [pl.BlockSpec((block, ROWS, LANES), lambda i: (i, 0, 0))]
    if spread:
        out_shapes = (shape((height, width), BF16),) * n_orb
        out_specs = tuple(whole(o) for o in out_shapes)
    else:
        out_shapes = (shape((n_orb, height, width), BF16),)
        out_specs = (pl.BlockSpec((block, height, width), lambda i: (i, 0, 0)),)
    values = pl.pallas_call(
        functools.partial(evaluate_kernel, count, sources, targets),
        grid=(n_orb // block,),
        out_shape=out_shapes,
        in_specs=point_specs + [whole(wavevectors), whole(derived), ANY],
        out_specs=out_specs,
        scratch_shapes=[
            pltpu.VMEM((block * 3 * count, plane), BF16),
            pltpu.VMEM((block * 2 * count, plane), BF16),
            pltpu.VMEM((block, 8, LANES), F32),
            pltpu.VMEM((3, 6 * count, LANES), F32),
        ],
        compiler_params=pltpu.CompilerParams(vmem_limit_bytes=8 * MIB),
        cost_estimate=pl.CostEstimate(
            flops=2 * n_orb * count * plane * width * 11,
            bytes_accessed=12 * plane * width,
            transcendentals=0,
        ),
    )(*points, wavevectors, derived, token_1)
    computed = values[0]
    if spread:
        values = [values[0]] + [
            lax.ppermute(values[s], "orb", pairs(n_orb, s)) for s in range(1, n_orb)
        ]
    else:
        values = values[0][:, :, :local]
        values = lax.all_to_all(values, "orb", split_axis=0, concat_axis=0, tiled=True)
        if width > local:
            values = values.transpose(1, 0, 2).reshape(1, height, electrons)
        values = [values]

    if n_grp == 4:
        y2, x2, token_2 = relay((own[2], own[1]), (y2, x2), (computed,))
        x3, y3 = send_x(y2), send_y(x2)
        arrays = own + [x1, x2, y1, y2, x3, y3]
        a1, a2, b1, b2, a3, b3 = range(chunks, chunks + 6)
        first, second, third, fourth = range(chunks)
        plan = [
            tuple((chunk, chunk) for chunk in range(chunks)),
            ((first, a1), (second, a2), (third, a3), (fourth, b3)),
            ((fourth, b1), (third, b2), (first, a3), (second, b3)),
            ((fourth, a2), (first, b2), (third, a3), (second, b3)),
        ]
        settled = chunks + 4

    columns = call(
        functools.partial(columns_kernel, count),
        shape((electrons, LANES), BF16),
        [HBM, VM, ANY],
        VM,
        scratch=[
            pltpu.VMEM((chunks, depth, electrons), F32),
            pltpu.SemaphoreType.DMA((chunks,)),
        ],
        flops=2 * electrons * electrons * LANES,
        moved=4 * electrons * electrons,
        vmem=8,
    )(*in_hbm(inverse), tiled, token_2)

    here = lax.axis_index("orb").astype(jnp.int32).reshape(1)
    early = 2
    work = 2 * electrons * 2 * count
    drift, laplacian, later, early_columns, products, total = call(
        functools.partial(middle_kernel, count, targets, plan),
        (
            shape((3, 1, count), F32),
            shape((1, 1, count), F32),
            shape((6 * count, electrons), BF16),
            shape((early, depth, LANES), BF16),
            shape((6 * count, LANES), F32),
            shape((2 * count, electrons), F32),
        ),
        [SM, SM, VM] + [VM] * (targets + 1) + [ANY] * settled,
        (VM,) * 6,
        scratch=[
            pltpu.VMEM((5 * count, electrons), BF16),
            pltpu.VMEM((early, depth, electrons), BF16),
            pltpu.SemaphoreType.DMA((early,)),
        ],
        flops=early * depth * work,
        moved=2 * early * depth * electrons + 44 * count * electrons,
        vmem=8,
    )(here, role, number, *values, columns, *in_hbm(*own), *arrays[chunks:settled])

    updated, drift, laplacian, new_weight = call(
        functools.partial(finish_kernel, count, plan),
        (
            shape((electrons, electrons), F32),
            shape((6, 1, count), F32),
            shape((2, 1, count), F32),
            shape((1, LANES), F32),
        ),
        [SM] + [VM] * 8 + [HBM] + [ANY] * len(arrays),
        (HBM, VM, VM, VM),
        scratch=[
            pltpu.VMEM((chunks, depth, electrons), BF16),
            pltpu.VMEM((chunks, depth, electrons), F32),
            pltpu.SemaphoreType.DMA((chunks,)),
            pltpu.SemaphoreType.DMA((chunks,)),
            pltpu.SemaphoreType.DMA((chunks,)),
        ],
        flops=2 * electrons * work,
        moved=6 * electrons * electrons,
        vmem=12,
    )(
        role,
        number,
        later,
        weight,
        drift,
        laplacian,
        early_columns,
        products,
        total,
        *in_hbm(inverse, *own),
        *arrays[chunks:],
    )

    return updated[None], drift.reshape(2, 1, 3, count), laplacian, new_weight[0, :1]


def solution(mesh):
    split = ("grp", "orb")
    return jax.shard_map(
        functools.partial(per_device, mesh.shape["grp"], mesh.shape["orb"]),
        mesh=mesh,
        in_specs=(
            P(),
            P(None, "orb"),
            P(split, None, None),
            P(split, None, None),
            P(None, split, None, None),
            P(None, split, None),
            P("orb"),
            P(split),
            P(split),
        ),
        out_specs=(
            P(split, None, None),
            P(None, split, None, None),
            P(None, split, None),
            P(split),
        ),
        check_vma=False,
    )
```

```python
import functools
import math

import jax
import jax.numpy as jnp
from jax import lax
from jax.experimental import pallas as pl
from jax.experimental.pallas import tpu as pltpu
from jax.sharding import PartitionSpec as P

F32 = jnp.float32
BF16 = jnp.bfloat16
LANES = 128
ROWS = 16
DIRECT_POINTS = False
DIRECT_VALUES = False
MIB = 1024 * 1024
precise = lax.Precision.HIGHEST

SIN_HALF = (4.4428679, -7.30744342, 3.59478808, -0.78437403)
COS_HALF = (1.4142135, -6.97885099, 5.73946117, -1.88356299, 0.31069819)


def dot(a, b, dims=((1,), (0,)), exact=False):
    return lax.dot_general(
        a, b, (dims, ((), ())), precision=precise if exact else None, preferred_element_type=F32
    )


def exact_dot(a, pick, dims=((1,), (0,))):
    high = a.astype(BF16)
    rest = a - high.astype(F32)
    middle = rest.astype(BF16)
    low = (rest - middle.astype(F32)).astype(BF16)
    rows = a.shape[0]
    parts = jnp.concatenate([high, middle, low], 0)
    found = dot(parts, pick, dims)
    return (found[0:rows] + found[rows : 2 * rows]) + found[2 * rows :]


def iota(shape, dim):
    return lax.broadcasted_iota(jnp.int32, shape, dim)


def call(
    kernel, out_shape, in_specs, out_specs, scratch=(), flops=0, moved=0, vmem=4, aliases=None
):
    return pl.pallas_call(
        kernel,
        out_shape=out_shape,
        input_output_aliases=aliases or {},
        in_specs=in_specs,
        out_specs=out_specs,
        scratch_shapes=list(scratch),
        compiler_params=pltpu.CompilerParams(vmem_limit_bytes=vmem * MIB),
        cost_estimate=pl.CostEstimate(flops=flops, bytes_accessed=moved, transcendentals=0),
    )


VM = pl.BlockSpec(memory_space=pltpu.VMEM)
SM = pl.BlockSpec(memory_space=pltpu.SMEM)
ANY = pl.BlockSpec(memory_space=pl.ANY)
HBM = pl.BlockSpec(memory_space=pltpu.HBM)


def shape(dims, dtype):
    return jax.ShapeDtypeStruct(dims, dtype)


def in_hbm(*arrays):
    return tuple(pltpu.with_memory_space_constraint(a, pltpu.HBM) for a in arrays)


def is_power(n):
    return n & (n - 1) == 0


def pairs(n, step):
    if is_power(n):
        return [(i, i ^ step) for i in range(n)]
    return [(i, (i + step) % n) for i in range(n)]


def distance(n, here, there):
    return here ^ there if is_power(n) else lax.rem(here - there + n, n)


def backward(n, step):
    return step if is_power(n) else (n - step) % n


def start_kernel(
    count,
    pos_hbm,
    moved_hbm,
    disp_hbm,
    weight_ref,
    out_ref,
    tiled_ref,
    shift_ref,
    pos_ref,
    moved_ref,
    disp_ref,
    sems,
):
    loads = [
        pltpu.make_async_copy(src, dst, sems.at[i])
        for i, (src, dst) in enumerate(
            (
                (moved_hbm, moved_ref),
                (disp_hbm, disp_ref),
                (pos_hbm, pos_ref),
            )
        )
    ]
    for load in loads:
        load.start()
    electrons = pos_ref.shape[2]
    copies = LANES // count
    loads[0].wait()
    tiled = jnp.concatenate([moved_ref[:, 0, :]] * copies, 1)
    tiled_ref[...] = tiled
    pick = (iota((electrons, LANES), 0) == tiled[0:1, :]).astype(F32).astype(BF16)
    block = iota((8, LANES), 1) // count
    zeros = jnp.zeros((5, LANES), F32)
    loads[1].wait()
    for update in range(2):
        shift = jnp.concatenate([disp_ref[3 * update : 3 * update + 3, 0, :]] * copies, 1)
        shift_ref[update] = jnp.concatenate([shift, zeros], 0)
    loads[2].wait()
    pos = jnp.concatenate([pos_ref[:, 0, :], jnp.zeros((5, electrons), F32)], 0)
    old = exact_dot(pos, pick)
    disp = shift_ref[0]
    points = old + jnp.where(block % 2 == 1, disp, 0.0)
    first = jnp.where(block == 0, disp, 0.0)
    out_ref[...] = pos + exact_dot(first, pick, ((1,), (1,)))
    out_ref[3:6, 0:LANES] = points[0:3]
    out_ref[6:7, 0:LANES] = tiled[0:1, :].astype(F32)
    out_ref[7:8, 0:LANES] = jnp.full((1, LANES), weight_ref[0], F32)


def rows_of(ref, chunk, depth):
    return ref.at[0, pl.ds(chunk * depth, depth)]


def round_kernel(wanted, inverse_hbm, after_ref, *refs):
    outs = refs[: len(wanted)]
    staged, rounded, in_sem, out_sem = refs[len(wanted) :]
    depth = staged.shape[1]
    loads, stores = [], []
    for slot, chunk in enumerate(wanted):
        load = pltpu.make_async_copy(
            rows_of(inverse_hbm, chunk, depth), staged.at[slot], in_sem.at[slot]
        )
        load.start()
        loads.append(load)
    for slot, out in enumerate(outs):
        loads[slot].wait()
        rounded[slot] = staged[slot].astype(BF16)
        store = pltpu.make_async_copy(rounded.at[slot], out, out_sem.at[slot])
        store.start()
        stores.append(store)
    for store in stores:
        store.wait()


def gate_kernel(*refs):
    token_ref = refs[-1]
    token_ref[...] = jnp.zeros(token_ref.shape, F32)


def relay_kernel(flag_ref, own_a, own_b, got_a, got_b, *refs):
    out_a, out_b, token_ref, staged, in_sem, out_sem = refs[-6:]
    pieces, depth, _ = staged.shape

    @pl.when(flag_ref[0] == 0)
    def _():
        loads, stores = [], []
        for piece in range(pieces):
            own, out = (own_a, out_a) if piece < pieces // 2 else (own_b, out_b)
            rows = pl.ds(piece % (pieces // 2) * depth, depth)
            loads.append(
                pltpu.make_async_copy(own.at[rows], staged.at[piece], in_sem.at[piece])
            )
            stores.append(
                pltpu.make_async_copy(staged.at[piece], out.at[rows], out_sem.at[piece])
            )
        for load in loads:
            load.start()
        for load, store in zip(loads, stores):
            load.wait()
            store.start()
        for store in stores:
            store.wait()

    token_ref[...] = jnp.zeros(token_ref.shape, F32)


def points_kernel(count, others, role_ref, *refs):
    own_ref = refs[0]
    received = refs[1 : 1 + others]
    moved_ref, disp_ref, after_ref, points_ref, weight_ref, number_ref = refs[1 + others :]
    role = role_ref[0]
    parent = own_ref[...]
    for step in range(others):
        parent = jnp.where(role == step + 1, received[step][...], parent)
    electrons = parent.shape[1]
    pick = (iota((electrons, LANES), 0) == moved_ref[1:2, :]).astype(F32).astype(BF16)
    block = iota((8, LANES), 1) // count
    old = exact_dot(parent, pick)
    later = old + jnp.where(block % 2 == 1, disp_ref[1], 0.0)
    zeros = jnp.zeros((5, LANES), F32)
    mine = jnp.concatenate([own_ref[3:6, 0:LANES], zeros], 0)
    theirs = jnp.concatenate([parent[3:6, 0:LANES], zeros], 0)
    points = jnp.where(block < 2, mine, jnp.where(block < 4, theirs, later))
    if len(points_ref.shape) == 2:
        points_ref[...] = points
    else:
        points = jnp.concatenate([points, jnp.zeros((ROWS - 8, LANES), F32)], 0)
        points_ref[...] = jnp.broadcast_to(points[None], points_ref.shape)
    weight_ref[...] = parent[7:8, 0:LANES]
    before = parent[6:7, 0:LANES].astype(jnp.int32)
    number_ref[...] = jnp.where(
        block[0:1] == 0, before, jnp.where(block[0:1] == 1, moved_ref[1:2, :], -1)
    )


def derive(coeff_ref, wave_ref, out_ref):
    waves = wave_ref.shape[1]
    width = coeff_ref.shape[1]
    wave = jnp.transpose(jnp.concatenate([wave_ref[...], jnp.zeros((5, waves), F32)], 0))
    out_ref[:, 0:width] = coeff_ref[...]
    cos_part = coeff_ref[0:waves].astype(F32)
    sin_part = coeff_ref[waves:].astype(F32)
    squared = None
    for a in range(3):
        scale = wave[:, a : a + 1]
        where = slice((a + 1) * width, (a + 2) * width)
        out_ref[0:waves, where] = (scale * sin_part).astype(BF16)
        out_ref[waves:, where] = (-scale * cos_part).astype(BF16)
        squared = scale * scale if a == 0 else squared + scale * scale
    where = slice(4 * width, 5 * width)
    out_ref[0:waves, where] = (-squared * cos_part).astype(BF16)
    out_ref[waves:, where] = (-squared * sin_part).astype(BF16)


def prepare_kernel(wanted, coeff_hbm, wave_hbm, inverse_hbm, after_ref, table_ref, *refs):
    outs = refs[: len(wanted)]
    coeff_ref, wave_ref, staged, rounded, small_sem, in_sem, out_sem = refs[len(wanted) :]
    depth = staged.shape[1]
    wave_load = pltpu.make_async_copy(wave_hbm, wave_ref, small_sem.at[0])
    coeff_load = pltpu.make_async_copy(coeff_hbm, coeff_ref, small_sem.at[1])
    wave_load.start()
    coeff_load.start()
    loads, stores = [], []
    for slot, chunk in enumerate(wanted):
        load = pltpu.make_async_copy(
            rows_of(inverse_hbm, chunk, depth), staged.at[slot], in_sem.at[slot]
        )
        load.start()
        loads.append(load)
    for slot, out in enumerate(outs):
        loads[slot].wait()
        rounded[slot] = staged[slot].astype(BF16)
        store = pltpu.make_async_copy(rounded.at[slot], out, out_sem.at[slot])
        store.start()
        stores.append(store)
    wave_load.wait()
    coeff_load.wait()
    derive(coeff_ref, wave_ref, table_ref)
    for store in stores:
        store.wait()


def horner(coefs, u):
    value = coefs[-1] * u + coefs[-2]
    for c in reversed(coefs[:-2]):
        value = value * u + c
    return value


def evaluate_kernel(count, sources, targets, *refs):
    points = refs[:sources]
    wave_ref, table_ref = refs[sources : sources + 2]
    outs = refs[sources + 3 : -4]
    diff, new, gathered, spread = refs[-4:]
    walkers = gathered.shape[0]
    for w in range(walkers):
        gathered[w] = points[w][...] if sources > 1 else points[0][w, 0:8]
    waves = wave_ref.shape[1]
    width = table_ref.shape[1] // 5
    step = math.gcd(waves, LANES)

    def one(w, carry):
        column = jnp.transpose(gathered[w])
        for a in range(3):
            spread[a] = jnp.broadcast_to(column[0 : 6 * count, a : a + 1], (6 * count, step))
        row_d = pl.multiple_of(w * (3 * count), count)
        row_n = pl.multiple_of(w * (2 * count), count)
        for at in range(0, waves, step):
            ks = [wave_ref[a : a + 1, at : at + step] * (0.5 / math.pi) for a in range(3)]
            for pair, diff_at, new_at in ((0, 2, 1), (1, 0, None), (2, 1, 0)):
                rows = slice(2 * pair * count, 2 * (pair + 1) * count)
                turn = spread[0, rows] * ks[0] + spread[1, rows] * ks[1] + spread[2, rows] * ks[2]
                r = turn - jnp.floor(turn + 0.5)
                u = r * r
                s = r * horner(SIN_HALF, u)
                c = horner(COS_HALF, u)
                for value, base in ((1.0 - s * s, 0), (s * c, waves)):
                    where = slice(base + at, base + at + step)
                    kept = value.astype(BF16)
                    wide = kept.astype(F32)
                    change = (wide[count:] - wide[:count]).astype(BF16)
                    diff[pl.ds(row_d + diff_at * count, count), where] = change
                    if new_at is not None:
                        new[pl.ds(row_n + new_at * count, count), where] = kept[count:]
        return carry

    lax.fori_loop(0, walkers, one, 0)
    change = dot(diff[...], table_ref[:, 0:width]).astype(BF16)
    rest = dot(new[...], table_ref[:, width:]).astype(BF16)
    for w in range(walkers):
        out_ref = outs[w] if targets > 1 else outs[0].at[w]
        at = w * 3 * count
        out_ref[0 : 2 * count] = change[at : at + 2 * count]
        out_ref[6 * count : 7 * count] = change[at + 2 * count : at + 3 * count]
        for half, base in ((0, 2 * count), (1, 7 * count)):
            row = (2 * w + half) * count
            for a in range(4):
                out_ref[base + a * count : base + (a + 1) * count] = rest[
                    row : row + count, a * width : (a + 1) * width
                ]


def pair_inverse(a, b, d):
    det = a * d - b * b
    scale = 1.0 / det
    return d * scale, -b * scale, a * scale, det


def sweep(matrix):
    size = matrix.shape[0]
    log = jnp.zeros((1, 1), F32)
    row = iota((size, size), 0)
    lane = iota((size, size), 1)
    place = iota((1, size), 1)
    for k in range(0, size, 4):
        columns = [jnp.broadcast_to(matrix[:, k + j : k + j + 1], (size, size)) for j in range(4)]
        lines = [matrix[k + i : k + i + 1, :] for i in range(4)]
        at = lambda i, j: columns[j][k + i : k + i + 1, :]
        a00, a01, a11, det_a = pair_inverse(at(0, 0), at(0, 1), at(1, 1))
        b00, b01, b10, b11 = at(0, 2), at(0, 3), at(1, 2), at(1, 3)
        t00, t01 = a00 * b00 + a01 * b10, a00 * b01 + a01 * b11
        t10, t11 = a01 * b00 + a11 * b10, a01 * b01 + a11 * b11
        d00 = at(2, 2) - (b00 * t00 + b10 * t10)
        d01 = at(2, 3) - (b00 * t01 + b10 * t11)
        d11 = at(3, 3) - (b01 * t01 + b11 * t11)
        s00, s01, s11, det_s = pair_inverse(d00, d01, d11)
        u00, u01 = -(t00 * s00 + t01 * s01), -(t00 * s01 + t01 * s11)
        u10, u11 = -(t10 * s00 + t11 * s01), -(t10 * s01 + t11 * s11)
        q00, q01 = a00 - (u00 * t00 + u01 * t01), a01 - (u00 * t10 + u01 * t11)
        q11 = a11 - (u10 * t10 + u11 * t11)
        pivot = (
            (q00, q01, u00, u01),
            (q01, q11, u10, u11),
            (u00, u10, s00, s01),
            (u01, u11, s01, s11),
        )
        reduced = matrix
        scaled, edges = [], []
        for i in range(4):
            line = pivot[i][0] * lines[0] + pivot[i][1] * lines[1]
            line = line + (pivot[i][2] * lines[2] + pivot[i][3] * lines[3])
            reduced = reduced - columns[i] * line
            for j in range(4):
                line = jnp.where(place == k + j, -pivot[i][j], line)
            scaled.append(line)
            edge = pivot[i][0] * columns[0] + pivot[i][1] * columns[1]
            edges.append(edge + (pivot[i][2] * columns[2] + pivot[i][3] * columns[3]))
        matrix = reduced
        for i in range(4):
            matrix = jnp.where(lane == k + i, edges[i], matrix)
        for i in range(4):
            matrix = jnp.where(row == k + i, scaled[i], matrix)
        log = log + (jnp.log(det_a[:, 0:1]) + jnp.log(det_s[:, 0:1]))
    return -matrix, log


def ratio_of(products, size):
    eye = jnp.where(iota((size, size), 0) == iota((size, size), 1), 1.0, 0.0)
    ratio = products[0:size, 0:size] + eye
    inverse, log = sweep(dot(ratio, ratio, ((0,), (0,)), exact=True))
    return ratio, inverse, 0.5 * log


def moved_sums(products, ratio, inverse, count):
    size = ratio.shape[0]
    turned = dot(ratio, inverse, exact=True)[size - count :]
    tile = jnp.concatenate([turned] * 4, 0)
    part = products[size : size + 4 * count, 0:size] * tile
    return dot(jnp.ones((8, size), F32), part, ((1,), (1,)), exact=True)[0:1]


def columns_kernel(count, inverse_hbm, moved_ref, after_ref, out_ref, staged, sem):
    chunks, depth, electrons = staged.shape
    loads = []
    for chunk in range(chunks):
        load = pltpu.make_async_copy(
            rows_of(inverse_hbm, chunk, depth), staged.at[chunk], sem.at[chunk]
        )
        load.start()
        loads.append(load)
    block = iota((1, LANES), 1) // count
    number = jnp.where(block == 0, moved_ref[0:1, :], -1)
    pick = (iota((electrons, LANES), 0) == number).astype(F32).astype(BF16)
    for chunk in range(chunks):
        loads[chunk].wait()
        found = dot(staged[chunk].astype(BF16), pick)
        out_ref[chunk * depth : (chunk + 1) * depth] = found.astype(BF16)


def pick_from(number_ref, electrons):
    return (iota((electrons, LANES), 0) == number_ref[...]).astype(F32).astype(BF16)


def chunk_at(plan, role, slot):
    chunk = jnp.int32(plan[0][slot][0])
    for which in range(1, len(plan)):
        chunk = jnp.where(role == which, plan[which][slot][0], chunk)
    return chunk


def load_slots(plan, slots, role, inputs, parent, sem):
    for slot in slots:
        for which in range(len(plan)):
            load = pltpu.make_async_copy(
                inputs[plan[which][slot][1]], parent.at[slot], sem.at[slot]
            )
            pl.when(role == which)(load.start)


def wait_slots(slots, inputs, parent, sem):
    for slot in slots:
        pltpu.make_async_copy(inputs[0], parent.at[slot], sem.at[slot]).wait()


def middle_kernel(count, sources, plan, me_ref, role_ref, number_ref, *refs):
    values = refs[:sources]
    own_columns = refs[sources]
    inputs = refs[sources + 1 : -9]
    drift_ref, lap_ref, later_ref, columns_ref, products_ref, total_ref = refs[-9:-3]
    vals, parent, sem = refs[-3:]
    slots, depth, electrons = parent.shape
    role = role_ref[0]
    load_slots(plan, range(slots), role, inputs, parent, sem)
    rows = later_ref.shape[0]
    if sources > 1:
        width = values[0].shape[1]
        for step in range(sources):
            at = pl.multiple_of((me_ref[0] ^ step) * width, width)
            later_ref[:, pl.ds(at, width)] = values[step][0:rows]
            vals[:, pl.ds(at, width)] = values[step][rows:]
    else:
        pieces, _, width = values[0].shape
        for piece in range(pieces):
            where = slice(piece * width, (piece + 1) * width)
            later_ref[:, where] = values[0][piece, 0:rows]
            vals[:, where] = values[0][piece, rows:]
    pick = pick_from(number_ref, electrons)
    wait_slots(range(slots), inputs, parent, sem)
    own = dot(vals[...], own_columns[...])
    products, total = None, None
    for slot in range(slots):
        columns = dot(parent[slot], pick).astype(BF16)
        columns_ref[slot] = columns
        at = pl.multiple_of(chunk_at(plan, role, slot) * depth, depth)
        part = later_ref[:, pl.ds(at, depth)]
        product = dot(part, columns)
        more = dot(part[0 : 2 * count], parent[slot])
        products = product if slot == 0 else products + product
        total = more if slot == 0 else total + more
    products_ref[...] = products
    total_ref[...] = total
    ratio, inverse, _ = ratio_of(own, count)
    sums = moved_sums(own, ratio, inverse, count)
    for a in range(3):
        drift_ref[a] = sums[:, a * count : (a + 1) * count]
    lap_ref[0] = sums[:, 3 * count : 4 * count]


def finish_kernel(
    count,
    plan,
    role_ref,
    number_ref,
    later_ref,
    weight_ref,
    drift_in,
    lap_in,
    early_ref,
    products_ref,
    total_ref,
    inverse_hbm,
    *refs,
):
    inputs = refs[:-9]
    out_ref, drift_ref, lap_ref, out_weight_ref = refs[-9:-5]
    parent, staged, in_sem, own_sem, out_sem = refs[-5:]
    chunks, depth, electrons = parent.shape
    done = early_ref.shape[0]
    late = range(done, chunks)
    size = 2 * count
    role = role_ref[0]
    own = [
        pltpu.make_async_copy(
            rows_of(inverse_hbm, plan[0][slot][0], depth), staged.at[slot], own_sem.at[slot]
        )
        for slot in range(chunks)
    ]
    load_slots(plan, list(late) + list(range(done)), role, inputs, parent, in_sem)
    pick = pick_from(number_ref, electrons)
    wait_slots(late, inputs, parent, in_sem)
    for load in own[done:] + own[:done]:
        pl.when(role == 0)(load.start)
    columns = [early_ref[slot] for slot in range(done)]
    products = products_ref[...]
    rows = []
    for slot in late:
        columns.append(dot(parent[slot], pick).astype(BF16))
        at = pl.multiple_of(chunk_at(plan, role, slot) * depth, depth)
        rows.append(later_ref[:, pl.ds(at, depth)])
        products = products + dot(rows[-1], columns[-1])
    ratio, inverse, log = ratio_of(products, size)
    total = total_ref[...]
    for slot, part in zip(late, rows):
        total = total + dot(part[0:size], parent[slot])
    small = dot(inverse, ratio, ((1,), (1,)), exact=True)
    high = small.astype(BF16)
    halves = jnp.concatenate([high, (small - high.astype(F32)).astype(BF16)], 1)
    rounded = total.astype(BF16)
    solved = dot(halves, jnp.concatenate([rounded, rounded], 0)).astype(BF16)
    solved = jnp.concatenate([solved, jnp.zeros((LANES - size, electrons), BF16)], 0)
    wait_slots(range(done), inputs, parent, in_sem)
    copies = []
    for slot in list(late) + list(range(done)):
        at = pl.multiple_of(chunk_at(plan, role, slot) * depth, depth)
        copy = pltpu.make_async_copy(
            staged.at[slot], out_ref.at[pl.ds(at, depth)], out_sem.at[slot]
        )
        copies.append((slot, copy))

    def kept(slot):
        own[slot].wait()
        return staged[slot]

    def write(before):
        for slot, copy in copies:
            staged[slot] = before(slot) - dot(columns[slot], solved)
            copy.start()

    pl.when(role == 0)(lambda: write(kept))
    pl.when(role != 0)(lambda: write(lambda slot: parent[slot].astype(F32)))
    sums = moved_sums(products, ratio, inverse, count)
    drift_ref[0:3] = drift_in[...]
    lap_ref[0:1] = lap_in[...]
    for a in range(3):
        drift_ref[3 + a] = sums[:, a * count : (a + 1) * count]
    lap_ref[1] = sums[:, 3 * count : 4 * count]
    out_weight_ref[...] = weight_ref[...] + log
    for _, copy in copies:
        copy.wait()


def per_device(
    n_grp,
    n_orb,
    wavevectors,
    coefficients,
    inverse,
    positions,
    displacements,
    moved,
    donor,
    take,
    log_weight,
):
    electrons = inverse.shape[1]
    count = moved.shape[2]
    plane = coefficients.shape[0]
    local = coefficients.shape[1]
    others = n_grp - 1
    chunks = 4

    apart = distance(n_grp, lax.axis_index("grp"), donor[0])
    role = jnp.where(take[0] == 1, apart, 0).astype(jnp.int32).reshape(1)
    apart = apart.astype(jnp.int32).reshape(1)

    record, tiled, disp = call(
        functools.partial(start_kernel, count),
        (
            shape((8, electrons), F32),
            shape((2, LANES), jnp.int32),
            shape((2, 8, LANES), F32),
        ),
        [HBM, HBM, HBM, SM],
        (VM, VM, VM),
        scratch=[
            pltpu.VMEM((3, 1, electrons), F32),
            pltpu.VMEM((2, 1, count), jnp.int32),
            pltpu.VMEM((6, 1, count), F32),
            pltpu.SemaphoreType.DMA((3,)),
        ],
    )(
        *in_hbm(
            positions.reshape(3, 1, electrons),
            moved,
            displacements.reshape(6, 1, count),
        ),
        log_weight,
    )
    records = [lax.ppermute(record, "grp", pairs(n_grp, s)) for s in range(1, n_grp)]

    depth = electrons // chunks
    kept = shape((depth, electrons), BF16)
    token = shape((8, LANES), F32)
    own = [None] * chunks
    ends = (0, chunks - 1)
    middle = tuple(range(1, chunks - 1))
    own[0], own[-1] = call(
        functools.partial(round_kernel, ends),
        (kept,) * 2,
        [HBM, ANY],
        (ANY,) * 2,
        scratch=[
            pltpu.VMEM((2, depth, electrons), F32),
            pltpu.VMEM((2, depth, electrons), BF16),
            pltpu.SemaphoreType.DMA((2,)),
            pltpu.SemaphoreType.DMA((2,)),
        ],
        moved=3 * electrons * electrons,
        vmem=6,
    )(*in_hbm(inverse), record)
    own[0], own[-1], token_0 = call(
        gate_kernel,
        (kept, kept, token),
        [ANY] * (2 + others),
        (ANY, ANY, VM),
        aliases={0: 0, 1: 1},
        vmem=1,
    )(own[0], own[-1], *records)

    few = is_power(n_orb) and local % LANES == 0
    direct = few and DIRECT_POINTS
    sources = n_orb if direct else 1
    points, weight, number = call(
        functools.partial(points_kernel, count, others),
        (
            shape((8, LANES) if direct else (n_orb, ROWS, LANES), F32),
            shape((1, LANES), F32),
            shape((1, LANES), jnp.int32),
        ),
        [SM] + [VM] * (others + 3) + [ANY],
        (VM, VM, VM),
    )(role, record, *records, tiled, disp, token_0)
    if direct:
        points = [points] + [lax.ppermute(points, "orb", pairs(n_orb, s)) for s in range(1, n_orb)]
    else:
        points = [lax.all_to_all(points, "orb", split_axis=0, concat_axis=0, tiled=True)]

    width = -(-local // LANES) * LANES
    coeff = jnp.pad(coefficients, ((0, 0), (0, width - local))) if width > local else coefficients
    derived, *prepared = call(
        functools.partial(prepare_kernel, middle),
        (shape((plane, 5 * width), BF16),)
        + (pltpu.HBM((depth, electrons), BF16),) * len(middle),
        [HBM, HBM, HBM, ANY],
        (VM,) + (ANY,) * len(middle),
        scratch=[
            pltpu.VMEM((plane, width), BF16),
            pltpu.VMEM(wavevectors.shape, F32),
            pltpu.VMEM((len(middle), depth, electrons), F32),
            pltpu.VMEM((len(middle), depth, electrons), BF16),
            pltpu.SemaphoreType.DMA((2,)),
            pltpu.SemaphoreType.DMA((len(middle),)),
            pltpu.SemaphoreType.DMA((len(middle),)),
        ],
        flops=8 * plane * width,
        moved=3 * electrons * electrons + 10 * plane * width,
        vmem=12,
    )(*in_hbm(coeff, wavevectors, inverse), weight)
    for chunk, ready in zip(middle, prepared):
        own[chunk] = ready

    arrays = list(own)
    if n_grp == 4:
        send_x = lambda block: lax.ppermute(block, "grp", pairs(n_grp, 1))
        send_y = lambda block: lax.ppermute(block, "grp", pairs(n_grp, 2))

        def relay(mine, got, first):
            return call(
                relay_kernel,
                (kept, kept, token),
                [SM] + [ANY] * (4 + len(first)),
                (ANY, ANY, VM),
                scratch=[
                    pltpu.VMEM((4, depth // 2, electrons), BF16),
                    pltpu.SemaphoreType.DMA((4,)),
                    pltpu.SemaphoreType.DMA((4,)),
                ],
                aliases={3: 0, 4: 1},
                vmem=2,
            )(apart, *in_hbm(*mine), *got, *first)

        x1, y1 = send_x(own[0]), send_y(own[3])
        y1, x1, token_1 = relay((own[1], own[2]), (y1, x1), (derived, *points))
        x2, y2 = send_x(y1), send_y(x1)
    else:
        token_1 = token_2 = jnp.zeros((8, LANES), F32)
        plan = [tuple((chunk, chunk) for chunk in range(chunks))]
        for step in range(1, n_grp):
            plan.append(tuple((chunk, len(arrays) + chunk) for chunk in range(chunks)))
            arrays += [lax.ppermute(block, "grp", pairs(n_grp, step)) for block in own]
        settled = len(arrays)

    height = 11 * count
    spread = few and DIRECT_VALUES
    targets = n_orb if spread else 1
    block = n_orb if few else math.gcd(n_orb, 8)
    whole = lambda array: pl.BlockSpec(array.shape, lambda i: (0,) * array.ndim)
    if direct:
        point_specs = [whole(p) for p in points]
    else:
        point_specs = [pl.BlockSpec((block, ROWS, LANES), lambda i: (i, 0, 0))]
    if spread:
        out_shapes = (shape((height, width), BF16),) * n_orb
        out_specs = tuple(whole(o) for o in out_shapes)
    else:
        out_shapes = (shape((n_orb, height, width), BF16),)
        out_specs = (pl.BlockSpec((block, height, width), lambda i: (i, 0, 0)),)
    values = pl.pallas_call(
        functools.partial(evaluate_kernel, count, sources, targets),
        grid=(n_orb // block,),
        out_shape=out_shapes,
        in_specs=point_specs + [whole(wavevectors), whole(derived), ANY],
        out_specs=out_specs,
        scratch_shapes=[
            pltpu.VMEM((block * 3 * count, plane), BF16),
            pltpu.VMEM((block * 2 * count, plane), BF16),
            pltpu.VMEM((block, 8, LANES), F32),
            pltpu.VMEM((3, 6 * count, LANES), F32),
        ],
        compiler_params=pltpu.CompilerParams(vmem_limit_bytes=8 * MIB),
        cost_estimate=pl.CostEstimate(
            flops=2 * n_orb * count * plane * width * 11,
            bytes_accessed=12 * plane * width,
            transcendentals=0,
        ),
    )(*points, wavevectors, derived, token_1)
    computed = values[0]
    if spread:
        values = [values[0]] + [
            lax.ppermute(values[s], "orb", pairs(n_orb, s)) for s in range(1, n_orb)
        ]
    else:
        values = values[0][:, :, :local]
        values = lax.all_to_all(values, "orb", split_axis=0, concat_axis=0, tiled=True)
        if width > local:
            values = values.transpose(1, 0, 2).reshape(1, height, electrons)
        values = [values]

    if n_grp == 4:
        y2, x2, token_2 = relay((own[2], own[1]), (y2, x2), (computed,))
        x3, y3 = send_x(y2), send_y(x2)
        arrays = own + [x1, x2, y1, y2, x3, y3]
        a1, a2, b1, b2, a3, b3 = range(chunks, chunks + 6)
        first, second, third, fourth = range(chunks)
        plan = [
            tuple((chunk, chunk) for chunk in range(chunks)),
            ((first, a1), (second, a2), (third, a3), (fourth, b3)),
            ((fourth, b1), (third, b2), (first, a3), (second, b3)),
            ((fourth, a2), (first, b2), (third, a3), (second, b3)),
        ]
        settled = chunks + 4

    columns = call(
        functools.partial(columns_kernel, count),
        shape((electrons, LANES), BF16),
        [HBM, VM, ANY],
        VM,
        scratch=[
            pltpu.VMEM((chunks, depth, electrons), F32),
            pltpu.SemaphoreType.DMA((chunks,)),
        ],
        flops=2 * electrons * electrons * LANES,
        moved=4 * electrons * electrons,
        vmem=8,
    )(*in_hbm(inverse), tiled, token_2)

    here = lax.axis_index("orb").astype(jnp.int32).reshape(1)
    early = 2
    work = 2 * electrons * 2 * count
    drift, laplacian, later, early_columns, products, total = call(
        functools.partial(middle_kernel, count, targets, plan),
        (
            shape((3, 1, count), F32),
            shape((1, 1, count), F32),
            shape((6 * count, electrons), BF16),
            shape((early, depth, LANES), BF16),
            shape((6 * count, LANES), F32),
            shape((2 * count, electrons), F32),
        ),
        [SM, SM, VM] + [VM] * (targets + 1) + [ANY] * settled,
        (VM,) * 6,
        scratch=[
            pltpu.VMEM((5 * count, electrons), BF16),
            pltpu.VMEM((early, depth, electrons), BF16),
            pltpu.SemaphoreType.DMA((early,)),
        ],
        flops=early * depth * work,
        moved=2 * early * depth * electrons + 44 * count * electrons,
        vmem=8,
    )(here, role, number, *values, columns, *in_hbm(*own), *arrays[chunks:settled])

    updated, drift, laplacian, new_weight = call(
        functools.partial(finish_kernel, count, plan),
        (
            shape((electrons, electrons), F32),
            shape((6, 1, count), F32),
            shape((2, 1, count), F32),
            shape((1, LANES), F32),
        ),
        [SM] + [VM] * 8 + [HBM] + [ANY] * len(arrays),
        (HBM, VM, VM, VM),
        scratch=[
            pltpu.VMEM((chunks, depth, electrons), BF16),
            pltpu.VMEM((chunks, depth, electrons), F32),
            pltpu.SemaphoreType.DMA((chunks,)),
            pltpu.SemaphoreType.DMA((chunks,)),
            pltpu.SemaphoreType.DMA((chunks,)),
        ],
        flops=2 * electrons * work,
        moved=6 * electrons * electrons,
        vmem=12,
    )(
        role,
        number,
        later,
        weight,
        drift,
        laplacian,
        early_columns,
        products,
        total,
        *in_hbm(inverse, *own),
        *arrays[chunks:],
    )

    return updated[None], drift.reshape(2, 1, 3, count), laplacian, new_weight[0, :1]


def solution(mesh):
    split = ("grp", "orb")
    return jax.shard_map(
        functools.partial(per_device, mesh.shape["grp"], mesh.shape["orb"]),
        mesh=mesh,
        in_specs=(
            P(),
            P(None, "orb"),
            P(split, None, None),
            P(split, None, None),
            P(None, split, None, None),
            P(None, split, None),
            P("orb"),
            P(split),
            P(split),
        ),
        out_specs=(
            P(split, None, None),
            P(None, split, None, None),
            P(None, split, None),
            P(split),
        ),
        check_vma=False,
    )
```

```python
import functools
import math

import jax
import jax.numpy as jnp
from jax import lax
from jax.experimental import pallas as pl
from jax.experimental.pallas import tpu as pltpu
from jax.sharding import PartitionSpec as P

F32 = jnp.float32
BF16 = jnp.bfloat16
LANES = 128
ROWS = 16
DIRECT_POINTS = False
DIRECT_VALUES = False
MIB = 1024 * 1024
precise = lax.Precision.HIGHEST

SIN_HALF = (4.4428679, -7.30744342, 3.59478808, -0.78437403)
COS_HALF = (1.4142135, -6.97885099, 5.73946117, -1.88356299, 0.31069819)


def dot(a, b, dims=((1,), (0,)), exact=False):
    return lax.dot_general(
        a, b, (dims, ((), ())), precision=precise if exact else None, preferred_element_type=F32
    )


def exact_dot(a, pick, dims=((1,), (0,))):
    high = a.astype(BF16)
    rest = a - high.astype(F32)
    middle = rest.astype(BF16)
    low = (rest - middle.astype(F32)).astype(BF16)
    rows = a.shape[0]
    parts = jnp.concatenate([high, middle, low], 0)
    found = dot(parts, pick, dims)
    return (found[0:rows] + found[rows : 2 * rows]) + found[2 * rows :]


def iota(shape, dim):
    return lax.broadcasted_iota(jnp.int32, shape, dim)


def call(
    kernel, out_shape, in_specs, out_specs, scratch=(), flops=0, moved=0, vmem=4, aliases=None
):
    return pl.pallas_call(
        kernel,
        out_shape=out_shape,
        input_output_aliases=aliases or {},
        in_specs=in_specs,
        out_specs=out_specs,
        scratch_shapes=list(scratch),
        compiler_params=pltpu.CompilerParams(vmem_limit_bytes=vmem * MIB),
        cost_estimate=pl.CostEstimate(flops=flops, bytes_accessed=moved, transcendentals=0),
    )


VM = pl.BlockSpec(memory_space=pltpu.VMEM)
SM = pl.BlockSpec(memory_space=pltpu.SMEM)
ANY = pl.BlockSpec(memory_space=pl.ANY)
HBM = pl.BlockSpec(memory_space=pltpu.HBM)


def shape(dims, dtype):
    return jax.ShapeDtypeStruct(dims, dtype)


def in_hbm(*arrays):
    return tuple(pltpu.with_memory_space_constraint(a, pltpu.HBM) for a in arrays)


def is_power(n):
    return n & (n - 1) == 0


def pairs(n, step):
    if is_power(n):
        return [(i, i ^ step) for i in range(n)]
    return [(i, (i + step) % n) for i in range(n)]


def distance(n, here, there):
    return here ^ there if is_power(n) else lax.rem(here - there + n, n)


def backward(n, step):
    return step if is_power(n) else (n - step) % n


def start_kernel(
    count,
    pos_hbm,
    moved_hbm,
    disp_hbm,
    weight_ref,
    out_ref,
    tiled_ref,
    shift_ref,
    pos_ref,
    moved_ref,
    disp_ref,
    sems,
):
    loads = [
        pltpu.make_async_copy(src, dst, sems.at[i])
        for i, (src, dst) in enumerate(
            (
                (moved_hbm, moved_ref),
                (disp_hbm, disp_ref),
                (pos_hbm, pos_ref),
            )
        )
    ]
    for load in loads:
        load.start()
    electrons = pos_ref.shape[2]
    copies = LANES // count
    loads[0].wait()
    tiled = jnp.concatenate([moved_ref[:, 0, :]] * copies, 1)
    tiled_ref[...] = tiled
    pick = (iota((electrons, LANES), 0) == tiled[0:1, :]).astype(F32).astype(BF16)
    block = iota((8, LANES), 1) // count
    zeros = jnp.zeros((5, LANES), F32)
    loads[1].wait()
    for update in range(2):
        shift = jnp.concatenate([disp_ref[3 * update : 3 * update + 3, 0, :]] * copies, 1)
        shift_ref[update] = jnp.concatenate([shift, zeros], 0)
    loads[2].wait()
    pos = jnp.concatenate([pos_ref[:, 0, :], jnp.zeros((5, electrons), F32)], 0)
    old = exact_dot(pos, pick)
    disp = shift_ref[0]
    points = old + jnp.where(block % 2 == 1, disp, 0.0)
    first = jnp.where(block == 0, disp, 0.0)
    out_ref[...] = pos + exact_dot(first, pick, ((1,), (1,)))
    out_ref[3:6, 0:LANES] = points[0:3]
    out_ref[6:7, 0:LANES] = tiled[0:1, :].astype(F32)
    out_ref[7:8, 0:LANES] = jnp.full((1, LANES), weight_ref[0], F32)


def rows_of(ref, chunk, depth):
    return ref.at[0, pl.ds(chunk * depth, depth)]


def round_kernel(wanted, inverse_hbm, after_ref, *refs):
    outs = refs[: len(wanted)]
    staged, rounded, in_sem, out_sem = refs[len(wanted) :]
    depth = staged.shape[1]
    loads, stores = [], []
    for slot, chunk in enumerate(wanted):
        load = pltpu.make_async_copy(
            rows_of(inverse_hbm, chunk, depth), staged.at[slot], in_sem.at[slot]
        )
        load.start()
        loads.append(load)
    for slot, out in enumerate(outs):
        loads[slot].wait()
        rounded[slot] = staged[slot].astype(BF16)
        store = pltpu.make_async_copy(rounded.at[slot], out, out_sem.at[slot])
        store.start()
        stores.append(store)
    for store in stores:
        store.wait()


def gate_kernel(*refs):
    token_ref = refs[-1]
    token_ref[...] = jnp.zeros(token_ref.shape, F32)


def relay_kernel(flag_ref, own_a, own_b, got_a, got_b, *refs):
    out_a, out_b, token_ref, staged, in_sem, out_sem = refs[-6:]
    pieces, depth, _ = staged.shape

    @pl.when(flag_ref[0] == 0)
    def _():
        loads, stores = [], []
        for piece in range(pieces):
            own, out = (own_a, out_a) if piece < pieces // 2 else (own_b, out_b)
            rows = pl.ds(piece % (pieces // 2) * depth, depth)
            loads.append(
                pltpu.make_async_copy(own.at[rows], staged.at[piece], in_sem.at[piece])
            )
            stores.append(
                pltpu.make_async_copy(staged.at[piece], out.at[rows], out_sem.at[piece])
            )
        for load in loads:
            load.start()
        for load, store in zip(loads, stores):
            load.wait()
            store.start()
        for store in stores:
            store.wait()

    token_ref[...] = jnp.zeros(token_ref.shape, F32)


def near_kernel(own_a, own_b, after_ref, near_a, near_b, sems):
    copies = [
        pltpu.make_async_copy(own_a, near_a, sems.at[0]),
        pltpu.make_async_copy(own_b, near_b, sems.at[1]),
    ]
    for copy in copies:
        copy.start()
    for copy in copies:
        copy.wait()


def near_relay_kernel(flag_ref, own_a, own_b, got_a, got_b, out_a, out_b, token_ref, sems):
    @pl.when(flag_ref[0] == 0)
    def _():
        copies = [
            pltpu.make_async_copy(own_a, out_a, sems.at[0]),
            pltpu.make_async_copy(own_b, out_b, sems.at[1]),
        ]
        for copy in copies:
            copy.start()
        for copy in copies:
            copy.wait()

    token_ref[...] = jnp.zeros(token_ref.shape, F32)


def points_kernel(count, others, role_ref, *refs):
    own_ref = refs[0]
    received = refs[1 : 1 + others]
    moved_ref, disp_ref, after_ref, points_ref, weight_ref, number_ref = refs[1 + others :]
    role = role_ref[0]
    parent = own_ref[...]
    for step in range(others):
        parent = jnp.where(role == step + 1, received[step][...], parent)
    electrons = parent.shape[1]
    pick = (iota((electrons, LANES), 0) == moved_ref[1:2, :]).astype(F32).astype(BF16)
    block = iota((8, LANES), 1) // count
    old = exact_dot(parent, pick)
    later = old + jnp.where(block % 2 == 1, disp_ref[1], 0.0)
    zeros = jnp.zeros((5, LANES), F32)
    mine = jnp.concatenate([own_ref[3:6, 0:LANES], zeros], 0)
    theirs = jnp.concatenate([parent[3:6, 0:LANES], zeros], 0)
    points = jnp.where(block < 2, mine, jnp.where(block < 4, theirs, later))
    if len(points_ref.shape) == 2:
        points_ref[...] = points
    else:
        points = jnp.concatenate([points, jnp.zeros((ROWS - 8, LANES), F32)], 0)
        points_ref[...] = jnp.broadcast_to(points[None], points_ref.shape)
    weight_ref[...] = parent[7:8, 0:LANES]
    before = parent[6:7, 0:LANES].astype(jnp.int32)
    number_ref[...] = jnp.where(
        block[0:1] == 0, before, jnp.where(block[0:1] == 1, moved_ref[1:2, :], -1)
    )


def derive(coeff_ref, wave_ref, out_ref):
    waves = wave_ref.shape[1]
    width = coeff_ref.shape[1]
    wave = jnp.transpose(jnp.concatenate([wave_ref[...], jnp.zeros((5, waves), F32)], 0))
    out_ref[:, 0:width] = coeff_ref[...]
    cos_part = coeff_ref[0:waves].astype(F32)
    sin_part = coeff_ref[waves:].astype(F32)
    squared = None
    for a in range(3):
        scale = wave[:, a : a + 1]
        where = slice((a + 1) * width, (a + 2) * width)
        out_ref[0:waves, where] = (scale * sin_part).astype(BF16)
        out_ref[waves:, where] = (-scale * cos_part).astype(BF16)
        squared = scale * scale if a == 0 else squared + scale * scale
    where = slice(4 * width, 5 * width)
    out_ref[0:waves, where] = (-squared * cos_part).astype(BF16)
    out_ref[waves:, where] = (-squared * sin_part).astype(BF16)


def prepare_kernel(wanted, coeff_hbm, wave_hbm, inverse_hbm, after_ref, table_ref, *refs):
    outs = refs[: len(wanted)]
    coeff_ref, wave_ref, staged, rounded, small_sem, in_sem, out_sem = refs[len(wanted) :]
    depth = staged.shape[1]
    wave_load = pltpu.make_async_copy(wave_hbm, wave_ref, small_sem.at[0])
    coeff_load = pltpu.make_async_copy(coeff_hbm, coeff_ref, small_sem.at[1])
    wave_load.start()
    coeff_load.start()
    loads, stores = [], []
    for slot, chunk in enumerate(wanted):
        load = pltpu.make_async_copy(
            rows_of(inverse_hbm, chunk, depth), staged.at[slot], in_sem.at[slot]
        )
        load.start()
        loads.append(load)
    for slot, out in enumerate(outs):
        loads[slot].wait()
        rounded[slot] = staged[slot].astype(BF16)
        store = pltpu.make_async_copy(rounded.at[slot], out, out_sem.at[slot])
        store.start()
        stores.append(store)
    wave_load.wait()
    coeff_load.wait()
    derive(coeff_ref, wave_ref, table_ref)
    for store in stores:
        store.wait()


def horner(coefs, u):
    value = coefs[-1] * u + coefs[-2]
    for c in reversed(coefs[:-2]):
        value = value * u + c
    return value


def evaluate_kernel(count, sources, targets, *refs):
    points = refs[:sources]
    wave_ref, table_ref = refs[sources : sources + 2]
    outs = refs[sources + 3 : -4]
    diff, new, gathered, spread = refs[-4:]
    walkers = gathered.shape[0]
    for w in range(walkers):
        gathered[w] = points[w][...] if sources > 1 else points[0][w, 0:8]
    waves = wave_ref.shape[1]
    width = table_ref.shape[1] // 5
    step = math.gcd(waves, LANES)

    def one(w, carry):
        column = jnp.transpose(gathered[w])
        for a in range(3):
            spread[a] = jnp.broadcast_to(column[0 : 6 * count, a : a + 1], (6 * count, step))
        row_d = pl.multiple_of(w * (3 * count), count)
        row_n = pl.multiple_of(w * (2 * count), count)
        for at in range(0, waves, step):
            ks = [wave_ref[a : a + 1, at : at + step] * (0.5 / math.pi) for a in range(3)]
            for pair, diff_at, new_at in ((0, 2, 1), (1, 0, None), (2, 1, 0)):
                rows = slice(2 * pair * count, 2 * (pair + 1) * count)
                turn = spread[0, rows] * ks[0] + spread[1, rows] * ks[1] + spread[2, rows] * ks[2]
                r = turn - jnp.floor(turn + 0.5)
                u = r * r
                s = r * horner(SIN_HALF, u)
                c = horner(COS_HALF, u)
                for value, base in ((1.0 - s * s, 0), (s * c, waves)):
                    where = slice(base + at, base + at + step)
                    kept = value.astype(BF16)
                    wide = kept.astype(F32)
                    change = (wide[count:] - wide[:count]).astype(BF16)
                    diff[pl.ds(row_d + diff_at * count, count), where] = change
                    if new_at is not None:
                        new[pl.ds(row_n + new_at * count, count), where] = kept[count:]
        return carry

    lax.fori_loop(0, walkers, one, 0)
    change = dot(diff[...], table_ref[:, 0:width]).astype(BF16)
    rest = dot(new[...], table_ref[:, width:]).astype(BF16)
    for w in range(walkers):
        out_ref = outs[w] if targets > 1 else outs[0].at[w]
        at = w * 3 * count
        out_ref[0 : 2 * count] = change[at : at + 2 * count]
        out_ref[6 * count : 7 * count] = change[at + 2 * count : at + 3 * count]
        for half, base in ((0, 2 * count), (1, 7 * count)):
            row = (2 * w + half) * count
            for a in range(4):
                out_ref[base + a * count : base + (a + 1) * count] = rest[
                    row : row + count, a * width : (a + 1) * width
                ]


def pair_inverse(a, b, d):
    det = a * d - b * b
    scale = 1.0 / det
    return d * scale, -b * scale, a * scale, det


def sweep(matrix):
    size = matrix.shape[0]
    log = jnp.zeros((1, 1), F32)
    row = iota((size, size), 0)
    lane = iota((size, size), 1)
    place = iota((1, size), 1)
    for k in range(0, size, 4):
        columns = [jnp.broadcast_to(matrix[:, k + j : k + j + 1], (size, size)) for j in range(4)]
        lines = [matrix[k + i : k + i + 1, :] for i in range(4)]
        at = lambda i, j: columns[j][k + i : k + i + 1, :]
        a00, a01, a11, det_a = pair_inverse(at(0, 0), at(0, 1), at(1, 1))
        b00, b01, b10, b11 = at(0, 2), at(0, 3), at(1, 2), at(1, 3)
        t00, t01 = a00 * b00 + a01 * b10, a00 * b01 + a01 * b11
        t10, t11 = a01 * b00 + a11 * b10, a01 * b01 + a11 * b11
        d00 = at(2, 2) - (b00 * t00 + b10 * t10)
        d01 = at(2, 3) - (b00 * t01 + b10 * t11)
        d11 = at(3, 3) - (b01 * t01 + b11 * t11)
        s00, s01, s11, det_s = pair_inverse(d00, d01, d11)
        u00, u01 = -(t00 * s00 + t01 * s01), -(t00 * s01 + t01 * s11)
        u10, u11 = -(t10 * s00 + t11 * s01), -(t10 * s01 + t11 * s11)
        q00, q01 = a00 - (u00 * t00 + u01 * t01), a01 - (u00 * t10 + u01 * t11)
        q11 = a11 - (u10 * t10 + u11 * t11)
        pivot = (
            (q00, q01, u00, u01),
            (q01, q11, u10, u11),
            (u00, u10, s00, s01),
            (u01, u11, s01, s11),
        )
        reduced = matrix
        scaled, edges = [], []
        for i in range(4):
            line = pivot[i][0] * lines[0] + pivot[i][1] * lines[1]
            line = line + (pivot[i][2] * lines[2] + pivot[i][3] * lines[3])
            reduced = reduced - columns[i] * line
            for j in range(4):
                line = jnp.where(place == k + j, -pivot[i][j], line)
            scaled.append(line)
            edge = pivot[i][0] * columns[0] + pivot[i][1] * columns[1]
            edges.append(edge + (pivot[i][2] * columns[2] + pivot[i][3] * columns[3]))
        matrix = reduced
        for i in range(4):
            matrix = jnp.where(lane == k + i, edges[i], matrix)
        for i in range(4):
            matrix = jnp.where(row == k + i, scaled[i], matrix)
        log = log + (jnp.log(det_a[:, 0:1]) + jnp.log(det_s[:, 0:1]))
    return -matrix, log


def ratio_of(products, size):
    eye = jnp.where(iota((size, size), 0) == iota((size, size), 1), 1.0, 0.0)
    ratio = products[0:size, 0:size] + eye
    inverse, log = sweep(dot(ratio, ratio, ((0,), (0,)), exact=True))
    return ratio, inverse, 0.5 * log


def moved_sums(products, ratio, inverse, count):
    size = ratio.shape[0]
    turned = dot(ratio, inverse, exact=True)[size - count :]
    tile = jnp.concatenate([turned] * 4, 0)
    part = products[size : size + 4 * count, 0:size] * tile
    return dot(jnp.ones((8, size), F32), part, ((1,), (1,)), exact=True)[0:1]


def columns_kernel(count, inverse_hbm, moved_ref, after_ref, out_ref, staged, sem):
    chunks, depth, electrons = staged.shape
    loads = []
    for chunk in range(chunks):
        load = pltpu.make_async_copy(
            rows_of(inverse_hbm, chunk, depth), staged.at[chunk], sem.at[chunk]
        )
        load.start()
        loads.append(load)
    block = iota((1, LANES), 1) // count
    number = jnp.where(block == 0, moved_ref[0:1, :], -1)
    pick = (iota((electrons, LANES), 0) == number).astype(F32).astype(BF16)
    for chunk in range(chunks):
        loads[chunk].wait()
        found = dot(staged[chunk].astype(BF16), pick)
        out_ref[chunk * depth : (chunk + 1) * depth] = found.astype(BF16)


def pick_from(number_ref, electrons):
    return (iota((electrons, LANES), 0) == number_ref[...]).astype(F32).astype(BF16)


def chunk_at(plan, role, slot):
    chunk = jnp.int32(plan[0][slot][0])
    for which in range(1, len(plan)):
        chunk = jnp.where(role == which, plan[which][slot][0], chunk)
    return chunk


def load_slots(plan, slots, role, inputs, parent, sem, first=0):
    for slot in slots:
        for which in range(first, len(plan)):
            load = pltpu.make_async_copy(
                inputs[plan[which][slot][1]], parent.at[slot], sem.at[slot]
            )
            pl.when(role == which)(load.start)


def wait_slots(slots, inputs, parent, sem):
    for slot in slots:
        pltpu.make_async_copy(inputs[0], parent.at[slot], sem.at[slot]).wait()


def middle_kernel(count, sources, plan, me_ref, role_ref, number_ref, *refs):
    values = refs[:sources]
    own_columns = refs[sources]
    inputs = refs[sources + 1 : -9]
    drift_ref, lap_ref, later_ref, columns_ref, products_ref, total_ref = refs[-9:-3]
    vals, parent, sem = refs[-3:]
    slots, depth, electrons = parent.shape
    role = role_ref[0]
    load_slots(plan, range(slots), role, inputs, parent, sem)
    rows = later_ref.shape[0]
    if sources > 1:
        width = values[0].shape[1]
        for step in range(sources):
            at = pl.multiple_of((me_ref[0] ^ step) * width, width)
            later_ref[:, pl.ds(at, width)] = values[step][0:rows]
            vals[:, pl.ds(at, width)] = values[step][rows:]
    else:
        pieces, _, width = values[0].shape
        for piece in range(pieces):
            where = slice(piece * width, (piece + 1) * width)
            later_ref[:, where] = values[0][piece, 0:rows]
            vals[:, where] = values[0][piece, rows:]
    pick = pick_from(number_ref, electrons)
    wait_slots(range(slots), inputs, parent, sem)
    own = dot(vals[...], own_columns[...])
    products, total = None, None
    for slot in range(slots):
        columns = dot(parent[slot], pick).astype(BF16)
        columns_ref[slot] = columns
        at = pl.multiple_of(chunk_at(plan, role, slot) * depth, depth)
        part = later_ref[:, pl.ds(at, depth)]
        product = dot(part, columns)
        more = dot(part[0 : 2 * count], parent[slot])
        products = product if slot == 0 else products + product
        total = more if slot == 0 else total + more
    products_ref[...] = products
    total_ref[...] = total
    ratio, inverse, _ = ratio_of(own, count)
    sums = moved_sums(own, ratio, inverse, count)
    for a in range(3):
        drift_ref[a] = sums[:, a * count : (a + 1) * count]
    lap_ref[0] = sums[:, 3 * count : 4 * count]


def finish_kernel(
    count,
    plan,
    role_ref,
    number_ref,
    later_ref,
    weight_ref,
    drift_in,
    lap_in,
    early_ref,
    products_ref,
    total_ref,
    inverse_hbm,
    *refs,
):
    inputs = refs[:-9]
    out_ref, drift_ref, lap_ref, out_weight_ref = refs[-9:-5]
    parent, staged, in_sem, own_sem, out_sem = refs[-5:]
    chunks, depth, electrons = parent.shape
    done = early_ref.shape[0]
    late = range(done, chunks)
    size = 2 * count
    role = role_ref[0]
    own = [
        pltpu.make_async_copy(
            rows_of(inverse_hbm, plan[0][slot][0], depth), staged.at[slot], own_sem.at[slot]
        )
        for slot in range(chunks)
    ]
    load_slots(plan, late, role, inputs, parent, in_sem)
    for load in own[done:] + own[:done]:
        pl.when(role == 0)(load.start)
    load_slots(plan, range(done), role, inputs, parent, in_sem, 1)
    pick = pick_from(number_ref, electrons)
    wait_slots(late, inputs, parent, in_sem)
    columns = [early_ref[slot] for slot in range(done)]
    products = products_ref[...]
    rows = []
    for slot in late:
        columns.append(dot(parent[slot], pick).astype(BF16))
        at = pl.multiple_of(chunk_at(plan, role, slot) * depth, depth)
        rows.append(later_ref[:, pl.ds(at, depth)])
        products = products + dot(rows[-1], columns[-1])
    ratio, inverse, log = ratio_of(products, size)
    total = total_ref[...]
    for slot, part in zip(late, rows):
        total = total + dot(part[0:size], parent[slot])
    small = dot(inverse, ratio, ((1,), (1,)), exact=True)
    high = small.astype(BF16)
    halves = jnp.concatenate([high, (small - high.astype(F32)).astype(BF16)], 1)
    rounded = total.astype(BF16)
    solved = dot(halves, jnp.concatenate([rounded, rounded], 0)).astype(BF16)
    solved = jnp.concatenate([solved, jnp.zeros((LANES - size, electrons), BF16)], 0)
    copies = []
    for slot in list(late) + list(range(done)):
        at = pl.multiple_of(chunk_at(plan, role, slot) * depth, depth)
        copy = pltpu.make_async_copy(
            staged.at[slot], out_ref.at[pl.ds(at, depth)], out_sem.at[slot]
        )
        copies.append((slot, copy))

    def kept(slot):
        own[slot].wait()
        return staged[slot]

    def write(before):
        for slot, copy in copies:
            staged[slot] = before(slot) - dot(columns[slot], solved)
            copy.start()

    def sent(slot):
        if slot < done:
            wait_slots([slot], inputs, parent, in_sem)
        return parent[slot].astype(F32)

    pl.when(role == 0)(lambda: write(kept))
    pl.when(role != 0)(lambda: write(sent))
    sums = moved_sums(products, ratio, inverse, count)
    drift_ref[0:3] = drift_in[...]
    lap_ref[0:1] = lap_in[...]
    for a in range(3):
        drift_ref[3 + a] = sums[:, a * count : (a + 1) * count]
    lap_ref[1] = sums[:, 3 * count : 4 * count]
    out_weight_ref[...] = weight_ref[...] + log
    for _, copy in copies:
        copy.wait()


def per_device(
    n_grp,
    n_orb,
    wavevectors,
    coefficients,
    inverse,
    positions,
    displacements,
    moved,
    donor,
    take,
    log_weight,
):
    electrons = inverse.shape[1]
    count = moved.shape[2]
    plane = coefficients.shape[0]
    local = coefficients.shape[1]
    others = n_grp - 1
    chunks = 4

    apart = distance(n_grp, lax.axis_index("grp"), donor[0])
    role = jnp.where(take[0] == 1, apart, 0).astype(jnp.int32).reshape(1)
    apart = apart.astype(jnp.int32).reshape(1)

    record, tiled, disp = call(
        functools.partial(start_kernel, count),
        (
            shape((8, electrons), F32),
            shape((2, LANES), jnp.int32),
            shape((2, 8, LANES), F32),
        ),
        [HBM, HBM, HBM, SM],
        (VM, VM, VM),
        scratch=[
            pltpu.VMEM((3, 1, electrons), F32),
            pltpu.VMEM((2, 1, count), jnp.int32),
            pltpu.VMEM((6, 1, count), F32),
            pltpu.SemaphoreType.DMA((3,)),
        ],
    )(
        *in_hbm(
            positions.reshape(3, 1, electrons),
            moved,
            displacements.reshape(6, 1, count),
        ),
        log_weight,
    )
    records = [lax.ppermute(record, "grp", pairs(n_grp, s)) for s in range(1, n_grp)]

    depth = electrons // chunks
    kept = shape((depth, electrons), BF16)
    token = shape((8, LANES), F32)
    own = [None] * chunks
    ends = (0, chunks - 1)
    middle = tuple(range(1, chunks - 1))
    own[0], own[-1] = call(
        functools.partial(round_kernel, ends),
        (kept,) * 2,
        [HBM, ANY],
        (ANY,) * 2,
        scratch=[
            pltpu.VMEM((2, depth, electrons), F32),
            pltpu.VMEM((2, depth, electrons), BF16),
            pltpu.SemaphoreType.DMA((2,)),
            pltpu.SemaphoreType.DMA((2,)),
        ],
        moved=3 * electrons * electrons,
        vmem=6,
    )(*in_hbm(inverse), record)
    own[0], own[-1], token_0 = call(
        gate_kernel,
        (kept, kept, token),
        [ANY] * (2 + others),
        (ANY, ANY, VM),
        aliases={0: 0, 1: 1},
        vmem=1,
    )(own[0], own[-1], *records)

    few = is_power(n_orb) and local % LANES == 0
    direct = few and DIRECT_POINTS
    sources = n_orb if direct else 1
    points, weight, number = call(
        functools.partial(points_kernel, count, others),
        (
            shape((8, LANES) if direct else (n_orb, ROWS, LANES), F32),
            shape((1, LANES), F32),
            shape((1, LANES), jnp.int32),
        ),
        [SM] + [VM] * (others + 3) + [ANY],
        (VM, VM, VM),
    )(role, record, *records, tiled, disp, token_0)
    if direct:
        points = [points] + [lax.ppermute(points, "orb", pairs(n_orb, s)) for s in range(1, n_orb)]
    else:
        points = [lax.all_to_all(points, "orb", split_axis=0, concat_axis=0, tiled=True)]

    width = -(-local // LANES) * LANES
    coeff = jnp.pad(coefficients, ((0, 0), (0, width - local))) if width > local else coefficients
    derived, *prepared = call(
        functools.partial(prepare_kernel, middle),
        (shape((plane, 5 * width), BF16),)
        + (pltpu.HBM((depth, electrons), BF16),) * len(middle),
        [HBM, HBM, HBM, ANY],
        (VM,) + (ANY,) * len(middle),
        scratch=[
            pltpu.VMEM((plane, width), BF16),
            pltpu.VMEM(wavevectors.shape, F32),
            pltpu.VMEM((len(middle), depth, electrons), F32),
            pltpu.VMEM((len(middle), depth, electrons), BF16),
            pltpu.SemaphoreType.DMA((2,)),
            pltpu.SemaphoreType.DMA((len(middle),)),
            pltpu.SemaphoreType.DMA((len(middle),)),
        ],
        flops=8 * plane * width,
        moved=3 * electrons * electrons + 10 * plane * width,
        vmem=12,
    )(*in_hbm(coeff, wavevectors, inverse), weight)
    for chunk, ready in zip(middle, prepared):
        own[chunk] = ready

    arrays = list(own)
    if n_grp == 4:
        send_x = lambda block: lax.ppermute(block, "grp", pairs(n_grp, 1))
        send_y = lambda block: lax.ppermute(block, "grp", pairs(n_grp, 2))

        def relay(mine, got, first):
            return call(
                relay_kernel,
                (kept, kept, token),
                [SM] + [ANY] * (4 + len(first)),
                (ANY, ANY, VM),
                scratch=[
                    pltpu.VMEM((4, depth // 2, electrons), BF16),
                    pltpu.SemaphoreType.DMA((4,)),
                    pltpu.SemaphoreType.DMA((4,)),
                ],
                aliases={3: 0, 4: 1},
                vmem=2,
            )(apart, *in_hbm(*mine), *got, *first)

        x1, y1 = send_x(own[0]), send_y(own[3])
        y1, x1, token_1 = relay((own[1], own[2]), (y1, x1), (derived, *points))
        x2, y2 = send_x(y1), send_y(x1)
    else:
        token_1 = token_2 = jnp.zeros((8, LANES), F32)
        plan = [tuple((chunk, chunk) for chunk in range(chunks))]
        for step in range(1, n_grp):
            plan.append(tuple((chunk, len(arrays) + chunk) for chunk in range(chunks)))
            arrays += [lax.ppermute(block, "grp", pairs(n_grp, step)) for block in own]
        settled = len(arrays)

    height = 11 * count
    spread = few and DIRECT_VALUES
    targets = n_orb if spread else 1
    block = n_orb if few else math.gcd(n_orb, 8)
    whole = lambda array: pl.BlockSpec(array.shape, lambda i: (0,) * array.ndim)
    if direct:
        point_specs = [whole(p) for p in points]
    else:
        point_specs = [pl.BlockSpec((block, ROWS, LANES), lambda i: (i, 0, 0))]
    if spread:
        out_shapes = (shape((height, width), BF16),) * n_orb
        out_specs = tuple(whole(o) for o in out_shapes)
    else:
        out_shapes = (shape((n_orb, height, width), BF16),)
        out_specs = (pl.BlockSpec((block, height, width), lambda i: (i, 0, 0)),)
    values = pl.pallas_call(
        functools.partial(evaluate_kernel, count, sources, targets),
        grid=(n_orb // block,),
        out_shape=out_shapes,
        in_specs=point_specs + [whole(wavevectors), whole(derived), ANY],
        out_specs=out_specs,
        scratch_shapes=[
            pltpu.VMEM((block * 3 * count, plane), BF16),
            pltpu.VMEM((block * 2 * count, plane), BF16),
            pltpu.VMEM((block, 8, LANES), F32),
            pltpu.VMEM((3, 6 * count, LANES), F32),
        ],
        compiler_params=pltpu.CompilerParams(vmem_limit_bytes=8 * MIB),
        cost_estimate=pl.CostEstimate(
            flops=2 * n_orb * count * plane * width * 11,
            bytes_accessed=12 * plane * width,
            transcendentals=0,
        ),
    )(*points, wavevectors, derived, token_1)
    computed = values[0]
    if spread:
        values = [values[0]] + [
            lax.ppermute(values[s], "orb", pairs(n_orb, s)) for s in range(1, n_orb)
        ]
    else:
        values = values[0][:, :, :local]
        values = lax.all_to_all(values, "orb", split_axis=0, concat_axis=0, tiled=True)
        if width > local:
            values = values.transpose(1, 0, 2).reshape(1, height, electrons)
        values = [values]

    if n_grp == 4:
        near = call(
            near_kernel,
            (kept, kept),
            [HBM, HBM, ANY],
            (VM, VM),
            scratch=[pltpu.SemaphoreType.DMA((2,))],
            vmem=3,
        )(*in_hbm(own[2], own[1]), computed)
        y2, x2, token_2 = call(
            near_relay_kernel,
            (kept, kept, token),
            [SM, VM, VM, ANY, ANY],
            (ANY, ANY, VM),
            scratch=[pltpu.SemaphoreType.DMA((2,))],
            aliases={3: 0, 4: 1},
            vmem=3,
        )(apart, *near, y2, x2)
        x3, y3 = send_x(y2), send_y(x2)
        arrays = own + [x1, x2, y1, y2, x3, y3]
        a1, a2, b1, b2, a3, b3 = range(chunks, chunks + 6)
        first, second, third, fourth = range(chunks)
        plan = [
            tuple((chunk, chunk) for chunk in range(chunks)),
            ((first, a1), (second, a2), (third, a3), (fourth, b3)),
            ((fourth, b1), (third, b2), (first, a3), (second, b3)),
            ((fourth, a2), (first, b2), (third, a3), (second, b3)),
        ]
        settled = chunks + 4

    columns = call(
        functools.partial(columns_kernel, count),
        shape((electrons, LANES), BF16),
        [HBM, VM, ANY],
        VM,
        scratch=[
            pltpu.VMEM((chunks, depth, electrons), F32),
            pltpu.SemaphoreType.DMA((chunks,)),
        ],
        flops=2 * electrons * electrons * LANES,
        moved=4 * electrons * electrons,
        vmem=8,
    )(*in_hbm(inverse), tiled, token_2)

    here = lax.axis_index("orb").astype(jnp.int32).reshape(1)
    early = 2
    work = 2 * electrons * 2 * count
    drift, laplacian, later, early_columns, products, total = call(
        functools.partial(middle_kernel, count, targets, plan),
        (
            shape((3, 1, count), F32),
            shape((1, 1, count), F32),
            shape((6 * count, electrons), BF16),
            shape((early, depth, LANES), BF16),
            shape((6 * count, LANES), F32),
            shape((2 * count, electrons), F32),
        ),
        [SM, SM, VM] + [VM] * (targets + 1) + [ANY] * settled,
        (VM,) * 6,
        scratch=[
            pltpu.VMEM((5 * count, electrons), BF16),
            pltpu.VMEM((early, depth, electrons), BF16),
            pltpu.SemaphoreType.DMA((early,)),
        ],
        flops=early * depth * work,
        moved=2 * early * depth * electrons + 44 * count * electrons,
        vmem=8,
    )(here, role, number, *values, columns, *in_hbm(*own), *arrays[chunks:settled])

    updated, drift, laplacian, new_weight = call(
        functools.partial(finish_kernel, count, plan),
        (
            shape((electrons, electrons), F32),
            shape((6, 1, count), F32),
            shape((2, 1, count), F32),
            shape((1, LANES), F32),
        ),
        [SM] + [VM] * 8 + [HBM] + [ANY] * len(arrays),
        (HBM, VM, VM, VM),
        scratch=[
            pltpu.VMEM((chunks, depth, electrons), BF16),
            pltpu.VMEM((chunks, depth, electrons), F32),
            pltpu.SemaphoreType.DMA((chunks,)),
            pltpu.SemaphoreType.DMA((chunks,)),
            pltpu.SemaphoreType.DMA((chunks,)),
        ],
        flops=2 * electrons * work,
        moved=6 * electrons * electrons,
        vmem=12,
    )(
        role,
        number,
        later,
        weight,
        drift,
        laplacian,
        early_columns,
        products,
        total,
        *in_hbm(inverse, *own),
        *arrays[chunks:],
    )

    return updated[None], drift.reshape(2, 1, 3, count), laplacian, new_weight[0, :1]


def solution(mesh):
    split = ("grp", "orb")
    return jax.shard_map(
        functools.partial(per_device, mesh.shape["grp"], mesh.shape["orb"]),
        mesh=mesh,
        in_specs=(
            P(),
            P(None, "orb"),
            P(split, None, None),
            P(split, None, None),
            P(None, split, None, None),
            P(None, split, None),
            P("orb"),
            P(split),
            P(split),
        ),
        out_specs=(
            P(split, None, None),
            P(None, split, None, None),
            P(None, split, None),
            P(split),
        ),
        check_vma=False,
    )
```

```python
import functools
import math

import jax
import jax.numpy as jnp
from jax import lax
from jax.experimental import pallas as pl
from jax.experimental.pallas import tpu as pltpu
from jax.sharding import PartitionSpec as P

F32 = jnp.float32
BF16 = jnp.bfloat16
LANES = 128
ROWS = 16
DIRECT_POINTS = False
DIRECT_VALUES = False
MIB = 1024 * 1024
precise = lax.Precision.HIGHEST

WHOLE = 1.5 * 2.0**23

SIN_HALF = (4.4428679, -7.30744342, 3.59478808, -0.78437403)
COS_HALF = (1.4142135, -6.97885099, 5.73946117, -1.88356299, 0.31069819)


def dot(a, b, dims=((1,), (0,)), exact=False):
    return lax.dot_general(
        a, b, (dims, ((), ())), precision=precise if exact else None, preferred_element_type=F32
    )


def exact_dot(a, pick, dims=((1,), (0,))):
    high = a.astype(BF16)
    rest = a - high.astype(F32)
    middle = rest.astype(BF16)
    low = (rest - middle.astype(F32)).astype(BF16)
    rows = a.shape[0]
    parts = jnp.concatenate([high, middle, low], 0)
    found = dot(parts, pick, dims)
    return (found[0:rows] + found[rows : 2 * rows]) + found[2 * rows :]


def iota(shape, dim):
    return lax.broadcasted_iota(jnp.int32, shape, dim)


def call(
    kernel, out_shape, in_specs, out_specs, scratch=(), flops=0, moved=0, vmem=4, aliases=None
):
    return pl.pallas_call(
        kernel,
        out_shape=out_shape,
        input_output_aliases=aliases or {},
        in_specs=in_specs,
        out_specs=out_specs,
        scratch_shapes=list(scratch),
        compiler_params=pltpu.CompilerParams(vmem_limit_bytes=vmem * MIB),
        cost_estimate=pl.CostEstimate(flops=flops, bytes_accessed=moved, transcendentals=0),
    )


VM = pl.BlockSpec(memory_space=pltpu.VMEM)
SM = pl.BlockSpec(memory_space=pltpu.SMEM)
ANY = pl.BlockSpec(memory_space=pl.ANY)
HBM = pl.BlockSpec(memory_space=pltpu.HBM)


def shape(dims, dtype):
    return jax.ShapeDtypeStruct(dims, dtype)


def in_hbm(*arrays):
    return tuple(pltpu.with_memory_space_constraint(a, pltpu.HBM) for a in arrays)


def is_power(n):
    return n & (n - 1) == 0


def pairs(n, step):
    if is_power(n):
        return [(i, i ^ step) for i in range(n)]
    return [(i, (i + step) % n) for i in range(n)]


def distance(n, here, there):
    return here ^ there if is_power(n) else lax.rem(here - there + n, n)


def backward(n, step):
    return step if is_power(n) else (n - step) % n


def start_kernel(
    count,
    pos_hbm,
    moved_hbm,
    disp_hbm,
    weight_ref,
    out_ref,
    tiled_ref,
    shift_ref,
    pos_ref,
    moved_ref,
    disp_ref,
    sems,
):
    loads = [
        pltpu.make_async_copy(src, dst, sems.at[i])
        for i, (src, dst) in enumerate(
            (
                (moved_hbm, moved_ref),
                (disp_hbm, disp_ref),
                (pos_hbm, pos_ref),
            )
        )
    ]
    for load in loads:
        load.start()
    electrons = pos_ref.shape[2]
    copies = LANES // count
    loads[0].wait()
    tiled = jnp.concatenate([moved_ref[:, 0, :]] * copies, 1)
    tiled_ref[...] = tiled
    pick = (iota((electrons, LANES), 0) == tiled[0:1, :]).astype(F32).astype(BF16)
    block = iota((8, LANES), 1) // count
    zeros = jnp.zeros((5, LANES), F32)
    loads[1].wait()
    for update in range(2):
        shift = jnp.concatenate([disp_ref[3 * update : 3 * update + 3, 0, :]] * copies, 1)
        shift_ref[update] = jnp.concatenate([shift, zeros], 0)
    loads[2].wait()
    pos = jnp.concatenate([pos_ref[:, 0, :], jnp.zeros((5, electrons), F32)], 0)
    old = exact_dot(pos, pick)
    disp = shift_ref[0]
    points = old + jnp.where(block % 2 == 1, disp, 0.0)
    first = jnp.where(block == 0, disp, 0.0)
    out_ref[...] = pos + exact_dot(first, pick, ((1,), (1,)))
    out_ref[3:6, 0:LANES] = points[0:3]
    out_ref[6:7, 0:LANES] = tiled[0:1, :].astype(F32)
    out_ref[7:8, 0:LANES] = jnp.full((1, LANES), weight_ref[0], F32)


def rows_of(ref, chunk, depth):
    return ref.at[0, pl.ds(chunk * depth, depth)]


def round_kernel(wanted, inverse_hbm, after_ref, *refs):
    outs = refs[: len(wanted)]
    staged, rounded, in_sem, out_sem = refs[len(wanted) :]
    depth = staged.shape[1]
    loads, stores = [], []
    for slot, chunk in enumerate(wanted):
        load = pltpu.make_async_copy(
            rows_of(inverse_hbm, chunk, depth), staged.at[slot], in_sem.at[slot]
        )
        load.start()
        loads.append(load)
    for slot, out in enumerate(outs):
        loads[slot].wait()
        rounded[slot] = staged[slot].astype(BF16)
        store = pltpu.make_async_copy(rounded.at[slot], out, out_sem.at[slot])
        store.start()
        stores.append(store)
    for store in stores:
        store.wait()


def gate_kernel(*refs):
    token_ref = refs[-1]
    token_ref[...] = jnp.zeros(token_ref.shape, F32)


def relay_kernel(flag_ref, own_a, own_b, got_a, got_b, *refs):
    out_a, out_b, token_ref, staged, in_sem, out_sem = refs[-6:]
    pieces, depth, _ = staged.shape

    @pl.when(flag_ref[0] == 0)
    def _():
        loads, stores = [], []
        for piece in range(pieces):
            own, out = (own_a, out_a) if piece < pieces // 2 else (own_b, out_b)
            rows = pl.ds(piece % (pieces // 2) * depth, depth)
            loads.append(
                pltpu.make_async_copy(own.at[rows], staged.at[piece], in_sem.at[piece])
            )
            stores.append(
                pltpu.make_async_copy(staged.at[piece], out.at[rows], out_sem.at[piece])
            )
        for load in loads:
            load.start()
        for load, store in zip(loads, stores):
            load.wait()
            store.start()
        for store in stores:
            store.wait()

    token_ref[...] = jnp.zeros(token_ref.shape, F32)


def near_kernel(own_a, own_b, after_ref, near_a, near_b, sems):
    copies = [
        pltpu.make_async_copy(own_a, near_a, sems.at[0]),
        pltpu.make_async_copy(own_b, near_b, sems.at[1]),
    ]
    for copy in copies:
        copy.start()
    for copy in copies:
        copy.wait()


def near_relay_kernel(flag_ref, own_a, own_b, got_a, got_b, out_a, out_b, token_ref, sems):
    @pl.when(flag_ref[0] == 0)
    def _():
        copies = [
            pltpu.make_async_copy(own_a, out_a, sems.at[0]),
            pltpu.make_async_copy(own_b, out_b, sems.at[1]),
        ]
        for copy in copies:
            copy.start()
        for copy in copies:
            copy.wait()

    token_ref[...] = jnp.zeros(token_ref.shape, F32)


def points_kernel(count, others, role_ref, *refs):
    own_ref = refs[0]
    received = refs[1 : 1 + others]
    moved_ref, disp_ref, after_ref, points_ref, weight_ref, number_ref = refs[1 + others :]
    role = role_ref[0]
    parent = own_ref[...]
    for step in range(others):
        parent = jnp.where(role == step + 1, received[step][...], parent)
    electrons = parent.shape[1]
    pick = (iota((electrons, LANES), 0) == moved_ref[1:2, :]).astype(F32).astype(BF16)
    block = iota((8, LANES), 1) // count
    old = exact_dot(parent, pick)
    later = old + jnp.where(block % 2 == 1, disp_ref[1], 0.0)
    zeros = jnp.zeros((5, LANES), F32)
    mine = jnp.concatenate([own_ref[3:6, 0:LANES], zeros], 0)
    theirs = jnp.concatenate([parent[3:6, 0:LANES], zeros], 0)
    points = jnp.where(block < 2, mine, jnp.where(block < 4, theirs, later))
    if len(points_ref.shape) == 2:
        points_ref[...] = points
    else:
        points = jnp.concatenate([points, jnp.zeros((ROWS - 8, LANES), F32)], 0)
        points_ref[...] = jnp.broadcast_to(points[None], points_ref.shape)
    weight_ref[...] = parent[7:8, 0:LANES]
    before = parent[6:7, 0:LANES].astype(jnp.int32)
    number_ref[...] = jnp.where(
        block[0:1] == 0, before, jnp.where(block[0:1] == 1, moved_ref[1:2, :], -1)
    )


def derive(coeff_ref, wave_ref, out_ref):
    waves = wave_ref.shape[1]
    width = coeff_ref.shape[1]
    wave = jnp.transpose(jnp.concatenate([wave_ref[...], jnp.zeros((5, waves), F32)], 0))
    out_ref[:, 0:width] = coeff_ref[...]
    cos_part = coeff_ref[0:waves].astype(F32)
    sin_part = coeff_ref[waves:].astype(F32)
    squared = None
    for a in range(3):
        scale = wave[:, a : a + 1]
        where = slice((a + 1) * width, (a + 2) * width)
        out_ref[0:waves, where] = (scale * sin_part).astype(BF16)
        out_ref[waves:, where] = (-scale * cos_part).astype(BF16)
        squared = scale * scale if a == 0 else squared + scale * scale
    where = slice(4 * width, 5 * width)
    out_ref[0:waves, where] = (-squared * cos_part).astype(BF16)
    out_ref[waves:, where] = (-squared * sin_part).astype(BF16)


def prepare_kernel(wanted, coeff_hbm, wave_hbm, inverse_hbm, after_ref, table_ref, *refs):
    outs = refs[: len(wanted)]
    coeff_ref, wave_ref, staged, rounded, small_sem, in_sem, out_sem = refs[len(wanted) :]
    depth = staged.shape[1]
    wave_load = pltpu.make_async_copy(wave_hbm, wave_ref, small_sem.at[0])
    coeff_load = pltpu.make_async_copy(coeff_hbm, coeff_ref, small_sem.at[1])
    wave_load.start()
    coeff_load.start()
    loads, stores = [], []
    for slot, chunk in enumerate(wanted):
        load = pltpu.make_async_copy(
            rows_of(inverse_hbm, chunk, depth), staged.at[slot], in_sem.at[slot]
        )
        load.start()
        loads.append(load)
    for slot, out in enumerate(outs):
        loads[slot].wait()
        rounded[slot] = staged[slot].astype(BF16)
        store = pltpu.make_async_copy(rounded.at[slot], out, out_sem.at[slot])
        store.start()
        stores.append(store)
    wave_load.wait()
    coeff_load.wait()
    derive(coeff_ref, wave_ref, table_ref)
    for store in stores:
        store.wait()


def horner(coefs, u):
    value = coefs[-1] * u + coefs[-2]
    for c in reversed(coefs[:-2]):
        value = value * u + c
    return value


def evaluate_kernel(count, sources, targets, *refs):
    points = refs[:sources]
    wave_ref, table_ref = refs[sources : sources + 2]
    outs = refs[sources + 3 : -4]
    diff, new, gathered, spread = refs[-4:]
    walkers = gathered.shape[0]
    for w in range(walkers):
        gathered[w] = points[w][...] if sources > 1 else points[0][w, 0:8]
    waves = wave_ref.shape[1]
    width = table_ref.shape[1] // 5
    step = math.gcd(waves, LANES)

    def one(w, carry):
        column = jnp.transpose(gathered[w])
        for a in range(3):
            spread[a] = jnp.broadcast_to(column[0 : 6 * count, a : a + 1], (6 * count, step))
        row_d = pl.multiple_of(w * (3 * count), count)
        row_n = pl.multiple_of(w * (2 * count), count)
        for at in range(0, waves, step):
            ks = [wave_ref[a : a + 1, at : at + step] * (0.5 / math.pi) for a in range(3)]
            for pair, diff_at, new_at in ((0, 2, 1), (1, 0, None), (2, 1, 0)):
                rows = slice(2 * pair * count, 2 * (pair + 1) * count)
                turn = spread[0, rows] * ks[0] + spread[1, rows] * ks[1] + spread[2, rows] * ks[2]
                r = turn - ((turn + WHOLE) - WHOLE)
                u = r * r
                s = r * horner(SIN_HALF, u)
                c = horner(COS_HALF, u)
                for value, base in ((1.0 - s * s, 0), (s * c, waves)):
                    where = slice(base + at, base + at + step)
                    kept = value.astype(BF16)
                    wide = kept.astype(F32)
                    change = (wide[count:] - wide[:count]).astype(BF16)
                    diff[pl.ds(row_d + diff_at * count, count), where] = change
                    if new_at is not None:
                        new[pl.ds(row_n + new_at * count, count), where] = kept[count:]
        return carry

    lax.fori_loop(0, walkers, one, 0)
    change = dot(diff[...], table_ref[:, 0:width]).astype(BF16)
    rest = dot(new[...], table_ref[:, width:]).astype(BF16)
    for w in range(walkers):
        out_ref = outs[w] if targets > 1 else outs[0].at[w]
        at = w * 3 * count
        out_ref[0 : 2 * count] = change[at : at + 2 * count]
        out_ref[6 * count : 7 * count] = change[at + 2 * count : at + 3 * count]
        for half, base in ((0, 2 * count), (1, 7 * count)):
            row = (2 * w + half) * count
            for a in range(4):
                out_ref[base + a * count : base + (a + 1) * count] = rest[
                    row : row + count, a * width : (a + 1) * width
                ]


def pair_inverse(a, b, d):
    det = a * d - b * b
    scale = 1.0 / det
    return d * scale, -b * scale, a * scale, det


def sweep(matrix):
    size = matrix.shape[0]
    log = jnp.zeros((1, 1), F32)
    row = iota((size, size), 0)
    lane = iota((size, size), 1)
    place = iota((1, size), 1)
    for k in range(0, size, 4):
        columns = [jnp.broadcast_to(matrix[:, k + j : k + j + 1], (size, size)) for j in range(4)]
        lines = [matrix[k + i : k + i + 1, :] for i in range(4)]
        at = lambda i, j: columns[j][k + i : k + i + 1, :]
        a00, a01, a11, det_a = pair_inverse(at(0, 0), at(0, 1), at(1, 1))
        b00, b01, b10, b11 = at(0, 2), at(0, 3), at(1, 2), at(1, 3)
        t00, t01 = a00 * b00 + a01 * b10, a00 * b01 + a01 * b11
        t10, t11 = a01 * b00 + a11 * b10, a01 * b01 + a11 * b11
        d00 = at(2, 2) - (b00 * t00 + b10 * t10)
        d01 = at(2, 3) - (b00 * t01 + b10 * t11)
        d11 = at(3, 3) - (b01 * t01 + b11 * t11)
        s00, s01, s11, det_s = pair_inverse(d00, d01, d11)
        u00, u01 = -(t00 * s00 + t01 * s01), -(t00 * s01 + t01 * s11)
        u10, u11 = -(t10 * s00 + t11 * s01), -(t10 * s01 + t11 * s11)
        q00, q01 = a00 - (u00 * t00 + u01 * t01), a01 - (u00 * t10 + u01 * t11)
        q11 = a11 - (u10 * t10 + u11 * t11)
        pivot = (
            (q00, q01, u00, u01),
            (q01, q11, u10, u11),
            (u00, u10, s00, s01),
            (u01, u11, s01, s11),
        )
        reduced = matrix
        scaled, edges = [], []
        for i in range(4):
            line = pivot[i][0] * lines[0] + pivot[i][1] * lines[1]
            line = line + (pivot[i][2] * lines[2] + pivot[i][3] * lines[3])
            reduced = reduced - columns[i] * line
            for j in range(4):
                line = jnp.where(place == k + j, -pivot[i][j], line)
            scaled.append(line)
            edge = pivot[i][0] * columns[0] + pivot[i][1] * columns[1]
            edges.append(edge + (pivot[i][2] * columns[2] + pivot[i][3] * columns[3]))
        matrix = reduced
        for i in range(4):
            matrix = jnp.where(lane == k + i, edges[i], matrix)
        for i in range(4):
            matrix = jnp.where(row == k + i, scaled[i], matrix)
        log = log + (jnp.log(det_a[:, 0:1]) + jnp.log(det_s[:, 0:1]))
    return -matrix, log


def ratio_of(products, size):
    eye = jnp.where(iota((size, size), 0) == iota((size, size), 1), 1.0, 0.0)
    ratio = products[0:size, 0:size] + eye
    inverse, log = sweep(dot(ratio, ratio, ((0,), (0,)), exact=True))
    return ratio, inverse, 0.5 * log


def moved_sums(products, ratio, inverse, count):
    size = ratio.shape[0]
    turned = dot(ratio, inverse, exact=True)[size - count :]
    tile = jnp.concatenate([turned] * 4, 0)
    part = products[size : size + 4 * count, 0:size] * tile
    return dot(jnp.ones((8, size), F32), part, ((1,), (1,)), exact=True)[0:1]


def columns_kernel(count, inverse_hbm, moved_ref, after_ref, out_ref, staged, sem):
    chunks, depth, electrons = staged.shape
    loads = []
    for chunk in range(chunks):
        load = pltpu.make_async_copy(
            rows_of(inverse_hbm, chunk, depth), staged.at[chunk], sem.at[chunk]
        )
        load.start()
        loads.append(load)
    block = iota((1, LANES), 1) // count
    number = jnp.where(block == 0, moved_ref[0:1, :], -1)
    pick = (iota((electrons, LANES), 0) == number).astype(F32).astype(BF16)
    for chunk in range(chunks):
        loads[chunk].wait()
        found = dot(staged[chunk].astype(BF16), pick)
        out_ref[chunk * depth : (chunk + 1) * depth] = found.astype(BF16)


def pick_from(number_ref, electrons):
    return (iota((electrons, LANES), 0) == number_ref[...]).astype(F32).astype(BF16)


def chunk_at(plan, role, slot):
    chunk = jnp.int32(plan[0][slot][0])
    for which in range(1, len(plan)):
        chunk = jnp.where(role == which, plan[which][slot][0], chunk)
    return chunk


def load_slots(plan, slots, role, inputs, parent, sem):
    for slot in slots:
        for which in range(len(plan)):
            load = pltpu.make_async_copy(
                inputs[plan[which][slot][1]], parent.at[slot], sem.at[slot]
            )
            pl.when(role == which)(load.start)


def wait_slots(slots, inputs, parent, sem):
    for slot in slots:
        pltpu.make_async_copy(inputs[0], parent.at[slot], sem.at[slot]).wait()


def middle_kernel(count, sources, plan, me_ref, role_ref, number_ref, inverse_hbm, *refs):
    values = refs[:sources]
    own_columns = refs[sources]
    inputs = refs[sources + 1 : -11]
    drift_ref, lap_ref, later_ref, columns_ref, products_ref, total_ref, held_ref = refs[-11:-4]
    vals, parent, sem, own_sem = refs[-4:]
    slots, depth, electrons = parent.shape
    role = role_ref[0]
    load_slots(plan, range(slots), role, inputs, parent, sem)
    wide = [
        pltpu.make_async_copy(
            rows_of(inverse_hbm, plan[0][slot][0], depth), held_ref.at[slot], own_sem.at[slot]
        )
        for slot in range(slots)
    ]
    for load in wide:
        pl.when(role == 0)(load.start)
    rows = later_ref.shape[0]
    if sources > 1:
        width = values[0].shape[1]
        for step in range(sources):
            at = pl.multiple_of((me_ref[0] ^ step) * width, width)
            later_ref[:, pl.ds(at, width)] = values[step][0:rows]
            vals[:, pl.ds(at, width)] = values[step][rows:]
    else:
        pieces, _, width = values[0].shape
        for piece in range(pieces):
            where = slice(piece * width, (piece + 1) * width)
            later_ref[:, where] = values[0][piece, 0:rows]
            vals[:, where] = values[0][piece, rows:]
    pick = pick_from(number_ref, electrons)
    wait_slots(range(slots), inputs, parent, sem)
    own = dot(vals[...], own_columns[...])
    products, total = None, None
    for slot in range(slots):
        columns = dot(parent[slot], pick).astype(BF16)
        columns_ref[slot] = columns
        at = pl.multiple_of(chunk_at(plan, role, slot) * depth, depth)
        part = later_ref[:, pl.ds(at, depth)]
        product = dot(part, columns)
        more = dot(part[0 : 2 * count], parent[slot])
        products = product if slot == 0 else products + product
        total = more if slot == 0 else total + more
    products_ref[...] = products
    total_ref[...] = total

    @pl.when(role == 0)
    def _():
        for load in wide:
            load.wait()

    @pl.when(role != 0)
    def _():
        for slot in range(slots):
            held_ref[slot] = parent[slot].astype(F32)

    ratio, inverse, _ = ratio_of(own, count)
    sums = moved_sums(own, ratio, inverse, count)
    for a in range(3):
        drift_ref[a] = sums[:, a * count : (a + 1) * count]
    lap_ref[0] = sums[:, 3 * count : 4 * count]


def finish_kernel(
    count,
    plan,
    role_ref,
    number_ref,
    later_ref,
    weight_ref,
    drift_in,
    lap_in,
    early_ref,
    products_ref,
    total_ref,
    held_ref,
    inverse_hbm,
    *refs,
):
    inputs = refs[:-9]
    out_ref, drift_ref, lap_ref, out_weight_ref = refs[-9:-5]
    parent, staged, in_sem, own_sem, out_sem = refs[-5:]
    chunks, depth, electrons = parent.shape
    done = early_ref.shape[0]
    late = range(done, chunks)
    size = 2 * count
    role = role_ref[0]
    own = [
        pltpu.make_async_copy(
            rows_of(inverse_hbm, plan[0][slot][0], depth), staged.at[slot], own_sem.at[slot]
        )
        for slot in range(chunks)
    ]
    load_slots(plan, late, role, inputs, parent, in_sem)
    for slot in late:
        pl.when(role == 0)(own[slot].start)
    pick = pick_from(number_ref, electrons)
    wait_slots(late, inputs, parent, in_sem)
    columns = [early_ref[slot] for slot in range(done)]
    products = products_ref[...]
    rows = []
    for slot in late:
        columns.append(dot(parent[slot], pick).astype(BF16))
        at = pl.multiple_of(chunk_at(plan, role, slot) * depth, depth)
        rows.append(later_ref[:, pl.ds(at, depth)])
        products = products + dot(rows[-1], columns[-1])
    ratio, inverse, log = ratio_of(products, size)
    total = total_ref[...]
    for slot, part in zip(late, rows):
        total = total + dot(part[0:size], parent[slot])
    small = dot(inverse, ratio, ((1,), (1,)), exact=True)
    high = small.astype(BF16)
    halves = jnp.concatenate([high, (small - high.astype(F32)).astype(BF16)], 1)
    rounded = total.astype(BF16)
    solved = dot(halves, jnp.concatenate([rounded, rounded], 0)).astype(BF16)
    solved = jnp.concatenate([solved, jnp.zeros((LANES - size, electrons), BF16)], 0)
    copies = []
    for slot in range(chunks):
        at = pl.multiple_of(chunk_at(plan, role, slot) * depth, depth)
        copies.append(
            pltpu.make_async_copy(
                staged.at[slot], out_ref.at[pl.ds(at, depth)], out_sem.at[slot]
            )
        )

    def write(slots, before):
        for slot in slots:
            staged[slot] = before(slot) - dot(columns[slot], solved)
            copies[slot].start()

    def kept(slot):
        own[slot].wait()
        return staged[slot]

    write(range(done), lambda slot: held_ref[slot])
    pl.when(role == 0)(lambda: write(late, kept))
    pl.when(role != 0)(lambda: write(late, lambda slot: parent[slot].astype(F32)))
    sums = moved_sums(products, ratio, inverse, count)
    drift_ref[0:3] = drift_in[...]
    lap_ref[0:1] = lap_in[...]
    for a in range(3):
        drift_ref[3 + a] = sums[:, a * count : (a + 1) * count]
    lap_ref[1] = sums[:, 3 * count : 4 * count]
    out_weight_ref[...] = weight_ref[...] + log
    for copy in copies:
        copy.wait()


def per_device(
    n_grp,
    n_orb,
    wavevectors,
    coefficients,
    inverse,
    positions,
    displacements,
    moved,
    donor,
    take,
    log_weight,
):
    electrons = inverse.shape[1]
    count = moved.shape[2]
    plane = coefficients.shape[0]
    local = coefficients.shape[1]
    others = n_grp - 1
    chunks = 4

    apart = distance(n_grp, lax.axis_index("grp"), donor[0])
    role = jnp.where(take[0] == 1, apart, 0).astype(jnp.int32).reshape(1)
    apart = apart.astype(jnp.int32).reshape(1)

    record, tiled, disp = call(
        functools.partial(start_kernel, count),
        (
            shape((8, electrons), F32),
            shape((2, LANES), jnp.int32),
            shape((2, 8, LANES), F32),
        ),
        [HBM, HBM, HBM, SM],
        (VM, VM, VM),
        scratch=[
            pltpu.VMEM((3, 1, electrons), F32),
            pltpu.VMEM((2, 1, count), jnp.int32),
            pltpu.VMEM((6, 1, count), F32),
            pltpu.SemaphoreType.DMA((3,)),
        ],
    )(
        *in_hbm(
            positions.reshape(3, 1, electrons),
            moved,
            displacements.reshape(6, 1, count),
        ),
        log_weight,
    )
    records = [lax.ppermute(record, "grp", pairs(n_grp, s)) for s in range(1, n_grp)]

    depth = electrons // chunks
    kept = shape((depth, electrons), BF16)
    token = shape((8, LANES), F32)
    own = [None] * chunks
    ends = (0, chunks - 1)
    middle = tuple(range(1, chunks - 1))
    own[0], own[-1] = call(
        functools.partial(round_kernel, ends),
        (kept,) * 2,
        [HBM, ANY],
        (ANY,) * 2,
        scratch=[
            pltpu.VMEM((2, depth, electrons), F32),
            pltpu.VMEM((2, depth, electrons), BF16),
            pltpu.SemaphoreType.DMA((2,)),
            pltpu.SemaphoreType.DMA((2,)),
        ],
        moved=3 * electrons * electrons,
        vmem=6,
    )(*in_hbm(inverse), record)
    own[0], own[-1], token_0 = call(
        gate_kernel,
        (kept, kept, token),
        [ANY] * (2 + others),
        (ANY, ANY, VM),
        aliases={0: 0, 1: 1},
        vmem=1,
    )(own[0], own[-1], *records)

    few = is_power(n_orb) and local % LANES == 0
    direct = few and DIRECT_POINTS
    sources = n_orb if direct else 1
    points, weight, number = call(
        functools.partial(points_kernel, count, others),
        (
            shape((8, LANES) if direct else (n_orb, ROWS, LANES), F32),
            shape((1, LANES), F32),
            shape((1, LANES), jnp.int32),
        ),
        [SM] + [VM] * (others + 3) + [ANY],
        (VM, VM, VM),
    )(role, record, *records, tiled, disp, token_0)
    if direct:
        points = [points] + [lax.ppermute(points, "orb", pairs(n_orb, s)) for s in range(1, n_orb)]
    else:
        points = [lax.all_to_all(points, "orb", split_axis=0, concat_axis=0, tiled=True)]

    width = -(-local // LANES) * LANES
    coeff = jnp.pad(coefficients, ((0, 0), (0, width - local))) if width > local else coefficients
    derived, *prepared = call(
        functools.partial(prepare_kernel, middle),
        (shape((plane, 5 * width), BF16),)
        + (pltpu.HBM((depth, electrons), BF16),) * len(middle),
        [HBM, HBM, HBM, ANY],
        (VM,) + (ANY,) * len(middle),
        scratch=[
            pltpu.VMEM((plane, width), BF16),
            pltpu.VMEM(wavevectors.shape, F32),
            pltpu.VMEM((len(middle), depth, electrons), F32),
            pltpu.VMEM((len(middle), depth, electrons), BF16),
            pltpu.SemaphoreType.DMA((2,)),
            pltpu.SemaphoreType.DMA((len(middle),)),
            pltpu.SemaphoreType.DMA((len(middle),)),
        ],
        flops=8 * plane * width,
        moved=3 * electrons * electrons + 10 * plane * width,
        vmem=12,
    )(*in_hbm(coeff, wavevectors, inverse), weight)
    for chunk, ready in zip(middle, prepared):
        own[chunk] = ready

    arrays = list(own)
    if n_grp == 4:
        send_x = lambda block: lax.ppermute(block, "grp", pairs(n_grp, 1))
        send_y = lambda block: lax.ppermute(block, "grp", pairs(n_grp, 2))

        def relay(mine, got, first):
            return call(
                relay_kernel,
                (kept, kept, token),
                [SM] + [ANY] * (4 + len(first)),
                (ANY, ANY, VM),
                scratch=[
                    pltpu.VMEM((4, depth // 2, electrons), BF16),
                    pltpu.SemaphoreType.DMA((4,)),
                    pltpu.SemaphoreType.DMA((4,)),
                ],
                aliases={3: 0, 4: 1},
                vmem=2,
            )(apart, *in_hbm(*mine), *got, *first)

        x1, y1 = send_x(own[0]), send_y(own[3])
        y1, x1, token_1 = relay((own[1], own[2]), (y1, x1), (derived, *points))
        x2, y2 = send_x(y1), send_y(x1)
    else:
        token_1 = token_2 = jnp.zeros((8, LANES), F32)
        plan = [tuple((chunk, chunk) for chunk in range(chunks))]
        for step in range(1, n_grp):
            plan.append(tuple((chunk, len(arrays) + chunk) for chunk in range(chunks)))
            arrays += [lax.ppermute(block, "grp", pairs(n_grp, step)) for block in own]
        settled = len(arrays)

    height = 11 * count
    spread = few and DIRECT_VALUES
    targets = n_orb if spread else 1
    block = n_orb if few else math.gcd(n_orb, 8)
    whole = lambda array: pl.BlockSpec(array.shape, lambda i: (0,) * array.ndim)
    if direct:
        point_specs = [whole(p) for p in points]
    else:
        point_specs = [pl.BlockSpec((block, ROWS, LANES), lambda i: (i, 0, 0))]
    if spread:
        out_shapes = (shape((height, width), BF16),) * n_orb
        out_specs = tuple(whole(o) for o in out_shapes)
    else:
        out_shapes = (shape((n_orb, height, width), BF16),)
        out_specs = (pl.BlockSpec((block, height, width), lambda i: (i, 0, 0)),)
    values = pl.pallas_call(
        functools.partial(evaluate_kernel, count, sources, targets),
        grid=(n_orb // block,),
        out_shape=out_shapes,
        in_specs=point_specs + [whole(wavevectors), whole(derived), ANY],
        out_specs=out_specs,
        scratch_shapes=[
            pltpu.VMEM((block * 3 * count, plane), BF16),
            pltpu.VMEM((block * 2 * count, plane), BF16),
            pltpu.VMEM((block, 8, LANES), F32),
            pltpu.VMEM((3, 6 * count, LANES), F32),
        ],
        compiler_params=pltpu.CompilerParams(vmem_limit_bytes=8 * MIB),
        cost_estimate=pl.CostEstimate(
            flops=2 * n_orb * count * plane * width * 11,
            bytes_accessed=12 * plane * width,
            transcendentals=0,
        ),
    )(*points, wavevectors, derived, token_1)
    computed = values[0]
    if spread:
        values = [values[0]] + [
            lax.ppermute(values[s], "orb", pairs(n_orb, s)) for s in range(1, n_orb)
        ]
    else:
        values = values[0][:, :, :local]
        values = lax.all_to_all(values, "orb", split_axis=0, concat_axis=0, tiled=True)
        if width > local:
            values = values.transpose(1, 0, 2).reshape(1, height, electrons)
        values = [values]

    if n_grp == 4:
        near = call(
            near_kernel,
            (kept, kept),
            [HBM, HBM, ANY],
            (VM, VM),
            scratch=[pltpu.SemaphoreType.DMA((2,))],
            vmem=3,
        )(*in_hbm(own[2], own[1]), computed)
        y2, x2, token_2 = call(
            near_relay_kernel,
            (kept, kept, token),
            [SM, VM, VM, ANY, ANY],
            (ANY, ANY, VM),
            scratch=[pltpu.SemaphoreType.DMA((2,))],
            aliases={3: 0, 4: 1},
            vmem=3,
        )(apart, *near, y2, x2)
        x3, y3 = send_x(y2), send_y(x2)
        arrays = own + [x1, x2, y1, y2, x3, y3]
        a1, a2, b1, b2, a3, b3 = range(chunks, chunks + 6)
        first, second, third, fourth = range(chunks)
        plan = [
            tuple((chunk, chunk) for chunk in range(chunks)),
            ((first, a1), (second, a2), (third, a3), (fourth, b3)),
            ((fourth, b1), (third, b2), (first, a3), (second, b3)),
            ((fourth, a2), (first, b2), (third, a3), (second, b3)),
        ]
        settled = chunks + 4

    columns = call(
        functools.partial(columns_kernel, count),
        shape((electrons, LANES), BF16),
        [HBM, VM, ANY],
        VM,
        scratch=[
            pltpu.VMEM((chunks, depth, electrons), F32),
            pltpu.SemaphoreType.DMA((chunks,)),
        ],
        flops=2 * electrons * electrons * LANES,
        moved=4 * electrons * electrons,
        vmem=8,
    )(*in_hbm(inverse), tiled, token_2)

    here = lax.axis_index("orb").astype(jnp.int32).reshape(1)
    early = 2
    work = 2 * electrons * 2 * count
    drift, laplacian, later, early_columns, products, total, held = call(
        functools.partial(middle_kernel, count, targets, plan),
        (
            shape((3, 1, count), F32),
            shape((1, 1, count), F32),
            shape((6 * count, electrons), BF16),
            shape((early, depth, LANES), BF16),
            shape((6 * count, LANES), F32),
            shape((2 * count, electrons), F32),
            shape((early, depth, electrons), F32),
        ),
        [SM, SM, VM, HBM] + [VM] * (targets + 1) + [ANY] * settled,
        (VM,) * 7,
        scratch=[
            pltpu.VMEM((5 * count, electrons), BF16),
            pltpu.VMEM((early, depth, electrons), BF16),
            pltpu.SemaphoreType.DMA((early,)),
            pltpu.SemaphoreType.DMA((early,)),
        ],
        flops=early * depth * work,
        moved=8 * early * depth * electrons + 44 * count * electrons,
        vmem=10,
    )(here, role, number, *in_hbm(inverse), *values, columns, *in_hbm(*own), *arrays[chunks:settled])

    updated, drift, laplacian, new_weight = call(
        functools.partial(finish_kernel, count, plan),
        (
            shape((electrons, electrons), F32),
            shape((6, 1, count), F32),
            shape((2, 1, count), F32),
            shape((1, LANES), F32),
        ),
        [SM] + [VM] * 9 + [HBM] + [ANY] * len(arrays),
        (HBM, VM, VM, VM),
        scratch=[
            pltpu.VMEM((chunks, depth, electrons), BF16),
            pltpu.VMEM((chunks, depth, electrons), F32),
            pltpu.SemaphoreType.DMA((chunks,)),
            pltpu.SemaphoreType.DMA((chunks,)),
            pltpu.SemaphoreType.DMA((chunks,)),
        ],
        flops=2 * electrons * work,
        moved=6 * electrons * electrons,
        vmem=12,
    )(
        role,
        number,
        later,
        weight,
        drift,
        laplacian,
        early_columns,
        products,
        total,
        held,
        *in_hbm(inverse, *own),
        *arrays[chunks:],
    )

    return updated[None], drift.reshape(2, 1, 3, count), laplacian, new_weight[0, :1]


def solution(mesh):
    split = ("grp", "orb")
    return jax.shard_map(
        functools.partial(per_device, mesh.shape["grp"], mesh.shape["orb"]),
        mesh=mesh,
        in_specs=(
            P(),
            P(None, "orb"),
            P(split, None, None),
            P(split, None, None),
            P(None, split, None, None),
            P(None, split, None),
            P("orb"),
            P(split),
            P(split),
        ),
        out_specs=(
            P(split, None, None),
            P(None, split, None, None),
            P(None, split, None),
            P(split),
        ),
        check_vma=False,
    )
```

```python
import functools
import math

import jax
import jax.numpy as jnp
from jax import lax
from jax.experimental import pallas as pl
from jax.experimental.pallas import tpu as pltpu
from jax.sharding import PartitionSpec as P

F32 = jnp.float32
BF16 = jnp.bfloat16
LANES = 128
ROWS = 64
DIRECT_POINTS = False
DIRECT_VALUES = False
MIB = 1024 * 1024
precise = lax.Precision.HIGHEST

WHOLE = 1.5 * 2.0**23

SIN_HALF = (4.4428679, -7.30744342, 3.59478808, -0.78437403)
COS_HALF = (1.4142135, -6.97885099, 5.73946117, -1.88356299, 0.31069819)


def dot(a, b, dims=((1,), (0,)), exact=False):
    return lax.dot_general(
        a, b, (dims, ((), ())), precision=precise if exact else None, preferred_element_type=F32
    )


def exact_dot(a, pick, dims=((1,), (0,))):
    high = a.astype(BF16)
    rest = a - high.astype(F32)
    middle = rest.astype(BF16)
    low = (rest - middle.astype(F32)).astype(BF16)
    rows = a.shape[0]
    parts = jnp.concatenate([high, middle, low], 0)
    found = dot(parts, pick, dims)
    return (found[0:rows] + found[rows : 2 * rows]) + found[2 * rows :]


def iota(shape, dim):
    return lax.broadcasted_iota(jnp.int32, shape, dim)


def call(
    kernel, out_shape, in_specs, out_specs, scratch=(), flops=0, moved=0, vmem=4, aliases=None
):
    return pl.pallas_call(
        kernel,
        out_shape=out_shape,
        input_output_aliases=aliases or {},
        in_specs=in_specs,
        out_specs=out_specs,
        scratch_shapes=list(scratch),
        compiler_params=pltpu.CompilerParams(vmem_limit_bytes=vmem * MIB),
        cost_estimate=pl.CostEstimate(flops=flops, bytes_accessed=moved, transcendentals=0),
    )


VM = pl.BlockSpec(memory_space=pltpu.VMEM)
SM = pl.BlockSpec(memory_space=pltpu.SMEM)
ANY = pl.BlockSpec(memory_space=pl.ANY)
HBM = pl.BlockSpec(memory_space=pltpu.HBM)


def shape(dims, dtype):
    return jax.ShapeDtypeStruct(dims, dtype)


def in_hbm(*arrays):
    return tuple(pltpu.with_memory_space_constraint(a, pltpu.HBM) for a in arrays)


def is_power(n):
    return n & (n - 1) == 0


def pairs(n, step):
    if is_power(n):
        return [(i, i ^ step) for i in range(n)]
    return [(i, (i + step) % n) for i in range(n)]


def distance(n, here, there):
    return here ^ there if is_power(n) else lax.rem(here - there + n, n)


def backward(n, step):
    return step if is_power(n) else (n - step) % n


def start_kernel(
    count,
    pos_hbm,
    moved_hbm,
    disp_hbm,
    weight_ref,
    out_ref,
    tiled_ref,
    shift_ref,
    pos_ref,
    moved_ref,
    disp_ref,
    sems,
):
    loads = [
        pltpu.make_async_copy(src, dst, sems.at[i])
        for i, (src, dst) in enumerate(
            (
                (moved_hbm, moved_ref),
                (disp_hbm, disp_ref),
                (pos_hbm, pos_ref),
            )
        )
    ]
    for load in loads:
        load.start()
    electrons = pos_ref.shape[2]
    copies = LANES // count
    loads[0].wait()
    tiled = jnp.concatenate([moved_ref[:, 0, :]] * copies, 1)
    tiled_ref[...] = tiled
    pick = (iota((electrons, LANES), 0) == tiled[0:1, :]).astype(F32).astype(BF16)
    block = iota((8, LANES), 1) // count
    zeros = jnp.zeros((5, LANES), F32)
    loads[1].wait()
    for update in range(2):
        shift = jnp.concatenate([disp_ref[3 * update : 3 * update + 3, 0, :]] * copies, 1)
        shift_ref[update] = jnp.concatenate([shift, zeros], 0)
    loads[2].wait()
    pos = jnp.concatenate([pos_ref[:, 0, :], jnp.zeros((5, electrons), F32)], 0)
    old = exact_dot(pos, pick)
    disp = shift_ref[0]
    points = old + jnp.where(block % 2 == 1, disp, 0.0)
    first = jnp.where(block == 0, disp, 0.0)
    out_ref[...] = pos + exact_dot(first, pick, ((1,), (1,)))
    out_ref[3:6, 0:LANES] = points[0:3]
    out_ref[6:7, 0:LANES] = tiled[0:1, :].astype(F32)
    out_ref[7:8, 0:LANES] = jnp.full((1, LANES), weight_ref[0], F32)


def rows_of(ref, chunk, depth):
    return ref.at[0, pl.ds(chunk * depth, depth)]


def round_kernel(wanted, inverse_hbm, after_ref, *refs):
    outs = refs[: len(wanted)]
    staged, rounded, in_sem, out_sem = refs[len(wanted) :]
    depth = staged.shape[1]
    loads, stores = [], []
    for slot, chunk in enumerate(wanted):
        load = pltpu.make_async_copy(
            rows_of(inverse_hbm, chunk, depth), staged.at[slot], in_sem.at[slot]
        )
        load.start()
        loads.append(load)
    for slot, out in enumerate(outs):
        loads[slot].wait()
        rounded[slot] = staged[slot].astype(BF16)
        store = pltpu.make_async_copy(rounded.at[slot], out, out_sem.at[slot])
        store.start()
        stores.append(store)
    for store in stores:
        store.wait()


def gate_kernel(*refs):
    token_ref = refs[-1]
    token_ref[...] = jnp.zeros(token_ref.shape, F32)


def relay_kernel(flag_ref, own_a, own_b, got_a, got_b, *refs):
    out_a, out_b, token_ref, staged, in_sem, out_sem = refs[-6:]
    pieces, depth, _ = staged.shape

    @pl.when(flag_ref[0] == 0)
    def _():
        loads, stores = [], []
        for piece in range(pieces):
            own, out = (own_a, out_a) if piece < pieces // 2 else (own_b, out_b)
            rows = pl.ds(piece % (pieces // 2) * depth, depth)
            loads.append(
                pltpu.make_async_copy(own.at[rows], staged.at[piece], in_sem.at[piece])
            )
            stores.append(
                pltpu.make_async_copy(staged.at[piece], out.at[rows], out_sem.at[piece])
            )
        for load in loads:
            load.start()
        for load, store in zip(loads, stores):
            load.wait()
            store.start()
        for store in stores:
            store.wait()

    token_ref[...] = jnp.zeros(token_ref.shape, F32)


def near_kernel(own_a, own_b, after_ref, near_a, near_b, sems):
    copies = [
        pltpu.make_async_copy(own_a, near_a, sems.at[0]),
        pltpu.make_async_copy(own_b, near_b, sems.at[1]),
    ]
    for copy in copies:
        copy.start()
    for copy in copies:
        copy.wait()


def near_relay_kernel(flag_ref, own_a, own_b, got_a, got_b, out_a, out_b, token_ref, sems):
    @pl.when(flag_ref[0] == 0)
    def _():
        copies = [
            pltpu.make_async_copy(own_a, out_a, sems.at[0]),
            pltpu.make_async_copy(own_b, out_b, sems.at[1]),
        ]
        for copy in copies:
            copy.start()
        for copy in copies:
            copy.wait()

    token_ref[...] = jnp.zeros(token_ref.shape, F32)


def points_kernel(count, others, role_ref, *refs):
    own_ref = refs[0]
    received = refs[1 : 1 + others]
    moved_ref, disp_ref, after_ref, points_ref, weight_ref, number_ref = refs[1 + others :]
    role = role_ref[0]
    parent = own_ref[...]
    for step in range(others):
        parent = jnp.where(role == step + 1, received[step][...], parent)
    electrons = parent.shape[1]
    pick = (iota((electrons, LANES), 0) == moved_ref[1:2, :]).astype(F32).astype(BF16)
    block = iota((8, LANES), 1) // count
    old = exact_dot(parent, pick)
    later = old + jnp.where(block % 2 == 1, disp_ref[1], 0.0)
    zeros = jnp.zeros((5, LANES), F32)
    mine = jnp.concatenate([own_ref[3:6, 0:LANES], zeros], 0)
    theirs = jnp.concatenate([parent[3:6, 0:LANES], zeros], 0)
    points = jnp.where(block < 2, mine, jnp.where(block < 4, theirs, later))
    if len(points_ref.shape) == 2:
        points_ref[...] = points
    else:
        points = jnp.concatenate([points, jnp.zeros((ROWS - 8, LANES), F32)], 0)
        points_ref[...] = jnp.broadcast_to(points[None], points_ref.shape)
    weight_ref[...] = parent[7:8, 0:LANES]
    before = parent[6:7, 0:LANES].astype(jnp.int32)
    number_ref[...] = jnp.where(
        block[0:1] == 0, before, jnp.where(block[0:1] == 1, moved_ref[1:2, :], -1)
    )


def derive(coeff_ref, wave_ref, out_ref):
    waves = wave_ref.shape[1]
    width = coeff_ref.shape[1]
    wave = jnp.transpose(jnp.concatenate([wave_ref[...], jnp.zeros((5, waves), F32)], 0))
    out_ref[:, 0:width] = coeff_ref[...]
    cos_part = coeff_ref[0:waves].astype(F32)
    sin_part = coeff_ref[waves:].astype(F32)
    squared = None
    for a in range(3):
        scale = wave[:, a : a + 1]
        where = slice((a + 1) * width, (a + 2) * width)
        out_ref[0:waves, where] = (scale * sin_part).astype(BF16)
        out_ref[waves:, where] = (-scale * cos_part).astype(BF16)
        squared = scale * scale if a == 0 else squared + scale * scale
    where = slice(4 * width, 5 * width)
    out_ref[0:waves, where] = (-squared * cos_part).astype(BF16)
    out_ref[waves:, where] = (-squared * sin_part).astype(BF16)


def prepare_kernel(wanted, coeff_hbm, wave_hbm, inverse_hbm, after_ref, table_ref, *refs):
    outs = refs[: len(wanted)]
    coeff_ref, wave_ref, staged, rounded, small_sem, in_sem, out_sem = refs[len(wanted) :]
    depth = staged.shape[1]
    wave_load = pltpu.make_async_copy(wave_hbm, wave_ref, small_sem.at[0])
    coeff_load = pltpu.make_async_copy(coeff_hbm, coeff_ref, small_sem.at[1])
    wave_load.start()
    coeff_load.start()
    loads, stores = [], []
    for slot, chunk in enumerate(wanted):
        load = pltpu.make_async_copy(
            rows_of(inverse_hbm, chunk, depth), staged.at[slot], in_sem.at[slot]
        )
        load.start()
        loads.append(load)
    for slot, out in enumerate(outs):
        loads[slot].wait()
        rounded[slot] = staged[slot].astype(BF16)
        store = pltpu.make_async_copy(rounded.at[slot], out, out_sem.at[slot])
        store.start()
        stores.append(store)
    wave_load.wait()
    coeff_load.wait()
    derive(coeff_ref, wave_ref, table_ref)
    for store in stores:
        store.wait()


def horner(coefs, u):
    value = coefs[-1] * u + coefs[-2]
    for c in reversed(coefs[:-2]):
        value = value * u + c
    return value


def evaluate_kernel(count, sources, targets, *refs):
    points = refs[:sources]
    wave_ref, table_ref = refs[sources : sources + 2]
    outs = refs[sources + 3 : -4]
    diff, new, gathered, spread = refs[-4:]
    walkers = gathered.shape[0]
    for w in range(walkers):
        gathered[w] = points[w][...] if sources > 1 else points[0][w, 0:8]
    waves = wave_ref.shape[1]
    width = table_ref.shape[1] // 5
    step = math.gcd(waves, LANES)

    def one(w, carry):
        column = jnp.transpose(gathered[w])
        for a in range(3):
            spread[a] = jnp.broadcast_to(column[0 : 6 * count, a : a + 1], (6 * count, step))
        row_d = pl.multiple_of(w * (3 * count), count)
        row_n = pl.multiple_of(w * (2 * count), count)
        for at in range(0, waves, step):
            ks = [wave_ref[a : a + 1, at : at + step] * (0.5 / math.pi) for a in range(3)]
            for pair, diff_at, new_at in ((0, 2, 1), (1, 0, None), (2, 1, 0)):
                rows = slice(2 * pair * count, 2 * (pair + 1) * count)
                turn = spread[0, rows] * ks[0] + spread[1, rows] * ks[1] + spread[2, rows] * ks[2]
                r = turn - ((turn + WHOLE) - WHOLE)
                u = r * r
                s = r * horner(SIN_HALF, u)
                c = horner(COS_HALF, u)
                for value, base in ((1.0 - s * s, 0), (s * c, waves)):
                    where = slice(base + at, base + at + step)
                    kept = value.astype(BF16)
                    wide = kept.astype(F32)
                    change = (wide[count:] - wide[:count]).astype(BF16)
                    diff[pl.ds(row_d + diff_at * count, count), where] = change
                    if new_at is not None:
                        new[pl.ds(row_n + new_at * count, count), where] = kept[count:]
        return carry

    lax.fori_loop(0, walkers, one, 0)
    change = dot(diff[...], table_ref[:, 0:width]).astype(BF16)
    rest = dot(new[...], table_ref[:, width:]).astype(BF16)
    for w in range(walkers):
        out_ref = outs[w] if targets > 1 else outs[0].at[w]
        at = w * 3 * count
        out_ref[0 : 2 * count] = change[at : at + 2 * count]
        out_ref[6 * count : 7 * count] = change[at + 2 * count : at + 3 * count]
        for half, base in ((0, 2 * count), (1, 7 * count)):
            row = (2 * w + half) * count
            for a in range(4):
                out_ref[base + a * count : base + (a + 1) * count] = rest[
                    row : row + count, a * width : (a + 1) * width
                ]


def pair_inverse(a, b, d):
    det = a * d - b * b
    scale = 1.0 / det
    return d * scale, -b * scale, a * scale, det


def sweep(matrix):
    size = matrix.shape[0]
    log = jnp.zeros((1, 1), F32)
    row = iota((size, size), 0)
    lane = iota((size, size), 1)
    place = iota((1, size), 1)
    for k in range(0, size, 4):
        columns = [jnp.broadcast_to(matrix[:, k + j : k + j + 1], (size, size)) for j in range(4)]
        lines = [matrix[k + i : k + i + 1, :] for i in range(4)]
        at = lambda i, j: columns[j][k + i : k + i + 1, :]
        a00, a01, a11, det_a = pair_inverse(at(0, 0), at(0, 1), at(1, 1))
        b00, b01, b10, b11 = at(0, 2), at(0, 3), at(1, 2), at(1, 3)
        t00, t01 = a00 * b00 + a01 * b10, a00 * b01 + a01 * b11
        t10, t11 = a01 * b00 + a11 * b10, a01 * b01 + a11 * b11
        d00 = at(2, 2) - (b00 * t00 + b10 * t10)
        d01 = at(2, 3) - (b00 * t01 + b10 * t11)
        d11 = at(3, 3) - (b01 * t01 + b11 * t11)
        s00, s01, s11, det_s = pair_inverse(d00, d01, d11)
        u00, u01 = -(t00 * s00 + t01 * s01), -(t00 * s01 + t01 * s11)
        u10, u11 = -(t10 * s00 + t11 * s01), -(t10 * s01 + t11 * s11)
        q00, q01 = a00 - (u00 * t00 + u01 * t01), a01 - (u00 * t10 + u01 * t11)
        q11 = a11 - (u10 * t10 + u11 * t11)
        pivot = (
            (q00, q01, u00, u01),
            (q01, q11, u10, u11),
            (u00, u10, s00, s01),
            (u01, u11, s01, s11),
        )
        reduced = matrix
        scaled, edges = [], []
        for i in range(4):
            line = pivot[i][0] * lines[0] + pivot[i][1] * lines[1]
            line = line + (pivot[i][2] * lines[2] + pivot[i][3] * lines[3])
            reduced = reduced - columns[i] * line
            for j in range(4):
                line = jnp.where(place == k + j, -pivot[i][j], line)
            scaled.append(line)
            edge = pivot[i][0] * columns[0] + pivot[i][1] * columns[1]
            edges.append(edge + (pivot[i][2] * columns[2] + pivot[i][3] * columns[3]))
        matrix = reduced
        for i in range(4):
            matrix = jnp.where(lane == k + i, edges[i], matrix)
        for i in range(4):
            matrix = jnp.where(row == k + i, scaled[i], matrix)
        log = log + (jnp.log(det_a[:, 0:1]) + jnp.log(det_s[:, 0:1]))
    return -matrix, log


def ratio_of(products, size):
    eye = jnp.where(iota((size, size), 0) == iota((size, size), 1), 1.0, 0.0)
    ratio = products[0:size, 0:size] + eye
    inverse, log = sweep(dot(ratio, ratio, ((0,), (0,)), exact=True))
    return ratio, inverse, 0.5 * log


def moved_sums(products, ratio, inverse, count):
    size = ratio.shape[0]
    turned = dot(ratio, inverse, exact=True)[size - count :]
    tile = jnp.concatenate([turned] * 4, 0)
    part = products[size : size + 4 * count, 0:size] * tile
    return dot(jnp.ones((8, size), F32), part, ((1,), (1,)), exact=True)[0:1]


def columns_kernel(count, inverse_hbm, moved_ref, after_ref, out_ref, staged, sem):
    chunks, depth, electrons = staged.shape
    loads = []
    for chunk in range(chunks):
        load = pltpu.make_async_copy(
            rows_of(inverse_hbm, chunk, depth), staged.at[chunk], sem.at[chunk]
        )
        load.start()
        loads.append(load)
    block = iota((1, LANES), 1) // count
    number = jnp.where(block == 0, moved_ref[0:1, :], -1)
    pick = (iota((electrons, LANES), 0) == number).astype(F32).astype(BF16)
    for chunk in range(chunks):
        loads[chunk].wait()
        found = dot(staged[chunk].astype(BF16), pick)
        out_ref[chunk * depth : (chunk + 1) * depth] = found.astype(BF16)


def pick_from(number_ref, electrons):
    return (iota((electrons, LANES), 0) == number_ref[...]).astype(F32).astype(BF16)


def chunk_at(plan, role, slot):
    chunk = jnp.int32(plan[0][slot][0])
    for which in range(1, len(plan)):
        chunk = jnp.where(role == which, plan[which][slot][0], chunk)
    return chunk


def load_slots(plan, slots, role, inputs, parent, sem, first=0):
    for slot in slots:
        for which in range(first, len(plan)):
            load = pltpu.make_async_copy(
                inputs[plan[which][slot][1]], parent.at[slot], sem.at[slot]
            )
            pl.when(role == which)(load.start)


def wait_slots(slots, inputs, parent, sem):
    for slot in slots:
        pltpu.make_async_copy(inputs[0], parent.at[slot], sem.at[slot]).wait()


def middle_kernel(count, sources, plan, me_ref, role_ref, number_ref, inverse_hbm, *refs):
    values = refs[:sources]
    own_columns = refs[sources]
    inputs = refs[sources + 1 : -13]
    drift_ref, lap_ref, later_ref, columns_ref, products_ref, total_ref = refs[-13:-7]
    held_ref, near_ref, vals, parent, sem, own_sem, near_sem = refs[-7:]
    slots, depth, electrons = parent.shape
    role = role_ref[0]
    load_slots(plan, range(slots), role, inputs, parent, sem)
    wide = [
        pltpu.make_async_copy(
            rows_of(inverse_hbm, plan[0][slot][0], depth), held_ref.at[slot], own_sem.at[slot]
        )
        for slot in range(slots)
    ]
    wide += [
        pltpu.make_async_copy(
            inputs[plan[0][slots + slot][1]], near_ref.at[slot], near_sem.at[slot]
        )
        for slot in range(near_ref.shape[0])
    ]
    for load in wide:
        pl.when(role == 0)(load.start)
    rows = later_ref.shape[0]
    if sources > 1:
        width = values[0].shape[1]
        for step in range(sources):
            at = pl.multiple_of((me_ref[0] ^ step) * width, width)
            later_ref[:, pl.ds(at, width)] = values[step][0:rows]
            vals[:, pl.ds(at, width)] = values[step][rows:]
    else:
        pieces, _, width = values[0].shape
        for piece in range(pieces):
            where = slice(piece * width, (piece + 1) * width)
            later_ref[:, where] = values[0][piece, 0:rows]
            vals[:, where] = values[0][piece, rows:]
    pick = pick_from(number_ref, electrons)
    wait_slots(range(slots), inputs, parent, sem)
    own = dot(vals[...], own_columns[...])
    products, total = None, None
    for slot in range(slots):
        columns = dot(parent[slot], pick).astype(BF16)
        columns_ref[slot] = columns
        at = pl.multiple_of(chunk_at(plan, role, slot) * depth, depth)
        part = later_ref[:, pl.ds(at, depth)]
        product = dot(part, columns)
        more = dot(part[0 : 2 * count], parent[slot])
        products = product if slot == 0 else products + product
        total = more if slot == 0 else total + more
    products_ref[...] = products
    total_ref[...] = total

    @pl.when(role == 0)
    def _():
        for load in wide:
            load.wait()

    @pl.when(role != 0)
    def _():
        for slot in range(slots):
            held_ref[slot] = parent[slot].astype(F32)

    ratio, inverse, _ = ratio_of(own, count)
    sums = moved_sums(own, ratio, inverse, count)
    for a in range(3):
        drift_ref[a] = sums[:, a * count : (a + 1) * count]
    lap_ref[0] = sums[:, 3 * count : 4 * count]


def finish_kernel(
    count,
    plan,
    role_ref,
    number_ref,
    later_ref,
    weight_ref,
    drift_in,
    lap_in,
    early_ref,
    products_ref,
    total_ref,
    held_ref,
    near_ref,
    inverse_hbm,
    *refs,
):
    inputs = refs[:-9]
    out_ref, drift_ref, lap_ref, out_weight_ref = refs[-9:-5]
    parent, staged, in_sem, own_sem, out_sem = refs[-5:]
    chunks, depth, electrons = parent.shape
    done = early_ref.shape[0]
    late = range(done, chunks)
    size = 2 * count
    role = role_ref[0]
    own = [
        pltpu.make_async_copy(
            rows_of(inverse_hbm, plan[0][slot][0], depth), staged.at[slot], own_sem.at[slot]
        )
        for slot in range(chunks)
    ]
    load_slots(plan, late, role, inputs, parent, in_sem, 1)
    for slot in late:
        close = pltpu.make_async_copy(
            near_ref.at[slot - done], parent.at[slot], in_sem.at[slot]
        )
        pl.when(role == 0)(close.start)
        pl.when(role == 0)(own[slot].start)
    pick = pick_from(number_ref, electrons)
    wait_slots(late, inputs, parent, in_sem)
    columns = [early_ref[slot] for slot in range(done)]
    products = products_ref[...]
    rows = []
    for slot in late:
        columns.append(dot(parent[slot], pick).astype(BF16))
        at = pl.multiple_of(chunk_at(plan, role, slot) * depth, depth)
        rows.append(later_ref[:, pl.ds(at, depth)])
        products = products + dot(rows[-1], columns[-1])
    ratio, inverse, log = ratio_of(products, size)
    total = total_ref[...]
    for slot, part in zip(late, rows):
        total = total + dot(part[0:size], parent[slot])
    small = dot(inverse, ratio, ((1,), (1,)), exact=True)
    high = small.astype(BF16)
    halves = jnp.concatenate([high, (small - high.astype(F32)).astype(BF16)], 1)
    rounded = total.astype(BF16)
    solved = dot(halves, jnp.concatenate([rounded, rounded], 0)).astype(BF16)
    solved = jnp.concatenate([solved, jnp.zeros((LANES - size, electrons), BF16)], 0)
    copies = []
    for slot in range(chunks):
        at = pl.multiple_of(chunk_at(plan, role, slot) * depth, depth)
        copies.append(
            pltpu.make_async_copy(
                staged.at[slot], out_ref.at[pl.ds(at, depth)], out_sem.at[slot]
            )
        )

    def write(slots, before):
        for slot in slots:
            staged[slot] = before(slot) - dot(columns[slot], solved)
            copies[slot].start()

    def kept(slot):
        own[slot].wait()
        return staged[slot]

    write(range(done), lambda slot: held_ref[slot])
    pl.when(role == 0)(lambda: write(late, kept))
    pl.when(role != 0)(lambda: write(late, lambda slot: parent[slot].astype(F32)))
    sums = moved_sums(products, ratio, inverse, count)
    drift_ref[0:3] = drift_in[...]
    lap_ref[0:1] = lap_in[...]
    for a in range(3):
        drift_ref[3 + a] = sums[:, a * count : (a + 1) * count]
    lap_ref[1] = sums[:, 3 * count : 4 * count]
    out_weight_ref[...] = weight_ref[...] + log
    for copy in copies:
        copy.wait()


def per_device(
    n_grp,
    n_orb,
    wavevectors,
    coefficients,
    inverse,
    positions,
    displacements,
    moved,
    donor,
    take,
    log_weight,
):
    electrons = inverse.shape[1]
    count = moved.shape[2]
    plane = coefficients.shape[0]
    local = coefficients.shape[1]
    others = n_grp - 1
    chunks = 4

    apart = distance(n_grp, lax.axis_index("grp"), donor[0])
    role = jnp.where(take[0] == 1, apart, 0).astype(jnp.int32).reshape(1)
    apart = apart.astype(jnp.int32).reshape(1)

    record, tiled, disp = call(
        functools.partial(start_kernel, count),
        (
            shape((8, electrons), F32),
            shape((2, LANES), jnp.int32),
            shape((2, 8, LANES), F32),
        ),
        [HBM, HBM, HBM, SM],
        (VM, VM, VM),
        scratch=[
            pltpu.VMEM((3, 1, electrons), F32),
            pltpu.VMEM((2, 1, count), jnp.int32),
            pltpu.VMEM((6, 1, count), F32),
            pltpu.SemaphoreType.DMA((3,)),
        ],
    )(
        *in_hbm(
            positions.reshape(3, 1, electrons),
            moved,
            displacements.reshape(6, 1, count),
        ),
        log_weight,
    )
    records = [lax.ppermute(record, "grp", pairs(n_grp, s)) for s in range(1, n_grp)]

    depth = electrons // chunks
    kept = shape((depth, electrons), BF16)
    token = shape((8, LANES), F32)
    own = [None] * chunks
    ends = (0, chunks - 1)
    middle = tuple(range(1, chunks - 1))
    own[0], own[-1] = call(
        functools.partial(round_kernel, ends),
        (kept,) * 2,
        [HBM, ANY],
        (ANY,) * 2,
        scratch=[
            pltpu.VMEM((2, depth, electrons), F32),
            pltpu.VMEM((2, depth, electrons), BF16),
            pltpu.SemaphoreType.DMA((2,)),
            pltpu.SemaphoreType.DMA((2,)),
        ],
        moved=3 * electrons * electrons,
        vmem=6,
    )(*in_hbm(inverse), record)
    own[0], own[-1], token_0 = call(
        gate_kernel,
        (kept, kept, token),
        [ANY] * (2 + others),
        (ANY, ANY, VM),
        aliases={0: 0, 1: 1},
        vmem=1,
    )(own[0], own[-1], *records)

    few = is_power(n_orb) and local % LANES == 0
    direct = few and DIRECT_POINTS
    sources = n_orb if direct else 1
    points, weight, number = call(
        functools.partial(points_kernel, count, others),
        (
            shape((8, LANES) if direct else (n_orb, ROWS, LANES), F32),
            shape((1, LANES), F32),
            shape((1, LANES), jnp.int32),
        ),
        [SM] + [VM] * (others + 3) + [ANY],
        (VM, VM, VM),
    )(role, record, *records, tiled, disp, token_0)
    if direct:
        points = [points] + [lax.ppermute(points, "orb", pairs(n_orb, s)) for s in range(1, n_orb)]
    else:
        points = [lax.all_to_all(points, "orb", split_axis=0, concat_axis=0, tiled=True)]

    width = -(-local // LANES) * LANES
    coeff = jnp.pad(coefficients, ((0, 0), (0, width - local))) if width > local else coefficients
    derived, *prepared = call(
        functools.partial(prepare_kernel, middle),
        (shape((plane, 5 * width), BF16),)
        + (pltpu.HBM((depth, electrons), BF16),) * len(middle),
        [HBM, HBM, HBM, ANY],
        (VM,) + (ANY,) * len(middle),
        scratch=[
            pltpu.VMEM((plane, width), BF16),
            pltpu.VMEM(wavevectors.shape, F32),
            pltpu.VMEM((len(middle), depth, electrons), F32),
            pltpu.VMEM((len(middle), depth, electrons), BF16),
            pltpu.SemaphoreType.DMA((2,)),
            pltpu.SemaphoreType.DMA((len(middle),)),
            pltpu.SemaphoreType.DMA((len(middle),)),
        ],
        flops=8 * plane * width,
        moved=3 * electrons * electrons + 10 * plane * width,
        vmem=12,
    )(*in_hbm(coeff, wavevectors, inverse), weight)
    for chunk, ready in zip(middle, prepared):
        own[chunk] = ready

    arrays = list(own)
    if n_grp == 4:
        send_x = lambda block: lax.ppermute(block, "grp", pairs(n_grp, 1))
        send_y = lambda block: lax.ppermute(block, "grp", pairs(n_grp, 2))

        def relay(mine, got, first):
            return call(
                relay_kernel,
                (kept, kept, token),
                [SM] + [ANY] * (4 + len(first)),
                (ANY, ANY, VM),
                scratch=[
                    pltpu.VMEM((4, depth // 2, electrons), BF16),
                    pltpu.SemaphoreType.DMA((4,)),
                    pltpu.SemaphoreType.DMA((4,)),
                ],
                aliases={3: 0, 4: 1},
                vmem=2,
            )(apart, *in_hbm(*mine), *got, *first)

        x1, y1 = send_x(own[0]), send_y(own[3])
        y1, x1, token_1 = relay((own[1], own[2]), (y1, x1), (derived,))
        x2, y2 = send_x(y1), send_y(x1)
    else:
        token_1 = token_2 = jnp.zeros((8, LANES), F32)
        plan = [tuple((chunk, chunk) for chunk in range(chunks))]
        for step in range(1, n_grp):
            plan.append(tuple((chunk, len(arrays) + chunk) for chunk in range(chunks)))
            arrays += [lax.ppermute(block, "grp", pairs(n_grp, step)) for block in own]
        settled = len(arrays)

    height = 11 * count
    spread = few and DIRECT_VALUES
    targets = n_orb if spread else 1
    block = n_orb if few else math.gcd(n_orb, 8)
    whole = lambda array: pl.BlockSpec(array.shape, lambda i: (0,) * array.ndim)
    if direct:
        point_specs = [whole(p) for p in points]
    else:
        point_specs = [pl.BlockSpec((block, ROWS, LANES), lambda i: (i, 0, 0))]
    if spread:
        out_shapes = (shape((height, width), BF16),) * n_orb
        out_specs = tuple(whole(o) for o in out_shapes)
    else:
        out_shapes = (shape((n_orb, height, width), BF16),)
        out_specs = (pl.BlockSpec((block, height, width), lambda i: (i, 0, 0)),)
    values = pl.pallas_call(
        functools.partial(evaluate_kernel, count, sources, targets),
        grid=(n_orb // block,),
        out_shape=out_shapes,
        in_specs=point_specs + [whole(wavevectors), whole(derived), ANY],
        out_specs=out_specs,
        scratch_shapes=[
            pltpu.VMEM((block * 3 * count, plane), BF16),
            pltpu.VMEM((block * 2 * count, plane), BF16),
            pltpu.VMEM((block, 8, LANES), F32),
            pltpu.VMEM((3, 6 * count, LANES), F32),
        ],
        compiler_params=pltpu.CompilerParams(vmem_limit_bytes=8 * MIB),
        cost_estimate=pl.CostEstimate(
            flops=2 * n_orb * count * plane * width * 11,
            bytes_accessed=12 * plane * width,
            transcendentals=0,
        ),
    )(*points, wavevectors, derived, token_1)
    computed = values[0]
    if spread:
        values = [values[0]] + [
            lax.ppermute(values[s], "orb", pairs(n_orb, s)) for s in range(1, n_orb)
        ]
    else:
        values = values[0][:, :, :local]
        values = lax.all_to_all(values, "orb", split_axis=0, concat_axis=0, tiled=True)
        if width > local:
            values = values.transpose(1, 0, 2).reshape(1, height, electrons)
        values = [values]

    if n_grp == 4:
        near = call(
            near_kernel,
            (kept, kept),
            [HBM, HBM, ANY],
            (VM, VM),
            scratch=[pltpu.SemaphoreType.DMA((2,))],
            vmem=3,
        )(*in_hbm(own[2], own[1]), computed)
        y2, x2, token_2 = call(
            near_relay_kernel,
            (kept, kept, token),
            [SM, VM, VM, ANY, ANY],
            (ANY, ANY, VM),
            scratch=[pltpu.SemaphoreType.DMA((2,))],
            aliases={3: 0, 4: 1},
            vmem=3,
        )(apart, *near, y2, x2)
        x3, y3 = send_x(y2), send_y(x2)
        arrays = own + [x1, x2, y1, y2, x3, y3]
        a1, a2, b1, b2, a3, b3 = range(chunks, chunks + 6)
        first, second, third, fourth = range(chunks)
        plan = [
            tuple((chunk, chunk) for chunk in range(chunks)),
            ((first, a1), (second, a2), (third, a3), (fourth, b3)),
            ((fourth, b1), (third, b2), (first, a3), (second, b3)),
            ((fourth, a2), (first, b2), (third, a3), (second, b3)),
        ]
        settled = chunks + 4

    columns = call(
        functools.partial(columns_kernel, count),
        shape((electrons, LANES), BF16),
        [HBM, VM, ANY],
        VM,
        scratch=[
            pltpu.VMEM((chunks, depth, electrons), F32),
            pltpu.SemaphoreType.DMA((chunks,)),
        ],
        flops=2 * electrons * electrons * LANES,
        moved=4 * electrons * electrons,
        vmem=8,
    )(*in_hbm(inverse), tiled, token_2)

    here = lax.axis_index("orb").astype(jnp.int32).reshape(1)
    early = 2
    work = 2 * electrons * 2 * count
    drift, laplacian, later, early_columns, products, total, held, near_own = call(
        functools.partial(middle_kernel, count, targets, plan),
        (
            shape((3, 1, count), F32),
            shape((1, 1, count), F32),
            shape((6 * count, electrons), BF16),
            shape((early, depth, LANES), BF16),
            shape((6 * count, LANES), F32),
            shape((2 * count, electrons), F32),
            shape((early, depth, electrons), F32),
            shape((chunks - early, depth, electrons), BF16),
        ),
        [SM, SM, VM, HBM] + [VM] * (targets + 1) + [ANY] * settled,
        (VM,) * 8,
        scratch=[
            pltpu.VMEM((5 * count, electrons), BF16),
            pltpu.VMEM((early, depth, electrons), BF16),
            pltpu.SemaphoreType.DMA((early,)),
            pltpu.SemaphoreType.DMA((early,)),
            pltpu.SemaphoreType.DMA((chunks - early,)),
        ],
        flops=early * depth * work,
        moved=8 * early * depth * electrons + 44 * count * electrons,
        vmem=10,
    )(here, role, number, *in_hbm(inverse), *values, columns, *in_hbm(*own), *arrays[chunks:settled])

    updated, drift, laplacian, new_weight = call(
        functools.partial(finish_kernel, count, plan),
        (
            shape((electrons, electrons), F32),
            shape((6, 1, count), F32),
            shape((2, 1, count), F32),
            shape((1, LANES), F32),
        ),
        [SM] + [VM] * 10 + [HBM] + [ANY] * len(arrays),
        (HBM, VM, VM, VM),
        scratch=[
            pltpu.VMEM((chunks, depth, electrons), BF16),
            pltpu.VMEM((chunks, depth, electrons), F32),
            pltpu.SemaphoreType.DMA((chunks,)),
            pltpu.SemaphoreType.DMA((chunks,)),
            pltpu.SemaphoreType.DMA((chunks,)),
        ],
        flops=2 * electrons * work,
        moved=6 * electrons * electrons,
        vmem=12,
    )(
        role,
        number,
        later,
        weight,
        drift,
        laplacian,
        early_columns,
        products,
        total,
        held,
        near_own,
        *in_hbm(inverse, *own),
        *arrays[chunks:],
    )

    return updated[None], drift.reshape(2, 1, 3, count), laplacian, new_weight[0, :1]


def solution(mesh):
    split = ("grp", "orb")
    return jax.shard_map(
        functools.partial(per_device, mesh.shape["grp"], mesh.shape["orb"]),
        mesh=mesh,
        in_specs=(
            P(),
            P(None, "orb"),
            P(split, None, None),
            P(split, None, None),
            P(None, split, None, None),
            P(None, split, None),
            P("orb"),
            P(split),
            P(split),
        ),
        out_specs=(
            P(split, None, None),
            P(None, split, None, None),
            P(None, split, None),
            P(split),
        ),
        check_vma=False,
    )
```
